32 devices in a mesh: mem: 8 (over y, x, core), seq: 4 (over z).
Axes of the slice: x: 2, y: 2, z: 4, core: 2. Of those that a mesh axis runs over, the one named last changes fastest.
Arguments:
- hidden_in: bfloat16 [8, 1024, 768], P('mem', 'seq'), may hold values from -6 to 6
- memory: bfloat16 [4, 768, 768], P(None, 'mem'), may hold values from -6 to 6
- cotangent: bfloat16 [8, 1024, 768], P('mem', 'seq'), may hold values from -6 to 6
- norm_self: bfloat16 [768], P(('mem', 'seq')), may hold values from 0.5 to 1.5
- query_self: bfloat16 [768, 768], P(('mem', 'seq')), may hold values from -0.21875 to 0.21875
- key_self: bfloat16 [768, 768], P(('mem', 'seq')), may hold values from -0.21875 to 0.21875
- value_self: bfloat16 [768, 768], P(('mem', 'seq')), may hold values from -0.21875 to 0.21875
- output_self: bfloat16 [768, 768], P(('mem', 'seq')), may hold values from -0.875 to 0.875
- norm_cross: bfloat16 [768], P(('mem', 'seq')), may hold values from 0.5 to 1.5
- query_cross: bfloat16 [768, 768], P(('mem', 'seq')), may hold values from -0.21875 to 0.21875
- key_cross: bfloat16 [768, 768], P(('mem', 'seq')), may hold values from -0.21875 to 0.21875
- value_cross: bfloat16 [768, 768], P(('mem', 'seq')), may hold values from -0.21875 to 0.21875
- output_cross: bfloat16 [768, 768], P(('mem', 'seq')), may hold values from -0.875 to 0.875
- norm_feed: bfloat16 [768], P(('mem', 'seq')), may hold values from 0.5 to 1.5
- gate_weight: bfloat16 [768, 2048], P(('mem', 'seq')), may hold values from -0.21875 to 0.21875
- up_weight: bfloat16 [768, 2048], P(('mem', 'seq')), may hold values from -0.21875 to 0.21875
- down_weight: bfloat16 [2048, 768], P(('mem', 'seq')), may hold values from -0.125 to 0.125
- block_counts: int32 [8], replicated, may hold values from 1 to 8, 32 in all
- memory_tail: int32 [8], replicated, may hold values from 1 to 96
- row_example: int32 [8], replicated, may hold values from 0 to 7, each once
Outputs:
- layer_out: bfloat16 [8, 1024, 768], P('mem', 'seq')
- hidden_grad: bfloat16 [8, 1024, 768], P('mem', 'seq')
- memory_grad: bfloat16 [4, 768, 768], P('seq', 'mem')
- norm_self_grad: float32 [768], P(('mem', 'seq'))
- query_self_grad: float32 [768, 768], P(('mem', 'seq'))
- key_self_grad: float32 [768, 768], P(('mem', 'seq'))
- value_self_grad: float32 [768, 768], P(('mem', 'seq'))
- output_self_grad: float32 [768, 768], P(('mem', 'seq'))
- norm_cross_grad: float32 [768], P(('mem', 'seq'))
- query_cross_grad: float32 [768, 768], P(('mem', 'seq'))
- key_cross_grad: float32 [768, 768], P(('mem', 'seq'))
- value_cross_grad: float32 [768, 768], P(('mem', 'seq'))
- output_cross_grad: float32 [768, 768], P(('mem', 'seq'))
- norm_feed_grad: float32 [768], P(('mem', 'seq'))
- gate_weight_grad: float32 [768, 2048], P(('mem', 'seq'))
- up_weight_grad: float32 [768, 2048], P(('mem', 'seq'))
- down_weight_grad: float32 [2048, 768], P(('mem', 'seq'))
The draws below stay inside these ranges and needn't reach their ends.
Inputs may be any that keep to these rules, and one draw needn't show every extreme that they name: block_counts sums to 32; the largest equals 8. `row_example`: each example stands in exactly one row.
All inputs are finite; a program needn't handle non-finite values.
Results may differ from the reference program's by a relative error of at most 0.025.
Values may be sent and summed in bfloat16 or wider, within the bound.
No kernel may reach another device: no remote copies, remote signals or barrier semaphores. Data moves between devices by JAX's collectives and lax.ppermute only.
A program may use at most 256 MiB of HBM per device.

```python
import math
import jax
import jax.numpy as jnp
import numpy as np
from jax import lax

D = 768
FF = 2048
HEADS = 12
HEAD_DIM = 64
INNER = 768
BLK = 96
BLK_DEV = 4
TARGET_LEN = 1024
MEM_ROWS = 768
N_MEM = 8


def place_ends(drawn, key, smallest, high):
    index_at = [jax.random.randint(jax.random.fold_in(key, axis), (), 0, length) for axis, length in enumerate(drawn.shape)]
    main_axis = drawn.shape.index(max(drawn.shape))
    neighbour = index_at[:main_axis] + [(index_at[main_axis] + 1) % drawn.shape[main_axis]] + index_at[main_axis + 1:]
    return drawn.at[tuple(index_at)].set(smallest).at[tuple(neighbour)].set(high)


def steps_of(own_key, shape, split, low, high):
    def one(position, parts):
        heights = jax.random.uniform(jax.random.fold_in(jax.random.fold_in(own_key, 6), position), (parts,), jnp.float32, low / len(split), high / len(split))
        return jnp.repeat(jnp.exp(heights), shape[position] // parts).reshape((-1,) + (1,) * (len(shape) - position - 1))

    factor_of = one(*split[0])
    for cut in split[1:]:
        factor_of = factor_of * one(*cut)
    return factor_of


def profile(count, total, bound, lean):
    loads = [(1 << 20) // math.isqrt(rank ** lean) + 1 for rank in range(2, count + 1)]
    surplus, counts = total - bound - (count - 1), [1] * (count - 1)
    while surplus > 0:
        candidates = [i for i in range(count - 1) if counts[i] < bound]
        mass, remaining = sum([loads[i] for i in candidates]), surplus
        for i in candidates:
            extra = min(bound - counts[i], max(1, remaining * loads[i] // mass), surplus)
            counts[i] = counts[i] + extra
            surplus = surplus - extra
    return np.array([bound] + counts)


def ragged_sizes(stream_key, number_of, total, limit, skew):
    if number_of == 2:
        one = jax.random.randint(stream_key, (), max(1, total - limit), min(limit, total - 1) + 1)
        return jnp.stack([one, total - one])
    sizes = jnp.asarray(profile(number_of, total, limit, skew), jnp.int32)
    twos = (number_of - 1) // 2
    source_of, taker = sizes[1:1 + 2 * twos:2], sizes[2:2 + 2 * twos:2]
    slack = jnp.minimum(source_of - 1, limit - taker)
    passed = jax.random.randint(jax.random.fold_in(stream_key, 1), (twos,), 0, 1 << 20) % (slack + 1)
    sizes = sizes.at[1:1 + 2 * twos:2].set(source_of - passed).at[2:2 + 2 * twos:2].set(taker + passed)
    return sizes[jax.random.permutation(jax.random.fold_in(stream_key, 2), number_of)]


def normal_values(rng, dims, width, bound, cuts=(), kind=jnp.bfloat16):
    entries = jax.random.normal(rng, dims, jnp.float32) * width
    if len(cuts) > 0:
        entries = steps_of(rng, dims, cuts, -0.22, 0.18) * entries
    return jnp.clip(entries, min=-bound, max=bound).astype(kind)


def setup_inputs(seed: int = 0) -> dict:
    streams_of = jax.random.split(jax.random.key(seed), 21)
    hidden_in = normal_values(streams_of[0], (N_MEM, TARGET_LEN, D), 1.0, 6.0, ((0, 8), (1, 4)))
    memory = normal_values(streams_of[1], (BLK_DEV, MEM_ROWS, D), 1.0, 6.0, ((1, 8),))
    cotangent = normal_values(streams_of[2], (N_MEM, TARGET_LEN, D), 1.0, 6.0, ((0, 8), (1, 4)))
    norm_self = jnp.clip(1.0 + 0.1 * jax.random.normal(streams_of[3], (D,), jnp.float32), 0.5, 1.5).astype(jnp.bfloat16)
    query_self = normal_values(streams_of[4], (D, INNER), D ** -0.5, 0.21875, ((0, 32),))
    key_self = normal_values(streams_of[5], (D, INNER), D ** -0.5, 0.21875, ((0, 32),))
    value_self = normal_values(streams_of[6], (D, INNER), D ** -0.5, 0.21875, ((0, 32),))
    output_self = normal_values(streams_of[7], (D, INNER), (INNER // 16) ** -0.5, 0.875, ((0, 32),))
    norm_cross = jnp.clip(1.0 + 0.1 * jax.random.normal(streams_of[8], (D,), jnp.float32), 0.5, 1.5).astype(jnp.bfloat16)
    query_cross = normal_values(streams_of[9], (D, INNER), D ** -0.5, 0.21875, ((0, 32),))
    key_cross = normal_values(streams_of[10], (D, INNER), D ** -0.5, 0.21875, ((0, 32),))
    value_cross = normal_values(streams_of[11], (D, INNER), D ** -0.5, 0.21875, ((0, 32),))
    output_cross = normal_values(streams_of[12], (D, INNER), (INNER // 16) ** -0.5, 0.875, ((0, 32),))
    norm_feed = jnp.clip(1.0 + 0.1 * jax.random.normal(streams_of[13], (D,), jnp.float32), 0.5, 1.5).astype(jnp.bfloat16)
    gate_weight = normal_values(streams_of[14], (D, FF), D ** -0.5, 0.21875, ((0, 32),))
    up_weight = normal_values(streams_of[15], (D, FF), D ** -0.5, 0.21875, ((0, 32),))
    down_weight = normal_values(streams_of[16], (FF, D), FF ** -0.5, 0.125, ((0, 32),))
    block_counts = ragged_sizes(streams_of[17], N_MEM, BLK_DEV * N_MEM, N_MEM, 2).astype(jnp.int32)
    memory_tail = place_ends(jax.random.randint(streams_of[18], (N_MEM,), 1, BLK + 1), jax.random.fold_in(streams_of[18], 1), 1, BLK).astype(jnp.int32)
    row_example = jax.random.permutation(streams_of[19], N_MEM).astype(jnp.int32)
    return {"hidden_in": hidden_in, "memory": memory, "cotangent": cotangent, "norm_self": norm_self, "query_self": query_self, "key_self": key_self, "value_self": value_self, "output_self": output_self, "norm_cross": norm_cross, "query_cross": query_cross, "key_cross": key_cross, "value_cross": value_cross, "output_cross": output_cross, "norm_feed": norm_feed, "gate_weight": gate_weight, "up_weight": up_weight, "down_weight": down_weight, "block_counts": block_counts, "memory_tail": memory_tail, "row_example": row_example}


@jax.custom_vjp
def low(v):
    return lax.optimization_barrier(v.astype(jnp.bfloat16)).astype(jnp.float32)

@jax.custom_vjp
def low_back(v):
    return v

def low_keep(v):
    return (low(v), None)

def low_pass(kept, grad):
    return (grad,)

def back_keep(v):
    return (v, None)

def back_low(kept, grad):
    return (low(grad),)
low.defvjp(low_keep, low_pass)
low_back.defvjp(back_keep, back_low)

def round_both(values):
    return low_back(low(values))

def product(left, right):
    return jnp.dot(left, right, precision=lax.Precision.HIGHEST)

def right_product(left, right):
    return jnp.einsum('qi,di->qd', left, right, precision=lax.Precision.HIGHEST)

def rms_norm(hidden, gain):
    return hidden * lax.rsqrt(lax.optimization_barrier(jnp.mean(hidden * hidden, axis=-1, keepdims=True)) + 1e-06) * gain

def gelu_tanh(values):
    return 0.5 * values * (1.0 + jnp.tanh(0.7978845608028654 * (values + 0.044715 * values * values * values)))

def block_tables(block_counts, memory_tail, blocks, block_width):
    ends = jnp.cumsum(block_counts).astype(jnp.int32)
    examples = jnp.arange(block_counts.shape[0], dtype=jnp.int32)
    block_owner = lax.optimization_barrier(jnp.sum((ends[None, :] <= blocks[:, None]).astype(jnp.int32), axis=1)).astype(jnp.int32)
    is_last = jnp.any(ends[None, :] - 1 == blocks[:, None], axis=1)
    tail_size = lax.optimization_barrier(jnp.sum(jnp.where(examples[None, :] == block_owner[:, None], memory_tail[None, :], 0), axis=1)).astype(jnp.int32)
    places = jnp.arange(block_width, dtype=jnp.int32)
    key_live = jnp.logical_or(jnp.logical_not(is_last)[:, None], places[None, :] < tail_size[:, None])
    return (jnp.repeat(block_owner, block_width), key_live.reshape(-1))

def forward(hidden_in, memory, norm_self, query_self, key_self, value_self, output_self, norm_cross, query_cross, key_cross, value_cross, output_cross, norm_feed, gate_weight, up_weight, down_weight, row_example, key_owner, key_live):
    scaling = HEAD_DIM ** (-0.5)
    inner_width = HEADS * HEAD_DIM
    memory_rows = memory.reshape(BLK_DEV, N_MEM, BLK, D).reshape(BLK_DEV * N_MEM * BLK, D)
    mem_keys = round_both(product(memory_rows, key_cross)).reshape(-1, HEADS, HEAD_DIM)
    mem_values = round_both(product(memory_rows, value_cross)).reshape(-1, HEADS, HEAD_DIM)
    length = hidden_in.shape[1]
    places = jnp.arange(length, dtype=jnp.int32)
    causal = places[None, :] <= places[:, None]

    def one_row(inputs):
        incoming, example = inputs
        normed = low(rms_norm(incoming, norm_self))
        queries = round_both(product(normed, query_self)).reshape(length, HEADS, HEAD_DIM)
        key_rows = round_both(product(normed, key_self)).reshape(length, HEADS, HEAD_DIM)
        values = round_both(product(normed, value_self)).reshape(length, HEADS, HEAD_DIM)
        scores = low_back(jnp.einsum('qhd,khd->hqk', queries, key_rows, precision=lax.Precision.HIGHEST)) * scaling
        chance = jax.nn.softmax(jnp.where(causal[None], scores, -1e+30), axis=-1)
        attended = round_both(jnp.einsum('hqk,khd->qhd', low(chance), values, precision=lax.Precision.HIGHEST).reshape(length, inner_width))
        after_self = incoming + low_back(right_product(attended, output_self))
        normed_cross = low(rms_norm(after_self, norm_cross))
        cross_queries = round_both(product(normed_cross, query_cross)).reshape(length, HEADS, HEAD_DIM)
        usable = jnp.logical_and(key_owner == example, key_live)
        cross_scores = low_back(jnp.einsum('qhd,khd->hqk', cross_queries, mem_keys, precision=lax.Precision.HIGHEST)) * scaling
        cross_scores = jnp.where(usable[None, None, :], cross_scores, -1e+30)
        row_peak = lax.optimization_barrier(jnp.max(cross_scores, axis=2, keepdims=True))
        powers = jnp.exp(cross_scores - row_peak)
        totals = lax.optimization_barrier(jnp.sum(powers, axis=2))
        summed = jnp.einsum('hqk,khd->qhd', low(powers), mem_values, precision=lax.Precision.HIGHEST)
        attended_cross = round_both((summed / totals.T[:, :, None]).reshape(length, inner_width))
        after_cross = after_self + low_back(right_product(attended_cross, output_cross))
        normed_feed = low(rms_norm(after_cross, norm_feed))
        gate = low_back(product(normed_feed, gate_weight))
        upper = low_back(product(normed_feed, up_weight))
        activated = low(gelu_tanh(gate) * upper)
        return after_cross + low_back(product(activated, down_weight))
    return lax.map(jax.checkpoint(one_row), (hidden_in, row_example))

def reference(hidden_in, memory, cotangent, norm_self, query_self, key_self, value_self, output_self, norm_cross, query_cross, key_cross, value_cross, output_cross, norm_feed, gate_weight, up_weight, down_weight, block_counts, memory_tail, row_example):
    blocks = jnp.arange(BLK_DEV * N_MEM, dtype=jnp.int32)
    key_owner, key_live = block_tables(block_counts, memory_tail, blocks, BLK)
    floats = [array.astype(jnp.float32) for array in (hidden_in, memory, norm_self, query_self, key_self, value_self, output_self, norm_cross, query_cross, key_cross, value_cross, output_cross, norm_feed, gate_weight, up_weight, down_weight)]

    def run(*arrays):
        return forward(*arrays, row_example, key_owner, key_live)
    layer_out, pullback = jax.vjp(run, *floats)
    gradients = pullback(cotangent.astype(jnp.float32))
    return (layer_out.astype(jnp.bfloat16), gradients[0].astype(jnp.bfloat16), gradients[1].astype(jnp.bfloat16), gradients[2], gradients[3], gradients[4], gradients[5], gradients[6], gradients[7], gradients[8], gradients[9], gradients[10], gradients[11], gradients[12], gradients[13], gradients[14], gradients[15])
```

```python
import functools

import jax
import jax.numpy as jnp
from jax import lax
from jax.experimental import pallas as pl
from jax.experimental.pallas import tpu as pltpu
from jax.sharding import PartitionSpec as P

HEADS = 12
HEAD_DIM = 64
SCALING = HEAD_DIM ** (-0.5)
LANES = 128
MASKED = -1e30
F32 = jnp.float32
BF16 = jnp.bfloat16


def product(left, right):
    return jnp.dot(left, right, preferred_element_type=F32)


def left_product(left, right):
    return lax.dot_general(left, right, (((0,), (0,)), ((), ())), preferred_element_type=F32)


def right_product(left, right):
    return lax.dot_general(left, right, (((1,), (1,)), ((), ())), preferred_element_type=F32)


def gelu_tanh(values):
    return (
        0.5
        * values
        * (1.0 + jnp.tanh(0.7978845608028654 * (values + 0.044715 * values * values * values)))
    )


def gated_unit(gate, upper):
    return gelu_tanh(gate) * upper


def norm_scale(hidden):
    return lax.rsqrt(jnp.mean(hidden * hidden, axis=-1, keepdims=True) + 1e-06)


def norm_hidden_grad(hidden, scale, gain, upstream):
    lifted = upstream * gain
    return scale * lifted - hidden * (scale * scale * scale) * jnp.mean(
        lifted * hidden, axis=-1, keepdims=True
    )


def shift(values, axis, step):
    size = lax.axis_size(axis)
    return lax.ppermute(values, axis, [(i, (i + step) % size) for i in range(size)])


def swap(values, axis, mask):
    size = lax.axis_size(axis)
    return lax.ppermute(values, axis, [(i, i ^ mask) for i in range(size)])


def place_kernel(moves, splits, places, *refs):
    sources = refs[: len(moves)]
    targets = refs[len(moves) : len(moves) + len(splits)]
    done = refs[-1]
    copies = []
    number = 0
    for source, count in zip(sources, moves):
        for block in range(count):
            for target, (first, last) in zip(targets, splits):
                part = source.at[block]
                if len(splits) > 1:
                    part = source.at[block, :, first:last]
                copies.append(
                    pltpu.make_async_copy(part, target.at[places[number]], done.at[len(copies)])
                )
            number += 1
    for copy in copies:
        copy.start()
    for copy in copies:
        copy.wait()


def place(pieces, places, widths=None):
    counts = [piece.shape[0] for piece in pieces]
    total = sum(counts)
    _, height, width = pieces[0].shape
    widths = widths or [width]
    edges = [sum(widths[:i]) for i in range(len(widths) + 1)]
    splits = list(zip(edges[:-1], edges[1:]))
    outs = [jax.ShapeDtypeStruct((total, height, w), pieces[0].dtype) for w in widths]
    size = total * height * width * 2
    result = pl.pallas_call(
        functools.partial(place_kernel, counts, splits),
        out_shape=outs,
        grid_spec=pltpu.PrefetchScalarGridSpec(
            num_scalar_prefetch=1,
            grid=(1,),
            in_specs=[pl.BlockSpec(memory_space=pl.ANY)] * len(pieces),
            out_specs=[
                pl.BlockSpec((total, height, w), lambda i, places: (0, 0, 0)) for w in widths
            ],
            scratch_shapes=[pltpu.SemaphoreType.DMA((total * len(splits),))],
        ),
        compiler_params=pltpu.CompilerParams(vmem_limit_bytes=3 * size + (4 << 20)),
        cost_estimate=pl.CostEstimate(flops=0, bytes_accessed=2 * size, transcendentals=0),
        name="place",
    )(places.astype(jnp.int32), *pieces)
    return result[0] if len(widths) == 1 else result


def after(values, *tokens):
    return lax.optimization_barrier((values,) + tokens)[0]


def gather_seq(values):
    size = lax.axis_size("seq")
    index = lax.axis_index("seq")
    pieces = [values[None]] + [shift(values, "seq", k)[None] for k in range(1, size)]
    return place(pieces, (index - jnp.arange(size)) % size)


def spread_seq(blocks):
    size = lax.axis_size("seq")
    index = lax.axis_index("seq")
    kept = lax.dynamic_index_in_dim(blocks, index, 0, keepdims=False)
    return [kept] + [
        shift(
            lax.dynamic_index_in_dim(blocks, (index + k) % size, 0, keepdims=False), "seq", k
        )
        for k in range(1, size)
    ]


def slot_masks(order):
    count = len(order)
    return [
        sum((((t >> (count - 1 - i)) & 1) << bit) for i, bit in enumerate(order))
        for t in range(1 << count)
    ]


def gather_mem(values, order):
    index = lax.axis_index("mem")
    held = values[None]
    masks = [0]
    for bit in order[:-1]:
        held = jnp.concatenate([held, swap(held, "mem", 1 << bit)], axis=0)
        masks = masks + [mask | (1 << bit) for mask in masks]
    other = swap(held, "mem", 1 << order[-1])
    masks = masks + [mask | (1 << order[-1]) for mask in masks]
    return place([held, other], index ^ jnp.array(masks, jnp.int32))


def scatter_mem(blocks, order):
    held = blocks
    for bit in order:
        half = held.shape[0] // 2
        arrived = swap(held[half:], "mem", 1 << bit)
        held = (held[:half].astype(F32) + arrived.astype(F32)).astype(BF16)
    return held


def scatter_all(blocks, order):
    held = scatter_mem(blocks, order)
    size = lax.axis_size("seq")
    pieces = spread_seq(held.reshape(size, held.shape[0] // size, held.shape[1]))
    return functools.reduce(jnp.add, [piece.astype(F32) for piece in pieces])


def head_mask(shape, head):
    return lax.broadcasted_iota(jnp.int32, shape, 1) // HEAD_DIM == head


def pick_head(values, head):
    return jnp.where(head_mask(values.shape, head), values, jnp.zeros_like(values))


def transposed(values):
    return values.astype(F32).T.astype(values.dtype)


def soft_parts(scores):
    peak = jnp.max(scores, axis=0, keepdims=True)
    powers = jnp.exp(scores - peak)
    return powers, 1.0 / jnp.sum(powers, axis=0, keepdims=True)


def causal_scores(keys, queries, first):
    scores = right_product(keys, queries) * SCALING
    key_place = lax.broadcasted_iota(jnp.int32, scores.shape, 0)
    query_place = lax.broadcasted_iota(jnp.int32, scores.shape, 1) + first
    return jnp.where(key_place <= query_place, scores, MASKED)


def self_forward_kernel(heads, chunk, q_ref, k_ref, v_ref, out_ref):
    values_t = transposed(v_ref[...])
    width = heads * HEAD_DIM
    for first in range(0, q_ref.shape[0], chunk):
        last = first + chunk
        queries = q_ref[first:last]
        parts = []
        for head in range(heads):
            scores = causal_scores(k_ref[:last], pick_head(queries, head), first)
            powers, inverse = soft_parts(scores)
            rows = values_t[head * HEAD_DIM : (head + 1) * HEAD_DIM, :last]
            parts.append(product(rows, powers.astype(BF16)) * inverse)
        out_ref[first:last] = jnp.concatenate(parts, axis=0).T[:, :width].astype(BF16)


def self_backward_kernel(heads, chunk, q_ref, k_ref, v_ref, up_ref, dq_ref, dk_ref, dv_ref, dk_sum, dv_sum):
    keys_t = transposed(k_ref[...])
    dk_sum[...] = jnp.zeros_like(dk_sum)
    dv_sum[...] = jnp.zeros_like(dv_sum)
    width = keys_t.shape[0]
    for first in range(0, q_ref.shape[0], chunk):
        last = first + chunk
        queries = q_ref[first:last]
        upstream = up_ref[first:last]
        parts = []
        for head in range(heads):
            own = pick_head(queries, head)
            up_own = pick_head(upstream, head)
            powers, inverse = soft_parts(causal_scores(k_ref[:last], own, first))
            chance = powers * inverse
            inner = right_product(v_ref[:last], up_own)
            spread = jnp.sum(chance * inner, axis=0, keepdims=True)
            grad = (chance * (inner - spread) * SCALING).astype(BF16)
            dv_sum[:last] += product(chance.astype(BF16), up_own)
            dk_sum[:last] += product(grad, own)
            rows = keys_t[head * HEAD_DIM : (head + 1) * HEAD_DIM, :last]
            parts.append(product(rows, grad))
        rest = jnp.zeros((width - heads * HEAD_DIM, chunk), F32)
        dq_ref[first:last] = jnp.concatenate(parts + [rest], axis=0).T.astype(BF16)
    dk_ref[...] = dk_sum[...].astype(BF16)
    dv_ref[...] = dv_sum[...].astype(BF16)


def cross_scores(keys, queries, live):
    return jnp.where(live > 0, right_product(keys, queries) * SCALING, MASKED)


def cross_forward_kernel(live_ref, q_ref, k_ref, v_ref, out_ref):
    values_t = transposed(v_ref[...])
    queries = q_ref[...]
    live = live_ref[...]
    parts = []
    for head in range(LANES // HEAD_DIM):
        powers, inverse = soft_parts(cross_scores(k_ref[...], pick_head(queries, head), live))
        rows = values_t[head * HEAD_DIM : (head + 1) * HEAD_DIM]
        parts.append(product(rows, powers.astype(BF16)) * inverse)
    out_ref[...] = jnp.concatenate(parts, axis=0).T.astype(BF16)


def cross_backward_kernel(live_ref, q_ref, k_ref, v_ref, up_ref, dq_ref, dk_ref, dv_ref):
    keys_t = transposed(k_ref[...])
    queries = q_ref[...]
    upstream = up_ref[...]
    live = live_ref[...]
    parts, dk, dv = [], 0.0, 0.0
    for head in range(LANES // HEAD_DIM):
        own = pick_head(queries, head)
        up_own = pick_head(upstream, head)
        powers, inverse = soft_parts(cross_scores(k_ref[...], own, live))
        chance = powers * inverse
        inner = right_product(v_ref[...], up_own)
        spread = jnp.sum(chance * inner, axis=0, keepdims=True)
        grad = (chance * (inner - spread) * SCALING).astype(BF16)
        dv = dv + product(chance.astype(BF16), up_own)
        dk = dk + product(grad, own)
        rows = keys_t[head * HEAD_DIM : (head + 1) * HEAD_DIM]
        parts.append(product(rows, grad))
    dq_ref[...] = jnp.concatenate(parts, axis=0).T.astype(BF16)
    dk_ref[...] = dk.astype(BF16)
    dv_ref[...] = dv.astype(BF16)


def vmem(mebibytes):
    return pltpu.CompilerParams(vmem_limit_bytes=mebibytes << 20)


def self_forward(qkv, heads, chunk):
    length, width = qkv.shape[0], qkv.shape[1] // 3
    spec = lambda j: pl.BlockSpec((length, width), lambda i, j=j: (0, j))
    return pl.pallas_call(
        functools.partial(self_forward_kernel, heads, chunk),
        out_shape=jax.ShapeDtypeStruct((length, heads * HEAD_DIM), BF16),
        grid=(1,),
        in_specs=[spec(0), spec(1), spec(2)],
        out_specs=pl.BlockSpec((length, heads * HEAD_DIM), lambda i: (0, 0)),
        compiler_params=vmem(32),
        name="self_forward",
    )(qkv, qkv, qkv)


def self_backward(qkv, upstream, heads, chunk):
    length, width = qkv.shape[0], qkv.shape[1] // 3
    spec = lambda j: pl.BlockSpec((length, width), lambda i, j=j: (0, j))
    whole = jax.ShapeDtypeStruct((length, width), BF16)
    return pl.pallas_call(
        functools.partial(self_backward_kernel, heads, chunk),
        out_shape=(whole, whole, whole),
        grid=(1,),
        in_specs=[spec(0), spec(1), spec(2), spec(0)],
        out_specs=(spec(0), spec(0), spec(0)),
        scratch_shapes=[pltpu.VMEM((length, width), F32), pltpu.VMEM((length, width), F32)],
        compiler_params=vmem(40),
        name="self_backward",
    )(qkv, qkv, qkv, upstream)


def cross_specs(rows, keys):
    return (
        pl.BlockSpec((keys, 1), lambda i: (0, 0)),
        pl.BlockSpec((rows, LANES), lambda i: (0, i)),
        pl.BlockSpec((keys, LANES), lambda i: (0, i)),
    )


def cross_room(keys):
    return vmem(max(24, keys * 8 // 1024 + 8))


def cross_forward(live, queries, keys, values):
    live_spec, row_spec, key_spec = cross_specs(queries.shape[0], keys.shape[0])
    return pl.pallas_call(
        cross_forward_kernel,
        out_shape=jax.ShapeDtypeStruct(queries.shape, BF16),
        grid=(queries.shape[1] // LANES,),
        in_specs=[live_spec, row_spec, key_spec, key_spec],
        out_specs=row_spec,
        compiler_params=cross_room(keys.shape[0]),
        name="cross_forward",
    )(live, queries, keys, values)


def cross_backward(live, queries, keys, values, upstream):
    live_spec, row_spec, key_spec = cross_specs(queries.shape[0], keys.shape[0])
    return pl.pallas_call(
        cross_backward_kernel,
        out_shape=(
            jax.ShapeDtypeStruct(queries.shape, BF16),
            jax.ShapeDtypeStruct(keys.shape, BF16),
            jax.ShapeDtypeStruct(keys.shape, BF16),
        ),
        grid=(queries.shape[1] // LANES,),
        in_specs=[live_spec, row_spec, key_spec, key_spec, row_spec],
        out_specs=(row_spec, key_spec, key_spec),
        compiler_params=cross_room(keys.shape[0]),
        name="cross_backward",
    )(live, queries, keys, values, upstream)


def local(
    hidden_in,
    memory,
    cotangent,
    norm_self,
    query_self,
    key_self,
    value_self,
    output_self,
    norm_cross,
    query_cross,
    key_cross,
    value_cross,
    output_cross,
    norm_feed,
    gate_weight,
    up_weight,
    down_weight,
    block_counts,
    memory_tail,
    row_example,
):
    mem_count, seq_count = lax.axis_size("mem"), lax.axis_size("seq")
    mem_place, seq_place = lax.axis_index("mem"), lax.axis_index("seq")
    rows, width = hidden_in.shape[1], hidden_in.shape[2]
    inner = HEADS * HEAD_DIM
    length = rows * seq_count
    near = HEADS // seq_count
    slim = near * HEAD_DIM
    broad = -(-(slim + 3) // LANES) * LANES
    share = norm_self.shape[0]
    feed_share = down_weight.shape[0]
    hidden_width = gate_weight.shape[1]
    bits = mem_count.bit_length() - 1
    orders = (
        [*range(1, bits), 0],
        [*range(bits - 1, 0, -1), 0],
    )
    back_orders = (
        [0, *range(1, bits)],
        [0, *range(bits - 1, 0, -1)],
    )

    with jax.named_scope("gather_hidden"):
        x_all = gather_seq(hidden_in[0]).reshape(length, width)

    with jax.named_scope("gather_self"):
        gains = jnp.stack([norm_self, norm_cross, norm_feed], axis=1)

        def by_seq(weight):
            return jnp.transpose(weight.reshape(share, seq_count, slim), (1, 0, 2))

        def padded(block, extra):
            return jnp.concatenate([block, extra], axis=2)

        gain_pad = jnp.broadcast_to(
            jnp.concatenate([gains, jnp.zeros((share, broad - slim - 3), BF16)], axis=1)[None],
            (seq_count, share, broad - slim),
        )
        zero_pad = jnp.zeros((seq_count, share, broad - slim), BF16)
        triple = jnp.concatenate(
            [
                padded(by_seq(query_self), gain_pad),
                padded(by_seq(key_self), zero_pad),
                padded(by_seq(value_self), zero_pad),
            ],
            axis=2,
        )
        triple_mine = place(
            [piece[None] for piece in spread_seq(triple)],
            (seq_place - jnp.arange(seq_count)) % seq_count,
        )
        w_self = gather_mem(triple_mine.reshape(seq_count * share, 3 * broad), orders[0])
        w_self = w_self.reshape(width, 3 * broad)
        gains_all = w_self[:, slim : slim + 3].astype(F32).T
        gain_self32, gain_cross32, gain_feed32 = gains_all[0:1], gains_all[1:2], gains_all[2:3]

    def gather_all(shard, order):
        across = gather_seq(shard)
        full = gather_mem(across.reshape(-1, shard.shape[1]), order)
        return full.reshape(-1, shard.shape[1])

    with jax.named_scope("gather_outer"):
        w_outer = gather_all(jnp.concatenate([output_self, query_cross], axis=1), orders[1])
        w_output_self, w_query_cross = w_outer[:, :inner], w_outer[:, inner:]

    with jax.named_scope("gather_memory"):
        ends = jnp.cumsum(block_counts)
        starts = ends - block_counts
        places = jnp.arange(mem_count, dtype=jnp.int32)

        def block_of(example, holder):
            first = starts[example]
            block = first + (holder - first) % mem_count
            return block, block < ends[example]

        pieces = []
        for mask in range(mem_count):
            block, _ = block_of(row_example[mem_place ^ mask], mem_place)
            slot = jnp.clip(block // mem_count, 0, memory.shape[0] - 1)
            piece = lax.dynamic_index_in_dim(memory, slot, 0, keepdims=False)
            pieces.append(swap(piece, "mem", mask) if mask else piece)
        block_width = memory.shape[1]
        keys_in = jnp.concatenate(pieces, axis=0)
        mine = row_example[mem_place]
        owned_block, owned = block_of(mine, mem_place ^ places)
        is_last = owned_block == ends[mine] - 1
        token = jnp.arange(block_width, dtype=jnp.int32)
        live = jnp.logical_and(
            owned[:, None],
            jnp.logical_or(jnp.logical_not(is_last)[:, None], token[None, :] < memory_tail[mine]),
        )
        live = live.astype(F32).reshape(-1, 1)

    with jax.named_scope("gather_cross"):
        w_cross = gather_all(
            jnp.concatenate([key_cross, value_cross, output_cross], axis=1), orders[0]
        )
        w_key_value, w_output_cross = w_cross[:, : 2 * inner], w_cross[:, 2 * inner :]

    with jax.named_scope("gather_feed"):
        w_feed = gather_all(jnp.concatenate([gate_weight, up_weight], axis=1), orders[1])
        w_down = gather_all(down_weight, orders[0])

    with jax.named_scope("self_attention"):
        x32 = x_all.astype(F32)
        scale_all = norm_scale(x32)
        n1_all = (x32 * scale_all * gain_self32).astype(BF16)
        qkv = product(n1_all, w_self).astype(BF16)
        o1 = self_forward(qkv, near, rows)

    def heads_to_rows(values):
        pieces = spread_seq(values.reshape(seq_count, rows, slim))
        stacked = jnp.stack(pieces)
        return jnp.concatenate(
            [
                lax.dynamic_index_in_dim(stacked, (seq_place - j) % seq_count, 0, keepdims=False)
                for j in range(seq_count)
            ],
            axis=1,
        )

    def rows_to_heads(values):
        blocks = jnp.transpose(values.reshape(rows, seq_count, slim), (1, 0, 2))
        return place(
            [piece[None] for piece in spread_seq(blocks)],
            (seq_place - jnp.arange(seq_count)) % seq_count,
        ).reshape(length, slim)

    with jax.named_scope("self_output"):
        a1 = heads_to_rows(o1)
        x_own = hidden_in[0].astype(F32)
        h1 = x_own + right_product(a1, w_output_self)
        scale_cross = norm_scale(h1)
        n2 = (h1 * scale_cross * gain_cross32).astype(BF16)
        q2 = product(n2, w_query_cross).astype(BF16)

    with jax.named_scope("cross_attention"):
        kv2 = product(keys_in, w_key_value).astype(BF16)
        k2, v2 = kv2[:, :inner], kv2[:, inner:]
        a2 = cross_forward(live, q2, k2, v2)
        h2 = h1 + right_product(a2, w_output_cross)

    with jax.named_scope("feed"):
        scale_feed = norm_scale(h2)
        n3 = (h2 * scale_feed * gain_feed32).astype(BF16)
        both = product(n3, w_feed)
        gate, upper = both[:, :hidden_width], both[:, hidden_width:]
        act = gated_unit(gate, upper).astype(BF16)
        layer_out = (h2 + product(act, w_down)).astype(BF16)

    def relative(order):
        masks = jnp.array(slot_masks(order), jnp.int32)
        column = jnp.arange(width, dtype=jnp.int32)
        block = width // mem_count
        source = block * (mem_place ^ jnp.repeat(masks, block)) + column % block
        return (column[:, None] == source[None, :]).astype(BF16)

    pick = [relative(order) for order in back_orders]

    def turned(values, which):
        return product(values, pick[which]).astype(BF16)

    def gain_column(values):
        ones = jnp.ones((values.shape[0], LANES), BF16)
        return left_product(values.astype(BF16), ones)

    with jax.named_scope("feed_back"):
        c3 = cotangent[0]
        act_places = jnp.argsort(mem_place ^ jnp.array(slot_masks(back_orders[0]), jnp.int32))
        g_down = left_product(act, c3).astype(BF16)
        g_down = place([g_down.reshape(mem_count, -1, width)], act_places)
        down_weight_grad = scatter_all(g_down.reshape(-1, width), back_orders[0])
        dact = right_product(c3, w_down)
        _, unit_pull = jax.vjp(gated_unit, gate, upper)
        dgate, dupper = unit_pull(dact)
        dboth = jnp.concatenate([dgate.astype(BF16), dupper.astype(BF16)], axis=1)
        n3_rel = turned(n3, 1)
        g_feed = scatter_all(left_product(n3_rel, dboth).astype(BF16), back_orders[1])
        dn3 = right_product(dboth, w_feed)
        dh2 = c3.astype(F32) + norm_hidden_grad(h2, scale_feed, gain_feed32, dn3)
        gain_feed_terms = jnp.sum(dn3 * h2 * scale_feed, axis=0)

    with jax.named_scope("cross_back"):
        c2 = dh2.astype(BF16)
        da2 = product(c2, w_output_cross).astype(BF16)
        dq2, dk2, dv2 = cross_backward(live, q2, k2, v2, da2)
        dn2 = right_product(dq2, w_query_cross)
        dh1 = dh2 + norm_hidden_grad(h1, scale_cross, gain_cross32, dn2)
        gain_cross_terms = jnp.sum(dn2 * h1 * scale_cross, axis=0)

    with jax.named_scope("self_back_rows"):
        c1 = dh1.astype(BF16)
        da1 = product(c1, w_output_self).astype(BF16)
        da1_heads = rows_to_heads(da1)
        da1_heads = jnp.pad(da1_heads, ((0, 0), (0, broad - slim)))

    with jax.named_scope("cross_weights"):
        dkv2 = jnp.concatenate([dk2, dv2], axis=1)
        dmem = right_product(dkv2, w_key_value).astype(BF16)
        dmem = dmem.reshape(mem_count, block_width, width)
        arrived = jnp.stack(
            [dmem[0]] + [swap(dmem[mask], "mem", mask) for mask in range(1, mem_count)]
        )
        slots = memory.shape[0]
        slot_block = jnp.arange(slots, dtype=jnp.int32) * mem_count + mem_place
        slot_owner = jnp.sum((ends[None, :] <= slot_block[:, None]).astype(jnp.int32), axis=1)
        slot_row = jnp.sum(
            jnp.where(row_example[None, :] == slot_owner[:, None], places[None, :], 0), axis=1
        )
        table = jnp.stack(
            [
                lax.dynamic_index_in_dim(arrived, slot_row[s] ^ mem_place, 0, keepdims=False)
                for s in range(slots)
            ]
        )
        table = table.reshape(seq_count, (slots // seq_count) * block_width, width)
        memory_grad = functools.reduce(
            jnp.add, [piece.astype(F32) for piece in spread_seq(table)]
        ).astype(BF16)
        memory_grad = memory_grad.reshape(slots // seq_count, block_width, width)
        g_kv = left_product(turned(keys_in, 0), dkv2).astype(BF16)
        g_q2 = left_product(turned(n2, 0), dq2).astype(BF16)
        g_o2 = left_product(turned(c2, 0), a2).astype(BF16)
        g_cross = scatter_all(jnp.concatenate([g_q2, g_kv, g_o2], axis=1), back_orders[0])

    with jax.named_scope("self_back"):
        dq1, dk1, dv1 = self_backward(qkv, da1_heads, near, rows)
        dqkv = jnp.concatenate([dq1, dk1, dv1], axis=1)
        w_clean = w_self
        dn1_part = right_product(dqkv, w_clean)
        gain_self_terms = jnp.sum(dn1_part * x32 * scale_all, axis=0)
        dn1_pieces = spread_seq(dn1_part.astype(BF16).reshape(seq_count, rows, width))
        dn1 = functools.reduce(jnp.add, [piece.astype(F32) for piece in dn1_pieces])
        hidden_grad = (
            dh1 + norm_hidden_grad(x_own, norm_scale(x_own), gain_self32, dn1)
        ).astype(BF16)

    with jax.named_scope("self_weights"):
        g_qkv = left_product(turned(n1_all, 1), dqkv).astype(BF16)
        g_o1 = left_product(turned(c1, 1), a1).astype(BF16)
        g_gain = jnp.stack([gain_self_terms, gain_cross_terms, gain_feed_terms], axis=1)
        g_gain = product(
            pick[1].T,
            jnp.pad(g_gain, ((0, 0), (0, LANES - 3))).astype(BF16),
        ).astype(BF16)
        held = scatter_mem(jnp.concatenate([g_qkv, g_o1, g_gain], axis=1), back_orders[1])
        held = held.reshape(seq_count, share, held.shape[1])
        triple_held = held[:, :, : 3 * broad]
        rest_pieces = spread_seq(held[:, :, 3 * broad :])
        rest = functools.reduce(jnp.add, [piece.astype(F32) for piece in rest_pieces])
        triple_pieces = jnp.stack(spread_seq(triple_held))
        triple_back = jnp.stack(
            [
                lax.dynamic_index_in_dim(
                    triple_pieces, (seq_place - j) % seq_count, 0, keepdims=False
                )
                for j in range(seq_count)
            ],
            axis=1,
        )
        triple_back = triple_back.reshape(share, seq_count, 3, broad)[:, :, :, :slim].astype(F32)
        self_grads = [triple_back[:, :, j].reshape(share, inner) for j in range(3)]

    return (
        layer_out[None],
        hidden_grad[None],
        memory_grad,
        rest[:, inner],
        self_grads[0],
        self_grads[1],
        self_grads[2],
        rest[:, :inner],
        rest[:, inner + 1],
        g_cross[:, :inner],
        g_cross[:, inner : 2 * inner],
        g_cross[:, 2 * inner : 3 * inner],
        g_cross[:, 3 * inner :],
        rest[:, inner + 2],
        g_feed[:, :hidden_width],
        g_feed[:, hidden_width:],
        down_weight_grad,
    )


def solution(mesh):
    every = P(("mem", "seq"), None)
    gain = P(("mem", "seq"))
    in_specs = (
        (P("mem", "seq", None), P(None, "mem", None), P("mem", "seq", None), gain)
        + (every,) * 4
        + (gain,)
        + (every,) * 4
        + (gain,)
        + (every,) * 3
        + (P(),) * 3
    )
    out_specs = (
        (P("mem", "seq", None), P("mem", "seq", None), P("seq", "mem", None), gain)
        + (every,) * 4
        + (gain,)
        + (every,) * 4
        + (gain,)
        + (every,) * 3
    )
    return jax.shard_map(local, mesh=mesh, in_specs=in_specs, out_specs=out_specs, check_vma=False)
```

```python
import functools

import jax
import jax.numpy as jnp
from jax import lax
from jax.experimental import pallas as pl
from jax.experimental.pallas import tpu as pltpu
from jax.sharding import PartitionSpec as P

HEADS = 12
HEAD_DIM = 64
SCALING = HEAD_DIM ** (-0.5)
LANES = 128
MASKED = -1e30
F32 = jnp.float32
BF16 = jnp.bfloat16


def product(left, right):
    return jnp.dot(left, right, preferred_element_type=F32)


def left_product(left, right):
    return lax.dot_general(left, right, (((0,), (0,)), ((), ())), preferred_element_type=F32)


def right_product(left, right):
    return lax.dot_general(left, right, (((1,), (1,)), ((), ())), preferred_element_type=F32)


def gelu_tanh(values):
    return (
        0.5
        * values
        * (1.0 + jnp.tanh(0.7978845608028654 * (values + 0.044715 * values * values * values)))
    )


def gated_unit(gate, upper):
    return gelu_tanh(gate) * upper


def norm_scale(hidden):
    return lax.rsqrt(jnp.mean(hidden * hidden, axis=-1, keepdims=True) + 1e-06)


def norm_hidden_grad(hidden, scale, gain, upstream):
    lifted = upstream * gain
    return scale * lifted - hidden * (scale * scale * scale) * jnp.mean(
        lifted * hidden, axis=-1, keepdims=True
    )


def shift(values, axis, step):
    size = lax.axis_size(axis)
    return lax.ppermute(values, axis, [(i, (i + step) % size) for i in range(size)])


def swap(values, axis, mask):
    size = lax.axis_size(axis)
    return lax.ppermute(values, axis, [(i, i ^ mask) for i in range(size)])


def place_kernel(counts, maps, places, *refs):
    sources = refs[: len(counts)]
    targets, done = refs[len(counts) : -1], refs[-1]
    copies = []
    number = 0
    for source, count, moves in zip(sources, counts, maps):
        for block in range(count):
            for goal, to, start, width in moves:
                part, target = source.at[block], targets[goal].at[places[number]]
                if len(moves) > 1 or width != source.shape[2]:
                    part = source.at[block, :, start : start + width]
                    target = targets[goal].at[places[number], :, to : to + width]
                copies.append(pltpu.make_async_copy(part, target, done.at[len(copies)]))
            number += 1
    for copy in copies:
        copy.start()
    for copy in copies:
        copy.wait()


def place(pieces, places, widths=None, maps=None):
    counts = [piece.shape[0] for piece in pieces]
    total = sum(counts)
    _, height, width = pieces[0].shape
    widths = widths or [width]
    if maps is None:
        plain = [(i, 0, sum(widths[:i]), w) for i, w in enumerate(widths)]
        maps = [plain] * len(pieces)
    copies = sum(count * len(moves) for count, moves in zip(counts, maps))
    outs = [((total, height, w), pieces[0].dtype) for w in widths]
    size = total * height * sum(widths) * 2
    result = pl.pallas_call(
        functools.partial(place_kernel, counts, maps),
        out_shape=far_out(outs),
        grid_spec=pltpu.PrefetchScalarGridSpec(
            num_scalar_prefetch=1,
            grid=(1,),
            in_specs=[HBM] * len(pieces),
            out_specs=[
                pl.BlockSpec((total, height, w), lambda i, places: (0, 0, 0)) for w in widths
            ],
            scratch_shapes=[pltpu.SemaphoreType.DMA((copies,))],
        ),
        compiler_params=pltpu.CompilerParams(vmem_limit_bytes=3 * size + (4 << 20)),
        cost_estimate=cost(1 + size / 1e6),
        name="place",
    )(places.astype(jnp.int32), *far(*pieces))
    return result[0] if len(widths) == 1 else result


def after(values, *tokens):
    return lax.optimization_barrier((values,) + tokens)[0]


def settle(*values):
    return lax.optimization_barrier(values)


def seq_masks(parity):
    return [0, 1 + parity, 2 - parity, 3]


def swap_seq(values, turn):
    mem, seq = lax.axis_size("mem"), lax.axis_size("seq")
    pairs = []
    for m in range(mem):
        mask = 1 + (m + turn) % 2
        pairs += [(m * seq + s, m * seq + (s ^ mask)) for s in range(seq)]
    return lax.ppermute(values, ("mem", "seq"), pairs)


def seq_places():
    parity = lax.axis_index("mem") % 2
    return lax.axis_index("seq") ^ jnp.stack(seq_masks(parity)).astype(jnp.int32)


def stack_seq(pieces, widths=None):
    return place(pieces, seq_places(), widths)


def send_seq(pieces):
    return [pieces[0]] + [shift(piece, "seq", k) for k, piece in enumerate(pieces) if k]


def total_of(pieces):
    return functools.reduce(jnp.add, [piece.astype(F32) for piece in pieces])


def join(blocks):
    return blocks[0] if len(blocks) == 1 else jnp.concatenate(blocks, axis=0)


def orders(count):
    bits = list(range(1, count.bit_length() - 1))
    return bits, bits[::-1]


def slot_masks(count):
    half = count // 2
    low = [
        [sum(((s >> j) & 1) << bit for j, bit in enumerate(order)) for s in range(half)]
        for order in orders(count)
    ]
    return low[0] + [m | 1 for m in low[1]], low[1] + [m | 1 for m in low[0]]


def swap_mem(values, turn):
    count = lax.axis_size("mem")
    pairs = []
    for i in range(count):
        order = [*orders(count)[i % 2], 0]
        pairs.append((i, i ^ (1 << order[turn])))
    return lax.ppermute(values, "mem", pairs)


def mem_masks():
    count = lax.axis_size("mem")
    even, odd = slot_masks(count)
    return jnp.where(
        lax.axis_index("mem") % 2 == 0, jnp.array(even, jnp.int32), jnp.array(odd, jnp.int32)
    )


def stack_mem(halves, widths=None):
    return place(halves, lax.axis_index("mem") ^ mem_masks(), widths)


def spread_weight(halves):
    if halves[0].shape[1] % 16 == 0:
        return list(halves)
    stacked = stack_mem(halves)
    return [stacked.reshape(1, -1, stacked.shape[-1])]


def add_low(left, right):
    return (left.astype(F32) + right.astype(F32)).astype(BF16)


def split_kernel(plans, spot_ref, *refs):
    tensors = len(plans)
    outs = list(refs[2 * tensors : -tensors])
    column = 0
    for i, ends in enumerate(plans):
        kept_ref, arrived_ref = refs[2 * i], refs[2 * i + 1]
        groups, rows, width = kept_ref.shape
        for g in range(groups):
            total = kept_ref[g].astype(F32) + arrived_ref[g].astype(F32)
            if not ends:
                outs[0][g] = total[: rows // 2].astype(BF16)
                outs[1][g] = total[rows // 2 :].astype(BF16)
                continue
            hold = refs[len(refs) - tensors + i]
            count = hold.shape[0]
            unit = rows // count
            for j in range(count):
                hold[j] = total[j * unit : (j + 1) * unit]
            for k, mask in enumerate(seq_masks(lax.rem(spot_ref[0], 2))):
                piece = hold[jnp.bitwise_xor(spot_ref[1], mask)].astype(BF16)
                outs[-2 + k // 2][k % 2, :, column : column + width] = piece
            column += width
        if not ends:
            del outs[:2]


def add_split(pairs, plans, spot):
    count = lax.axis_size("seq")
    shapes = []
    ended = 0
    for (kept, _), ends in zip(pairs, plans):
        groups, rows, width = kept.shape
        if ends:
            ended += groups * width
            unit = rows // count
        else:
            shapes += [(groups, rows // 2, width)] * 2
    if ended:
        shapes += [(2, unit, ended)] * 2
    whole = lambda shape: pl.BlockSpec(shape, lambda i, spot: (0, 0, 0))
    holds = [
        pltpu.VMEM((count, kept.shape[1] // count, kept.shape[2]) if ends else (1, 8, 128), F32)
        for (kept, _), ends in zip(pairs, plans)
    ]
    size = sum(kept.size for kept, _ in pairs)
    flat = [array for pair in pairs for array in pair]
    outs = pl.pallas_call(
        functools.partial(split_kernel, plans),
        out_shape=far_out([(shape, BF16) for shape in shapes]),
        grid_spec=pltpu.PrefetchScalarGridSpec(
            num_scalar_prefetch=1,
            grid=(1,),
            in_specs=[whole(a.shape) for a in flat],
            out_specs=[whole(shape) for shape in shapes],
            scratch_shapes=holds,
        ),
        compiler_params=vmem(min(56, 12 + (size * 24 >> 20))),
        cost_estimate=cost(1 + size / 1e6),
        name="add_split",
    )(spot, *far(*flat))
    outs = list(outs)
    return (outs[:-2], outs[-2:]) if ended else (outs, None)


class Scatter:
    def __init__(self, kept, sent):
        self.kept, self.sent = [a if a.ndim == 3 else a[None] for a in (kept, sent)]
        self.left = (lax.axis_size("mem") // 2).bit_length() - 1
        self.turn = self.left

    def move(self):
        self.arrived = swap_mem(self.sent, self.turn)

    def parts(self):
        return [self.kept, self.sent]

    def take(self, parts):
        self.kept, self.sent = parts


def advance(scatters, spot):
    count = lax.axis_size("seq")
    pairs = [(s.kept, s.arrived) for s in scatters]
    plans = [s.left == 0 for s in scatters]
    for s in scatters:
        s.left -= 1
        s.turn = s.left
    exact = all(
        kept.shape[1] // (count if ends else 2) % 8 == 0
        for (kept, _), ends in zip(pairs, plans)
    )
    if exact:
        results, pieces = add_split(pairs, plans, spot)
    else:
        results, ended = [], []
        for pair, ends in zip(pairs, plans):
            total = add_low(*pair)
            groups, rows, width = total.shape
            if ends:
                blocks = total.reshape(groups, count, rows // count, width)
                blocks = jnp.concatenate(list(blocks), axis=2)
                ended.append(jnp.take(blocks, seq_places(), axis=0))
            else:
                results += [total[:, : rows // 2], total[:, rows // 2 :]]
        pieces = None
        if ended:
            ended = jnp.concatenate(ended, axis=2)
            pieces = [ended[:2], ended[2:]]
    for s, ends in zip(scatters, plans):
        if not ends:
            s.kept, s.sent = results[:2]
            results = results[2:]
    return pieces


def onward(kept, arrived, summed=None):
    half = kept.shape[0] // 2
    mine, theirs = kept[half:], arrived[half:]
    if summed is None:
        return add_low(mine, theirs)
    return jnp.concatenate(
        [add_low(mine[..., :summed], theirs[..., :summed]), mine[..., summed:], theirs[..., summed:]],
        axis=-1,
    )


def part_blocks(blocks, turn):
    count = blocks.shape[0]
    parts = blocks.reshape((count >> (turn + 1), 2, 1 << turn) + blocks.shape[1:])
    return parts[:, 0], parts[:, 1]


def join_blocks(stay, arrived):
    joined = jnp.stack([stay, arrived], axis=1)
    return joined.reshape((-1,) + joined.shape[3:])


HBM = pl.BlockSpec(memory_space=pltpu.HBM)


def far(*arrays):
    return [pltpu.with_memory_space_constraint(a, pltpu.HBM) for a in arrays]


def far_out(shapes):
    return [pltpu.HBM(shape, dtype) for shape, dtype in shapes]


def vmem(mebibytes):
    return pltpu.CompilerParams(vmem_limit_bytes=mebibytes << 20)


def cost(microseconds):
    return pl.CostEstimate(
        flops=int(microseconds * 1.1e9), bytes_accessed=0, transcendentals=0
    )


def run(copies):
    for copy in copies:
        copy.start()
    for copy in copies:
        copy.wait()


def prepare_kernel(
    slim, broad, scalars_ref, spot_ref,
    q_ref, k_ref, v_ref, o1_ref, q2_ref, k2_ref, v2_ref, o2_ref, gate_ref, up_ref,
    gain_ref, memory_ref,
    own_ref, two_ref, one_ref, second_ref, blocks_ref, live_ref,
    turn, triple, held, done,
):
    mem_count, height = blocks_ref.shape[0], memory_ref.shape[1]
    share, width = q_ref.shape
    half = mem_count // 2
    me, seq = spot_ref[0], spot_ref[1]
    parity = lax.rem(me, 2)
    counts_at, tails_at, rows_at = 0, mem_count, 2 * mem_count
    moves = [(ref, triple.at[i]) for i, ref in enumerate((q_ref, k_ref, v_ref))]
    moves += [(memory_ref, held)]
    for ref, base in ((own_ref, 3 * broad), (one_ref, 3 * broad), (two_ref, 6 * broad)):
        for i, source in enumerate((o1_ref, q2_ref, k2_ref, v2_ref, o2_ref)):
            moves += [(source, ref.at[:, base + i * width : base + (i + 1) * width])]
    hidden = gate_ref.shape[1]
    moves += [(gate_ref, second_ref.at[:, :hidden]), (up_ref, second_ref.at[:, hidden:])]
    copies = [pltpu.make_async_copy(a, b, done.at[i]) for i, (a, b) in enumerate(moves)]
    for copy in copies:
        copy.start()
    turn[...] = jnp.zeros_like(turn)
    turn[0:3, 0:share] = gain_ref[...].astype(F32)
    gains = turn[...].T[:share]
    lane = lax.broadcasted_iota(jnp.int32, (share, broad - slim), 1)
    extra = jnp.zeros((share, broad - slim), F32)
    for i in range(3):
        extra = jnp.where(lane == i, gains[:, i : i + 1], extra)
    extra = extra.astype(BF16)
    blank = jnp.zeros((share, broad - slim), BF16)
    token = lax.broadcasted_iota(jnp.int32, (height, 1), 0)

    def first_block(example):
        return lax.fori_loop(
            0, example, lambda i, total: total + scalars_ref[counts_at + i], jnp.int32(0)
        )

    mine = scalars_ref[rows_at + me]
    mine_start = first_block(mine)
    mine_end = mine_start + scalars_ref[counts_at + mine]

    for copy in copies[:4]:
        copy.wait()

    order, contrary = orders(mem_count)

    def one(t, carry):
        low = lax.rem(t, half)
        first, second = jnp.int32(0), jnp.int32(0)
        for j in range(len(order)):
            bit = lax.rem(lax.shift_right_logical(low, jnp.int32(j)), 2)
            first = first + bit * (1 << order[j])
            second = second + bit * (1 << contrary[j])
        flip = parity == 1
        first, second = jnp.where(flip, second, first), jnp.where(flip, first, second)
        upper = t >= half
        goal = jnp.bitwise_xor(me, jnp.where(upper, first + 1, first))
        start = first_block(scalars_ref[rows_at + goal])
        block = start + lax.rem(me - lax.rem(start, mem_count) + mem_count, mem_count)
        slot = jnp.minimum(block // mem_count, memory_ref.shape[0] - 1)
        blocks_ref[t] = held[slot]
        holder = jnp.bitwise_xor(me, jnp.where(upper, second + 1, first))
        block = mine_start + lax.rem(
            holder - lax.rem(mine_start, mem_count) + mem_count, mem_count
        )
        bound = jnp.where(block == mine_end - 1, scalars_ref[tails_at + mine], height)
        bound = jnp.where(block < mine_end, bound, 0)
        live_ref[t] = (token < bound).astype(F32)
        return carry

    lax.fori_loop(0, mem_count, one, 0)
    seq_steps = seq_masks(parity)
    for ref, base, mask in (
        (own_ref, 0, seq_steps[0]),
        (two_ref, 0, seq_steps[1]),
        (one_ref, 0, seq_steps[2]),
        (two_ref, 1, seq_steps[3]),
    ):
        goal = jnp.bitwise_xor(seq, mask)
        for i in range(3):
            weight = triple[i].astype(F32)
            chosen = weight[:, :slim]
            for j in range(1, width // slim):
                chosen = jnp.where(goal == j, weight[:, j * slim : (j + 1) * slim], chosen)
            start = (3 * base + i) * broad
            ref[:, start : start + broad] = jnp.concatenate(
                [chosen.astype(BF16), blank if i else extra], axis=1
            )
    for copy in copies[4:]:
        copy.wait()


def prepare(weights, gains, memory, scalars, spot, slim, broad):
    mem_count = lax.axis_size("mem")
    share, width = weights[0].shape
    first = 3 * broad + 5 * width
    second = sum(w.shape[1] for w in weights[8:])
    height = memory.shape[1]
    whole = lambda shape: pl.BlockSpec(shape, lambda *_: (0,) * len(shape))
    outs = [
        ((share, first), BF16),
        ((share, first + 3 * broad), BF16),
        ((share, first), BF16),
        ((share, second), BF16),
        ((mem_count, height, width), BF16),
        ((mem_count, height, 1), F32),
    ]
    return pl.pallas_call(
        functools.partial(prepare_kernel, slim, broad),
        out_shape=far_out(outs),
        grid_spec=pltpu.PrefetchScalarGridSpec(
            num_scalar_prefetch=2,
            grid=(1,),
            in_specs=[HBM] * len(weights) + [whole(gains.shape), HBM],
            out_specs=[whole(shape) for shape, _ in outs],
            scratch_shapes=[
                pltpu.VMEM((8, 128), F32),
                pltpu.VMEM((3, share, width), BF16),
                pltpu.VMEM(memory.shape, BF16),
                pltpu.SemaphoreType.DMA((4 + 15 + 2,)),
            ],
        ),
        compiler_params=vmem(16 + 3 * mem_count // 8),
        cost_estimate=cost(3),
        name="prepare",
    )(scalars, spot, *far(*weights), gains, *far(memory))


def slots_kernel(per, scalars_ref, spot_ref, blocks_ref, keep_ref, send_ref, done):
    mem_count = blocks_ref.shape[0]
    me, seq = spot_ref[0], spot_ref[1]
    parity = lax.rem(me, 2)
    copies = []
    for k, mask in enumerate(seq_masks(parity)):
        for s in range(per):
            slot = jnp.bitwise_xor(seq, mask) * per + s
            block = slot * mem_count + me

            def scan(i, carry):
                end, owner = carry
                end = end + scalars_ref[i]
                return end, owner + jnp.where(end <= block, 1, 0)

            _, owner = lax.fori_loop(0, mem_count, scan, (jnp.int32(0), jnp.int32(0)))
            row = lax.fori_loop(
                0,
                mem_count,
                lambda i, r: jnp.where(scalars_ref[2 * mem_count + i] == owner, i, r),
                jnp.int32(0),
            )
            gap = jnp.bitwise_xor(row, me)
            bit = lambda b: lax.rem(lax.shift_right_logical(gap, jnp.int32(b)), 2)
            spots = [
                sum(bit(b) * (1 << j) for j, b in enumerate(order)) for order in orders(mem_count)
            ]
            at = jnp.where(parity == 1, spots[1], spots[0]) + bit(0) * (mem_count // 2)
            copies.append(
                pltpu.make_async_copy(
                    blocks_ref.at[at],
                    (keep_ref, send_ref)[k // 2].at[k % 2 * per + s],
                    done.at[len(copies)],
                )
            )
    for copy in copies:
        copy.start()
    for copy in copies:
        copy.wait()


def pick_slots(blocks, slots, scalars, spot):
    per = slots // lax.axis_size("seq")
    shape = (2 * per,) + blocks.shape[1:]
    return pl.pallas_call(
        functools.partial(slots_kernel, per),
        out_shape=far_out([(shape, BF16)] * 2),
        grid_spec=pltpu.PrefetchScalarGridSpec(
            num_scalar_prefetch=2,
            grid=(1,),
            in_specs=[HBM],
            out_specs=[pl.BlockSpec(shape, lambda *_: (0, 0, 0))] * 2,
            scratch_shapes=[pltpu.SemaphoreType.DMA((slots,))],
        ),
        compiler_params=vmem(8),
        cost_estimate=cost(2),
        name="pick_slots",
    )(scalars, spot, *far(blocks))


def feed_kernel(
    order_ref, h2_ref, n3_ref, c3_ref, gain_ref, source_ref,
    gate_a_ref, gate_b_ref, up_a_ref, up_b_ref, down_a_ref, down_b_ref,
    out_ref, dh2_ref, c2_ref, gain_grad_ref, gboth_a_ref, gboth_b_ref, gdown_a_ref, gdown_b_ref,
    turn, n3_rel, n3_rel_t, total, dn3, gate_w, up_w,
):
    step, steps = pl.program_id(0), pl.num_programs(0)
    half = gate_a_ref.shape[0]
    width = n3_ref.shape[1]

    @pl.when(step == 0)
    def _():
        columns = lax.broadcasted_iota(jnp.int32, (width, width), 1)
        turn[...] = (columns == source_ref[...]).astype(F32).astype(BF16)
        n3_rel[...] = right_product(n3_ref[...], turn[...]).astype(BF16)
        n3_rel_t[...] = right_product(turn[...], n3_ref[...]).astype(BF16)
        total[...] = jnp.zeros_like(total)
        dn3[...] = jnp.zeros_like(dn3)

    gate_w[:half] = gate_a_ref[...]
    gate_w[half:] = gate_b_ref[...]
    up_w[:half] = up_a_ref[...]
    up_w[half:] = up_b_ref[...]
    first = step < steps // 2
    down = jnp.where(first, down_a_ref[...], down_b_ref[...])
    n3, c3 = n3_rel[...], c3_ref[...]
    gate = product(n3, gate_w[...])
    upper = product(n3, up_w[...])
    dact = right_product(c3, down)
    inner = 0.7978845608028654 * (gate + 0.044715 * gate * gate * gate)
    bent = jnp.tanh(inner)
    gelu = 0.5 * gate * (1.0 + bent)
    slope = 0.5 * (1.0 + bent) + 0.5 * gate * (1.0 - bent * bent) * (
        0.7978845608028654 * (1.0 + 3.0 * 0.044715 * gate * gate)
    )
    act = (gelu * upper).astype(BF16)
    dgate = (dact * upper * slope).astype(BF16)
    dupper = (dact * gelu).astype(BF16)
    total[...] += product(act, down)
    gdown = left_product(act, c3).astype(BF16)

    @pl.when(first)
    def _():
        gdown_a_ref[...] = gdown

    @pl.when(jnp.logical_not(first))
    def _():
        gdown_b_ref[...] = gdown

    dn3[...] += right_product(dgate, gate_w[...]) + right_product(dupper, up_w[...])
    ggate = product(n3_rel_t[...], dgate).astype(BF16)
    gup = product(n3_rel_t[...], dupper).astype(BF16)
    gboth_a_ref[0] = ggate[:half]
    gboth_b_ref[0] = ggate[half:]
    gboth_a_ref[1] = gup[:half]
    gboth_b_ref[1] = gup[half:]

    @pl.when(step == steps - 1)
    def _():
        h2 = h2_ref[...]
        out_ref[...] = (h2 + total[...]).astype(BF16)
        high = dn3[...].astype(BF16)
        rest = (dn3[...] - high.astype(F32)).astype(BF16)
        upstream = product(high, turn[...]) + product(rest, turn[...])
        scale = norm_scale(h2)
        dh2 = c3_ref[...].astype(F32) + norm_hidden_grad(h2, scale, gain_ref[...], upstream)
        dh2_ref[...] = dh2
        c2_ref[...] = dh2.astype(BF16)
        gain_grad_ref[...] = jnp.sum(upstream * h2 * scale, axis=0, keepdims=True)


def feed(order, h2, n3, c3, gain, source, both, down):
    rows, width = h2.shape
    half, hidden = both[0].shape
    hidden = hidden // 2
    steps = order.shape[0]
    unit = hidden // steps
    middle = steps // 2
    whole = lambda shape: pl.BlockSpec(shape, lambda i, o: (0, 0))
    column = pl.BlockSpec((half, unit), lambda i, o: (0, o[i]))
    beside = pl.BlockSpec((half, unit), lambda i, o: (0, o[i] + steps))
    twice = pl.BlockSpec((2, half, unit), lambda i, o: (0, 0, o[i]))
    early = pl.BlockSpec((unit, width), lambda i, o: (jnp.minimum(i, middle - 1), 0))
    late = pl.BlockSpec((unit, width), lambda i, o: (jnp.maximum(i - middle, 0), 0))
    flat = (rows, width)
    return pl.pallas_call(
        feed_kernel,
        out_shape=far_out(
            [(flat, BF16), (flat, F32), (flat, BF16), ((1, width), F32)]
            + [((2, half, hidden), BF16)] * 2
            + [((hidden // 2, width), BF16)] * 2
        ),
        grid_spec=pltpu.PrefetchScalarGridSpec(
            num_scalar_prefetch=1,
            grid=(steps,),
            in_specs=[whole(flat)] * 3
            + [whole((1, width)), whole((width, 1))]
            + [column, column, beside, beside]
            + [early, late],
            out_specs=[whole(flat)] * 3 + [whole((1, width)), twice, twice, early, late],
            scratch_shapes=[
                pltpu.VMEM((width, width), BF16),
                pltpu.VMEM(flat, BF16),
                pltpu.VMEM((width, rows), BF16),
                pltpu.VMEM(flat, F32),
                pltpu.VMEM(flat, F32),
                pltpu.VMEM((2 * half, unit), BF16),
                pltpu.VMEM((2 * half, unit), BF16),
            ],
        ),
        compiler_params=vmem(48),
        cost_estimate=cost(19),
        name="feed",
    )(order, *far(h2, n3, c3), gain, source, *far(*both, *both, *down))


def head_mask(shape, head):
    return lax.broadcasted_iota(jnp.int32, shape, 1) // HEAD_DIM == head


def pick_head(values, head):
    return jnp.where(head_mask(values.shape, head), values, jnp.zeros_like(values))


def transposed(values):
    return values.astype(F32).T.astype(values.dtype)


def soft_parts(scores):
    peak = jnp.max(scores, axis=0, keepdims=True)
    powers = jnp.exp(scores - peak)
    return powers, 1.0 / jnp.sum(powers, axis=0, keepdims=True)


def causal_scores(keys, queries, first):
    scores = right_product(keys, queries) * SCALING
    key_place = lax.broadcasted_iota(jnp.int32, scores.shape, 0)
    query_place = lax.broadcasted_iota(jnp.int32, scores.shape, 1) + first
    return jnp.where(key_place <= query_place, scores, MASKED)


def cross_scores(keys, queries, live):
    return jnp.where(live > 0, right_product(keys, queries) * SCALING, MASKED)


def weight_copies(refs, masks, me, columns, target, done, base):
    copies = []
    for ref in refs:
        for block in range(ref.shape[0]):
            number = len(copies)
            spot = 0
            if len(refs) > 1:
                mask = masks[0][number]
                if masks[1][number] != mask:
                    mask = jnp.where(lax.rem(me, 2) == 1, masks[1][number], mask)
                spot = pl.multiple_of(jnp.bitwise_xor(me, mask) * ref.shape[1], 16)
            copies.append(
                pltpu.make_async_copy(
                    ref.at[block, :, columns[0] : columns[1]],
                    target.at[pl.ds(spot, ref.shape[1])],
                    done.at[base + number],
                )
            )
    return copies


def blocks_in(refs):
    return sum(ref.shape[0] for ref in refs)


def self_rows_kernel(heads, masks, counts, spot_ref, *refs):
    seq_count, weights = counts
    x_refs, refs = refs[:3], refs[3:]
    x_list = [x_refs[0], x_refs[1], x_refs[2].at[0], x_refs[2].at[1]]
    w_refs, refs = refs[:weights], refs[weights:]
    o_refs, refs = refs[:seq_count], refs[seq_count:]
    n1_ref, qkv_ref, gain_ref, x_all, w_all, o_all, done = refs
    rows, width = x_refs[0].shape
    broad = w_all.shape[1] // 3
    me, seq = spot_ref[0], spot_ref[1]
    copies = weight_copies(w_refs, masks, me, (0, 3 * broad), w_all, done, 0)
    base = len(copies)
    copies += [
        pltpu.make_async_copy(ref, x_all.at[jnp.bitwise_xor(seq, mask)], done.at[base + k])
        for k, (ref, mask) in enumerate(zip(x_list, seq_masks(lax.rem(me, 2))))
    ]
    run(copies)
    slim = heads * HEAD_DIM
    edge = slim // LANES * LANES
    gains = w_all[:, edge : edge + LANES].astype(F32).T[slim - edge : slim - edge + 8]
    gain_ref[...] = gains
    for j in range(seq_count):
        x = x_all[j].astype(F32)
        n1 = (x * norm_scale(x) * gains[0:1]).astype(BF16)
        n1_ref[j * rows : (j + 1) * rows] = n1
        qkv_ref[j * rows : (j + 1) * rows] = product(n1, w_all[...]).astype(BF16)
    values_t = transposed(qkv_ref[:, 2 * broad :])
    for j in range(seq_count):
        first, last = j * rows, (j + 1) * rows
        queries = qkv_ref[first:last, :broad]
        parts = []
        for head in range(heads):
            scores = causal_scores(
                qkv_ref[:last, broad : 2 * broad], pick_head(queries, head), first
            )
            powers, inverse = soft_parts(scores)
            lines = values_t[head * HEAD_DIM : (head + 1) * HEAD_DIM, :last]
            parts.append(product(lines, powers.astype(BF16)) * inverse)
        o_all[j] = jnp.concatenate(parts, axis=0).T.astype(BF16)
    for k, ref in enumerate(o_refs):
        ref[...] = o_all[lax.rem(seq + k, seq_count)]


def self_rows(x_pieces, weights, spot, heads, broad, masks):
    count = lax.axis_size("seq")
    rows, width = x_pieces[0].shape
    length, slim = rows * count, heads * HEAD_DIM
    whole = lambda shape: pl.BlockSpec(shape, lambda i, spot: (0, 0))
    shapes = [((rows, slim), BF16)] * count + [
        ((length, width), BF16),
        ((length, 3 * broad), BF16),
        ((8, width), F32),
    ]
    outs = pl.pallas_call(
        functools.partial(self_rows_kernel, heads, masks, (count, len(weights))),
        out_shape=far_out(shapes),
        grid_spec=pltpu.PrefetchScalarGridSpec(
            num_scalar_prefetch=1,
            grid=(1,),
            in_specs=[HBM] * (3 + len(weights)),
            out_specs=[whole(s) for s, _ in shapes],
            scratch_shapes=[
                pltpu.VMEM((count, rows, width), BF16),
                pltpu.VMEM((width, 3 * broad), BF16),
                pltpu.VMEM((count, rows, slim), BF16),
                pltpu.SemaphoreType.DMA((blocks_in(weights) + count,)),
            ],
        ),
        compiler_params=vmem(40),
        cost_estimate=cost(10),
        name="self_rows",
    )(spot, *far(*x_pieces, *weights))
    return outs[:count], *outs[count:]


def key_values_kernel(masks, number, edge, spot_ref, keys_ref, *refs):
    w_refs, (out_ref, w_all, done) = refs[:number], refs[number:]

    @pl.when(pl.program_id(0) == 0)
    def _():
        columns = (edge, edge + w_all.shape[1])
        run(weight_copies(w_refs, masks, spot_ref[0], columns, w_all, done, 0))

    out_ref[...] = product(keys_ref[...], w_all[...]).astype(BF16)


def key_values(keys, weights, spot, chunk, edge, masks):
    width = keys.shape[1]
    columns = 2 * width
    return pl.pallas_call(
        functools.partial(key_values_kernel, masks, len(weights), edge),
        out_shape=pltpu.HBM((keys.shape[0], columns), BF16),
        grid_spec=pltpu.PrefetchScalarGridSpec(
            num_scalar_prefetch=1,
            grid=(keys.shape[0] // chunk,),
            in_specs=[pl.BlockSpec((chunk, width), lambda i, spot: (i, 0))] + [HBM] * len(weights),
            out_specs=pl.BlockSpec((chunk, columns), lambda i, spot: (i, 0)),
            scratch_shapes=[
                pltpu.VMEM((width, columns), BF16),
                pltpu.SemaphoreType.DMA((blocks_in(weights),)),
            ],
        ),
        compiler_params=vmem(32),
        cost_estimate=cost(4),
        name="key_values",
    )(spot, *far(keys, *weights))


def rows_forward_kernel(masks, counts, broad, spot_ref, *refs):
    seq_count, weights = counts
    a_refs, refs = refs[:seq_count], refs[seq_count:]
    w_refs, refs = refs[:weights], refs[weights:]
    x_ref, gain_ref, live_ref, k_ref, v_ref = refs[:5]
    a1_ref, n2_ref, q2_ref, a2_ref, h1_ref, h2_ref, n3_ref = refs[5:12]
    a_all, w_o1, w_q2, w_o2, q_parts, o_parts, done = refs[12:]
    step = pl.program_id(0)
    me, seq = spot_ref[0], spot_ref[1]
    width = x_ref.shape[1]
    parts = q_parts.shape[0]

    @pl.when(step == 0)
    def _():
        copies = [
            pltpu.make_async_copy(
                ref, a_all.at[lax.rem(seq - k + seq_count, seq_count)], done.at[k]
            )
            for k, ref in enumerate(a_refs)
        ]
        edge = 3 * broad
        for i, target in ((0, w_o1), (1, w_q2), (4, w_o2)):
            columns = (edge + i * width, edge + (i + 1) * width)
            copies += weight_copies(w_refs, masks, me, columns, target, done, len(copies))
        run(copies)
        a1 = jnp.concatenate([a_all[j] for j in range(seq_count)], axis=1)
        a1_ref[...] = a1
        h1 = x_ref[...].astype(F32) + right_product(a1, w_o1[...])
        h1_ref[...] = h1
        n2 = (h1 * norm_scale(h1) * gain_ref[1:2]).astype(BF16)
        n2_ref[...] = n2
        q2 = product(n2, w_q2[...]).astype(BF16)
        q2_ref[...] = q2
        for i in range(parts):
            q_parts[i] = q2[:, i * LANES : (i + 1) * LANES]

    values_t = transposed(v_ref[...])
    queries = q_parts[step]
    live = live_ref[...]
    pieces = []
    for head in range(LANES // HEAD_DIM):
        powers, inverse = soft_parts(cross_scores(k_ref[...], pick_head(queries, head), live))
        lines = values_t[head * HEAD_DIM : (head + 1) * HEAD_DIM]
        pieces.append(product(lines, powers.astype(BF16)) * inverse)
    o_parts[step] = jnp.concatenate(pieces, axis=0).T.astype(BF16)

    @pl.when(step == parts - 1)
    def _():
        a2 = jnp.concatenate([o_parts[i] for i in range(parts)], axis=1)
        a2_ref[...] = a2
        h2 = h1_ref[...] + right_product(a2, w_o2[...])
        h2_ref[...] = h2
        n3_ref[...] = (h2 * norm_scale(h2) * gain_ref[2:3]).astype(BF16)


def rows_forward(a_pieces, weights, x, gains, live, kv, spot, broad, masks):
    count = len(a_pieces)
    rows, width = x.shape
    keys = kv.shape[0]
    parts = width // LANES
    slim = a_pieces[0].shape[1]
    flat = (rows, width)
    whole = lambda shape: pl.BlockSpec(shape, lambda i, spot: (0, 0))
    key = pl.BlockSpec((keys, LANES), lambda i, spot: (0, i))
    value = pl.BlockSpec((keys, LANES), lambda i, spot: (0, i + parts))
    low, full = (flat, BF16), (flat, F32)
    square = pltpu.VMEM((width, width), BF16)
    piece = pltpu.VMEM((parts, rows, LANES), BF16)
    return pl.pallas_call(
        functools.partial(rows_forward_kernel, masks, (count, len(weights)), broad),
        out_shape=far_out([low, low, low, low, full, full, low]),
        grid_spec=pltpu.PrefetchScalarGridSpec(
            num_scalar_prefetch=1,
            grid=(parts,),
            in_specs=[HBM] * (count + len(weights))
            + [whole(flat), whole(gains.shape), whole(live.shape), key, value],
            out_specs=[whole(flat)] * 7,
            scratch_shapes=[
                pltpu.VMEM((count, rows, slim), BF16),
                square, square, square, piece, piece,
                pltpu.SemaphoreType.DMA((count + 3 * blocks_in(weights),)),
            ],
        ),
        compiler_params=vmem(max(40, keys * 8 // 1024 + 8)),
        cost_estimate=cost(14),
        name="rows_forward",
    )(spot, *far(*a_pieces, *weights, x, gains, live, kv, kv))


def cross_backward(queries, upstream, live, keys, values):
    keys_t = transposed(keys)
    pieces, dk, dv = [], 0.0, 0.0
    for head in range(LANES // HEAD_DIM):
        own = pick_head(queries, head)
        up_own = pick_head(upstream, head)
        powers, inverse = soft_parts(cross_scores(keys, own, live))
        chance = powers * inverse
        inner = right_product(values, up_own)
        spread = jnp.sum(chance * inner, axis=0, keepdims=True)
        grad = (chance * (inner - spread) * SCALING).astype(BF16)
        dv = dv + product(chance.astype(BF16), up_own)
        dk = dk + product(grad, own)
        lines = keys_t[head * HEAD_DIM : (head + 1) * HEAD_DIM]
        pieces.append(product(lines, grad))
    return jnp.concatenate(pieces, axis=0).T.astype(BF16), dk.astype(BF16), dv.astype(BF16)


def rows_early_kernel(masks, weights, edge, spot_ref, *refs):
    w_refs, refs = refs[:weights], refs[weights:]
    c2_ref, live_ref, q_ref, k_ref, v_ref, up_ref, dq_ref, dk_ref, dv_ref = refs[:9]
    w_o2, up_parts, done = refs[9:]
    width = c2_ref.shape[1]

    @pl.when(pl.program_id(0) == 0)
    def _():
        columns = (edge + 4 * width, edge + 5 * width)
        run(weight_copies(w_refs, masks, spot_ref[0], columns, w_o2, done, 0))
        up = product(c2_ref[...], w_o2[...]).astype(BF16)
        up_ref[...] = up
        for i in range(up_parts.shape[0]):
            up_parts[i] = up[:, i * LANES : (i + 1) * LANES]

    dq_ref[...], dk_ref[...], dv_ref[...] = cross_backward(
        q_ref[...], up_parts[pl.program_id(0)], live_ref[...], k_ref[...], v_ref[...]
    )


def rows_late_kernel(masks, counts, edge, spot_ref, *refs):
    seq_count, weights = counts
    w_refs, refs = refs[:weights], refs[weights:]
    up_ref, dq_early_ref, dh2_ref, h1_ref, gain_ref, live_ref, q_ref, k_ref, v_ref = refs[:9]
    da_refs, refs = refs[9 : 9 + seq_count], refs[9 + seq_count :]
    dq2_ref, dk_ref, dv_ref, dh1_ref, c1_ref, gain_grad_ref = refs[:6]
    w_o1, w_q2, dq_parts, da_all, done = refs[6:]
    step = pl.program_id(0)
    me, seq = spot_ref[0], spot_ref[1]
    width = dh2_ref.shape[1]
    parts = dq_parts.shape[0]
    copies = weight_copies(
        w_refs, masks, me, (edge + width, edge + 2 * width), w_q2, done, 0
    )
    copies += weight_copies(w_refs, masks, me, (edge, edge + width), w_o1, done, len(copies))

    @pl.when(step == 0)
    def _():
        for copy in copies:
            copy.start()

    dq_parts[step], dk_ref[...], dv_ref[...] = cross_backward(
        q_ref[...], up_ref[...], live_ref[...], k_ref[...], v_ref[...]
    )

    @pl.when(step == parts - 1)
    def _():
        for copy in copies:
            copy.wait()
        dq2 = jnp.concatenate([dq_early_ref[...]] + [dq_parts[i] for i in range(parts)], axis=1)
        dq2_ref[...] = dq2
        dn2 = right_product(dq2, w_q2[...])
        h1 = h1_ref[...]
        scale = norm_scale(h1)
        dh1 = dh2_ref[...] + norm_hidden_grad(h1, scale, gain_ref[1:2], dn2)
        dh1_ref[...] = dh1
        gain_grad_ref[...] = jnp.sum(dn2 * h1 * scale, axis=0, keepdims=True)
        c1 = dh1.astype(BF16)
        c1_ref[...] = c1
        up = product(c1, w_o1[...])
        slim = da_all.shape[2]
        for j in range(seq_count):
            da_all[j] = up[:, j * slim : (j + 1) * slim].astype(BF16)
        for k, ref in enumerate(da_refs):
            ref[...] = da_all[lax.rem(seq + k, seq_count)]


def rows_specs(rows, keys, width, start):
    parts = width // LANES
    row = pl.BlockSpec((rows, LANES), lambda i, spot: (0, i + start))
    key = pl.BlockSpec((keys, LANES), lambda i, spot: (0, i + start))
    value = pl.BlockSpec((keys, LANES), lambda i, spot: (0, i + start + parts))
    return row, key, value


def rows_early(weights, c2, live, q2, kv, spot, edge, masks):
    rows, width = c2.shape
    keys = kv.shape[0]
    parts = width // LANES // 2
    whole = lambda shape: pl.BlockSpec(shape, lambda i, spot: (0, 0))
    row, key, value = rows_specs(rows, keys, width, 0)
    half = width // 2
    shapes = [((rows, width), BF16), ((rows, half), BF16)] + [((keys, half), BF16)] * 2
    return pl.pallas_call(
        functools.partial(rows_early_kernel, masks, len(weights), edge),
        out_shape=far_out(shapes),
        grid_spec=pltpu.PrefetchScalarGridSpec(
            num_scalar_prefetch=1,
            grid=(parts,),
            in_specs=[HBM] * len(weights)
            + [whole((rows, width)), whole(live.shape), row, key, value],
            out_specs=[whole((rows, width)), row, key, key],
            scratch_shapes=[
                pltpu.VMEM((width, width), BF16),
                pltpu.VMEM((2 * parts, rows, LANES), BF16),
                pltpu.SemaphoreType.DMA((blocks_in(weights),)),
            ],
        ),
        compiler_params=vmem(max(40, keys * 8 // 1024 + 12)),
        cost_estimate=cost(10),
        name="rows_early",
    )(spot, *far(*weights, c2, live, q2, kv, kv))


def rows_late(weights, up, dq_early, dh2, h1, gains, live, q2, kv, spot, edge, masks):
    count = lax.axis_size("seq")
    rows, width = dh2.shape
    keys = kv.shape[0]
    parts = width // LANES // 2
    slim = width // count
    flat = (rows, width)
    half = width // 2
    whole = lambda shape: pl.BlockSpec(shape, lambda i, spot: (0, 0))
    row, key, value = rows_specs(rows, keys, width, parts)
    key_out = pl.BlockSpec((keys, LANES), lambda i, spot: (0, i))
    shapes = [((rows, slim), BF16)] * count + [
        (flat, BF16), ((keys, half), BF16), ((keys, half), BF16),
        (flat, F32), (flat, BF16), ((1, width), F32),
    ]
    square = pltpu.VMEM((width, width), BF16)
    outs = pl.pallas_call(
        functools.partial(rows_late_kernel, masks, (count, len(weights)), edge),
        out_shape=far_out(shapes),
        grid_spec=pltpu.PrefetchScalarGridSpec(
            num_scalar_prefetch=1,
            grid=(parts,),
            in_specs=[HBM] * len(weights)
            + [row, whole((rows, half)), whole(flat), whole(flat)]
            + [whole(gains.shape), whole(live.shape), row, key, value],
            out_specs=[whole((rows, slim))] * count
            + [whole(flat), key_out, key_out, whole(flat), whole(flat), whole((1, width))],
            scratch_shapes=[
                square, square,
                pltpu.VMEM((parts, rows, LANES), BF16),
                pltpu.VMEM((count, rows, slim), BF16),
                pltpu.SemaphoreType.DMA((2 * blocks_in(weights),)),
            ],
        ),
        compiler_params=vmem(max(40, keys * 8 // 1024 + 12)),
        cost_estimate=cost(11),
        name="rows_late",
    )(spot, *far(*weights, up, dq_early, dh2, h1, gains, live, q2, kv, kv))
    return outs[:count], *outs[count:]


def turn_of(source_ref, width):
    columns = lax.broadcasted_iota(jnp.int32, (width, width), 1)
    return (columns == source_ref[...]).astype(F32).astype(BF16)


def cross_weights_kernel(masks, number, edge, spot_ref, *refs):
    w_refs, refs = refs[:number], refs[number:]
    source_ref, n2_ref, dq2_ref, c2_ref, a2_ref, keys_ref = refs[:6]
    parts, refs = refs[6:10], refs[10:]
    near_ref, far_ref, dmem_ref = refs[:3]
    w_all, turn, dk_sum, dv_sum, done = refs[3:]
    dk = jnp.concatenate([parts[0][...], parts[1][...]], axis=1)
    dv = jnp.concatenate([parts[2][...], parts[3][...]], axis=1)
    step, steps = pl.program_id(0), pl.num_programs(0)
    width = dq2_ref.shape[1]
    half = width // 2
    columns = (edge + 2 * width, edge + 4 * width)
    copies = weight_copies(w_refs, masks, spot_ref[0], columns, w_all, done, 0)

    def put(column, values):
        values = values.astype(BF16)
        near_ref[:, column : column + width] = values[:half]
        far_ref[:, column : column + width] = values[half:]

    @pl.when(step == 0)
    def _():
        for copy in copies:
            copy.start()
        turn[...] = turn_of(source_ref, width)
        n2_t = right_product(turn[...], n2_ref[...]).astype(BF16)
        put(0, product(n2_t, dq2_ref[...]))
        c2_t = right_product(turn[...], c2_ref[...]).astype(BF16)
        put(3 * width, product(c2_t, a2_ref[...]))
        dk_sum[...] = jnp.zeros_like(dk_sum)
        dv_sum[...] = jnp.zeros_like(dv_sum)

    keys_t = right_product(turn[...], keys_ref[...]).astype(BF16)
    dk_sum[...] += product(keys_t, dk)
    dv_sum[...] += product(keys_t, dv)

    @pl.when(step == 0)
    def _():
        for copy in copies:
            copy.wait()

    dmem_ref[...] = (
        right_product(dk, w_all[:, :width]) + right_product(dv, w_all[:, width:])
    ).astype(BF16)

    @pl.when(step == steps - 1)
    def _():
        put(width, dk_sum[...])
        put(2 * width, dv_sum[...])


def cross_weights(weights, source, n2, dq2, c2, a2, keys, grads, spot, chunk, edge, masks):
    rows, width = n2.shape
    whole = lambda shape: pl.BlockSpec(shape, lambda i, spot: (0, 0))
    part = pl.BlockSpec((chunk, width), lambda i, spot: (i, 0))
    half = ((width // 2, 4 * width), BF16)
    return pl.pallas_call(
        functools.partial(cross_weights_kernel, masks, len(weights), edge),
        out_shape=far_out([half, half, (keys.shape, BF16)]),
        grid_spec=pltpu.PrefetchScalarGridSpec(
            num_scalar_prefetch=1,
            grid=(keys.shape[0] // chunk,),
            in_specs=[HBM] * len(weights)
            + [whole(source.shape)]
            + [whole((rows, width))] * 4
            + [part]
            + [pl.BlockSpec((chunk, width // 2), lambda i, spot: (i, 0))] * 4,
            out_specs=[whole(half[0]), whole(half[0]), part],
            scratch_shapes=[
                pltpu.VMEM((width, 2 * width), BF16),
                pltpu.VMEM((width, width), BF16),
                pltpu.VMEM((width, width), F32),
                pltpu.VMEM((width, width), F32),
                pltpu.SemaphoreType.DMA((blocks_in(weights),)),
            ],
        ),
        compiler_params=vmem(48),
        cost_estimate=cost(10),
        name="cross_weights",
    )(spot, *far(*weights, source, n2, dq2, c2, a2, keys, *grads))


def self_backward_kernel(heads, masks, counts, spot_ref, *refs):
    seq_count, weights = counts
    up_refs, refs = refs[:seq_count], refs[seq_count:]
    x_refs, refs = refs[:3], refs[3:]
    x_list = [x_refs[0], x_refs[1], x_refs[2].at[0], x_refs[2].at[1]]
    w_refs, refs = refs[:weights], refs[weights:]
    qkv_ref, refs = refs[0], refs[1:]
    dn_refs, refs = refs[:2], refs[2:]
    steps = seq_masks(lax.rem(spot_ref[0], 2))
    dqkv_ref, gain_grad_ref = refs[:2]
    up_all, x_all, w_all, dn_all, dk_sum, dv_sum, done = refs[2:]
    rows = up_refs[0].shape[0]
    broad = w_all.shape[1] // 3
    slim = heads * HEAD_DIM
    me, seq = spot_ref[0], spot_ref[1]
    spots = [lax.rem(seq - k + seq_count, seq_count) for k in range(seq_count)]
    early = [
        pltpu.make_async_copy(ref, up_all.at[spots[k]], done.at[k])
        for k, ref in enumerate(up_refs)
    ]
    late = [
        pltpu.make_async_copy(ref, x_all.at[jnp.bitwise_xor(seq, mask)], done.at[seq_count + k])
        for k, (ref, mask) in enumerate(zip(x_list, steps))
    ]
    late += weight_copies(w_refs, masks, me, (0, 3 * broad), w_all, done, 2 * seq_count)
    for copy in early + late:
        copy.start()
    keys_t = transposed(qkv_ref[:, broad : 2 * broad])
    dk_sum[...] = jnp.zeros_like(dk_sum)
    dv_sum[...] = jnp.zeros_like(dv_sum)
    blank = jnp.zeros((rows, broad - slim), BF16)
    for copy in early:
        copy.wait()
    for j in range(seq_count):
        first, last = j * rows, (j + 1) * rows
        queries = qkv_ref[first:last, :broad]
        upstream = jnp.concatenate([up_all[j], blank], axis=1)
        parts = []
        for head in range(heads):
            own = pick_head(queries, head)
            up_own = pick_head(upstream, head)
            keys = qkv_ref[:last, broad : 2 * broad]
            powers, inverse = soft_parts(causal_scores(keys, own, first))
            chance = powers * inverse
            inner = right_product(qkv_ref[:last, 2 * broad :], up_own)
            spread = jnp.sum(chance * inner, axis=0, keepdims=True)
            grad = (chance * (inner - spread) * SCALING).astype(BF16)
            dv_sum[:last] += product(chance.astype(BF16), up_own)
            dk_sum[:last] += product(grad, own)
            lines = keys_t[head * HEAD_DIM : (head + 1) * HEAD_DIM, :last]
            parts.append(product(lines, grad))
        rest = jnp.zeros((broad - slim, rows), F32)
        dqkv_ref[first:last, :broad] = jnp.concatenate(parts + [rest], axis=0).T.astype(BF16)
    dqkv_ref[:, broad : 2 * broad] = dk_sum[...].astype(BF16)
    dqkv_ref[:, 2 * broad :] = dv_sum[...].astype(BF16)
    for copy in late:
        copy.wait()
    total = 0.0
    for j in range(seq_count):
        dn1 = right_product(dqkv_ref[j * rows : (j + 1) * rows], w_all[...])
        x = x_all[j].astype(F32)
        total = total + jnp.sum(dn1 * x * norm_scale(x), axis=0, keepdims=True)
        dn_all[j] = dn1.astype(BF16)
    gain_grad_ref[...] = total
    for k, mask in enumerate(steps):
        dn_refs[k // 2][k % 2] = dn_all[jnp.bitwise_xor(seq, mask)]


def self_backward(up_pieces, x_pieces, weights, qkv, spot, heads, masks):
    count = len(up_pieces)
    rows, width = x_pieces[0].shape
    slim = up_pieces[0].shape[1]
    length, broad = qkv.shape[0], qkv.shape[1] // 3
    whole = lambda shape: pl.BlockSpec(shape, lambda i, spot: (0, 0))
    shapes = [((2, rows, width), BF16)] * 2 + [(qkv.shape, BF16), ((1, width), F32)]
    outs = pl.pallas_call(
        functools.partial(self_backward_kernel, heads, masks, (count, len(weights))),
        out_shape=far_out(shapes),
        grid_spec=pltpu.PrefetchScalarGridSpec(
            num_scalar_prefetch=1,
            grid=(1,),
            in_specs=[HBM] * (count + 3 + len(weights)) + [whole(qkv.shape)],
            out_specs=[
                pl.BlockSpec(s, lambda i, spot, n=len(s): (0,) * n) for s, _ in shapes
            ],
            scratch_shapes=[
                pltpu.VMEM((count, rows, slim), BF16),
                pltpu.VMEM((count, rows, width), BF16),
                pltpu.VMEM((width, 3 * broad), BF16),
                pltpu.VMEM((count, rows, width), BF16),
                pltpu.VMEM((length, broad), F32),
                pltpu.VMEM((length, broad), F32),
                pltpu.SemaphoreType.DMA((2 * count + blocks_in(weights),)),
            ],
        ),
        compiler_params=vmem(48),
        cost_estimate=cost(13),
        name="self_backward",
    )(spot, *far(*up_pieces, *x_pieces, *weights, qkv))
    return outs


def self_weights_kernel(source_ref, n1_ref, dqkv_ref, c1_ref, a1_ref, gain_ref, near_ref, far_ref):
    width = n1_ref.shape[1]
    half = width // 2
    turn = turn_of(source_ref, width)
    column = 0

    def put(values):
        nonlocal column
        values = values.astype(BF16)
        near_ref[:, column : column + values.shape[1]] = values[:half]
        far_ref[:, column : column + values.shape[1]] = values[half:]
        column += values.shape[1]

    c1_t = right_product(turn, c1_ref[...]).astype(BF16)
    put(product(c1_t, a1_ref[...]))
    put(right_product(turn, gain_ref[...].astype(BF16)))
    n1_t = right_product(turn, n1_ref[...]).astype(BF16)
    put(product(n1_t, dqkv_ref[...]))


def self_weights(source, n1, dqkv, c1, a1, gain_grads):
    width = n1.shape[1]
    half = ((width // 2, width + LANES + dqkv.shape[1]), BF16)
    return pl.pallas_call(
        self_weights_kernel,
        out_shape=far_out([half, half]),
        compiler_params=vmem(40),
        cost_estimate=cost(6),
        name="self_weights",
    )(*far(source, n1, dqkv, c1, a1), gain_grads)


def last_rows_kernel(keep_ref, one_ref, two_ref, x_ref, dh1_ref, gain_ref, out_ref):
    dn1 = keep_ref[0].astype(F32) + one_ref[0].astype(F32) + two_ref[...].astype(F32)
    x = x_ref[...].astype(F32)
    out_ref[...] = (
        dh1_ref[...] + norm_hidden_grad(x, norm_scale(x), gain_ref[0:1], dn1)
    ).astype(BF16)


def last_rows(keep, one, two, x, dh1, gains):
    return pl.pallas_call(
        last_rows_kernel,
        out_shape=pltpu.HBM(x.shape, BF16),
        compiler_params=vmem(16),
        cost_estimate=cost(2),
        name="last_rows",
    )(*far(keep, one, two, x, dh1, gains))


def finish_kernel(slim, broad, spot_ref, *refs):
    sources, outs, hold = refs[:9], refs[9:-1], refs[-1]

    def total(refs, columns):
        keep, one, two = refs
        return (
            keep[0, :, columns[0] : columns[1]].astype(F32)
            + one[0, :, columns[0] : columns[1]].astype(F32)
            + two[0, :, columns[0] : columns[1]].astype(F32)
        )

    pair, down, rest = sources[0:3], sources[3:6], sources[6:9]
    hidden, width = outs[0].shape[1], outs[2].shape[1]
    outs[0][...] = total(pair, (0, hidden))
    outs[1][...] = total(pair, (hidden, 2 * hidden))
    outs[2][...] = total(down, (0, width))
    for i in range(5):
        outs[3 + i][...] = total(rest, (i * width, (i + 1) * width))
    edge = 5 * width
    outs[-1][...] = total(rest, (edge, edge + LANES))
    edge = edge + LANES
    far_edge = edge + 3 * broad
    keep, one, two = rest
    steps = [jnp.bitwise_xor(spot_ref[1], m) for m in seq_masks(lax.rem(spot_ref[0], 2))]
    hold[steps[0]] = keep[0, :, edge:far_edge].astype(F32)
    hold[steps[1]] = two[0, :, edge:far_edge].astype(F32)
    hold[steps[2]] = one[0, :, edge:far_edge].astype(F32)
    hold[steps[3]] = two[0, :, far_edge : far_edge + 3 * broad].astype(F32)
    for i in range(3):
        outs[8 + i][...] = jnp.concatenate(
            [hold[j][:, i * broad : i * broad + slim] for j in range(hold.shape[0])], axis=1
        )


def finish(pair, down, rest, spot, hidden, slim, broad):
    share, feed_share, width = pair[0].shape[1], down[0].shape[1], down[0].shape[2]
    count = lax.axis_size("seq")
    shapes = (
        [(share, hidden)] * 2 + [(feed_share, width)] + [(share, width)] * 8 + [(share, LANES)]
    )
    whole = lambda shape: pl.BlockSpec(shape, lambda i, spot: (0,) * len(shape))
    flat = [*pair, *down, *rest]
    return pl.pallas_call(
        functools.partial(finish_kernel, slim, broad),
        out_shape=far_out([(shape, F32) for shape in shapes]),
        grid_spec=pltpu.PrefetchScalarGridSpec(
            num_scalar_prefetch=1,
            grid=(1,),
            in_specs=[whole(a.shape) for a in flat],
            out_specs=[whole(shape) for shape in shapes],
            scratch_shapes=[pltpu.VMEM((count, share, 3 * broad), F32)],
        ),
        compiler_params=vmem(24),
        cost_estimate=cost(3),
        name="finish",
    )(spot, *far(*flat))


def local(
    hidden_in,
    memory,
    cotangent,
    norm_self,
    query_self,
    key_self,
    value_self,
    output_self,
    norm_cross,
    query_cross,
    key_cross,
    value_cross,
    output_cross,
    norm_feed,
    gate_weight,
    up_weight,
    down_weight,
    block_counts,
    memory_tail,
    row_example,
):
    mem_count, seq_count = lax.axis_size("mem"), lax.axis_size("seq")
    mem_place, seq_place = lax.axis_index("mem"), lax.axis_index("seq")
    rows, width = hidden_in.shape[1], hidden_in.shape[2]
    inner = HEADS * HEAD_DIM
    near = HEADS // seq_count
    slim = near * HEAD_DIM
    broad = -(-(slim + 8) // LANES) * LANES
    share = norm_self.shape[0]
    hidden_width = gate_weight.shape[1]
    spot = jnp.stack([mem_place, seq_place]).astype(jnp.int32)
    scalars = jnp.concatenate([block_counts, memory_tail, row_example])
    masks = slot_masks(mem_count)
    mask_array = mem_masks()
    block = width // mem_count
    column = jnp.arange(width, dtype=jnp.int32)
    source = (block * (mem_place ^ jnp.repeat(mask_array, block)) + column % block).reshape(width, 1)
    gain_stack = jnp.stack([norm_self, norm_cross, norm_feed], axis=0)
    x_own = hidden_in[0]
    edge = 3 * broad
    turns = mem_count.bit_length() - 2
    flat = lambda stacked: stacked.reshape((1, -1) + stacked.shape[2:])

    with jax.named_scope("gather"):
        own, two, one, second, blocks, live = prepare(
            (query_self, key_self, value_self, output_self, query_cross)
            + (key_cross, value_cross, output_cross, gate_weight, up_weight),
            gain_stack, memory, scalars, spot, slim, broad,
        )
        live = live.reshape(-1, 1)
        stay, go = part_blocks(blocks, 0)
        two, arrived = swap_seq(two, 0), swap_mem(go, 0)
        two, blocks, one, second, x_in, down_in = settle(
            two, join_blocks(stay, arrived), one, second, x_own, down_weight
        )
        three = swap_seq(jnp.stack([one, two[:, edge:]]), 1)
        for turn in range(1, turns):
            stay, go = part_blocks(blocks, turn)
            blocks = join_blocks(stay, swap_mem(go, turn))
        three, blocks, second, x_in, down_in = settle(three, blocks, second, x_in, down_in)
        first_width = edge + 5 * width
        first = flat(
            place(
                [own[None], two[None], three],
                seq_places(),
                [first_width],
                [
                    [(0, 0, 0, first_width)],
                    [(0, 0, 0, edge), (0, edge, 2 * edge, 5 * width)],
                    [(0, 0, 0, first_width)],
                ],
            )
        )
        held = [first]
        held.append(swap_mem(first, 0))
        stay, go = part_blocks(blocks, turns)
        keys_in = join_blocks(stay, swap_mem(go, turns)).reshape(-1, width)
        second_a, x_a = swap_seq(second, 0), swap_seq(x_in, 0)
        held, keys_in, second_a, x_a, second, x_in, down_in = settle(
            held, keys_in, second_a, x_a, second, x_in, down_in
        )
        for turn in range(1, turns):
            held.append(swap_mem(join(held), turn))
        second_b = swap_seq(jnp.stack([second, second_a]), 1)
        x_b = swap_seq(jnp.stack([x_in, x_a]), 1)
        held, second_b, x_b, second_a, second, x_a, x_in, down_in = settle(
            held, second_b, x_b, second_a, second, x_a, x_in, down_in
        )
        held = join(held)
        other = swap_mem(held, turns)
        both = [flat(stack_seq([second[None], second_a[None], second_b]))]
        both.append(swap_mem(both[0], 0))
        down_a = swap_seq(down_in, 0)
        held, other, both, down_a, down_in, x_in, x_a, x_b = settle(
            held, other, both, down_a, down_in, x_in, x_a, x_b
        )
        packed = spread_weight([held, other])

    key_chunk = width

    with jax.named_scope("forward"):
        x_pieces = [x_in, x_a, x_b]
        o_pieces, n1, qkv, gains = self_rows(x_pieces, packed, spot, near, broad, masks)
        for turn in range(1, turns):
            both.append(swap_mem(join(both), turn))
        down_b = swap_seq(jnp.stack([down_in, down_a]), 1)
        o_pieces, down_b, down_a, down_in, gains = settle(o_pieces, down_b, down_a, down_in, gains)
        a_pieces = send_seq(o_pieces)
        kv2 = key_values(keys_in, packed, spot, key_chunk, edge + 2 * width, masks)
        downs = [flat(stack_seq([down_in[None], down_a[None], down_b]))]
        downs.append(swap_mem(downs[0], 0))
        a_pieces, kv2, downs, both, keys_in = settle(a_pieces, kv2, downs, both, keys_in)
        a1, n2, q2, a2, h1, h2, n3 = rows_forward(
            a_pieces, packed, x_own, gains, live, kv2, spot, broad, masks
        )
        both = join(both)
        both_other = swap_mem(both, turns)
        for turn in range(1, turns):
            downs.append(swap_mem(join(downs), turn))
        h2, n3, both_other, both, downs = settle(h2, n3, both_other, both, downs)
        downs = join(downs)
        downs = [downs, swap_mem(downs, turns)]
        both = [w.reshape(-1, 2 * hidden_width) for w in (both, both_other)]
        unit = hidden_width // mem_count
        narrow = unit % LANES != 0
        if narrow:
            unit = 2 * LANES
            downs = stack_mem(downs).reshape(2, -1, width)
            downs = (downs[0], downs[1])
            feed_order = jnp.arange(hidden_width // unit, dtype=jnp.int32)
        else:
            feed_order = mem_place ^ mask_array
        downs = [w.reshape(-1, width) for w in downs]
        layer_out, dh2, c2, gain_feed_terms, *g_feed = feed(
            feed_order, h2, n3, cotangent[0], gains[2:3], source, both, downs
        )

    with jax.named_scope("backward"):
        g_both, g_down = g_feed[0:2], g_feed[2:4]
        if narrow:
            g_down = place(
                [jnp.concatenate(g_down).reshape(mem_count, -1, width)],
                jnp.argsort(mem_place ^ mask_array),
            ).reshape(2, -1, width)
        feeding, downing = Scatter(*g_both), Scatter(*g_down)
        feeding.move()
        downing.move()
        up, dq_early, dk_early, dv_early = rows_early(
            packed, c2, live, q2, kv2, spot, edge, masks
        )
        feeding.arrived, downing.arrived, up, dq_early = settle(
            feeding.arrived, downing.arrived, up, dq_early
        )
        advance([feeding, downing], spot)
        feeding.kept, feeding.sent, downing.kept, downing.sent, up = settle(
            feeding.kept, feeding.sent, downing.kept, downing.sent, up
        )
        feeding.move()
        da_pieces, dq2, dk_late, dv_late, dh1, c1, gain_cross_terms = rows_late(
            packed, up, dq_early, dh2, h1, gains, live, q2, kv2, spot, edge, masks
        )
        da_pieces, dq2 = settle(da_pieces, dq2)
        da_pieces = send_seq(da_pieces)
        *g_cross, dmem = cross_weights(
            packed, source, n2, dq2, c2, a2, keys_in,
            [dk_early, dk_late, dv_early, dv_late], spot, key_chunk, edge, masks,
        )
        crossing = Scatter(*g_cross)
        da_pieces, crossing.kept, crossing.sent, feeding.arrived, downing.sent, dmem = settle(
            da_pieces, crossing.kept, crossing.sent, feeding.arrived, downing.sent, dmem
        )
        crossing.move()
        downing.move()
        keep_dn, send_dn, dqkv, gain_self_terms = self_backward(
            da_pieces, x_pieces, packed, qkv, spot, near, masks
        )
        dmem = dmem.reshape(mem_count, -1, width)
        stay, go = part_blocks(dmem, turns)
        dmem = join_blocks(stay, swap_mem(go, turns))
        crossing.arrived, downing.arrived, keep_dn, send_dn, dqkv, dmem = settle(
            crossing.arrived, downing.arrived, keep_dn, send_dn, dqkv, dmem
        )
        one_dn = swap_seq(send_dn, 1)
        ends = [None, None, None]
        ends[0] = advance([feeding, crossing, downing], spot)
        for s in (feeding, crossing, downing):
            if s.left >= 0:
                s.move()
        gain_grads = jnp.concatenate(
            [gain_self_terms, gain_cross_terms, gain_feed_terms, jnp.zeros((LANES - 3, width), F32)]
        )
        g_self = self_weights(source, n1, dqkv, c1, a1, gain_grads)
        selfing = Scatter(*g_self)
        one_dn, keep_dn, feeding.arrived, crossing.arrived, downing.arrived, dmem = settle(
            one_dn, keep_dn, feeding.arrived, crossing.arrived, downing.arrived, dmem
        )
        two_dn = swap_seq(onward(keep_dn, one_dn)[0], 0)
        selfing.move()
        stay, go = part_blocks(dmem, 0)
        dmem = join_blocks(stay, swap_mem(go, 0))
        pending = [feeding, downing, crossing]
        while any(s.left > 0 for s in pending):
            for s in pending:
                if s.left > 0:
                    advance([s], spot)
                    s.move()
        ends[0] = advance([feeding], spot)
        ends[1] = advance([downing], spot)
        crossing.arrived, selfing.arrived, two_dn, dmem, ends[0], ends[1] = settle(
            crossing.arrived, selfing.arrived, two_dn, dmem, ends[0], ends[1]
        )
        hidden_grad = last_rows(keep_dn, one_dn, two_dn, x_own, dh1, gains)
        one_both, one_down = swap_seq(ends[0][1], 1), swap_seq(ends[1][1], 1)
        advance([selfing], spot)
        selfing.move()
        for turn in range(1, turns):
            stay, go = part_blocks(dmem, turn)
            dmem = join_blocks(stay, swap_mem(go, turn))
        one_both, one_down, selfing.arrived, dmem, hidden_grad = settle(
            one_both, one_down, selfing.arrived, dmem, hidden_grad
        )
        two_both = swap_seq(onward(ends[0][0], one_both), 0)
        two_down = swap_seq(onward(ends[1][0], one_down), 0)
        while selfing.left > 0:
            advance([selfing], spot)
            selfing.move()
        mem_keep, mem_send = pick_slots(dmem, memory.shape[0], scalars, spot)
        mem_one = swap_seq(mem_send, 1)
        two_both, two_down, selfing.arrived, mem_one, mem_keep = settle(
            two_both, two_down, selfing.arrived, mem_one, mem_keep
        )
        ends[2] = advance([crossing, selfing], spot)
        one_rest = swap_seq(ends[2][1], 1)
        mem_two = swap_seq(onward(mem_keep, mem_one), 0)
        one_rest, mem_two = settle(one_rest, mem_two)
        two_rest = swap_seq(onward(ends[2][0], one_rest, 4 * width + width + LANES), 0)
        per = mem_two.shape[0]
        memory_grad = total_of([mem_keep[:per], mem_one[:per], mem_two]).astype(BF16)
        *finals, gain_finals = finish(
            (ends[0][0], one_both, two_both),
            (ends[1][0], one_down, two_down),
            (ends[2][0], one_rest, two_rest),
            spot, hidden_width, slim, broad,
        )
    g_gate, g_up, g_down, g_q2, g_k2, g_v2, g_o2, g_o1, g_q1, g_k1, g_v1 = finals
    return (
        layer_out[None],
        hidden_grad[None],
        memory_grad,
        gain_finals[:, 0],
        g_q1,
        g_k1,
        g_v1,
        g_o1,
        gain_finals[:, 1],
        g_q2,
        g_k2,
        g_v2,
        g_o2,
        gain_finals[:, 2],
        g_gate,
        g_up,
        g_down,
    )


def solution(mesh):
    every = P(("mem", "seq"), None)
    gain = P(("mem", "seq"))
    in_specs = (
        (P("mem", "seq", None), P(None, "mem", None), P("mem", "seq", None), gain)
        + (every,) * 4
        + (gain,)
        + (every,) * 4
        + (gain,)
        + (every,) * 3
        + (P(),) * 3
    )
    out_specs = (
        (P("mem", "seq", None), P("mem", "seq", None), P("seq", "mem", None), gain)
        + (every,) * 4
        + (gain,)
        + (every,) * 4
        + (gain,)
        + (every,) * 3
    )
    return jax.shard_map(local, mesh=mesh, in_specs=in_specs, out_specs=out_specs, check_vma=False)
```

```python
import functools

import jax
import jax.numpy as jnp
from jax import lax
from jax.experimental import pallas as pl
from jax.experimental.pallas import tpu as pltpu
from jax.sharding import PartitionSpec as P

HEADS = 12
HEAD_DIM = 64
SCALING = HEAD_DIM ** (-0.5)
LANES = 128
MASKED = -1e30
F32 = jnp.float32
BF16 = jnp.bfloat16


def product(left, right):
    return jnp.dot(left, right, preferred_element_type=F32)


def left_product(left, right):
    return lax.dot_general(left, right, (((0,), (0,)), ((), ())), preferred_element_type=F32)


def right_product(left, right):
    return lax.dot_general(left, right, (((1,), (1,)), ((), ())), preferred_element_type=F32)


def gelu_tanh(values):
    return (
        0.5
        * values
        * (1.0 + jnp.tanh(0.7978845608028654 * (values + 0.044715 * values * values * values)))
    )


def gated_unit(gate, upper):
    return gelu_tanh(gate) * upper


def norm_scale(hidden):
    return lax.rsqrt(jnp.mean(hidden * hidden, axis=-1, keepdims=True) + 1e-06)


def norm_hidden_grad(hidden, scale, gain, upstream):
    lifted = upstream * gain
    return scale * lifted - hidden * (scale * scale * scale) * jnp.mean(
        lifted * hidden, axis=-1, keepdims=True
    )


def shift(values, axis, step):
    size = lax.axis_size(axis)
    return lax.ppermute(values, axis, [(i, (i + step) % size) for i in range(size)])


def swap(values, axis, mask):
    size = lax.axis_size(axis)
    return lax.ppermute(values, axis, [(i, i ^ mask) for i in range(size)])


def place_kernel(counts, maps, places, *refs):
    sources = refs[: len(counts)]
    targets, done = refs[len(counts) : -1], refs[-1]
    copies = []
    number = 0
    for source, count, moves in zip(sources, counts, maps):
        for block in range(count):
            for goal, to, start, width in moves:
                part, target = source.at[block], targets[goal].at[places[number]]
                if len(moves) > 1 or width != source.shape[2]:
                    part = source.at[block, :, start : start + width]
                    target = targets[goal].at[places[number], :, to : to + width]
                copies.append(pltpu.make_async_copy(part, target, done.at[len(copies)]))
            number += 1
    for copy in copies:
        copy.start()
    for copy in copies:
        copy.wait()


def place(pieces, places, widths=None, maps=None):
    counts = [piece.shape[0] for piece in pieces]
    total = sum(counts)
    _, height, width = pieces[0].shape
    widths = widths or [width]
    if maps is None:
        plain = [(i, 0, sum(widths[:i]), w) for i, w in enumerate(widths)]
        maps = [plain] * len(pieces)
    copies = sum(count * len(moves) for count, moves in zip(counts, maps))
    outs = [((total, height, w), pieces[0].dtype) for w in widths]
    size = total * height * sum(widths) * 2
    result = pl.pallas_call(
        functools.partial(place_kernel, counts, maps),
        out_shape=shaped(outs),
        grid_spec=pltpu.PrefetchScalarGridSpec(
            num_scalar_prefetch=1,
            grid=(1,),
            in_specs=[HBM] * len(pieces),
            out_specs=[
                pl.BlockSpec((total, height, w), lambda i, places: (0, 0, 0)) for w in widths
            ],
            scratch_shapes=[pltpu.SemaphoreType.DMA((copies,))],
        ),
        compiler_params=pltpu.CompilerParams(vmem_limit_bytes=3 * size + (4 << 20)),
        cost_estimate=cost(1 + size / 1e6),
        name="place",
    )(places.astype(jnp.int32), *pieces)
    return result[0] if len(widths) == 1 else result


def after(values, *tokens):
    return lax.optimization_barrier((values,) + tokens)[0]


def settle(*values):
    return lax.optimization_barrier(values)


def seq_masks(parity):
    return [0, 1 + parity, 2 - parity, 3]


def swap_seq(values, turn):
    mem, seq = lax.axis_size("mem"), lax.axis_size("seq")
    pairs = []
    for m in range(mem):
        mask = 1 + (m + turn) % 2
        pairs += [(m * seq + s, m * seq + (s ^ mask)) for s in range(seq)]
    return lax.ppermute(values, ("mem", "seq"), pairs)


def seq_places():
    parity = lax.axis_index("mem") % 2
    return lax.axis_index("seq") ^ jnp.stack(seq_masks(parity)).astype(jnp.int32)


def stack_seq(pieces, widths=None):
    return place(pieces, seq_places(), widths)


def send_seq(pieces):
    return [pieces[0]] + [shift(piece, "seq", k) for k, piece in enumerate(pieces) if k]


def total_of(pieces):
    return functools.reduce(jnp.add, [piece.astype(F32) for piece in pieces])


def join(blocks):
    return blocks[0] if len(blocks) == 1 else jnp.concatenate(blocks, axis=0)


def orders(count):
    bits = list(range(1, count.bit_length() - 1))
    return bits, bits[::-1]


def slot_masks(count):
    half = count // 2
    low = [
        [sum(((s >> j) & 1) << bit for j, bit in enumerate(order)) for s in range(half)]
        for order in orders(count)
    ]
    return low[0] + [m | 1 for m in low[1]], low[1] + [m | 1 for m in low[0]]


def swap_mem(values, turn):
    count = lax.axis_size("mem")
    pairs = []
    for i in range(count):
        order = [*orders(count)[i % 2], 0]
        pairs.append((i, i ^ (1 << order[turn])))
    return lax.ppermute(values, "mem", pairs)


def mem_masks():
    count = lax.axis_size("mem")
    even, odd = slot_masks(count)
    return jnp.where(
        lax.axis_index("mem") % 2 == 0, jnp.array(even, jnp.int32), jnp.array(odd, jnp.int32)
    )


def stack_mem(halves, widths=None):
    return place(halves, lax.axis_index("mem") ^ mem_masks(), widths)


def spread_weight(halves):
    if halves[0].shape[1] % 16 == 0:
        return list(halves)
    stacked = stack_mem(halves)
    return [stacked.reshape(1, -1, stacked.shape[-1])]


def add_low(left, right):
    return (left.astype(F32) + right.astype(F32)).astype(BF16)


def total_kernel(plans, spot_ref, *refs):
    terms = sum(number for number, _ in plans)
    sources, refs = list(refs[:terms]), refs[terms:]
    outs, holds = list(refs[: len(refs) - len(plans)]), refs[len(refs) - len(plans) :]
    column = 0
    for (number, ends), hold in zip(plans, holds):
        mine, sources = sources[:number], sources[number:]
        groups, rows, width = mine[0].shape
        for g in range(groups):
            total = mine[0][g].astype(F32)
            for ref in mine[1:]:
                total = total + ref[g].astype(F32)
            if not ends:
                outs[0][g] = total.astype(BF16)
                continue
            count = hold.shape[0]
            unit = rows // count
            for j in range(count):
                hold[j] = total[j * unit : (j + 1) * unit]
            for k, mask in enumerate(seq_masks(lax.rem(spot_ref[0], 2))):
                piece = hold[jnp.bitwise_xor(spot_ref[1], mask)].astype(BF16)
                outs[-2 + k // 2][k % 2, :, column : column + width] = piece
            column += width
        if not ends:
            del outs[:1]


class Scatter:
    def __init__(self, kept, sent):
        self.terms = [kept if kept.ndim == 3 else kept[None]]
        self.sent = sent if sent.ndim == 3 else sent[None]
        self.left = (lax.axis_size("mem") // 2).bit_length() - 1
        self.rows = self.terms[0].shape[1]

    def move(self):
        self.terms.append(swap_mem(self.sent, self.left))

    def hold(self):
        return [self.terms, self.sent]

    def take(self, held):
        self.terms, self.sent = held


def advance(scatters, spot):
    count = lax.axis_size("seq")
    plans, shapes, specs, flat, holds = [], [], [], [], []
    ended, exact = 0, True
    whole = lambda shape: pl.BlockSpec(shape, lambda i, spot: (0, 0, 0))
    for s in scatters:
        ends = s.left == 0
        groups, _, width = s.terms[0].shape
        rows = s.rows if ends else s.rows // 2
        exact = exact and rows // (count if ends else 1) % 8 == 0
        plans.append((len(s.terms), ends))
        part = (groups, rows, width)
        if ends:
            specs += [whole(part)] * len(s.terms)
            ended += groups * width
            unit = rows // count
            holds.append(pltpu.VMEM((count, unit, width), F32))
        else:
            specs += [pl.BlockSpec(part, lambda i, spot: (0, 1, 0))] * len(s.terms)
            shapes.append(part)
            holds.append(pltpu.VMEM((1, 8, 128), F32))
        flat += s.terms
    if ended:
        shapes += [(2, unit, ended)] * 2
    if exact:
        size = sum(spec.block_shape[0] * spec.block_shape[1] * spec.block_shape[2] for spec in specs)
        outs = pl.pallas_call(
            functools.partial(total_kernel, plans),
            out_shape=shaped([(shape, BF16) for shape in shapes]),
            grid_spec=pltpu.PrefetchScalarGridSpec(
                num_scalar_prefetch=1,
                grid=(1,),
                in_specs=specs,
                out_specs=[whole(shape) for shape in shapes],
                scratch_shapes=holds,
            ),
            compiler_params=vmem(6 + (size * 8 >> 20)),
            cost_estimate=cost(1 + size / 1e6),
            name="total",
        )(spot, *(far(*flat) if size > 1 << 20 else flat))
        outs = list(outs)
    else:
        outs, ends_at = [], []
        for s in scatters:
            low = 0 if s.left == 0 else s.rows // 2
            high = s.rows if s.left == 0 else 2 * low
            total = total_of([term[:, low:high] for term in s.terms]).astype(BF16)
            if s.left:
                outs.append(total)
                continue
            groups, rows, width = total.shape
            blocks = total.reshape(groups, count, rows // count, width)
            ends_at.append(jnp.take(jnp.concatenate(list(blocks), axis=2), seq_places(), axis=0))
        if ends_at:
            blocks = jnp.concatenate(ends_at, axis=2)
            outs += [blocks[:2], blocks[2:]]
    for s in scatters:
        if s.left:
            s.sent, s.rows = outs.pop(0), s.rows // 2
        s.left -= 1
    return outs or None


def onward(kept, arrived, summed=None):
    half = kept.shape[0] // 2
    mine, theirs = kept[half:], arrived[half:]
    if summed is None:
        return add_low(mine, theirs)
    return jnp.concatenate(
        [add_low(mine[..., :summed], theirs[..., :summed]), mine[..., summed:], theirs[..., summed:]],
        axis=-1,
    )


def part_blocks(blocks, turn):
    count = blocks.shape[0]
    parts = blocks.reshape((count >> (turn + 1), 2, 1 << turn) + blocks.shape[1:])
    return parts[:, 0], parts[:, 1]


def join_blocks(stay, arrived):
    joined = jnp.stack([stay, arrived], axis=1)
    return joined.reshape((-1,) + joined.shape[3:])


HBM = pl.BlockSpec(memory_space=pltpu.HBM)


def far(*arrays):
    return [pltpu.with_memory_space_constraint(array, pltpu.HBM) for array in arrays]


def shaped(shapes, distant=()):
    return [
        jax.ShapeDtypeStruct(shape, dtype)
        for i, (shape, dtype) in enumerate(shapes)
    ]


def vmem(mebibytes):
    return pltpu.CompilerParams(vmem_limit_bytes=mebibytes << 20)


def cost(microseconds):
    return pl.CostEstimate(
        flops=int(microseconds * 1.1e9), bytes_accessed=0, transcendentals=0
    )


def run(copies):
    for copy in copies:
        copy.start()
    for copy in copies:
        copy.wait()


def prepare_kernel(
    slim, broad, scalars_ref, spot_ref,
    q_ref, k_ref, v_ref, o1_ref, q2_ref, k2_ref, v2_ref, o2_ref, gate_ref, up_ref,
    gain_ref, memory_ref,
    own_ref, two_ref, one_ref, second_ref, blocks_ref, live_ref,
    turn, triple, held, done,
):
    mem_count, height = blocks_ref.shape[0], memory_ref.shape[1]
    share, width = q_ref.shape
    half = mem_count // 2
    me, seq = spot_ref[0], spot_ref[1]
    parity = lax.rem(me, 2)
    counts_at, tails_at, rows_at = 0, mem_count, 2 * mem_count
    moves = [(ref, triple.at[i]) for i, ref in enumerate((q_ref, k_ref, v_ref))]
    moves += [(memory_ref, held)]
    for ref, base in ((own_ref, 3 * broad), (one_ref, 3 * broad), (two_ref, 6 * broad)):
        for i, source in enumerate((o1_ref, q2_ref, k2_ref, v2_ref, o2_ref)):
            moves += [(source, ref.at[:, base + i * width : base + (i + 1) * width])]
    hidden = gate_ref.shape[1]
    moves += [(gate_ref, second_ref.at[:, :hidden]), (up_ref, second_ref.at[:, hidden:])]
    copies = [pltpu.make_async_copy(a, b, done.at[i]) for i, (a, b) in enumerate(moves)]
    for copy in copies:
        copy.start()
    turn[...] = jnp.zeros_like(turn)
    turn[0:3, 0:share] = gain_ref[...].astype(F32)
    gains = turn[...].T[:share]
    lane = lax.broadcasted_iota(jnp.int32, (share, broad - slim), 1)
    extra = jnp.zeros((share, broad - slim), F32)
    for i in range(3):
        extra = jnp.where(lane == i, gains[:, i : i + 1], extra)
    extra = extra.astype(BF16)
    blank = jnp.zeros((share, broad - slim), BF16)
    token = lax.broadcasted_iota(jnp.int32, (height, 1), 0)

    def first_block(example):
        return lax.fori_loop(
            0, example, lambda i, total: total + scalars_ref[counts_at + i], jnp.int32(0)
        )

    mine = scalars_ref[rows_at + me]
    mine_start = first_block(mine)
    mine_end = mine_start + scalars_ref[counts_at + mine]

    for copy in copies[:4]:
        copy.wait()

    order, contrary = orders(mem_count)

    def one(t, carry):
        low = lax.rem(t, half)
        first, second = jnp.int32(0), jnp.int32(0)
        for j in range(len(order)):
            bit = lax.rem(lax.shift_right_logical(low, jnp.int32(j)), 2)
            first = first + bit * (1 << order[j])
            second = second + bit * (1 << contrary[j])
        flip = parity == 1
        first, second = jnp.where(flip, second, first), jnp.where(flip, first, second)
        upper = t >= half
        goal = jnp.bitwise_xor(me, jnp.where(upper, first + 1, first))
        start = first_block(scalars_ref[rows_at + goal])
        block = start + lax.rem(me - lax.rem(start, mem_count) + mem_count, mem_count)
        slot = jnp.minimum(block // mem_count, memory_ref.shape[0] - 1)
        blocks_ref[t] = held[slot]
        holder = jnp.bitwise_xor(me, jnp.where(upper, second + 1, first))
        block = mine_start + lax.rem(
            holder - lax.rem(mine_start, mem_count) + mem_count, mem_count
        )
        bound = jnp.where(block == mine_end - 1, scalars_ref[tails_at + mine], height)
        bound = jnp.where(block < mine_end, bound, 0)
        live_ref[t] = jnp.where(token < bound, 0.0, MASKED)
        return carry

    lax.fori_loop(0, mem_count, one, 0)
    seq_steps = seq_masks(parity)
    for ref, base, mask in (
        (own_ref, 0, seq_steps[0]),
        (two_ref, 0, seq_steps[1]),
        (one_ref, 0, seq_steps[2]),
        (two_ref, 1, seq_steps[3]),
    ):
        goal = jnp.bitwise_xor(seq, mask)
        for i in range(3):
            weight = triple[i].astype(F32)
            chosen = weight[:, :slim]
            for j in range(1, width // slim):
                chosen = jnp.where(goal == j, weight[:, j * slim : (j + 1) * slim], chosen)
            start = (3 * base + i) * broad
            ref[:, start : start + broad] = jnp.concatenate(
                [chosen.astype(BF16), blank if i else extra], axis=1
            )
    for copy in copies[4:]:
        copy.wait()


def prepare(weights, gains, memory, scalars, spot, slim, broad):
    mem_count = lax.axis_size("mem")
    share, width = weights[0].shape
    first = 3 * broad + 5 * width
    second = sum(w.shape[1] for w in weights[8:])
    height = memory.shape[1]
    whole = lambda shape: pl.BlockSpec(shape, lambda *_: (0,) * len(shape))
    outs = [
        ((share, first), BF16),
        ((share, first + 3 * broad), BF16),
        ((share, first), BF16),
        ((share, second), BF16),
        ((mem_count, height, width), BF16),
        ((mem_count, height, 1), F32),
    ]
    return pl.pallas_call(
        functools.partial(prepare_kernel, slim, broad),
        out_shape=shaped(outs),
        grid_spec=pltpu.PrefetchScalarGridSpec(
            num_scalar_prefetch=2,
            grid=(1,),
            in_specs=[HBM] * len(weights) + [whole(gains.shape), HBM],
            out_specs=[whole(shape) for shape, _ in outs],
            scratch_shapes=[
                pltpu.VMEM((8, 128), F32),
                pltpu.VMEM((3, share, width), BF16),
                pltpu.VMEM(memory.shape, BF16),
                pltpu.SemaphoreType.DMA((4 + 15 + 2,)),
            ],
        ),
        compiler_params=vmem(16 + 3 * mem_count // 8),
        cost_estimate=cost(3),
        name="prepare",
    )(scalars, spot, *far(*weights), gains, *far(memory))


def slots_kernel(per, scalars_ref, spot_ref, blocks_ref, keep_ref, send_ref, done):
    mem_count = blocks_ref.shape[0]
    me, seq = spot_ref[0], spot_ref[1]
    parity = lax.rem(me, 2)
    copies = []
    for k, mask in enumerate(seq_masks(parity)):
        for s in range(per):
            slot = jnp.bitwise_xor(seq, mask) * per + s
            block = slot * mem_count + me

            def scan(i, carry):
                end, owner = carry
                end = end + scalars_ref[i]
                return end, owner + jnp.where(end <= block, 1, 0)

            _, owner = lax.fori_loop(0, mem_count, scan, (jnp.int32(0), jnp.int32(0)))
            row = lax.fori_loop(
                0,
                mem_count,
                lambda i, r: jnp.where(scalars_ref[2 * mem_count + i] == owner, i, r),
                jnp.int32(0),
            )
            gap = jnp.bitwise_xor(row, me)
            bit = lambda b: lax.rem(lax.shift_right_logical(gap, jnp.int32(b)), 2)
            spots = [
                sum(bit(b) * (1 << j) for j, b in enumerate(order)) for order in orders(mem_count)
            ]
            at = jnp.where(parity == 1, spots[1], spots[0]) + bit(0) * (mem_count // 2)
            copies.append(
                pltpu.make_async_copy(
                    blocks_ref.at[at],
                    (keep_ref, send_ref)[k // 2].at[k % 2 * per + s],
                    done.at[len(copies)],
                )
            )
    for copy in copies:
        copy.start()
    for copy in copies:
        copy.wait()


def pick_slots(blocks, slots, scalars, spot):
    per = slots // lax.axis_size("seq")
    shape = (2 * per,) + blocks.shape[1:]
    return pl.pallas_call(
        functools.partial(slots_kernel, per),
        out_shape=shaped([(shape, BF16)] * 2),
        grid_spec=pltpu.PrefetchScalarGridSpec(
            num_scalar_prefetch=2,
            grid=(1,),
            in_specs=[HBM],
            out_specs=[pl.BlockSpec(shape, lambda *_: (0, 0, 0))] * 2,
            scratch_shapes=[pltpu.SemaphoreType.DMA((slots,))],
        ),
        compiler_params=vmem(8),
        cost_estimate=cost(2),
        name="pick_slots",
    )(scalars, spot, blocks)


def feed_kernel(
    order_ref, h2_ref, c3_ref, gain_ref, source_ref,
    gate_a_ref, gate_b_ref, up_a_ref, up_b_ref, *refs,
):
    down_refs, refs = refs[:-16], refs[-16:]
    out_ref, dh2_ref, c2_ref, gain_grad_ref = refs[:4]
    gboth_a_ref, gboth_b_ref, gdown_a_ref, gdown_b_ref = refs[4:8]
    turn, n3_rel, n3_rel_t, total, dn3, gate_w, up_w, down_w = refs[8:]
    step, steps = pl.program_id(0), pl.num_programs(0)
    half = gate_a_ref.shape[0]
    width = h2_ref.shape[1]

    @pl.when(step == 0)
    def _():
        columns = lax.broadcasted_iota(jnp.int32, (width, width), 1)
        turn[...] = (columns == source_ref[...]).astype(F32).astype(BF16)
        h2 = h2_ref[...]
        n3 = (h2 * norm_scale(h2) * gain_ref[2:3]).astype(BF16)
        n3_rel[...] = right_product(n3, turn[...]).astype(BF16)
        n3_rel_t[...] = right_product(turn[...], n3).astype(BF16)
        total[...] = jnp.zeros_like(total)
        dn3[...] = jnp.zeros_like(dn3)

    base = 0
    for ref in down_refs:
        number = ref.shape[0]
        for block in range(number):

            @pl.when(step == base + block)
            def _(ref=ref, block=block):
                down_w[...] = ref[block]

        base += number
    gate_w[:half] = gate_a_ref[...]
    gate_w[half:] = gate_b_ref[...]
    up_w[:half] = up_a_ref[...]
    up_w[half:] = up_b_ref[...]
    first = step < steps // 2
    down = down_w[...]
    n3, c3 = n3_rel[...], c3_ref[...]
    gate = product(n3, gate_w[...])
    upper = product(n3, up_w[...])
    dact = right_product(c3, down)
    inner = 0.7978845608028654 * (gate + 0.044715 * gate * gate * gate)
    bent = jnp.tanh(inner)
    gelu = 0.5 * gate * (1.0 + bent)
    slope = 0.5 * (1.0 + bent) + 0.5 * gate * (1.0 - bent * bent) * (
        0.7978845608028654 * (1.0 + 3.0 * 0.044715 * gate * gate)
    )
    act = (gelu * upper).astype(BF16)
    dgate = (dact * upper * slope).astype(BF16)
    dupper = (dact * gelu).astype(BF16)
    total[...] += product(act, down)
    gdown = left_product(act, c3).astype(BF16)

    @pl.when(first)
    def _():
        gdown_a_ref[...] = gdown

    @pl.when(jnp.logical_not(first))
    def _():
        gdown_b_ref[...] = gdown

    dn3[...] += right_product(dgate, gate_w[...]) + right_product(dupper, up_w[...])
    ggate = product(n3_rel_t[...], dgate).astype(BF16)
    gup = product(n3_rel_t[...], dupper).astype(BF16)
    gboth_a_ref[0] = ggate[:half]
    gboth_b_ref[0] = ggate[half:]
    gboth_a_ref[1] = gup[:half]
    gboth_b_ref[1] = gup[half:]

    @pl.when(step == steps - 1)
    def _():
        h2 = h2_ref[...]
        out_ref[...] = (h2 + total[...]).astype(BF16)
        high = dn3[...].astype(BF16)
        rest = (dn3[...] - high.astype(F32)).astype(BF16)
        upstream = product(high, turn[...]) + product(rest, turn[...])
        scale = norm_scale(h2)
        dh2 = c3_ref[...].astype(F32) + norm_hidden_grad(h2, scale, gain_ref[2:3], upstream)
        dh2_ref[...] = dh2
        c2_ref[...] = dh2.astype(BF16)
        gain_grad_ref[...] = jnp.sum(upstream * h2 * scale, axis=0, keepdims=True)


def feed(order, h2, c3, gains, source, both, down):
    rows, width = h2.shape
    half, hidden = both[0].shape
    hidden = hidden // 2
    steps = order.shape[0]
    unit = hidden // steps
    middle = steps // 2
    whole = lambda shape: pl.BlockSpec(shape, lambda i, o: (0, 0))
    column = pl.BlockSpec((half, unit), lambda i, o: (0, o[i]))
    beside = pl.BlockSpec((half, unit), lambda i, o: (0, o[i] + steps))
    twice = pl.BlockSpec((2, half, unit), lambda i, o: (0, 0, o[i]))
    early = pl.BlockSpec((unit, width), lambda i, o: (jnp.minimum(i, middle - 1), 0))
    late = pl.BlockSpec((unit, width), lambda i, o: (jnp.maximum(i - middle, 0), 0))
    flat = (rows, width)
    return pl.pallas_call(
        feed_kernel,
        out_shape=shaped(
            [(flat, BF16), (flat, F32), (flat, BF16), ((1, width), F32)]
            + [((2, half, hidden), BF16)] * 2
            + [((hidden // 2, width), BF16)] * 2,
            (0, 1, 2, 4, 6),
        ),
        grid_spec=pltpu.PrefetchScalarGridSpec(
            num_scalar_prefetch=1,
            grid=(steps,),
            in_specs=[whole(flat)] * 2
            + [whole(gains.shape), whole((width, 1))]
            + [column, column, beside, beside]
            + [pl.BlockSpec(w.shape, lambda i, o: (0, 0, 0)) for w in down],
            out_specs=[whole(flat)] * 3 + [whole((1, width)), twice, twice, early, late],
            scratch_shapes=[
                pltpu.VMEM((width, width), BF16),
                pltpu.VMEM(flat, BF16),
                pltpu.VMEM((width, rows), BF16),
                pltpu.VMEM(flat, F32),
                pltpu.VMEM(flat, F32),
                pltpu.VMEM((2 * half, unit), BF16),
                pltpu.VMEM((2 * half, unit), BF16),
                pltpu.VMEM((unit, width), BF16),
            ],
        ),
        compiler_params=vmem(20),
        cost_estimate=cost(19),
        name="feed",
    )(order, h2, *far(c3), gains, source, *far(*both, *both), *down)


def head_mask(shape, head):
    return lax.broadcasted_iota(jnp.int32, shape, 1) // HEAD_DIM == head


def pick_head(values, head):
    return jnp.where(head_mask(values.shape, head), values, jnp.zeros_like(values))


def transposed(values):
    return values.astype(F32).T.astype(values.dtype)


LOG2E = 1.4426950408889634
SHRINK = SCALING * LOG2E


def soft_parts(scores, axis=0):
    peak = jnp.max(scores, axis=0, keepdims=True)
    powers = jnp.exp2(scores - peak)
    total = jnp.sum(powers, axis=0, keepdims=True)
    return powers, 1.0 / total, peak + jnp.log2(total)


def causal_scores(keys, queries):
    scores = right_product(keys, queries) * SHRINK
    last = scores.shape[0] - scores.shape[1]
    corner = scores[last:]
    key_place = lax.broadcasted_iota(jnp.int32, corner.shape, 0)
    query_place = lax.broadcasted_iota(jnp.int32, corner.shape, 1)
    corner = jnp.where(key_place <= query_place, corner, MASKED)
    return corner if last == 0 else jnp.concatenate([scores[:last], corner], axis=0)


def cross_scores(keys, queries, bias):
    return right_product(keys, queries) * SHRINK + bias


def score_grads(scores, logs, inner):
    chance = jnp.exp2(scores - logs)
    spread = jnp.sum(chance * inner, axis=0, keepdims=True)
    return chance.astype(BF16), (chance * (inner - spread)).astype(BF16)


def weight_copies(refs, masks, me, columns, target, done, base):
    copies = []
    for ref in refs:
        for block in range(ref.shape[0]):
            number = len(copies)
            spot = 0
            if len(refs) > 1:
                mask = masks[0][number]
                if masks[1][number] != mask:
                    mask = jnp.where(lax.rem(me, 2) == 1, masks[1][number], mask)
                spot = pl.multiple_of(jnp.bitwise_xor(me, mask) * ref.shape[1], 16)
            copies.append(
                pltpu.make_async_copy(
                    ref.at[block, :, columns[0] : columns[1]],
                    target.at[pl.ds(spot, ref.shape[1])],
                    done.at[base + number],
                )
            )
    return copies


def blocks_in(refs):
    return sum(ref.shape[0] for ref in refs)


def self_rows_kernel(heads, masks, counts, spot_ref, *refs):
    seq_count, weights = counts
    x_refs, refs = refs[:3], refs[3:]
    x_list = [x_refs[0], x_refs[1], x_refs[2].at[0], x_refs[2].at[1]]
    w_refs, refs = refs[:weights], refs[weights:]
    o_refs, refs = refs[:seq_count], refs[seq_count:]
    n1_ref, qkv_ref, gain_ref, log_ref, x_all, w_all, o_all, done = refs
    rows, width = x_refs[0].shape
    broad = w_all.shape[1] // 3
    me, seq = spot_ref[0], spot_ref[1]
    copies = weight_copies(w_refs, masks, me, (0, 3 * broad), w_all, done, 0)
    base = len(copies)
    copies += [
        pltpu.make_async_copy(ref, x_all.at[jnp.bitwise_xor(seq, mask)], done.at[base + k])
        for k, (ref, mask) in enumerate(zip(x_list, seq_masks(lax.rem(me, 2))))
    ]
    run(copies)
    slim = heads * HEAD_DIM
    edge = slim // LANES * LANES
    gains = w_all[:, edge : edge + LANES].astype(F32).T[slim - edge : slim - edge + 8]
    gain_ref[...] = gains
    for j in range(seq_count):
        x = x_all[j].astype(F32)
        n1 = (x * norm_scale(x) * gains[0:1]).astype(BF16)
        n1_ref[j * rows : (j + 1) * rows] = n1
        qkv_ref[j * rows : (j + 1) * rows] = product(n1, w_all[...]).astype(BF16)
    values_t = transposed(qkv_ref[:, 2 * broad :])
    for j in range(seq_count):
        first, last = j * rows, (j + 1) * rows
        queries = qkv_ref[first:last, :broad]
        parts = []
        for head in range(heads):
            scores = causal_scores(qkv_ref[:last, broad : 2 * broad], pick_head(queries, head))
            powers, inverse, logs = soft_parts(scores)
            log_ref[head : head + 1, first:last] = logs
            lines = values_t[head * HEAD_DIM : (head + 1) * HEAD_DIM, :last]
            parts.append(product(lines, powers.astype(BF16)) * inverse)
        o_all[j] = jnp.concatenate(parts, axis=0).T.astype(BF16)
    for k, ref in enumerate(o_refs):
        ref[...] = o_all[lax.rem(seq + k, seq_count)]


def self_rows(x_pieces, weights, spot, heads, broad, masks):
    count = lax.axis_size("seq")
    rows, width = x_pieces[0].shape
    length, slim = rows * count, heads * HEAD_DIM
    whole = lambda shape: pl.BlockSpec(shape, lambda i, spot: (0, 0))
    shapes = [((rows, slim), BF16)] * count + [
        ((length, width), BF16),
        ((length, 3 * broad), BF16),
        ((8, width), F32),
        ((8, length), F32),
    ]
    outs = pl.pallas_call(
        functools.partial(self_rows_kernel, heads, masks, (count, len(weights))),
        out_shape=shaped(shapes, (count, count + 1, count + 3)),
        grid_spec=pltpu.PrefetchScalarGridSpec(
            num_scalar_prefetch=1,
            grid=(1,),
            in_specs=[HBM] * (3 + len(weights)),
            out_specs=[whole(s) for s, _ in shapes],
            scratch_shapes=[
                pltpu.VMEM((count, rows, width), BF16),
                pltpu.VMEM((width, 3 * broad), BF16),
                pltpu.VMEM((count, rows, slim), BF16),
                pltpu.SemaphoreType.DMA((blocks_in(weights) + count,)),
            ],
        ),
        compiler_params=vmem(14),
        cost_estimate=cost(10),
        name="self_rows",
    )(spot, *x_pieces, *weights)
    return outs[:count], *outs[count:]


def key_values_kernel(masks, number, edge, spot_ref, keys_ref, *refs):
    w_refs, (out_ref, w_all, done) = refs[:number], refs[number:]

    @pl.when(pl.program_id(0) == 0)
    def _():
        columns = (edge, edge + w_all.shape[1])
        run(weight_copies(w_refs, masks, spot_ref[0], columns, w_all, done, 0))

    out_ref[...] = product(keys_ref[...], w_all[...]).astype(BF16)


def key_values(keys, weights, spot, chunk, edge, masks):
    width = keys.shape[1]
    columns = 2 * width
    return pl.pallas_call(
        functools.partial(key_values_kernel, masks, len(weights), edge),
        out_shape=jax.ShapeDtypeStruct((keys.shape[0], columns), BF16),
        grid_spec=pltpu.PrefetchScalarGridSpec(
            num_scalar_prefetch=1,
            grid=(keys.shape[0] // chunk,),
            in_specs=[pl.BlockSpec((chunk, width), lambda i, spot: (i, 0))] + [HBM] * len(weights),
            out_specs=pl.BlockSpec((chunk, columns), lambda i, spot: (i, 0)),
            scratch_shapes=[
                pltpu.VMEM((width, columns), BF16),
                pltpu.SemaphoreType.DMA((blocks_in(weights),)),
            ],
        ),
        compiler_params=vmem(12),
        cost_estimate=cost(4),
        name="key_values",
    )(spot, keys, *weights)


def rows_forward_kernel(masks, counts, broad, spot_ref, *refs):
    seq_count, weights = counts
    a_refs, refs = refs[:seq_count], refs[seq_count:]
    w_refs, refs = refs[:weights], refs[weights:]
    x_ref, gain_ref, live_ref, k_ref, v_ref = refs[:5]
    q2_ref, a2_ref, h1_ref, h2_ref, log_ref = refs[5:10]
    a_all, w_o1, w_q2, w_o2, q_parts, o_parts, done = refs[10:]
    step = pl.program_id(0)
    me, seq = spot_ref[0], spot_ref[1]
    width = x_ref.shape[1]
    parts = q_parts.shape[0]
    edge = 3 * broad

    def weights_at(i, base, target):
        columns = (edge + i * width, edge + (i + 1) * width)
        return weight_copies(w_refs, masks, me, columns, target, done, base)

    last = weights_at(4, seq_count + 2 * blocks_in(w_refs), w_o2)

    @pl.when(step == 0)
    def _():
        copies = [
            pltpu.make_async_copy(
                ref, a_all.at[lax.rem(seq - k + seq_count, seq_count)], done.at[k]
            )
            for k, ref in enumerate(a_refs)
        ]
        copies += weights_at(0, len(copies), w_o1)
        later = weights_at(1, len(copies), w_q2)
        for copy in copies + later + last:
            copy.start()
        for copy in copies:
            copy.wait()
        a1 = jnp.concatenate([a_all[j] for j in range(seq_count)], axis=1)
        h1 = x_ref[...].astype(F32) + right_product(a1, w_o1[...])
        h1_ref[...] = h1
        n2 = (h1 * norm_scale(h1) * gain_ref[1:2]).astype(BF16)
        for copy in later:
            copy.wait()
        q2 = product(n2, w_q2[...]).astype(BF16)
        q2_ref[...] = q2
        for i in range(parts):
            q_parts[i] = q2[:, i * LANES : (i + 1) * LANES]

    values_t = transposed(v_ref[...])
    queries = q_parts[step]
    live = live_ref[...]
    pieces = []
    for head in range(LANES // HEAD_DIM):
        powers, inverse, logs = soft_parts(
            cross_scores(k_ref[...], pick_head(queries, head), live)
        )
        log_ref[0, head : head + 1] = logs
        lines = values_t[head * HEAD_DIM : (head + 1) * HEAD_DIM]
        pieces.append(product(lines, powers.astype(BF16)) * inverse)
    o_parts[step] = jnp.concatenate(pieces, axis=0).T.astype(BF16)

    @pl.when(step == parts - 1)
    def _():
        for copy in last:
            copy.wait()
        a2 = jnp.concatenate([o_parts[i] for i in range(parts)], axis=1)
        a2_ref[...] = a2
        h2 = h1_ref[...] + right_product(a2, w_o2[...])
        h2_ref[...] = h2


def rows_forward(a_pieces, weights, x, gains, live, kv, spot, broad, masks):
    count = len(a_pieces)
    rows, width = x.shape
    keys = kv.shape[0]
    parts = width // LANES
    slim = a_pieces[0].shape[1]
    flat = (rows, width)
    whole = lambda shape: pl.BlockSpec(shape, lambda i, spot: (0, 0))
    key = pl.BlockSpec((keys, LANES), lambda i, spot: (0, i))
    value = pl.BlockSpec((keys, LANES), lambda i, spot: (0, i + parts))
    low, full = (flat, BF16), (flat, F32)
    square = pltpu.VMEM((width, width), BF16)
    piece = pltpu.VMEM((parts, rows, LANES), BF16)
    return pl.pallas_call(
        functools.partial(rows_forward_kernel, masks, (count, len(weights)), broad),
        out_shape=shaped([low, low, full, full, ((parts, 8, rows), F32)]),
        grid_spec=pltpu.PrefetchScalarGridSpec(
            num_scalar_prefetch=1,
            grid=(parts,),
            in_specs=[HBM] * (count + len(weights))
            + [whole(flat), whole(gains.shape), whole(live.shape), key, value],
            out_specs=[whole(flat)] * 4 + [pl.BlockSpec((1, 8, rows), lambda i, spot: (i, 0, 0))],
            scratch_shapes=[
                pltpu.VMEM((count, rows, slim), BF16),
                square, square, square, piece, piece,
                pltpu.SemaphoreType.DMA((count + 3 * blocks_in(weights),)),
            ],
        ),
        compiler_params=vmem(max(16, keys * 8 // 1024 + 8)),
        cost_estimate=cost(14),
        name="rows_forward",
    )(spot, *a_pieces, *weights, x, gains, live, kv, kv)


def cross_backward(queries, upstream, live, keys, values, logs):
    keys_t = transposed(keys)
    pieces, dk, dv = [], 0.0, 0.0
    for head in range(LANES // HEAD_DIM):
        own = pick_head(queries, head)
        up_own = pick_head(upstream, head)
        inner = right_product(values, up_own)
        chance, grad = score_grads(cross_scores(keys, own, live), logs[head : head + 1], inner)
        dv = dv + product(chance, up_own)
        dk = dk + product(grad, own)
        lines = keys_t[head * HEAD_DIM : (head + 1) * HEAD_DIM]
        pieces.append(product(lines, grad))
    dq = jnp.concatenate(pieces, axis=0).T * SCALING
    return dq.astype(BF16), (dk * SCALING).astype(BF16), dv.astype(BF16)


def rows_early_kernel(masks, weights, edge, spot_ref, *refs):
    w_refs, refs = refs[:weights], refs[weights:]
    c2_ref, live_ref, log_ref, q_ref, k_ref, v_ref, up_ref, dq_ref, dk_ref, dv_ref = refs[:10]
    w_o2, up_parts, done = refs[10:]
    width = c2_ref.shape[1]

    @pl.when(pl.program_id(0) == 0)
    def _():
        columns = (edge + 4 * width, edge + 5 * width)
        run(weight_copies(w_refs, masks, spot_ref[0], columns, w_o2, done, 0))
        up = product(c2_ref[...], w_o2[...]).astype(BF16)
        up_ref[...] = up
        for i in range(up_parts.shape[0]):
            up_parts[i] = up[:, i * LANES : (i + 1) * LANES]

    dq_ref[...], dk_ref[...], dv_ref[...] = cross_backward(
        q_ref[...], up_parts[pl.program_id(0)], live_ref[...], k_ref[...], v_ref[...], log_ref[0]
    )


def rows_late_kernel(masks, counts, edge, spot_ref, *refs):
    seq_count, weights = counts
    w_refs, refs = refs[:weights], refs[weights:]
    up_ref, dq_early_ref, dh2_ref, h1_ref, gain_ref, live_ref, log_ref, q_ref, k_ref, v_ref = refs[:10]
    da_refs, refs = refs[10 : 10 + seq_count], refs[10 + seq_count :]
    dq2_ref, dk_ref, dv_ref, dh1_ref, gain_grad_ref = refs[:5]
    w_o1, w_q2, dq_parts, da_all, done = refs[5:]
    step = pl.program_id(0)
    me, seq = spot_ref[0], spot_ref[1]
    width = dh2_ref.shape[1]
    parts = dq_parts.shape[0]
    copies = weight_copies(
        w_refs, masks, me, (edge + width, edge + 2 * width), w_q2, done, 0
    )
    copies += weight_copies(w_refs, masks, me, (edge, edge + width), w_o1, done, len(copies))

    @pl.when(step == 0)
    def _():
        for copy in copies:
            copy.start()

    dq_parts[step], dk_ref[...], dv_ref[...] = cross_backward(
        q_ref[...], up_ref[...], live_ref[...], k_ref[...], v_ref[...], log_ref[0]
    )

    @pl.when(step == parts - 1)
    def _():
        for copy in copies:
            copy.wait()
        dq2 = jnp.concatenate([dq_early_ref[...]] + [dq_parts[i] for i in range(parts)], axis=1)
        dq2_ref[...] = dq2
        dn2 = right_product(dq2, w_q2[...])
        h1 = h1_ref[...]
        scale = norm_scale(h1)
        dh1 = dh2_ref[...] + norm_hidden_grad(h1, scale, gain_ref[1:2], dn2)
        dh1_ref[...] = dh1
        gain_grad_ref[...] = jnp.sum(dn2 * h1 * scale, axis=0, keepdims=True)
        c1 = dh1.astype(BF16)
        up = product(c1, w_o1[...])
        slim = da_all.shape[2]
        for j in range(seq_count):
            da_all[j] = up[:, j * slim : (j + 1) * slim].astype(BF16)
        for k, ref in enumerate(da_refs):
            ref[...] = da_all[lax.rem(seq + k, seq_count)]


def rows_specs(rows, keys, width, start):
    parts = width // LANES
    row = pl.BlockSpec((rows, LANES), lambda i, spot: (0, i + start))
    key = pl.BlockSpec((keys, LANES), lambda i, spot: (0, i + start))
    value = pl.BlockSpec((keys, LANES), lambda i, spot: (0, i + start + parts))
    log = pl.BlockSpec((1, 8, rows), lambda i, spot: (i + start, 0, 0))
    return log, row, key, value


def rows_early(weights, c2, live, logs, q2, kv, spot, edge, masks):
    rows, width = c2.shape
    keys = kv.shape[0]
    parts = width // LANES // 2
    whole = lambda shape: pl.BlockSpec(shape, lambda i, spot: (0, 0))
    log, row, key, value = rows_specs(rows, keys, width, 0)
    half = width // 2
    shapes = [((rows, width), BF16), ((rows, half), BF16)] + [((keys, half), BF16)] * 2
    return pl.pallas_call(
        functools.partial(rows_early_kernel, masks, len(weights), edge),
        out_shape=shaped(shapes, (2, 3)),
        grid_spec=pltpu.PrefetchScalarGridSpec(
            num_scalar_prefetch=1,
            grid=(parts,),
            in_specs=[HBM] * len(weights)
            + [whole((rows, width)), whole(live.shape), log, row, key, value],
            out_specs=[whole((rows, width)), row, key, key],
            scratch_shapes=[
                pltpu.VMEM((width, width), BF16),
                pltpu.VMEM((2 * parts, rows, LANES), BF16),
                pltpu.SemaphoreType.DMA((blocks_in(weights),)),
            ],
        ),
        compiler_params=vmem(max(12, keys * 8 // 1024 + 12)),
        cost_estimate=cost(10),
        name="rows_early",
    )(spot, *weights, c2, live, logs, q2, kv, kv)


def rows_late(weights, up, dq_early, dh2, h1, gains, live, logs, q2, kv, spot, edge, masks):
    count = lax.axis_size("seq")
    rows, width = dh2.shape
    keys = kv.shape[0]
    parts = width // LANES // 2
    slim = width // count
    flat = (rows, width)
    half = width // 2
    whole = lambda shape: pl.BlockSpec(shape, lambda i, spot: (0, 0))
    log, row, key, value = rows_specs(rows, keys, width, parts)
    key_out = pl.BlockSpec((keys, LANES), lambda i, spot: (0, i))
    shapes = [((rows, slim), BF16)] * count + [
        (flat, BF16), ((keys, half), BF16), ((keys, half), BF16),
        (flat, F32), ((1, width), F32),
    ]
    square = pltpu.VMEM((width, width), BF16)
    outs = pl.pallas_call(
        functools.partial(rows_late_kernel, masks, (count, len(weights)), edge),
        out_shape=shaped(shapes, range(count, count + 6)),
        grid_spec=pltpu.PrefetchScalarGridSpec(
            num_scalar_prefetch=1,
            grid=(parts,),
            in_specs=[HBM] * len(weights)
            + [row, whole((rows, half)), whole(flat), whole(flat)]
            + [whole(gains.shape), whole(live.shape), log, row, key, value],
            out_specs=[whole((rows, slim))] * count
            + [whole(flat), key_out, key_out, whole(flat), whole((1, width))],
            scratch_shapes=[
                square, square,
                pltpu.VMEM((parts, rows, LANES), BF16),
                pltpu.VMEM((count, rows, slim), BF16),
                pltpu.SemaphoreType.DMA((2 * blocks_in(weights),)),
            ],
        ),
        compiler_params=vmem(max(18, keys * 8 // 1024 + 12)),
        cost_estimate=cost(11),
        name="rows_late",
    )(spot, *weights, up, dq_early, dh2, h1, gains, live, logs, q2, kv, kv)
    return outs[:count], *outs[count:]


def turn_of(source_ref, width):
    columns = lax.broadcasted_iota(jnp.int32, (width, width), 1)
    return (columns == source_ref[...]).astype(F32).astype(BF16)


def cross_weights_kernel(masks, number, edge, spot_ref, *refs):
    w_refs, refs = refs[:number], refs[number:]
    source_ref, h1_ref, gain_ref, dq2_ref, c2_ref, a2_ref, keys_ref = refs[:7]
    parts, refs = refs[7:11], refs[11:]
    near_ref, far_ref, dmem_ref = refs[:3]
    w_all, turn, dk_sum, dv_sum, done = refs[3:]
    dk = jnp.concatenate([parts[0][...], parts[1][...]], axis=1)
    dv = jnp.concatenate([parts[2][...], parts[3][...]], axis=1)
    step, steps = pl.program_id(0), pl.num_programs(0)
    width = dq2_ref.shape[1]
    half = width // 2
    columns = (edge + 2 * width, edge + 4 * width)
    copies = weight_copies(w_refs, masks, spot_ref[0], columns, w_all, done, 0)

    def put(column, values):
        values = values.astype(BF16)
        near_ref[:, column : column + width] = values[:half]
        far_ref[:, column : column + width] = values[half:]

    @pl.when(step == 0)
    def _():
        for copy in copies:
            copy.start()
        turn[...] = turn_of(source_ref, width)
        h1 = h1_ref[...]
        n2 = (h1 * norm_scale(h1) * gain_ref[1:2]).astype(BF16)
        n2_t = right_product(turn[...], n2).astype(BF16)
        put(0, product(n2_t, dq2_ref[...]))
        c2_t = right_product(turn[...], c2_ref[...]).astype(BF16)
        put(3 * width, product(c2_t, a2_ref[...]))
        dk_sum[...] = jnp.zeros_like(dk_sum)
        dv_sum[...] = jnp.zeros_like(dv_sum)

    keys_t = right_product(turn[...], keys_ref[...]).astype(BF16)
    dk_sum[...] += product(keys_t, dk)
    dv_sum[...] += product(keys_t, dv)

    @pl.when(step == 0)
    def _():
        for copy in copies:
            copy.wait()

    dmem_ref[...] = (
        right_product(dk, w_all[:, :width]) + right_product(dv, w_all[:, width:])
    ).astype(BF16)

    @pl.when(step == steps - 1)
    def _():
        put(width, dk_sum[...])
        put(2 * width, dv_sum[...])


def cross_weights(weights, source, h1, gains, dq2, c2, a2, keys, grads, spot, chunk, edge, masks):
    rows, width = h1.shape
    whole = lambda shape: pl.BlockSpec(shape, lambda i, spot: (0, 0))
    part = pl.BlockSpec((chunk, width), lambda i, spot: (i, 0))
    half = ((width // 2, 4 * width), BF16)
    return pl.pallas_call(
        functools.partial(cross_weights_kernel, masks, len(weights), edge),
        out_shape=shaped([half, half, (keys.shape, BF16)], (0,)),
        grid_spec=pltpu.PrefetchScalarGridSpec(
            num_scalar_prefetch=1,
            grid=(keys.shape[0] // chunk,),
            in_specs=[HBM] * len(weights)
            + [whole(source.shape), whole((rows, width)), whole(gains.shape)]
            + [whole((rows, width))] * 3
            + [part]
            + [pl.BlockSpec((chunk, width // 2), lambda i, spot: (i, 0))] * 4,
            out_specs=[whole(half[0]), whole(half[0]), part],
            scratch_shapes=[
                pltpu.VMEM((width, 2 * width), BF16),
                pltpu.VMEM((width, width), BF16),
                pltpu.VMEM((width, width), F32),
                pltpu.VMEM((width, width), F32),
                pltpu.SemaphoreType.DMA((blocks_in(weights),)),
            ],
        ),
        compiler_params=vmem(24),
        cost_estimate=cost(10),
        name="cross_weights",
    )(spot, *weights, source, h1, gains, dq2, c2, a2, keys, *grads)


def self_backward_kernel(heads, masks, counts, spot_ref, *refs):
    seq_count, weights = counts
    up_refs, refs = refs[:seq_count], refs[seq_count:]
    x_refs, refs = refs[:3], refs[3:]
    x_list = [x_refs[0], x_refs[1], x_refs[2].at[0], x_refs[2].at[1]]
    w_refs, refs = refs[:weights], refs[weights:]
    qkv_ref, log_ref, refs = refs[0], refs[1], refs[2:]
    dn_refs, refs = refs[:2], refs[2:]
    steps = seq_masks(lax.rem(spot_ref[0], 2))
    dqkv_ref, gain_grad_ref = refs[:2]
    up_all, x_all, w_all, dn_all, dk_sum, dv_sum, done = refs[2:]
    rows = up_refs[0].shape[0]
    broad = w_all.shape[1] // 3
    slim = heads * HEAD_DIM
    me, seq = spot_ref[0], spot_ref[1]
    spots = [lax.rem(seq - k + seq_count, seq_count) for k in range(seq_count)]
    early = [
        pltpu.make_async_copy(ref, up_all.at[spots[k]], done.at[k])
        for k, ref in enumerate(up_refs)
    ]
    late = [
        pltpu.make_async_copy(ref, x_all.at[jnp.bitwise_xor(seq, mask)], done.at[seq_count + k])
        for k, (ref, mask) in enumerate(zip(x_list, steps))
    ]
    late += weight_copies(w_refs, masks, me, (0, 3 * broad), w_all, done, 2 * seq_count)
    for copy in early + late:
        copy.start()
    keys_t = transposed(qkv_ref[:, broad : 2 * broad])
    dk_sum[...] = jnp.zeros_like(dk_sum)
    dv_sum[...] = jnp.zeros_like(dv_sum)
    blank = jnp.zeros((rows, broad - slim), BF16)
    for copy in early:
        copy.wait()
    for j in range(seq_count):
        first, last = j * rows, (j + 1) * rows
        queries = qkv_ref[first:last, :broad]
        upstream = jnp.concatenate([up_all[j], blank], axis=1)
        parts = []
        for head in range(heads):
            own = pick_head(queries, head)
            up_own = pick_head(upstream, head)
            keys = qkv_ref[:last, broad : 2 * broad]
            inner = right_product(qkv_ref[:last, 2 * broad :], up_own)
            chance, grad = score_grads(
                causal_scores(keys, own), log_ref[head : head + 1, first:last], inner
            )
            dv_sum[:last] += product(chance, up_own)
            dk_sum[:last] += product(grad, own)
            lines = keys_t[head * HEAD_DIM : (head + 1) * HEAD_DIM, :last]
            parts.append(product(lines, grad))
        rest = jnp.zeros((broad - slim, rows), F32)
        dq = jnp.concatenate(parts + [rest], axis=0).T * SCALING
        dqkv_ref[first:last, :broad] = dq.astype(BF16)
    dqkv_ref[:, broad : 2 * broad] = (dk_sum[...] * SCALING).astype(BF16)
    dqkv_ref[:, 2 * broad :] = dv_sum[...].astype(BF16)
    for copy in late:
        copy.wait()
    total = 0.0
    for j in range(seq_count):
        dn1 = right_product(dqkv_ref[j * rows : (j + 1) * rows], w_all[...])
        x = x_all[j].astype(F32)
        total = total + jnp.sum(dn1 * x * norm_scale(x), axis=0, keepdims=True)
        dn_all[j] = dn1.astype(BF16)
    gain_grad_ref[...] = total
    for k, mask in enumerate(steps):
        dn_refs[k // 2][k % 2] = dn_all[jnp.bitwise_xor(seq, mask)]


def self_backward(up_pieces, x_pieces, weights, qkv, logs, spot, heads, masks):
    count = len(up_pieces)
    rows, width = x_pieces[0].shape
    slim = up_pieces[0].shape[1]
    length, broad = qkv.shape[0], qkv.shape[1] // 3
    whole = lambda shape: pl.BlockSpec(shape, lambda i, spot: (0, 0))
    shapes = [((2, rows, width), BF16)] * 2 + [(qkv.shape, BF16), ((1, width), F32)]
    outs = pl.pallas_call(
        functools.partial(self_backward_kernel, heads, masks, (count, len(weights))),
        out_shape=shaped(shapes),
        grid_spec=pltpu.PrefetchScalarGridSpec(
            num_scalar_prefetch=1,
            grid=(1,),
            in_specs=[HBM] * (count + 3 + len(weights)) + [whole(qkv.shape), whole(logs.shape)],
            out_specs=[
                pl.BlockSpec(s, lambda i, spot, n=len(s): (0,) * n) for s, _ in shapes
            ],
            scratch_shapes=[
                pltpu.VMEM((count, rows, slim), BF16),
                pltpu.VMEM((count, rows, width), BF16),
                pltpu.VMEM((width, 3 * broad), BF16),
                pltpu.VMEM((count, rows, width), BF16),
                pltpu.VMEM((length, broad), F32),
                pltpu.VMEM((length, broad), F32),
                pltpu.SemaphoreType.DMA((2 * count + blocks_in(weights),)),
            ],
        ),
        compiler_params=vmem(18),
        cost_estimate=cost(13),
        name="self_backward",
    )(spot, *up_pieces, *x_pieces, *weights, qkv, logs)
    return outs


def self_weights_kernel(
    spot_ref, source_ref, n1_ref, dqkv_ref, dh1_ref, gain_ref, *refs
):
    a_refs, (near_ref, far_ref, a_all) = refs[:-3], refs[-3:]
    width = n1_ref.shape[1]
    half = width // 2
    count = len(a_refs)
    turn = turn_of(source_ref, width)
    column = 0

    def put(values):
        nonlocal column
        values = values.astype(BF16)
        near_ref[:, column : column + values.shape[1]] = values[:half]
        far_ref[:, column : column + values.shape[1]] = values[half:]
        column += values.shape[1]

    for k, ref in enumerate(a_refs):
        a_all[lax.rem(spot_ref[1] - k + count, count)] = ref[...]
    a1 = jnp.concatenate([a_all[j] for j in range(count)], axis=1)
    c1_t = right_product(turn, dh1_ref[...].astype(BF16)).astype(BF16)
    put(product(c1_t, a1))
    put(right_product(turn, gain_ref[...].astype(BF16)))
    n1_t = right_product(turn, n1_ref[...]).astype(BF16)
    put(product(n1_t, dqkv_ref[...]))


def self_weights(source, n1, dqkv, dh1, gain_grads, a_pieces, spot):
    width = n1.shape[1]
    half = ((width // 2, width + LANES + dqkv.shape[1]), BF16)
    whole = lambda shape: pl.BlockSpec(shape, lambda i, spot: (0, 0))
    ins = [source, n1, dqkv, dh1, gain_grads, *a_pieces]
    return pl.pallas_call(
        self_weights_kernel,
        out_shape=shaped([half, half]),
        grid_spec=pltpu.PrefetchScalarGridSpec(
            num_scalar_prefetch=1,
            grid=(1,),
            in_specs=[whole(a.shape) for a in ins],
            out_specs=[whole(half[0])] * 2,
            scratch_shapes=[pltpu.VMEM((len(a_pieces),) + a_pieces[0].shape, BF16)],
        ),
        compiler_params=vmem(16),
        cost_estimate=cost(6),
        name="self_weights",
    )(spot, *ins)


def last_rows_kernel(keep_ref, one_ref, two_ref, x_ref, dh1_ref, gain_ref, out_ref):
    dn1 = keep_ref[0].astype(F32) + one_ref[0].astype(F32) + two_ref[...].astype(F32)
    x = x_ref[...].astype(F32)
    out_ref[...] = (
        dh1_ref[...] + norm_hidden_grad(x, norm_scale(x), gain_ref[0:1], dn1)
    ).astype(BF16)


def last_rows(keep, one, two, x, dh1, gains):
    return pl.pallas_call(
        last_rows_kernel,
        out_shape=jax.ShapeDtypeStruct(x.shape, BF16),
        compiler_params=vmem(8),
        cost_estimate=cost(2),
        name="last_rows",
    )(keep, one, two, x, dh1, gains)


def finish_kernel(slim, broad, spot_ref, *refs):
    sources, outs, hold = refs[:12], refs[12:-1], refs[-1]

    def total(refs, columns):
        keep, one, two = refs
        return (
            keep[0, :, columns[0] : columns[1]].astype(F32)
            + one[0, :, columns[0] : columns[1]].astype(F32)
            + two[0, :, columns[0] : columns[1]].astype(F32)
        )

    pair, down, cross, rest = sources[0:3], sources[3:6], sources[6:9], sources[9:12]
    hidden, width = outs[0].shape[1], outs[2].shape[1]
    outs[0][...] = total(pair, (0, hidden))
    outs[1][...] = total(pair, (hidden, 2 * hidden))
    outs[2][...] = total(down, (0, width))
    for i in range(4):
        outs[3 + i][...] = total(cross, (i * width, (i + 1) * width))
    outs[7][...] = total(rest, (0, width))
    edge = width
    outs[-1][...] = total(rest, (edge, edge + LANES))
    edge = edge + LANES
    far_edge = edge + 3 * broad
    keep, one, two = rest
    steps = [jnp.bitwise_xor(spot_ref[1], m) for m in seq_masks(lax.rem(spot_ref[0], 2))]
    hold[steps[0]] = keep[0, :, edge:far_edge].astype(F32)
    hold[steps[1]] = two[0, :, edge:far_edge].astype(F32)
    hold[steps[2]] = one[0, :, edge:far_edge].astype(F32)
    hold[steps[3]] = two[0, :, far_edge : far_edge + 3 * broad].astype(F32)
    for i in range(3):
        outs[8 + i][...] = jnp.concatenate(
            [hold[j][:, i * broad : i * broad + slim] for j in range(hold.shape[0])], axis=1
        )


def finish(pair, down, cross, rest, spot, hidden, slim, broad):
    share, feed_share, width = pair[0].shape[1], down[0].shape[1], down[0].shape[2]
    count = lax.axis_size("seq")
    shapes = (
        [(share, hidden)] * 2 + [(feed_share, width)] + [(share, width)] * 8 + [(share, LANES)]
    )
    whole = lambda shape: pl.BlockSpec(shape, lambda i, spot: (0,) * len(shape))
    flat = [*pair, *down, *cross, *rest]
    return pl.pallas_call(
        functools.partial(finish_kernel, slim, broad),
        out_shape=shaped([(shape, F32) for shape in shapes]),
        grid_spec=pltpu.PrefetchScalarGridSpec(
            num_scalar_prefetch=1,
            grid=(1,),
            in_specs=[whole(a.shape) for a in flat],
            out_specs=[whole(shape) for shape in shapes],
            scratch_shapes=[pltpu.VMEM((count, share, 3 * broad), F32)],
        ),
        compiler_params=vmem(12),
        cost_estimate=cost(3),
        name="finish",
    )(spot, *flat)


def local(
    hidden_in,
    memory,
    cotangent,
    norm_self,
    query_self,
    key_self,
    value_self,
    output_self,
    norm_cross,
    query_cross,
    key_cross,
    value_cross,
    output_cross,
    norm_feed,
    gate_weight,
    up_weight,
    down_weight,
    block_counts,
    memory_tail,
    row_example,
):
    mem_count, seq_count = lax.axis_size("mem"), lax.axis_size("seq")
    mem_place, seq_place = lax.axis_index("mem"), lax.axis_index("seq")
    rows, width = hidden_in.shape[1], hidden_in.shape[2]
    inner = HEADS * HEAD_DIM
    near = HEADS // seq_count
    slim = near * HEAD_DIM
    broad = -(-(slim + 8) // LANES) * LANES
    share = norm_self.shape[0]
    hidden_width = gate_weight.shape[1]
    spot = jnp.stack([mem_place, seq_place]).astype(jnp.int32)
    scalars = jnp.concatenate([block_counts, memory_tail, row_example])
    masks = slot_masks(mem_count)
    mask_array = mem_masks()
    block = width // mem_count
    column = jnp.arange(width, dtype=jnp.int32)
    source = (block * (mem_place ^ jnp.repeat(mask_array, block)) + column % block).reshape(width, 1)
    gain_stack = jnp.stack([norm_self, norm_cross, norm_feed], axis=0)
    x_own = hidden_in[0]
    edge = 3 * broad
    turns = mem_count.bit_length() - 2
    flat = lambda stacked: stacked.reshape((1, -1) + stacked.shape[2:])

    with jax.named_scope("gather"):
        own, two, one, second, blocks, live = prepare(
            (query_self, key_self, value_self, output_self, query_cross)
            + (key_cross, value_cross, output_cross, gate_weight, up_weight),
            gain_stack, memory, scalars, spot, slim, broad,
        )
        live = live.reshape(-1, 1)
        stay, go = part_blocks(blocks, 0)
        two, arrived = swap_seq(two, 0), swap_mem(go, 0)
        two, blocks, one, second, x_in, down_in = settle(
            two, join_blocks(stay, arrived), one, second, x_own, down_weight
        )
        three = swap_seq(jnp.stack([one, two[:, edge:]]), 1)
        for turn in range(1, turns):
            stay, go = part_blocks(blocks, turn)
            blocks = join_blocks(stay, swap_mem(go, turn))
        three, blocks, second, x_in, down_in, source = settle(
            three, blocks, second, x_in, down_in, source
        )
        first_width = edge + 5 * width
        first = flat(
            place(
                [own[None], two[None], three],
                seq_places(),
                [first_width],
                [
                    [(0, 0, 0, first_width)],
                    [(0, 0, 0, edge), (0, edge, 2 * edge, 5 * width)],
                    [(0, 0, 0, first_width)],
                ],
            )
        )
        held = [first]
        held.append(swap_mem(first, 0))
        stay, go = part_blocks(blocks, turns)
        keys_in = join_blocks(stay, swap_mem(go, turns)).reshape(-1, width)
        second_a, x_a = swap_seq(second, 0), swap_seq(x_in, 0)
        held, keys_in, second_a, x_a, second, x_in, down_in = settle(
            held, keys_in, second_a, x_a, second, x_in, down_in
        )
        for turn in range(1, turns):
            held.append(swap_mem(join(held), turn))
        second_b = swap_seq(jnp.stack([second, second_a]), 1)
        x_b = swap_seq(jnp.stack([x_in, x_a]), 1)
        held, second_b, x_b, second_a, second, x_a, x_in, down_in = settle(
            held, second_b, x_b, second_a, second, x_a, x_in, down_in
        )
        held = join(held)
        other = swap_mem(held, turns)
        both = [flat(stack_seq([second[None], second_a[None], second_b]))]
        both.append(swap_mem(both[0], 0))
        down_a = swap_seq(down_in, 0)
        held, other, both, down_a, down_in, x_in, x_a, x_b = settle(
            held, other, both, down_a, down_in, x_in, x_a, x_b
        )
        packed = spread_weight([held, other])

    key_chunk = width

    with jax.named_scope("forward"):
        x_pieces = [x_in, x_a, x_b]
        o_pieces, n1, qkv, gains, self_logs = self_rows(x_pieces, packed, spot, near, broad, masks)
        for turn in range(1, turns):
            both.append(swap_mem(join(both), turn))
        down_b = swap_seq(jnp.stack([down_in, down_a]), 1)
        o_pieces, down_b, down_a, down_in, gains = settle(o_pieces, down_b, down_a, down_in, gains)
        a_pieces = send_seq(o_pieces)
        kv2 = key_values(keys_in, packed, spot, key_chunk, edge + 2 * width, masks)
        downs = [flat(stack_seq([down_in[None], down_a[None], down_b]))]
        downs.append(swap_mem(downs[0], 0))
        others = [swap_mem(downs[0], turns)]
        a_pieces, kv2, downs, others, both, keys_in = settle(
            a_pieces, kv2, downs, others, both, keys_in
        )
        q2, a2, h1, h2, cross_logs = rows_forward(
            a_pieces, packed, x_own, gains, live, kv2, spot, broad, masks
        )
        both = join(both)
        both_other = swap_mem(both, turns)
        for turn in range(1, turns):
            downs.append(swap_mem(join(downs), turn))
        others.append(swap_mem(downs[1], turns))
        h2, both_other, both, downs, others = settle(h2, both_other, both, downs, others)
        others += [swap_mem(piece, turns) for piece in downs[2:]]
        both = [w.reshape(-1, 2 * hidden_width) for w in (both, both_other)]
        unit = hidden_width // mem_count
        narrow = unit % LANES != 0
        if narrow:
            unit = 2 * LANES
            downs = [stack_mem(downs + others).reshape(-1, unit, width)]
            feed_order = jnp.arange(hidden_width // unit, dtype=jnp.int32)
        else:
            feed_order = mem_place ^ mask_array
            downs = downs + others
        layer_out, dh2, c2, gain_feed_terms, *g_feed = feed(
            feed_order, h2, cotangent[0], gains, source, both, downs
        )

    with jax.named_scope("backward"):
        g_both, g_down = g_feed[0:2], g_feed[2:4]
        if narrow:
            g_down = place(
                [jnp.concatenate(g_down).reshape(mem_count, -1, width)],
                jnp.argsort(mem_place ^ mask_array),
            ).reshape(2, -1, width)
        feeding, downing = Scatter(*g_both), Scatter(*g_down)
        feeding.move()
        downing.move()
        up, dq_early, dk_early, dv_early = rows_early(
            packed, c2, live, cross_logs, q2, kv2, spot, edge, masks
        )
        feeding.terms, downing.terms, up, dq_early = settle(
            feeding.terms, downing.terms, up, dq_early
        )
        advance([feeding, downing], spot)
        feeding.sent, downing.sent, up = settle(feeding.sent, downing.sent, up)
        feeding.move()
        downing.move()
        da_pieces, dq2, dk_late, dv_late, dh1, gain_cross_terms = rows_late(
            packed, up, dq_early, dh2, h1, gains, live, cross_logs, q2, kv2, spot, edge, masks
        )
        da_pieces, dq2 = settle(da_pieces, dq2)
        da_pieces = send_seq(da_pieces)
        *g_cross, dmem = cross_weights(
            packed, source, h1, gains, dq2, c2, a2, keys_in,
            [dk_early, dk_late, dv_early, dv_late], spot, key_chunk, edge, masks,
        )
        crossing = Scatter(*g_cross)
        advance([feeding, downing], spot)
        da_pieces, crossing.sent, feeding.sent, downing.sent, dmem = settle(
            da_pieces, crossing.sent, feeding.sent, downing.sent, dmem
        )
        crossing.move()
        feeding.move()
        downing.move()
        keep_dn, send_dn, dqkv, gain_self_terms = self_backward(
            da_pieces, x_pieces, packed, qkv, self_logs, spot, near, masks
        )
        dmem = dmem.reshape(mem_count, -1, width)
        stay, go = part_blocks(dmem, turns)
        dmem = join_blocks(stay, swap_mem(go, turns))
        crossing.terms, feeding.terms, downing.terms, keep_dn, send_dn, dqkv, dmem = settle(
            crossing.terms, feeding.terms, downing.terms, keep_dn, send_dn, dqkv, dmem
        )
        one_dn = swap_seq(send_dn, 1)
        stay, go = part_blocks(dmem, 0)
        dmem = join_blocks(stay, swap_mem(go, 0))
        ends = [None] * 4
        while feeding.left > 0:
            advance([feeding, downing], spot)
            feeding.move()
            downing.move()
        ends[0] = advance([feeding], spot)
        ends[1] = advance([downing], spot)
        advance([crossing], spot)
        gain_grads = jnp.concatenate(
            [gain_self_terms, gain_cross_terms, gain_feed_terms, jnp.zeros((LANES - 3, width), F32)]
        )
        g_self = self_weights(source, n1, dqkv, dh1, gain_grads, a_pieces, spot)
        selfing = Scatter(*g_self)
        one_dn, keep_dn, crossing.sent, dmem, ends[0], ends[1], selfing.sent = settle(
            one_dn, keep_dn, crossing.sent, dmem, ends[0], ends[1], selfing.sent
        )
        two_dn = swap_seq(onward(keep_dn, one_dn)[0], 0)
        one_both = swap_seq(ends[0][1], 1)
        crossing.move()
        selfing.move()
        for turn in range(1, turns):
            stay, go = part_blocks(dmem, turn)
            dmem = join_blocks(stay, swap_mem(go, turn))
        two_dn, one_both, selfing.terms, crossing.terms, dmem, ends[1] = settle(
            two_dn, one_both, selfing.terms, crossing.terms, dmem, ends[1]
        )
        two_both = swap_seq(onward(ends[0][0], one_both), 0)
        one_down = swap_seq(ends[1][1], 1)
        while crossing.left > 0:
            advance([crossing], spot)
            crossing.move()
        advance([selfing], spot)
        selfing.move()
        mem_keep, mem_send = pick_slots(dmem, memory.shape[0], scalars, spot)
        hidden_grad = last_rows(keep_dn, one_dn, two_dn, x_own, dh1, gains)
        two_both, one_down, crossing.terms, selfing.terms, mem_send, mem_keep, hidden_grad = settle(
            two_both, one_down, crossing.terms, selfing.terms, mem_send, mem_keep, hidden_grad
        )
        ends[2] = advance([crossing], spot)
        one_cross = swap_seq(ends[2][1], 1)
        two_down = swap_seq(onward(ends[1][0], one_down), 0)
        mem_one = swap_seq(mem_send, 1)
        while selfing.left > 0:
            advance([selfing], spot)
            selfing.move()
        one_cross, mem_one, mem_keep, selfing.terms, two_down = settle(
            one_cross, mem_one, mem_keep, selfing.terms, two_down
        )
        ends[3] = advance([selfing], spot)
        one_self = swap_seq(ends[3][1], 1)
        two_cross = swap_seq(onward(ends[2][0], one_cross), 0)
        mem_two = swap_seq(onward(mem_keep, mem_one), 0)
        one_self, two_cross, mem_two = settle(one_self, two_cross, mem_two)
        two_self = swap_seq(onward(ends[3][0], one_self, width + LANES), 0)
        per = mem_two.shape[0]
        memory_grad = total_of([mem_keep[:per], mem_one[:per], mem_two]).astype(BF16)
        *finals, gain_finals = finish(
            (ends[0][0], one_both, two_both),
            (ends[1][0], one_down, two_down),
            (ends[2][0], one_cross, two_cross),
            (ends[3][0], one_self, two_self),
            spot, hidden_width, slim, broad,
        )
    g_gate, g_up, g_down, g_q2, g_k2, g_v2, g_o2, g_o1, g_q1, g_k1, g_v1 = finals
    return (
        layer_out[None],
        hidden_grad[None],
        memory_grad,
        gain_finals[:, 0],
        g_q1,
        g_k1,
        g_v1,
        g_o1,
        gain_finals[:, 1],
        g_q2,
        g_k2,
        g_v2,
        g_o2,
        gain_finals[:, 2],
        g_gate,
        g_up,
        g_down,
    )


def solution(mesh):
    every = P(("mem", "seq"), None)
    gain = P(("mem", "seq"))
    in_specs = (
        (P("mem", "seq", None), P(None, "mem", None), P("mem", "seq", None), gain)
        + (every,) * 4
        + (gain,)
        + (every,) * 4
        + (gain,)
        + (every,) * 3
        + (P(),) * 3
    )
    out_specs = (
        (P("mem", "seq", None), P("mem", "seq", None), P("seq", "mem", None), gain)
        + (every,) * 4
        + (gain,)
        + (every,) * 4
        + (gain,)
        + (every,) * 3
    )
    return jax.shard_map(local, mesh=mesh, in_specs=in_specs, out_specs=out_specs, check_vma=False)
```

```python
import functools

import jax
import jax.numpy as jnp
from jax import lax
from jax.experimental import pallas as pl
from jax.experimental.pallas import tpu as pltpu
from jax.sharding import PartitionSpec as P

HEADS = 12
HEAD_DIM = 64
SCALING = HEAD_DIM ** (-0.5)
LANES = 128
MASKED = -1e30
F32 = jnp.float32
BF16 = jnp.bfloat16


def product(left, right):
    return jnp.dot(left, right, preferred_element_type=F32)


def left_product(left, right):
    return lax.dot_general(left, right, (((0,), (0,)), ((), ())), preferred_element_type=F32)


def right_product(left, right):
    return lax.dot_general(left, right, (((1,), (1,)), ((), ())), preferred_element_type=F32)


def gelu_tanh(values):
    return (
        0.5
        * values
        * (1.0 + jnp.tanh(0.7978845608028654 * (values + 0.044715 * values * values * values)))
    )


def gated_unit(gate, upper):
    return gelu_tanh(gate) * upper


def norm_scale(hidden):
    return lax.rsqrt(jnp.mean(hidden * hidden, axis=-1, keepdims=True) + 1e-06)


def norm_hidden_grad(hidden, scale, gain, upstream):
    lifted = upstream * gain
    return scale * lifted - hidden * (scale * scale * scale) * jnp.mean(
        lifted * hidden, axis=-1, keepdims=True
    )


def shift(values, axis, step):
    size = lax.axis_size(axis)
    return lax.ppermute(values, axis, [(i, (i + step) % size) for i in range(size)])


def swap(values, axis, mask):
    size = lax.axis_size(axis)
    return lax.ppermute(values, axis, [(i, i ^ mask) for i in range(size)])


def place_kernel(counts, maps, places, *refs):
    sources = refs[: len(counts)]
    targets, done = refs[len(counts) : -1], refs[-1]
    copies = []
    number = 0
    for source, count, moves in zip(sources, counts, maps):
        for block in range(count):
            for goal, to, start, width in moves:
                part, target = source.at[block], targets[goal].at[places[number]]
                if len(moves) > 1 or width != source.shape[2]:
                    part = source.at[block, :, start : start + width]
                    target = targets[goal].at[places[number], :, to : to + width]
                copies.append(pltpu.make_async_copy(part, target, done.at[len(copies)]))
            number += 1
    for copy in copies:
        copy.start()
    for copy in copies:
        copy.wait()


def place(pieces, places, widths=None, maps=None):
    counts = [piece.shape[0] for piece in pieces]
    total = sum(counts)
    _, height, width = pieces[0].shape
    widths = widths or [width]
    if maps is None:
        plain = [(i, 0, sum(widths[:i]), w) for i, w in enumerate(widths)]
        maps = [plain] * len(pieces)
    copies = sum(count * len(moves) for count, moves in zip(counts, maps))
    outs = [((total, height, w), pieces[0].dtype) for w in widths]
    size = total * height * sum(widths) * 2
    result = pl.pallas_call(
        functools.partial(place_kernel, counts, maps),
        out_shape=shaped(outs),
        grid_spec=pltpu.PrefetchScalarGridSpec(
            num_scalar_prefetch=1,
            grid=(1,),
            in_specs=[HBM] * len(pieces),
            out_specs=[
                pl.BlockSpec((total, height, w), lambda i, places: (0, 0, 0)) for w in widths
            ],
            scratch_shapes=[pltpu.SemaphoreType.DMA((copies,))],
        ),
        compiler_params=pltpu.CompilerParams(vmem_limit_bytes=3 * size + (4 << 20)),
        cost_estimate=cost(1 + size / 1e6),
        name="place",
    )(places.astype(jnp.int32), *pieces)
    return result[0] if len(widths) == 1 else result


def after(values, *tokens):
    return lax.optimization_barrier((values,) + tokens)[0]


def settle(*values):
    return lax.optimization_barrier(values)


def seq_masks(parity):
    return [0, 1 + parity, 2 - parity, 3]


def swap_seq(values, turn):
    mem, seq = lax.axis_size("mem"), lax.axis_size("seq")
    pairs = []
    for m in range(mem):
        mask = 1 + (m + turn) % 2
        pairs += [(m * seq + s, m * seq + (s ^ mask)) for s in range(seq)]
    return lax.ppermute(values, ("mem", "seq"), pairs)


def seq_places():
    parity = lax.axis_index("mem") % 2
    return lax.axis_index("seq") ^ jnp.stack(seq_masks(parity)).astype(jnp.int32)


def stack_seq(pieces, widths=None):
    return place(pieces, seq_places(), widths)


def send_seq(pieces):
    return [pieces[0]] + [shift(piece, "seq", k) for k, piece in enumerate(pieces) if k]


def total_of(pieces):
    return functools.reduce(jnp.add, [piece.astype(F32) for piece in pieces])


def join(blocks):
    return blocks[0] if len(blocks) == 1 else jnp.concatenate(blocks, axis=0)


def orders(count):
    bits = list(range(1, count.bit_length() - 1))
    return bits, bits[::-1]


def slot_masks(count):
    half = count // 2
    low = [
        [sum(((s >> j) & 1) << bit for j, bit in enumerate(order)) for s in range(half)]
        for order in orders(count)
    ]
    return low[0] + [m | 1 for m in low[1]], low[1] + [m | 1 for m in low[0]]


def swap_mem(values, turn):
    count = lax.axis_size("mem")
    pairs = []
    for i in range(count):
        order = [*orders(count)[i % 2], 0]
        pairs.append((i, i ^ (1 << order[turn])))
    return lax.ppermute(values, "mem", pairs)


def mem_masks():
    count = lax.axis_size("mem")
    even, odd = slot_masks(count)
    return jnp.where(
        lax.axis_index("mem") % 2 == 0, jnp.array(even, jnp.int32), jnp.array(odd, jnp.int32)
    )


def stack_mem(halves, widths=None):
    return place(halves, lax.axis_index("mem") ^ mem_masks(), widths)


def spread_weight(halves):
    if halves[0].shape[1] % 16 == 0:
        return list(halves)
    stacked = stack_mem(halves)
    return [stacked.reshape(1, -1, stacked.shape[-1])]


def add_low(left, right):
    return (left.astype(F32) + right.astype(F32)).astype(BF16)


def total_kernel(plans, spot_ref, *refs):
    terms = sum(number for number, _ in plans)
    sources, refs = list(refs[:terms]), refs[terms:]
    outs, holds = list(refs[: len(refs) - len(plans)]), refs[len(refs) - len(plans) :]
    column = 0
    for (number, ends), hold in zip(plans, holds):
        mine, sources = sources[:number], sources[number:]
        groups, rows, width = mine[0].shape
        for g in range(groups):
            total = mine[0][g].astype(F32)
            for ref in mine[1:]:
                total = total + ref[g].astype(F32)
            if not ends:
                outs[0][g] = total.astype(BF16)
                continue
            count = hold.shape[0]
            unit = rows // count
            for j in range(count):
                hold[j] = total[j * unit : (j + 1) * unit]
            for k, mask in enumerate(seq_masks(lax.rem(spot_ref[0], 2))):
                piece = hold[jnp.bitwise_xor(spot_ref[1], mask)].astype(BF16)
                outs[-2 + k // 2][k % 2, :, column : column + width] = piece
            column += width
        if not ends:
            del outs[:1]


class Scatter:
    def __init__(self, kept, sent, taken=0):
        self.terms = [kept if kept.ndim == 3 else kept[None]]
        self.sent = sent if sent.ndim == 3 else sent[None]
        self.left = (lax.axis_size("mem") // 2).bit_length() - 1 - taken
        self.rows = self.terms[0].shape[1]

    def move(self):
        self.terms.append(swap_mem(self.sent, self.left))

    def hold(self):
        return [self.terms, self.sent]

    def take(self, held):
        self.terms, self.sent = held


def advance(scatters, spot):
    count = lax.axis_size("seq")
    plans, shapes, specs, flat, holds = [], [], [], [], []
    ended, exact = 0, True
    whole = lambda shape: pl.BlockSpec(shape, lambda i, spot: (0, 0, 0))
    for s in scatters:
        ends = s.left == 0
        groups, _, width = s.terms[0].shape
        rows = s.rows if ends else s.rows // 2
        exact = exact and rows // (count if ends else 1) % 8 == 0
        plans.append((len(s.terms), ends))
        part = (groups, rows, width)
        if ends:
            specs += [whole(part)] * len(s.terms)
            ended += groups * width
            unit = rows // count
            holds.append(pltpu.VMEM((count, unit, width), F32))
        else:
            specs += [pl.BlockSpec(part, lambda i, spot: (0, 1, 0))] * len(s.terms)
            shapes.append(part)
            holds.append(pltpu.VMEM((1, 8, 128), F32))
        flat += s.terms
    if ended:
        shapes += [(2, unit, ended)] * 2
    if exact:
        size = sum(spec.block_shape[0] * spec.block_shape[1] * spec.block_shape[2] for spec in specs)
        outs = pl.pallas_call(
            functools.partial(total_kernel, plans),
            out_shape=shaped([(shape, BF16) for shape in shapes]),
            grid_spec=pltpu.PrefetchScalarGridSpec(
                num_scalar_prefetch=1,
                grid=(1,),
                in_specs=specs,
                out_specs=[whole(shape) for shape in shapes],
                scratch_shapes=holds,
            ),
            compiler_params=vmem(6 + (size * 8 >> 20)),
            cost_estimate=cost(1 + size / 1e6),
            name="total",
        )(spot, *(far(*flat) if size > 1 << 20 else flat))
        outs = list(outs)
    else:
        outs, ends_at = [], []
        for s in scatters:
            low = 0 if s.left == 0 else s.rows // 2
            high = s.rows if s.left == 0 else 2 * low
            total = total_of([term[:, low:high] for term in s.terms]).astype(BF16)
            if s.left:
                outs.append(total)
                continue
            groups, rows, width = total.shape
            blocks = total.reshape(groups, count, rows // count, width)
            ends_at.append(jnp.take(jnp.concatenate(list(blocks), axis=2), seq_places(), axis=0))
        if ends_at:
            blocks = jnp.concatenate(ends_at, axis=2)
            outs += [blocks[:2], blocks[2:]]
    for s in scatters:
        if s.left:
            s.sent, s.rows = outs.pop(0), s.rows // 2
        s.left -= 1
    return outs or None


def onward(kept, arrived, summed=None):
    half = kept.shape[0] // 2
    mine, theirs = kept[half:], arrived[half:]
    if summed is None:
        return add_low(mine, theirs)
    return jnp.concatenate(
        [add_low(mine[..., :summed], theirs[..., :summed]), mine[..., summed:], theirs[..., summed:]],
        axis=-1,
    )


def part_blocks(blocks, turn):
    count = blocks.shape[0]
    parts = blocks.reshape((count >> (turn + 1), 2, 1 << turn) + blocks.shape[1:])
    return parts[:, 0], parts[:, 1]


def join_blocks(stay, arrived):
    joined = jnp.stack([stay, arrived], axis=1)
    return joined.reshape((-1,) + joined.shape[3:])


HBM = pl.BlockSpec(memory_space=pltpu.HBM)


def far(*arrays):
    return [pltpu.with_memory_space_constraint(array, pltpu.HBM) for array in arrays]


def shaped(shapes, distant=()):
    return [
        jax.ShapeDtypeStruct(shape, dtype)
        for i, (shape, dtype) in enumerate(shapes)
    ]


def vmem(mebibytes):
    return pltpu.CompilerParams(vmem_limit_bytes=mebibytes << 20)


def cost(microseconds):
    return pl.CostEstimate(
        flops=int(microseconds * 1.1e9), bytes_accessed=0, transcendentals=0
    )


def run(copies):
    for copy in copies:
        copy.start()
    for copy in copies:
        copy.wait()


def prepare_kernel(
    slim, broad, scalars_ref, spot_ref,
    q_ref, k_ref, v_ref, o1_ref, q2_ref, k2_ref, v2_ref, o2_ref, gate_ref, up_ref,
    gain_ref, memory_ref,
    own_ref, two_ref, one_ref, second_ref, blocks_ref, live_ref,
    turn, triple, held, done,
):
    mem_count, height = blocks_ref.shape[0], memory_ref.shape[1]
    share, width = q_ref.shape
    half = mem_count // 2
    me, seq = spot_ref[0], spot_ref[1]
    parity = lax.rem(me, 2)
    counts_at, tails_at, rows_at = 0, mem_count, 2 * mem_count
    moves = [(ref, triple.at[i]) for i, ref in enumerate((q_ref, k_ref, v_ref))]
    moves += [(memory_ref, held)]
    for ref, base in ((own_ref, 3 * broad), (one_ref, 3 * broad), (two_ref, 6 * broad)):
        for i, source in enumerate((o1_ref, q2_ref, k2_ref, v2_ref, o2_ref)):
            moves += [(source, ref.at[:, base + i * width : base + (i + 1) * width])]
    hidden = gate_ref.shape[1]
    moves += [(gate_ref, second_ref.at[:, :hidden]), (up_ref, second_ref.at[:, hidden:])]
    copies = [pltpu.make_async_copy(a, b, done.at[i]) for i, (a, b) in enumerate(moves)]
    for copy in copies:
        copy.start()
    turn[...] = jnp.zeros_like(turn)
    turn[0:3, 0:share] = gain_ref[...].astype(F32)
    gains = turn[...].T[:share]
    lane = lax.broadcasted_iota(jnp.int32, (share, broad - slim), 1)
    extra = jnp.zeros((share, broad - slim), F32)
    for i in range(3):
        extra = jnp.where(lane == i, gains[:, i : i + 1], extra)
    extra = extra.astype(BF16)
    blank = jnp.zeros((share, broad - slim), BF16)
    token = lax.broadcasted_iota(jnp.int32, (height, 1), 0)

    def first_block(example):
        return lax.fori_loop(
            0, example, lambda i, total: total + scalars_ref[counts_at + i], jnp.int32(0)
        )

    mine = scalars_ref[rows_at + me]
    mine_start = first_block(mine)
    mine_end = mine_start + scalars_ref[counts_at + mine]

    for copy in copies[:4]:
        copy.wait()

    order, contrary = orders(mem_count)

    def one(t, carry):
        low = lax.rem(t, half)
        first, second = jnp.int32(0), jnp.int32(0)
        for j in range(len(order)):
            bit = lax.rem(lax.shift_right_logical(low, jnp.int32(j)), 2)
            first = first + bit * (1 << order[j])
            second = second + bit * (1 << contrary[j])
        flip = parity == 1
        first, second = jnp.where(flip, second, first), jnp.where(flip, first, second)
        upper = t >= half
        goal = jnp.bitwise_xor(me, jnp.where(upper, first + 1, first))
        start = first_block(scalars_ref[rows_at + goal])
        block = start + lax.rem(me - lax.rem(start, mem_count) + mem_count, mem_count)
        slot = jnp.minimum(block // mem_count, memory_ref.shape[0] - 1)
        blocks_ref[t] = held[slot]
        holder = jnp.bitwise_xor(me, jnp.where(upper, second + 1, first))
        block = mine_start + lax.rem(
            holder - lax.rem(mine_start, mem_count) + mem_count, mem_count
        )
        bound = jnp.where(block == mine_end - 1, scalars_ref[tails_at + mine], height)
        bound = jnp.where(block < mine_end, bound, 0)
        live_ref[t] = jnp.where(token < bound, 0.0, MASKED)
        return carry

    lax.fori_loop(0, mem_count, one, 0)
    seq_steps = seq_masks(parity)
    for ref, base, mask in (
        (own_ref, 0, seq_steps[0]),
        (two_ref, 0, seq_steps[1]),
        (one_ref, 0, seq_steps[2]),
        (two_ref, 1, seq_steps[3]),
    ):
        goal = jnp.bitwise_xor(seq, mask)
        for i in range(3):
            weight = triple[i].astype(F32)
            chosen = weight[:, :slim]
            for j in range(1, width // slim):
                chosen = jnp.where(goal == j, weight[:, j * slim : (j + 1) * slim], chosen)
            start = (3 * base + i) * broad
            ref[:, start : start + broad] = jnp.concatenate(
                [chosen.astype(BF16), blank if i else extra], axis=1
            )
    for copy in copies[4:]:
        copy.wait()


def prepare(weights, gains, memory, scalars, spot, slim, broad):
    mem_count = lax.axis_size("mem")
    share, width = weights[0].shape
    first = 3 * broad + 5 * width
    second = sum(w.shape[1] for w in weights[8:])
    height = memory.shape[1]
    whole = lambda shape: pl.BlockSpec(shape, lambda *_: (0,) * len(shape))
    outs = [
        ((share, first), BF16),
        ((share, first + 3 * broad), BF16),
        ((share, first), BF16),
        ((share, second), BF16),
        ((mem_count, height, width), BF16),
        ((mem_count, height, 1), F32),
    ]
    return pl.pallas_call(
        functools.partial(prepare_kernel, slim, broad),
        out_shape=shaped(outs),
        grid_spec=pltpu.PrefetchScalarGridSpec(
            num_scalar_prefetch=2,
            grid=(1,),
            in_specs=[HBM] * len(weights) + [whole(gains.shape), HBM],
            out_specs=[whole(shape) for shape, _ in outs],
            scratch_shapes=[
                pltpu.VMEM((8, 128), F32),
                pltpu.VMEM((3, share, width), BF16),
                pltpu.VMEM(memory.shape, BF16),
                pltpu.SemaphoreType.DMA((4 + 15 + 2,)),
            ],
        ),
        compiler_params=vmem(16 + 3 * mem_count // 8),
        cost_estimate=cost(3),
        name="prepare",
    )(scalars, spot, *far(*weights), gains, *far(memory))


def slots_kernel(per, scalars_ref, spot_ref, blocks_ref, keep_ref, send_ref, done):
    mem_count = blocks_ref.shape[0]
    me, seq = spot_ref[0], spot_ref[1]
    parity = lax.rem(me, 2)
    copies = []
    for k, mask in enumerate(seq_masks(parity)):
        for s in range(per):
            slot = jnp.bitwise_xor(seq, mask) * per + s
            block = slot * mem_count + me

            def scan(i, carry):
                end, owner = carry
                end = end + scalars_ref[i]
                return end, owner + jnp.where(end <= block, 1, 0)

            _, owner = lax.fori_loop(0, mem_count, scan, (jnp.int32(0), jnp.int32(0)))
            row = lax.fori_loop(
                0,
                mem_count,
                lambda i, r: jnp.where(scalars_ref[2 * mem_count + i] == owner, i, r),
                jnp.int32(0),
            )
            gap = jnp.bitwise_xor(row, me)
            bit = lambda b: lax.rem(lax.shift_right_logical(gap, jnp.int32(b)), 2)
            spots = [
                sum(bit(b) * (1 << j) for j, b in enumerate(order)) for order in orders(mem_count)
            ]
            at = jnp.where(parity == 1, spots[1], spots[0]) + bit(0) * (mem_count // 2)
            copies.append(
                pltpu.make_async_copy(
                    blocks_ref.at[at],
                    (keep_ref, send_ref)[k // 2].at[k % 2 * per + s],
                    done.at[len(copies)],
                )
            )
    for copy in copies:
        copy.start()
    for copy in copies:
        copy.wait()


def pick_slots(blocks, slots, scalars, spot):
    per = slots // lax.axis_size("seq")
    shape = (2 * per,) + blocks.shape[1:]
    return pl.pallas_call(
        functools.partial(slots_kernel, per),
        out_shape=shaped([(shape, BF16)] * 2),
        grid_spec=pltpu.PrefetchScalarGridSpec(
            num_scalar_prefetch=2,
            grid=(1,),
            in_specs=[HBM],
            out_specs=[pl.BlockSpec(shape, lambda *_: (0, 0, 0))] * 2,
            scratch_shapes=[pltpu.SemaphoreType.DMA((slots,))],
        ),
        compiler_params=vmem(8),
        cost_estimate=cost(2),
        name="pick_slots",
    )(scalars, spot, blocks)


def feed_kernel(
    order_ref, h2_ref, c3_ref, gain_ref, source_ref,
    gate_a_ref, gate_b_ref, up_a_ref, up_b_ref, *refs,
):
    down_refs, refs = refs[:-15], refs[-15:]
    out_ref, dh2_ref, c2_ref, gain_grad_ref, bundle_ref, act_near_ref, n3_near_ref = refs[:7]
    turn, n3_rel, total, dn3, gate_w, up_w, down_w, act_all = refs[7:]
    step, steps = pl.program_id(0), pl.num_programs(0)
    half, unit = gate_a_ref.shape
    width = h2_ref.shape[1]
    hidden = unit * steps
    slim = width // 2

    @pl.when(step == 0)
    def _():
        columns = lax.broadcasted_iota(jnp.int32, (width, width), 1)
        turn[...] = (columns == source_ref[...]).astype(F32).astype(BF16)
        h2 = h2_ref[...]
        n3 = (h2 * norm_scale(h2) * gain_ref[2:3]).astype(BF16)
        rel = right_product(n3, turn[...]).astype(BF16)
        n3_rel[...] = rel
        n3_near_ref[...] = rel[:, :slim]
        bundle_ref[:, 2 * hidden + hidden // 2 :] = rel[:, slim:]
        total[...] = jnp.zeros_like(total)
        dn3[...] = jnp.zeros_like(dn3)

    base = 0
    for ref in down_refs:
        number = ref.shape[0]
        for block in range(number):

            @pl.when(step == base + block)
            def _(ref=ref, block=block):
                down_w[...] = ref[block]

        base += number
    gate_w[:half] = gate_a_ref[...]
    gate_w[half:] = gate_b_ref[...]
    up_w[:half] = up_a_ref[...]
    up_w[half:] = up_b_ref[...]
    down = down_w[...]
    n3, c3 = n3_rel[...], c3_ref[...]
    gate = product(n3, gate_w[...])
    upper = product(n3, up_w[...])
    dact = right_product(c3, down)
    inner = 0.7978845608028654 * (gate + 0.044715 * gate * gate * gate)
    bent = jnp.tanh(inner)
    gelu = 0.5 * gate * (1.0 + bent)
    slope = 0.5 * (1.0 + bent) + 0.5 * gate * (1.0 - bent * bent) * (
        0.7978845608028654 * (1.0 + 3.0 * 0.044715 * gate * gate)
    )
    act = (gelu * upper).astype(BF16)
    dgate = (dact * upper * slope).astype(BF16)
    dupper = (dact * gelu).astype(BF16)
    total[...] += product(act, down)
    act_all[step] = act
    column = pl.multiple_of(order_ref[step] * unit, LANES)
    bundle_ref[:, pl.ds(column, unit)] = dgate
    bundle_ref[:, pl.ds(pl.multiple_of(hidden + column, LANES), unit)] = dupper
    dn3[...] += right_product(dgate, gate_w[...]) + right_product(dupper, up_w[...])

    @pl.when(step == steps - 1)
    def _():
        middle = act_all.shape[0] // 2
        for t in range(middle):
            act_near_ref[:, t * unit : (t + 1) * unit] = act_all[t]
            first = 2 * hidden + t * unit
            bundle_ref[:, first : first + unit] = act_all[middle + t]
        h2 = h2_ref[...]
        out_ref[...] = (h2 + total[...]).astype(BF16)
        high = dn3[...].astype(BF16)
        rest = (dn3[...] - high.astype(F32)).astype(BF16)
        upstream = product(high, turn[...]) + product(rest, turn[...])
        scale = norm_scale(h2)
        dh2 = c3_ref[...].astype(F32) + norm_hidden_grad(h2, scale, gain_ref[2:3], upstream)
        dh2_ref[...] = dh2
        c2_ref[...] = dh2.astype(BF16)
        gain_grad_ref[...] = jnp.sum(upstream * h2 * scale, axis=0, keepdims=True)


def feed(order, h2, c3, gains, source, both, down):
    rows, width = h2.shape
    half, hidden = both[0].shape
    hidden = hidden // 2
    steps = order.shape[0]
    unit = hidden // steps
    whole = lambda shape: pl.BlockSpec(shape, lambda i, o: (0, 0))
    column = pl.BlockSpec((half, unit), lambda i, o: (0, o[i]))
    beside = pl.BlockSpec((half, unit), lambda i, o: (0, o[i] + steps))
    flat = (rows, width)
    shapes = [
        (flat, BF16),
        (flat, F32),
        (flat, BF16),
        ((1, width), F32),
        ((rows, 2 * hidden + hidden // 2 + width // 2), BF16),
        ((rows, hidden // 2), BF16),
        ((rows, width // 2), BF16),
    ]
    return pl.pallas_call(
        feed_kernel,
        out_shape=shaped(shapes, (0,)),
        grid_spec=pltpu.PrefetchScalarGridSpec(
            num_scalar_prefetch=1,
            grid=(steps,),
            in_specs=[whole(flat)] * 2
            + [whole(gains.shape), whole((width, 1))]
            + [column, column, beside, beside]
            + [pl.BlockSpec(w.shape, lambda i, o: (0, 0, 0)) for w in down],
            out_specs=[whole(shape) for shape, _ in shapes],
            scratch_shapes=[
                pltpu.VMEM((width, width), BF16),
                pltpu.VMEM(flat, BF16),
                pltpu.VMEM(flat, F32),
                pltpu.VMEM(flat, F32),
                pltpu.VMEM((2 * half, unit), BF16),
                pltpu.VMEM((2 * half, unit), BF16),
                pltpu.VMEM((unit, width), BF16),
                pltpu.VMEM((steps, rows, unit), BF16),
            ],
        ),
        compiler_params=vmem(22),
        cost_estimate=cost(13),
        name="feed",
    )(order, h2, *far(c3), gains, source, *far(*both, *both), *down)


def feed_weights_kernel(
    own_ref, other_ref, act_ref, n3_ref, c3_ref, c3_other_ref,
    both_keep_ref, both_send_ref, down_keep_ref, down_send_ref,
):
    hidden = both_keep_ref.shape[2]
    units = act_ref.shape[1]
    quarter, third = both_keep_ref.shape[1], down_keep_ref.shape[0]
    edge = 2 * hidden + units
    mine = transposed(n3_ref[...])
    theirs = transposed(other_ref[:, edge:])
    step = hidden // 2
    for first in range(0, 2 * hidden, step):
        grad = product(mine, own_ref[:, first : first + step])
        grad = grad + product(theirs, other_ref[:, first : first + step])
        grad = grad.astype(BF16)
        part, column = first // hidden, first % hidden
        both_keep_ref[part, :, column : column + step] = grad[:quarter]
        both_send_ref[part, :, column : column + step] = grad[quarter:]
    c3, c3_other = c3_ref[...], c3_other_ref[...]
    for k, ref in enumerate((down_keep_ref, down_send_ref)):
        first = k * third
        mine = transposed(act_ref[:, first : first + third])
        theirs = transposed(other_ref[:, 2 * hidden + first : 2 * hidden + first + third])
        ref[...] = (product(mine, c3) + product(theirs, c3_other)).astype(BF16)


def feed_weights(own, other, act, n3, c3, c3_other):
    rows, width = c3.shape
    units = act.shape[1]
    hidden = 2 * units
    pair = ((2, width // 4, hidden), BF16)
    single = ((units // 2, width), BF16)
    return pl.pallas_call(
        feed_weights_kernel,
        out_shape=shaped([pair, pair, single, single]),
        compiler_params=vmem(24),
        cost_estimate=cost(5),
        name="feed_weights",
    )(own, other, act, n3, c3, c3_other)


def head_mask(shape, head):
    return lax.broadcasted_iota(jnp.int32, shape, 1) // HEAD_DIM == head


def pick_head(values, head):
    return jnp.where(head_mask(values.shape, head), values, jnp.zeros_like(values))


def transposed(values):
    return values.astype(F32).T.astype(values.dtype)


LOG2E = 1.4426950408889634
SHRINK = SCALING * LOG2E


def soft_parts(scores, axis=0):
    peak = jnp.max(scores, axis=0, keepdims=True)
    powers = jnp.exp2(scores - peak)
    total = jnp.sum(powers, axis=0, keepdims=True)
    return powers, 1.0 / total, peak + jnp.log2(total)


def causal_scores(keys, queries):
    scores = right_product(keys, queries) * SHRINK
    last = scores.shape[0] - scores.shape[1]
    corner = scores[last:]
    key_place = lax.broadcasted_iota(jnp.int32, corner.shape, 0)
    query_place = lax.broadcasted_iota(jnp.int32, corner.shape, 1)
    corner = jnp.where(key_place <= query_place, corner, MASKED)
    return corner if last == 0 else jnp.concatenate([scores[:last], corner], axis=0)


def cross_scores(keys, queries, bias):
    return right_product(keys, queries) * SHRINK + bias


def score_grads(scores, logs, inner):
    chance = jnp.exp2(scores - logs)
    spread = jnp.sum(chance * inner, axis=0, keepdims=True)
    return chance.astype(BF16), (chance * (inner - spread)).astype(BF16)


def weight_copies(refs, masks, me, columns, target, done, base):
    copies = []
    for ref in refs:
        for block in range(ref.shape[0]):
            number = len(copies)
            spot = 0
            if len(refs) > 1:
                mask = masks[0][number]
                if masks[1][number] != mask:
                    mask = jnp.where(lax.rem(me, 2) == 1, masks[1][number], mask)
                spot = pl.multiple_of(jnp.bitwise_xor(me, mask) * ref.shape[1], 16)
            copies.append(
                pltpu.make_async_copy(
                    ref.at[block, :, columns[0] : columns[1]],
                    target.at[pl.ds(spot, ref.shape[1])],
                    done.at[base + number],
                )
            )
    return copies


def blocks_in(refs):
    return sum(ref.shape[0] for ref in refs)


def self_rows_kernel(heads, masks, counts, spot_ref, *refs):
    seq_count, weights = counts
    x_refs, refs = refs[:3], refs[3:]
    x_list = [x_refs[0], x_refs[1], x_refs[2].at[0], x_refs[2].at[1]]
    w_refs, refs = refs[:weights], refs[weights:]
    o_refs, refs = refs[:seq_count], refs[seq_count:]
    n1_ref, qkv_ref, gain_ref, log_ref, x_all, w_all, o_all, done = refs
    rows, width = x_refs[0].shape
    broad = w_all.shape[1] // 3
    me, seq = spot_ref[0], spot_ref[1]
    copies = weight_copies(w_refs, masks, me, (0, 3 * broad), w_all, done, 0)
    base = len(copies)
    copies += [
        pltpu.make_async_copy(ref, x_all.at[jnp.bitwise_xor(seq, mask)], done.at[base + k])
        for k, (ref, mask) in enumerate(zip(x_list, seq_masks(lax.rem(me, 2))))
    ]
    run(copies)
    slim = heads * HEAD_DIM
    edge = slim // LANES * LANES
    gains = w_all[:, edge : edge + LANES].astype(F32).T[slim - edge : slim - edge + 8]
    gain_ref[...] = gains
    for j in range(seq_count):
        x = x_all[j].astype(F32)
        n1 = (x * norm_scale(x) * gains[0:1]).astype(BF16)
        n1_ref[j * rows : (j + 1) * rows] = n1
        qkv_ref[j * rows : (j + 1) * rows] = product(n1, w_all[...]).astype(BF16)
    values_t = transposed(qkv_ref[:, 2 * broad :])
    for j in range(seq_count):
        first, last = j * rows, (j + 1) * rows
        queries = qkv_ref[first:last, :broad]
        parts = []
        for head in range(heads):
            scores = causal_scores(qkv_ref[:last, broad : 2 * broad], pick_head(queries, head))
            powers, inverse, logs = soft_parts(scores)
            log_ref[head : head + 1, first:last] = logs
            lines = values_t[head * HEAD_DIM : (head + 1) * HEAD_DIM, :last]
            parts.append(product(lines, powers.astype(BF16)) * inverse)
        o_all[j] = jnp.concatenate(parts, axis=0).T.astype(BF16)
    for k, ref in enumerate(o_refs):
        ref[...] = o_all[lax.rem(seq + k, seq_count)]


def self_rows(x_pieces, weights, spot, heads, broad, masks):
    count = lax.axis_size("seq")
    rows, width = x_pieces[0].shape
    length, slim = rows * count, heads * HEAD_DIM
    whole = lambda shape: pl.BlockSpec(shape, lambda i, spot: (0, 0))
    shapes = [((rows, slim), BF16)] * count + [
        ((length, width), BF16),
        ((length, 3 * broad), BF16),
        ((8, width), F32),
        ((8, length), F32),
    ]
    outs = pl.pallas_call(
        functools.partial(self_rows_kernel, heads, masks, (count, len(weights))),
        out_shape=shaped(shapes, (count, count + 1, count + 3)),
        grid_spec=pltpu.PrefetchScalarGridSpec(
            num_scalar_prefetch=1,
            grid=(1,),
            in_specs=[HBM] * (3 + len(weights)),
            out_specs=[whole(s) for s, _ in shapes],
            scratch_shapes=[
                pltpu.VMEM((count, rows, width), BF16),
                pltpu.VMEM((width, 3 * broad), BF16),
                pltpu.VMEM((count, rows, slim), BF16),
                pltpu.SemaphoreType.DMA((blocks_in(weights) + count,)),
            ],
        ),
        compiler_params=vmem(14),
        cost_estimate=cost(10),
        name="self_rows",
    )(spot, *x_pieces, *weights)
    return outs[:count], *outs[count:]


def key_values_kernel(masks, number, edge, spot_ref, keys_ref, *refs):
    w_refs, (out_ref, w_all, done) = refs[:number], refs[number:]

    @pl.when(pl.program_id(0) == 0)
    def _():
        columns = (edge, edge + w_all.shape[1])
        run(weight_copies(w_refs, masks, spot_ref[0], columns, w_all, done, 0))

    out_ref[...] = product(keys_ref[...], w_all[...]).astype(BF16)


def key_values(keys, weights, spot, chunk, edge, masks):
    width = keys.shape[1]
    columns = 2 * width
    return pl.pallas_call(
        functools.partial(key_values_kernel, masks, len(weights), edge),
        out_shape=jax.ShapeDtypeStruct((keys.shape[0], columns), BF16),
        grid_spec=pltpu.PrefetchScalarGridSpec(
            num_scalar_prefetch=1,
            grid=(keys.shape[0] // chunk,),
            in_specs=[pl.BlockSpec((chunk, width), lambda i, spot: (i, 0))] + [HBM] * len(weights),
            out_specs=pl.BlockSpec((chunk, columns), lambda i, spot: (i, 0)),
            scratch_shapes=[
                pltpu.VMEM((width, columns), BF16),
                pltpu.SemaphoreType.DMA((blocks_in(weights),)),
            ],
        ),
        compiler_params=vmem(12),
        cost_estimate=cost(4),
        name="key_values",
    )(spot, keys, *weights)


def cross_attend(queries, keys, values, live, log_ref):
    values_t = transposed(values)
    pieces = []
    for head in range(LANES // HEAD_DIM):
        powers, inverse, logs = soft_parts(cross_scores(keys, pick_head(queries, head), live))
        log_ref[0, head : head + 1] = logs
        lines = values_t[head * HEAD_DIM : (head + 1) * HEAD_DIM]
        pieces.append(product(lines, powers.astype(BF16)) * inverse)
    return jnp.concatenate(pieces, axis=0).T.astype(BF16)


def rows_first_kernel(masks, counts, edge, spot_ref, *refs):
    seq_count, weights = counts
    a_refs, refs = refs[:seq_count], refs[seq_count:]
    w_refs, refs = refs[:weights], refs[weights:]
    x_ref, gain_ref, live_ref, k_ref, v_ref = refs[:5]
    q2_ref, a2_ref, h1_ref, log_ref = refs[5:9]
    a_all, w_o1, w_q2, q_parts, done = refs[9:]
    step = pl.program_id(0)
    me, seq = spot_ref[0], spot_ref[1]
    width = x_ref.shape[1]

    @pl.when(step == 0)
    def _():
        copies = [
            pltpu.make_async_copy(
                ref, a_all.at[lax.rem(seq - k + seq_count, seq_count)], done.at[k]
            )
            for k, ref in enumerate(a_refs)
        ]
        copies += weight_copies(w_refs, masks, me, (edge, edge + width), w_o1, done, seq_count)
        later = weight_copies(
            w_refs, masks, me, (edge + width, edge + 2 * width), w_q2, done, len(copies)
        )
        for copy in copies + later:
            copy.start()
        for copy in copies:
            copy.wait()
        a1 = jnp.concatenate([a_all[j] for j in range(seq_count)], axis=1)
        h1 = x_ref[...].astype(F32) + right_product(a1, w_o1[...])
        h1_ref[...] = h1
        n2 = (h1 * norm_scale(h1) * gain_ref[1:2]).astype(BF16)
        for copy in later:
            copy.wait()
        q2 = product(n2, w_q2[...]).astype(BF16)
        q2_ref[...] = q2
        for i in range(q_parts.shape[0]):
            q_parts[i] = q2[:, i * LANES : (i + 1) * LANES]

    a2_ref[...] = cross_attend(q_parts[step], k_ref[...], v_ref[...], live_ref[...], log_ref)


def rows_second_kernel(masks, weights, edge, spot_ref, *refs):
    w_refs, refs = refs[:weights], refs[weights:]
    h1_ref, early_ref, live_ref, q_ref, k_ref, v_ref, a2_ref, h2_ref, log_ref = refs[:9]
    w_o2, o_parts, done = refs[9:]
    step, parts = pl.program_id(0), o_parts.shape[0]
    width = h1_ref.shape[1]
    columns = (edge + 4 * width, edge + 5 * width)
    copies = weight_copies(w_refs, masks, spot_ref[0], columns, w_o2, done, 0)

    @pl.when(step == 0)
    def _():
        for copy in copies:
            copy.start()

    o_parts[step] = cross_attend(q_ref[...], k_ref[...], v_ref[...], live_ref[...], log_ref)

    @pl.when(step == parts - 1)
    def _():
        for copy in copies:
            copy.wait()
        a2 = jnp.concatenate([early_ref[...]] + [o_parts[i] for i in range(parts)], axis=1)
        a2_ref[...] = a2
        h2_ref[...] = h1_ref[...] + right_product(a2, w_o2[...])


def rows_first(a_pieces, weights, x, gains, live, kv, spot, edge, masks):
    count = len(a_pieces)
    rows, width = x.shape
    keys = kv.shape[0]
    parts = width // LANES
    flat = (rows, width)
    whole = lambda shape: pl.BlockSpec(shape, lambda i, spot: (0, 0))
    _, row, key, value = rows_specs(rows, keys, width, 0)
    log = pl.BlockSpec((1, 8, rows), lambda i, spot: (i, 0, 0))
    shapes = [
        (flat, BF16), ((rows, width // 2), BF16), (flat, F32), ((parts // 2, 8, rows), F32)
    ]
    square = pltpu.VMEM((width, width), BF16)
    return pl.pallas_call(
        functools.partial(rows_first_kernel, masks, (count, len(weights)), edge),
        out_shape=shaped(shapes),
        grid_spec=pltpu.PrefetchScalarGridSpec(
            num_scalar_prefetch=1,
            grid=(parts // 2,),
            in_specs=[HBM] * (count + len(weights))
            + [whole(flat), whole(gains.shape), whole(live.shape), key, value],
            out_specs=[whole(flat), row, whole(flat), log],
            scratch_shapes=[
                pltpu.VMEM((count,) + a_pieces[0].shape, BF16),
                square, square,
                pltpu.VMEM((parts, rows, LANES), BF16),
                pltpu.SemaphoreType.DMA((count + 2 * blocks_in(weights),)),
            ],
        ),
        compiler_params=vmem(max(16, keys * 8 // 1024 + 8)),
        cost_estimate=cost(7),
        name="rows_first",
    )(spot, *a_pieces, *weights, x, gains, live, kv, kv)


def rows_second(weights, h1, early, live, q2, kv, spot, edge, masks):
    rows, width = h1.shape
    keys = kv.shape[0]
    parts = width // LANES // 2
    flat = (rows, width)
    whole = lambda shape: pl.BlockSpec(shape, lambda i, spot: (0, 0))
    _, row, key, value = rows_specs(rows, keys, width, parts)
    log = pl.BlockSpec((1, 8, rows), lambda i, spot: (i, 0, 0))
    return pl.pallas_call(
        functools.partial(rows_second_kernel, masks, len(weights), edge),
        out_shape=shaped([(flat, BF16), (flat, F32), ((parts, 8, rows), F32)]),
        grid_spec=pltpu.PrefetchScalarGridSpec(
            num_scalar_prefetch=1,
            grid=(parts,),
            in_specs=[HBM] * len(weights)
            + [whole(flat), whole(early.shape), whole(live.shape), row, key, value],
            out_specs=[whole(flat), whole(flat), log],
            scratch_shapes=[
                pltpu.VMEM((width, width), BF16),
                pltpu.VMEM((parts, rows, LANES), BF16),
                pltpu.SemaphoreType.DMA((blocks_in(weights),)),
            ],
        ),
        compiler_params=vmem(max(14, keys * 8 // 1024 + 8)),
        cost_estimate=cost(6),
        name="rows_second",
    )(spot, *weights, h1, early, live, q2, kv, kv)


def cross_backward(queries, upstream, live, keys, values, logs):
    keys_t = transposed(keys)
    pieces, dk, dv = [], 0.0, 0.0
    for head in range(LANES // HEAD_DIM):
        own = pick_head(queries, head)
        up_own = pick_head(upstream, head)
        inner = right_product(values, up_own)
        chance, grad = score_grads(cross_scores(keys, own, live), logs[head : head + 1], inner)
        dv = dv + product(chance, up_own)
        dk = dk + product(grad, own)
        lines = keys_t[head * HEAD_DIM : (head + 1) * HEAD_DIM]
        pieces.append(product(lines, grad))
    dq = jnp.concatenate(pieces, axis=0).T * SCALING
    return dq.astype(BF16), (dk * SCALING).astype(BF16), dv.astype(BF16)


def rows_early_kernel(masks, weights, edge, spot_ref, *refs):
    w_refs, refs = refs[:weights], refs[weights:]
    c2_ref, live_ref, log_ref, q_ref, k_ref, v_ref, up_ref, dq_ref, dk_ref, dv_ref = refs[:10]
    w_o2, up_parts, done = refs[10:]
    width = c2_ref.shape[1]

    @pl.when(pl.program_id(0) == 0)
    def _():
        columns = (edge + 4 * width, edge + 5 * width)
        run(weight_copies(w_refs, masks, spot_ref[0], columns, w_o2, done, 0))
        up = product(c2_ref[...], w_o2[...]).astype(BF16)
        up_ref[...] = up
        for i in range(up_parts.shape[0]):
            up_parts[i] = up[:, i * LANES : (i + 1) * LANES]

    dq_ref[...], dk_ref[...], dv_ref[...] = cross_backward(
        q_ref[...], up_parts[pl.program_id(0)], live_ref[...], k_ref[...], v_ref[...], log_ref[0]
    )


def rows_late_kernel(masks, counts, edge, spot_ref, *refs):
    seq_count, weights = counts
    w_refs, refs = refs[:weights], refs[weights:]
    up_ref, dq_early_ref, dh2_ref, h1_ref, gain_ref, live_ref, log_ref, q_ref, k_ref, v_ref = refs[:10]
    da_refs, refs = refs[10 : 10 + seq_count], refs[10 + seq_count :]
    dq2_ref, dk_ref, dv_ref, dh1_ref, gain_grad_ref = refs[:5]
    w_o1, w_q2, dq_parts, da_all, done = refs[5:]
    step = pl.program_id(0)
    me, seq = spot_ref[0], spot_ref[1]
    width = dh2_ref.shape[1]
    parts = dq_parts.shape[0]
    copies = weight_copies(
        w_refs, masks, me, (edge + width, edge + 2 * width), w_q2, done, 0
    )
    copies += weight_copies(w_refs, masks, me, (edge, edge + width), w_o1, done, len(copies))

    @pl.when(step == 0)
    def _():
        for copy in copies:
            copy.start()

    dq_parts[step], dk_ref[...], dv_ref[...] = cross_backward(
        q_ref[...], up_ref[...], live_ref[...], k_ref[...], v_ref[...], log_ref[0]
    )

    @pl.when(step == parts - 1)
    def _():
        for copy in copies:
            copy.wait()
        dq2 = jnp.concatenate([dq_early_ref[...]] + [dq_parts[i] for i in range(parts)], axis=1)
        dq2_ref[...] = dq2
        dn2 = right_product(dq2, w_q2[...])
        h1 = h1_ref[...]
        scale = norm_scale(h1)
        dh1 = dh2_ref[...] + norm_hidden_grad(h1, scale, gain_ref[1:2], dn2)
        dh1_ref[...] = dh1
        gain_grad_ref[...] = jnp.sum(dn2 * h1 * scale, axis=0, keepdims=True)
        c1 = dh1.astype(BF16)
        up = product(c1, w_o1[...])
        slim = da_all.shape[2]
        for j in range(seq_count):
            da_all[j] = up[:, j * slim : (j + 1) * slim].astype(BF16)
        for k, ref in enumerate(da_refs):
            ref[...] = da_all[lax.rem(seq + k, seq_count)]


def rows_specs(rows, keys, width, start):
    parts = width // LANES
    row = pl.BlockSpec((rows, LANES), lambda i, spot: (0, i + start))
    key = pl.BlockSpec((keys, LANES), lambda i, spot: (0, i + start))
    value = pl.BlockSpec((keys, LANES), lambda i, spot: (0, i + start + parts))
    log = pl.BlockSpec((1, 8, rows), lambda i, spot: (i, 0, 0))
    return log, row, key, value


def rows_early(weights, c2, live, logs, q2, kv, spot, edge, masks):
    rows, width = c2.shape
    keys = kv.shape[0]
    parts = width // LANES // 2
    whole = lambda shape: pl.BlockSpec(shape, lambda i, spot: (0, 0))
    log, row, key, value = rows_specs(rows, keys, width, 0)
    half = width // 2
    shapes = [((rows, width), BF16), ((rows, half), BF16)] + [((keys, half), BF16)] * 2
    return pl.pallas_call(
        functools.partial(rows_early_kernel, masks, len(weights), edge),
        out_shape=shaped(shapes, (2, 3)),
        grid_spec=pltpu.PrefetchScalarGridSpec(
            num_scalar_prefetch=1,
            grid=(parts,),
            in_specs=[HBM] * len(weights)
            + [whole((rows, width)), whole(live.shape), log, row, key, value],
            out_specs=[whole((rows, width)), row, key, key],
            scratch_shapes=[
                pltpu.VMEM((width, width), BF16),
                pltpu.VMEM((2 * parts, rows, LANES), BF16),
                pltpu.SemaphoreType.DMA((blocks_in(weights),)),
            ],
        ),
        compiler_params=vmem(max(12, keys * 8 // 1024 + 12)),
        cost_estimate=cost(10),
        name="rows_early",
    )(spot, *weights, c2, live, logs, q2, kv, kv)


def rows_late(weights, up, dq_early, dh2, h1, gains, live, logs, q2, kv, spot, edge, masks):
    count = lax.axis_size("seq")
    rows, width = dh2.shape
    keys = kv.shape[0]
    parts = width // LANES // 2
    slim = width // count
    flat = (rows, width)
    half = width // 2
    whole = lambda shape: pl.BlockSpec(shape, lambda i, spot: (0, 0))
    log, row, key, value = rows_specs(rows, keys, width, parts)
    key_out = pl.BlockSpec((keys, LANES), lambda i, spot: (0, i))
    shapes = [((rows, slim), BF16)] * count + [
        (flat, BF16), ((keys, half), BF16), ((keys, half), BF16),
        (flat, F32), ((1, width), F32),
    ]
    square = pltpu.VMEM((width, width), BF16)
    outs = pl.pallas_call(
        functools.partial(rows_late_kernel, masks, (count, len(weights)), edge),
        out_shape=shaped(shapes, range(count, count + 6)),
        grid_spec=pltpu.PrefetchScalarGridSpec(
            num_scalar_prefetch=1,
            grid=(parts,),
            in_specs=[HBM] * len(weights)
            + [row, whole((rows, half)), whole(flat), whole(flat)]
            + [whole(gains.shape), whole(live.shape), log, row, key, value],
            out_specs=[whole((rows, slim))] * count
            + [whole(flat), key_out, key_out, whole(flat), whole((1, width))],
            scratch_shapes=[
                square, square,
                pltpu.VMEM((parts, rows, LANES), BF16),
                pltpu.VMEM((count, rows, slim), BF16),
                pltpu.SemaphoreType.DMA((2 * blocks_in(weights),)),
            ],
        ),
        compiler_params=vmem(max(18, keys * 8 // 1024 + 12)),
        cost_estimate=cost(11),
        name="rows_late",
    )(spot, *weights, up, dq_early, dh2, h1, gains, live, logs, q2, kv, kv)
    return outs[:count], *outs[count:]


def turn_of(source_ref, width):
    columns = lax.broadcasted_iota(jnp.int32, (width, width), 1)
    return (columns == source_ref[...]).astype(F32).astype(BF16)


def cross_weights_kernel(masks, number, edge, spot_ref, *refs):
    w_refs, refs = refs[:number], refs[number:]
    source_ref, h1_ref, gain_ref, dq2_ref, c2_ref, a2_ref, keys_ref = refs[:7]
    parts, refs = refs[7:11], refs[11:]
    near_ref, far_ref, dmem_ref = refs[:3]
    w_all, turn, dk_sum, dv_sum, done = refs[3:]
    dk = jnp.concatenate([parts[0][...], parts[1][...]], axis=1)
    dv = jnp.concatenate([parts[2][...], parts[3][...]], axis=1)
    step, steps = pl.program_id(0), pl.num_programs(0)
    width = dq2_ref.shape[1]
    half = width // 2
    columns = (edge + 2 * width, edge + 4 * width)
    copies = weight_copies(w_refs, masks, spot_ref[0], columns, w_all, done, 0)

    def put(column, values):
        values = values.astype(BF16)
        near_ref[:, column : column + width] = values[:half]
        far_ref[:, column : column + width] = values[half:]

    @pl.when(step == 0)
    def _():
        for copy in copies:
            copy.start()
        turn[...] = turn_of(source_ref, width)
        h1 = h1_ref[...]
        n2 = (h1 * norm_scale(h1) * gain_ref[1:2]).astype(BF16)
        n2_t = right_product(turn[...], n2).astype(BF16)
        put(0, product(n2_t, dq2_ref[...]))
        c2_t = right_product(turn[...], c2_ref[...]).astype(BF16)
        put(3 * width, product(c2_t, a2_ref[...]))
        dk_sum[...] = jnp.zeros_like(dk_sum)
        dv_sum[...] = jnp.zeros_like(dv_sum)

    keys_t = right_product(turn[...], keys_ref[...]).astype(BF16)
    dk_sum[...] += product(keys_t, dk)
    dv_sum[...] += product(keys_t, dv)

    @pl.when(step == 0)
    def _():
        for copy in copies:
            copy.wait()

    dmem_ref[...] = (
        right_product(dk, w_all[:, :width]) + right_product(dv, w_all[:, width:])
    ).astype(BF16)

    @pl.when(step == steps - 1)
    def _():
        put(width, dk_sum[...])
        put(2 * width, dv_sum[...])


def cross_weights(weights, source, h1, gains, dq2, c2, a2, keys, grads, spot, chunk, edge, masks):
    rows, width = h1.shape
    whole = lambda shape: pl.BlockSpec(shape, lambda i, spot: (0, 0))
    part = pl.BlockSpec((chunk, width), lambda i, spot: (i, 0))
    half = ((width // 2, 4 * width), BF16)
    return pl.pallas_call(
        functools.partial(cross_weights_kernel, masks, len(weights), edge),
        out_shape=shaped([half, half, (keys.shape, BF16)], (0,)),
        grid_spec=pltpu.PrefetchScalarGridSpec(
            num_scalar_prefetch=1,
            grid=(keys.shape[0] // chunk,),
            in_specs=[HBM] * len(weights)
            + [whole(source.shape), whole((rows, width)), whole(gains.shape)]
            + [whole((rows, width))] * 3
            + [part]
            + [pl.BlockSpec((chunk, width // 2), lambda i, spot: (i, 0))] * 4,
            out_specs=[whole(half[0]), whole(half[0]), part],
            scratch_shapes=[
                pltpu.VMEM((width, 2 * width), BF16),
                pltpu.VMEM((width, width), BF16),
                pltpu.VMEM((width, width), F32),
                pltpu.VMEM((width, width), F32),
                pltpu.SemaphoreType.DMA((blocks_in(weights),)),
            ],
        ),
        compiler_params=vmem(24),
        cost_estimate=cost(10),
        name="cross_weights",
    )(spot, *weights, source, h1, gains, dq2, c2, a2, keys, *grads)


def self_backward_kernel(heads, masks, counts, spot_ref, *refs):
    seq_count, weights = counts
    up_refs, refs = refs[:seq_count], refs[seq_count:]
    x_refs, refs = refs[:3], refs[3:]
    x_list = [x_refs[0], x_refs[1], x_refs[2].at[0], x_refs[2].at[1]]
    w_refs, refs = refs[:weights], refs[weights:]
    qkv_ref, log_ref, refs = refs[0], refs[1], refs[2:]
    dn_refs, refs = refs[:2], refs[2:]
    steps = seq_masks(lax.rem(spot_ref[0], 2))
    dqkv_ref, gain_grad_ref = refs[:2]
    up_all, x_all, w_all, dn_all, dk_sum, dv_sum, done = refs[2:]
    rows = up_refs[0].shape[0]
    broad = w_all.shape[1] // 3
    slim = heads * HEAD_DIM
    me, seq = spot_ref[0], spot_ref[1]
    spots = [lax.rem(seq - k + seq_count, seq_count) for k in range(seq_count)]
    early = [
        pltpu.make_async_copy(ref, up_all.at[spots[k]], done.at[k])
        for k, ref in enumerate(up_refs)
    ]
    late = [
        pltpu.make_async_copy(ref, x_all.at[jnp.bitwise_xor(seq, mask)], done.at[seq_count + k])
        for k, (ref, mask) in enumerate(zip(x_list, steps))
    ]
    late += weight_copies(w_refs, masks, me, (0, 3 * broad), w_all, done, 2 * seq_count)
    for copy in early + late:
        copy.start()
    keys_t = transposed(qkv_ref[:, broad : 2 * broad])
    dk_sum[...] = jnp.zeros_like(dk_sum)
    dv_sum[...] = jnp.zeros_like(dv_sum)
    blank = jnp.zeros((rows, broad - slim), BF16)
    for copy in early:
        copy.wait()
    for j in range(seq_count):
        first, last = j * rows, (j + 1) * rows
        queries = qkv_ref[first:last, :broad]
        upstream = jnp.concatenate([up_all[j], blank], axis=1)
        parts = []
        for head in range(heads):
            own = pick_head(queries, head)
            up_own = pick_head(upstream, head)
            keys = qkv_ref[:last, broad : 2 * broad]
            inner = right_product(qkv_ref[:last, 2 * broad :], up_own)
            chance, grad = score_grads(
                causal_scores(keys, own), log_ref[head : head + 1, first:last], inner
            )
            dv_sum[:last] += product(chance, up_own)
            dk_sum[:last] += product(grad, own)
            lines = keys_t[head * HEAD_DIM : (head + 1) * HEAD_DIM, :last]
            parts.append(product(lines, grad))
        rest = jnp.zeros((broad - slim, rows), F32)
        dq = jnp.concatenate(parts + [rest], axis=0).T * SCALING
        dqkv_ref[first:last, :broad] = dq.astype(BF16)
    dqkv_ref[:, broad : 2 * broad] = (dk_sum[...] * SCALING).astype(BF16)
    dqkv_ref[:, 2 * broad :] = dv_sum[...].astype(BF16)
    for copy in late:
        copy.wait()
    total = 0.0
    for j in range(seq_count):
        dn1 = right_product(dqkv_ref[j * rows : (j + 1) * rows], w_all[...])
        x = x_all[j].astype(F32)
        total = total + jnp.sum(dn1 * x * norm_scale(x), axis=0, keepdims=True)
        dn_all[j] = dn1.astype(BF16)
    gain_grad_ref[...] = total
    for k, mask in enumerate(steps):
        dn_refs[k // 2][k % 2] = dn_all[jnp.bitwise_xor(seq, mask)]


def self_backward(up_pieces, x_pieces, weights, qkv, logs, spot, heads, masks):
    count = len(up_pieces)
    rows, width = x_pieces[0].shape
    slim = up_pieces[0].shape[1]
    length, broad = qkv.shape[0], qkv.shape[1] // 3
    whole = lambda shape: pl.BlockSpec(shape, lambda i, spot: (0, 0))
    shapes = [((2, rows, width), BF16)] * 2 + [(qkv.shape, BF16), ((1, width), F32)]
    outs = pl.pallas_call(
        functools.partial(self_backward_kernel, heads, masks, (count, len(weights))),
        out_shape=shaped(shapes),
        grid_spec=pltpu.PrefetchScalarGridSpec(
            num_scalar_prefetch=1,
            grid=(1,),
            in_specs=[HBM] * (count + 3 + len(weights)) + [whole(qkv.shape), whole(logs.shape)],
            out_specs=[
                pl.BlockSpec(s, lambda i, spot, n=len(s): (0,) * n) for s, _ in shapes
            ],
            scratch_shapes=[
                pltpu.VMEM((count, rows, slim), BF16),
                pltpu.VMEM((count, rows, width), BF16),
                pltpu.VMEM((width, 3 * broad), BF16),
                pltpu.VMEM((count, rows, width), BF16),
                pltpu.VMEM((length, broad), F32),
                pltpu.VMEM((length, broad), F32),
                pltpu.SemaphoreType.DMA((2 * count + blocks_in(weights),)),
            ],
        ),
        compiler_params=vmem(18),
        cost_estimate=cost(13),
        name="self_backward",
    )(spot, *up_pieces, *x_pieces, *weights, qkv, logs)
    return outs


def self_weights_kernel(
    spot_ref, source_ref, n1_ref, dqkv_ref, dh1_ref, gain_ref, *refs
):
    a_refs, (near_ref, far_ref, a_all) = refs[:-3], refs[-3:]
    width = n1_ref.shape[1]
    half = width // 2
    count = len(a_refs)
    turn = turn_of(source_ref, width)
    column = 0

    def put(values):
        nonlocal column
        values = values.astype(BF16)
        near_ref[:, column : column + values.shape[1]] = values[:half]
        far_ref[:, column : column + values.shape[1]] = values[half:]
        column += values.shape[1]

    for k, ref in enumerate(a_refs):
        a_all[lax.rem(spot_ref[1] - k + count, count)] = ref[...]
    a1 = jnp.concatenate([a_all[j] for j in range(count)], axis=1)
    c1_t = right_product(turn, dh1_ref[...].astype(BF16)).astype(BF16)
    put(product(c1_t, a1))
    put(right_product(turn, gain_ref[...].astype(BF16)))
    n1_t = right_product(turn, n1_ref[...]).astype(BF16)
    put(product(n1_t, dqkv_ref[...]))


def self_weights(source, n1, dqkv, dh1, gain_grads, a_pieces, spot):
    width = n1.shape[1]
    half = ((width // 2, width + LANES + dqkv.shape[1]), BF16)
    whole = lambda shape: pl.BlockSpec(shape, lambda i, spot: (0, 0))
    ins = [source, n1, dqkv, dh1, gain_grads, *a_pieces]
    return pl.pallas_call(
        self_weights_kernel,
        out_shape=shaped([half, half]),
        grid_spec=pltpu.PrefetchScalarGridSpec(
            num_scalar_prefetch=1,
            grid=(1,),
            in_specs=[whole(a.shape) for a in ins],
            out_specs=[whole(half[0])] * 2,
            scratch_shapes=[pltpu.VMEM((len(a_pieces),) + a_pieces[0].shape, BF16)],
        ),
        compiler_params=vmem(16),
        cost_estimate=cost(6),
        name="self_weights",
    )(spot, *ins)


def last_rows_kernel(keep_ref, one_ref, two_ref, x_ref, dh1_ref, gain_ref, out_ref):
    dn1 = keep_ref[0].astype(F32) + one_ref[0].astype(F32) + two_ref[...].astype(F32)
    x = x_ref[...].astype(F32)
    out_ref[...] = (
        dh1_ref[...] + norm_hidden_grad(x, norm_scale(x), gain_ref[0:1], dn1)
    ).astype(BF16)


def last_rows(keep, one, two, x, dh1, gains):
    return pl.pallas_call(
        last_rows_kernel,
        out_shape=jax.ShapeDtypeStruct(x.shape, BF16),
        compiler_params=vmem(8),
        cost_estimate=cost(2),
        name="last_rows",
    )(keep, one, two, x, dh1, gains)


def finish_kernel(slim, broad, spot_ref, *refs):
    sources, outs, hold = refs[:12], refs[12:-1], refs[-1]

    def total(refs, columns):
        keep, one, two = refs
        return (
            keep[0, :, columns[0] : columns[1]].astype(F32)
            + one[0, :, columns[0] : columns[1]].astype(F32)
            + two[0, :, columns[0] : columns[1]].astype(F32)
        )

    pair, down, cross, rest = sources[0:3], sources[3:6], sources[6:9], sources[9:12]
    hidden, width = outs[0].shape[1], outs[2].shape[1]
    outs[0][...] = total(pair, (0, hidden))
    outs[1][...] = total(pair, (hidden, 2 * hidden))
    outs[2][...] = total(down, (0, width))
    for i in range(4):
        outs[3 + i][...] = total(cross, (i * width, (i + 1) * width))
    outs[7][...] = total(rest, (0, width))
    edge = width
    outs[-1][...] = total(rest, (edge, edge + LANES))
    edge = edge + LANES
    far_edge = edge + 3 * broad
    keep, one, two = rest
    steps = [jnp.bitwise_xor(spot_ref[1], m) for m in seq_masks(lax.rem(spot_ref[0], 2))]
    hold[steps[0]] = keep[0, :, edge:far_edge].astype(F32)
    hold[steps[1]] = two[0, :, edge:far_edge].astype(F32)
    hold[steps[2]] = one[0, :, edge:far_edge].astype(F32)
    hold[steps[3]] = two[0, :, far_edge : far_edge + 3 * broad].astype(F32)
    for i in range(3):
        outs[8 + i][...] = jnp.concatenate(
            [hold[j][:, i * broad : i * broad + slim] for j in range(hold.shape[0])], axis=1
        )


def finish(pair, down, cross, rest, spot, hidden, slim, broad):
    share, feed_share, width = pair[0].shape[1], down[0].shape[1], down[0].shape[2]
    count = lax.axis_size("seq")
    shapes = (
        [(share, hidden)] * 2 + [(feed_share, width)] + [(share, width)] * 8 + [(share, LANES)]
    )
    whole = lambda shape: pl.BlockSpec(shape, lambda i, spot: (0,) * len(shape))
    flat = [*pair, *down, *cross, *rest]
    return pl.pallas_call(
        functools.partial(finish_kernel, slim, broad),
        out_shape=shaped([(shape, F32) for shape in shapes]),
        grid_spec=pltpu.PrefetchScalarGridSpec(
            num_scalar_prefetch=1,
            grid=(1,),
            in_specs=[whole(a.shape) for a in flat],
            out_specs=[whole(shape) for shape in shapes],
            scratch_shapes=[pltpu.VMEM((count, share, 3 * broad), F32)],
        ),
        compiler_params=vmem(12),
        cost_estimate=cost(3),
        name="finish",
    )(spot, *flat)


def local(
    hidden_in,
    memory,
    cotangent,
    norm_self,
    query_self,
    key_self,
    value_self,
    output_self,
    norm_cross,
    query_cross,
    key_cross,
    value_cross,
    output_cross,
    norm_feed,
    gate_weight,
    up_weight,
    down_weight,
    block_counts,
    memory_tail,
    row_example,
):
    mem_count, seq_count = lax.axis_size("mem"), lax.axis_size("seq")
    mem_place, seq_place = lax.axis_index("mem"), lax.axis_index("seq")
    rows, width = hidden_in.shape[1], hidden_in.shape[2]
    inner = HEADS * HEAD_DIM
    near = HEADS // seq_count
    slim = near * HEAD_DIM
    broad = -(-(slim + 8) // LANES) * LANES
    share = norm_self.shape[0]
    hidden_width = gate_weight.shape[1]
    spot = jnp.stack([mem_place, seq_place]).astype(jnp.int32)
    scalars = jnp.concatenate([block_counts, memory_tail, row_example])
    masks = slot_masks(mem_count)
    mask_array = mem_masks()
    block = width // mem_count
    column = jnp.arange(width, dtype=jnp.int32)
    source = (block * (mem_place ^ jnp.repeat(mask_array, block)) + column % block).reshape(width, 1)
    gain_stack = jnp.stack([norm_self, norm_cross, norm_feed], axis=0)
    x_own = hidden_in[0]
    edge = 3 * broad
    turns = mem_count.bit_length() - 2
    flat = lambda stacked: stacked.reshape((1, -1) + stacked.shape[2:])

    with jax.named_scope("gather"):
        own, two, one, second, blocks, live = prepare(
            (query_self, key_self, value_self, output_self, query_cross)
            + (key_cross, value_cross, output_cross, gate_weight, up_weight),
            gain_stack, memory, scalars, spot, slim, broad,
        )
        live = live.reshape(-1, 1)
        stay, go = part_blocks(blocks, 0)
        two, arrived = swap_seq(two, 0), swap_mem(go, 0)
        c3 = cotangent[0]
        c3_other = swap_mem(c3, turns)
        two, blocks, one, second, x_in, down_in, c3_other = settle(
            two, join_blocks(stay, arrived), one, second, x_own, down_weight, c3_other
        )
        three = swap_seq(jnp.stack([one, two[:, edge:]]), 1)
        second_a = swap_seq(second, 0)
        for turn in range(1, turns):
            stay, go = part_blocks(blocks, turn)
            blocks = join_blocks(stay, swap_mem(go, turn))
        three, blocks, second_a, second, x_in, down_in, source = settle(
            three, blocks, second_a, second, x_in, down_in, source
        )
        plain = [(0, 0, 0, edge), (1, 0, edge, 5 * width)]
        skipping = [(0, 0, 0, edge), (1, 0, 2 * edge, 5 * width)]
        heads, outer = place(
            [own[None], two[None], three],
            seq_places(),
            [edge, 5 * width],
            [plain, skipping, plain],
        )
        heads, outer = [flat(heads)], [flat(outer)]
        heads.append(swap_mem(heads[0], 0))
        outer.append(swap_mem(outer[0], 0))
        stay, go = part_blocks(blocks, turns)
        keys_in = join_blocks(stay, swap_mem(go, turns)).reshape(-1, width)
        second_b = swap_seq(jnp.stack([second, second_a]), 1)
        heads, outer, keys_in, second_a, second_b, second, x_in, down_in = settle(
            heads, outer, keys_in, second_a, second_b, second, x_in, down_in
        )
        x_a = swap_seq(x_in, 0)
        for turn in range(1, turns):
            heads.append(swap_mem(join(heads), turn))
            outer.append(swap_mem(join(outer), turn))
        both = [flat(stack_seq([second[None], second_a[None], second_b]))]
        x_a, x_in, both, down_in = settle(x_a, x_in, both, down_in)
        x_b = swap_seq(jnp.stack([x_in, x_a]), 1)
        both.append(swap_mem(both[0], 0))
        down_a = swap_seq(down_in, 0)
        heads, outer, both, x_b, x_a, x_in, down_a, down_in = settle(
            heads, outer, both, x_b, x_a, x_in, down_a, down_in
        )
        heads, outer = join(heads), join(outer)
        heads = [heads, swap_mem(heads, turns)]
        outer = [outer, swap_mem(outer, turns)]
        for turn in range(1, turns):
            both.append(swap_mem(join(both), turn))
        down_b = swap_seq(jnp.stack([down_in, down_a]), 1)
        heads, x_in, x_a, x_b = settle(heads, x_in, x_a, x_b)
        packed_heads = spread_weight(heads)

    key_chunk = width

    with jax.named_scope("forward"):
        x_pieces = [x_in, x_a, x_b]
        o_pieces, n1, qkv, gains, self_logs = self_rows(
            x_pieces, packed_heads, spot, near, broad, masks
        )
        o_pieces, gains, outer, down_a, down_b, down_in = settle(
            o_pieces, gains, outer, down_a, down_b, down_in
        )
        packed = spread_weight(outer)
        downs = [flat(stack_seq([down_in[None], down_a[None], down_b]))]
        a_pieces = send_seq(o_pieces)
        kv2 = key_values(keys_in, packed, spot, key_chunk, 2 * width, masks)
        downs.append(swap_mem(downs[0], 0))
        a_pieces, kv2, downs, keys_in, both = settle(a_pieces, kv2, downs, keys_in, both)
        q2, a2_early, h1, logs_first = rows_first(
            a_pieces, packed, x_own, gains, live, kv2, spot, 0, masks
        )
        both = join(both)
        both_other = swap_mem(both, turns)
        for turn in range(1, turns):
            downs.append(swap_mem(join(downs), turn))
        others = [swap_mem(downs[0], turns), swap_mem(downs[1], turns)]
        a2_early, h1, q2, both, both_other, others, downs = settle(
            a2_early, h1, q2, both, both_other, others, downs
        )
        a2, h2, logs_second = rows_second(
            packed, h1, a2_early, live, q2, kv2, spot, 0, masks
        )
        others += [swap_mem(piece, turns) for piece in downs[2:]]
        h2, both_other, both, downs, others = settle(h2, both_other, both, downs, others)
        both = [w.reshape(-1, 2 * hidden_width) for w in (both, both_other)]
        unit = hidden_width // mem_count
        narrow = unit % LANES != 0
        if narrow:
            unit = 2 * LANES
            downs = [stack_mem(downs + others).reshape(-1, unit, width)]
            feed_order = jnp.arange(hidden_width // unit, dtype=jnp.int32)
        else:
            feed_order = mem_place ^ mask_array
            downs = downs + others
        layer_out, dh2, c2, gain_feed_terms, bundle, act_near, n3_near = feed(
            feed_order, h2, c3, gains, source, both, downs
        )

    with jax.named_scope("backward"):
        bundle_other = swap_mem(bundle, turns)
        up, dq_early, dk_early, dv_early = rows_early(
            packed, c2, live, logs_first, q2, kv2, spot, 0, masks
        )
        bundle_other, up, dq_early = settle(bundle_other, up, dq_early)
        if narrow:
            acts = jnp.concatenate([act_near, bundle[:, 2 * hidden_width : -(width // 2)]], axis=1)
            g_down = left_product(acts, c3).astype(BF16).reshape(mem_count, -1, width)
            g_down = place([g_down], jnp.argsort(mem_place ^ mask_array)).reshape(2, -1, width)
            normed = jnp.concatenate([n3_near, bundle[:, -(width // 2) :]], axis=1)
            g_both = jnp.stack(
                [
                    left_product(normed, bundle[:, k * hidden_width : (k + 1) * hidden_width])
                    for k in range(2)
                ]
            ).astype(BF16)
            feeding = Scatter(g_both[:, : width // 2], g_both[:, width // 2 :])
            downing = Scatter(g_down[0], g_down[1])
            for s in (feeding, downing):
                s.move()
            advance([feeding, downing], spot)
        else:
            g_feed = feed_weights(bundle, bundle_other, act_near, n3_near, c3, c3_other)
            feeding, downing = Scatter(*g_feed[0:2], 1), Scatter(*g_feed[2:4], 1)
        feeding.sent, up = settle(feeding.sent, up)
        feeding.move()
        da_pieces, dq2, dk_late, dv_late, dh1, gain_cross_terms = rows_late(
            packed, up, dq_early, dh2, h1, gains, live, logs_second, q2, kv2, spot, 0, masks
        )
        da_pieces, dq2 = settle(da_pieces, dq2)
        da_pieces = send_seq(da_pieces)
        *g_cross, dmem = cross_weights(
            packed, source, h1, gains, dq2, c2, a2, keys_in,
            [dk_early, dk_late, dv_early, dv_late], spot, key_chunk, 0, masks,
        )
        crossing = Scatter(*g_cross)
        advance([feeding], spot)
        da_pieces, crossing.sent, feeding.sent, downing.sent, dmem = settle(
            da_pieces, crossing.sent, feeding.sent, downing.sent, dmem
        )
        crossing.move()
        feeding.move()
        keep_dn, send_dn, dqkv, gain_self_terms = self_backward(
            da_pieces, x_pieces, packed_heads, qkv, self_logs, spot, near, masks
        )
        dmem = dmem.reshape(mem_count, -1, width)
        stay, go = part_blocks(dmem, turns)
        dmem = join_blocks(stay, swap_mem(go, turns))
        crossing.terms, feeding.terms, downing.sent, keep_dn, send_dn, dqkv, dmem = settle(
            crossing.terms, feeding.terms, downing.sent, keep_dn, send_dn, dqkv, dmem
        )
        one_dn = swap_seq(send_dn, 1)
        downing.move()
        stay, go = part_blocks(dmem, 0)
        dmem = join_blocks(stay, swap_mem(go, 0))
        while feeding.left > 0:
            advance([feeding], spot)
            feeding.move()
        ends = [advance([feeding], spot), None, None, None]
        advance([crossing], spot)
        gain_grads = jnp.concatenate(
            [gain_self_terms, gain_cross_terms, gain_feed_terms, jnp.zeros((LANES - 3, width), F32)]
        )
        g_self = self_weights(source, n1, dqkv, dh1, gain_grads, a_pieces, spot)
        selfing = Scatter(*g_self)
        one_dn, keep_dn, crossing.sent, downing.terms, dmem, ends[0], selfing.sent = settle(
            one_dn, keep_dn, crossing.sent, downing.terms, dmem, ends[0], selfing.sent
        )
        two_dn = swap_seq(onward(keep_dn, one_dn)[0], 0)
        one_both = swap_seq(ends[0][1], 1)
        crossing.move()
        selfing.move()
        for turn in range(1, turns):
            stay, go = part_blocks(dmem, turn)
            dmem = join_blocks(stay, swap_mem(go, turn))
        while downing.left > 0:
            advance([downing], spot)
            downing.move()
        ends[1] = advance([downing], spot)
        while crossing.left > 0:
            advance([crossing], spot)
            crossing.move()
        while selfing.left > 0:
            advance([selfing], spot)
            selfing.move()
        two_both = swap_seq(onward(ends[0][0], one_both), 0)
        mem_keep, mem_send = pick_slots(dmem, memory.shape[0], scalars, spot)
        mem_one = swap_seq(mem_send, 1)
        one_down = swap_seq(ends[1][1], 1)
        ends[2] = advance([crossing], spot)
        one_cross = swap_seq(ends[2][1], 1)
        mem_two = swap_seq(onward(mem_keep, mem_one), 0)
        ends[3] = advance([selfing], spot)
        one_self = swap_seq(ends[3][1], 1)
        two_down = swap_seq(onward(ends[1][0], one_down), 0)
        two_cross = swap_seq(onward(ends[2][0], one_cross), 0)
        two_self = swap_seq(onward(ends[3][0], one_self, width + LANES), 0)
        hidden_grad = last_rows(keep_dn, one_dn, after(two_dn, ends[3][1]), x_own, dh1, gains)
        per = mem_two.shape[0]
        memory_grad = total_of([mem_keep[:per], mem_one[:per], mem_two]).astype(BF16)
        *finals, gain_finals = finish(
            (ends[0][0], one_both, two_both),
            (ends[1][0], one_down, two_down),
            (ends[2][0], one_cross, two_cross),
            (ends[3][0], one_self, two_self),
            spot, hidden_width, slim, broad,
        )
    g_gate, g_up, g_down, g_q2, g_k2, g_v2, g_o2, g_o1, g_q1, g_k1, g_v1 = finals
    return (
        layer_out[None],
        hidden_grad[None],
        memory_grad,
        gain_finals[:, 0],
        g_q1,
        g_k1,
        g_v1,
        g_o1,
        gain_finals[:, 1],
        g_q2,
        g_k2,
        g_v2,
        g_o2,
        gain_finals[:, 2],
        g_gate,
        g_up,
        g_down,
    )


def solution(mesh):
    every = P(("mem", "seq"), None)
    gain = P(("mem", "seq"))
    in_specs = (
        (P("mem", "seq", None), P(None, "mem", None), P("mem", "seq", None), gain)
        + (every,) * 4
        + (gain,)
        + (every,) * 4
        + (gain,)
        + (every,) * 3
        + (P(),) * 3
    )
    out_specs = (
        (P("mem", "seq", None), P("mem", "seq", None), P("seq", "mem", None), gain)
        + (every,) * 4
        + (gain,)
        + (every,) * 4
        + (gain,)
        + (every,) * 3
    )
    return jax.shard_map(local, mesh=mesh, in_specs=in_specs, out_specs=out_specs, check_vma=False)
```

```python
import functools

import jax
import jax.numpy as jnp
from jax import lax
from jax.experimental import pallas as pl
from jax.experimental.pallas import tpu as pltpu
from jax.sharding import PartitionSpec as P

HEADS = 12
HEAD_DIM = 64
SCALING = HEAD_DIM ** (-0.5)
LANES = 128
MASKED = -1e30
F32 = jnp.float32
BF16 = jnp.bfloat16


def product(left, right):
    return jnp.dot(left, right, preferred_element_type=F32)


def left_product(left, right):
    return lax.dot_general(left, right, (((0,), (0,)), ((), ())), preferred_element_type=F32)


def right_product(left, right):
    return lax.dot_general(left, right, (((1,), (1,)), ((), ())), preferred_element_type=F32)


def gelu_tanh(values):
    return (
        0.5
        * values
        * (1.0 + jnp.tanh(0.7978845608028654 * (values + 0.044715 * values * values * values)))
    )


def gated_unit(gate, upper):
    return gelu_tanh(gate) * upper


def norm_scale(hidden):
    return lax.rsqrt(jnp.mean(hidden * hidden, axis=-1, keepdims=True) + 1e-06)


def norm_hidden_grad(hidden, scale, gain, upstream):
    lifted = upstream * gain
    return scale * lifted - hidden * (scale * scale * scale) * jnp.mean(
        lifted * hidden, axis=-1, keepdims=True
    )


def shift(values, axis, step):
    size = lax.axis_size(axis)
    return lax.ppermute(values, axis, [(i, (i + step) % size) for i in range(size)])


def swap(values, axis, mask):
    size = lax.axis_size(axis)
    return lax.ppermute(values, axis, [(i, i ^ mask) for i in range(size)])


def place_kernel(counts, maps, places, *refs):
    sources = refs[: len(counts)]
    targets, done = refs[len(counts) : -1], refs[-1]
    copies = []
    number = 0
    for source, count, moves in zip(sources, counts, maps):
        for block in range(count):
            for goal, to, start, width in moves:
                part, target = source.at[block], targets[goal].at[places[number]]
                if len(moves) > 1 or width != source.shape[2]:
                    part = source.at[block, :, start : start + width]
                    target = targets[goal].at[places[number], :, to : to + width]
                copies.append(pltpu.make_async_copy(part, target, done.at[len(copies)]))
            number += 1
    for copy in copies:
        copy.start()
    for copy in copies:
        copy.wait()


def place(pieces, places, widths=None, maps=None):
    counts = [piece.shape[0] for piece in pieces]
    total = sum(counts)
    _, height, width = pieces[0].shape
    widths = widths or [width]
    if maps is None:
        plain = [(i, 0, sum(widths[:i]), w) for i, w in enumerate(widths)]
        maps = [plain] * len(pieces)
    copies = sum(count * len(moves) for count, moves in zip(counts, maps))
    outs = [((total, height, w), pieces[0].dtype) for w in widths]
    size = total * height * sum(widths) * 2
    result = pl.pallas_call(
        functools.partial(place_kernel, counts, maps),
        out_shape=shaped(outs),
        grid_spec=pltpu.PrefetchScalarGridSpec(
            num_scalar_prefetch=1,
            grid=(1,),
            in_specs=[HBM] * len(pieces),
            out_specs=[
                pl.BlockSpec((total, height, w), lambda i, places: (0, 0, 0)) for w in widths
            ],
            scratch_shapes=[pltpu.SemaphoreType.DMA((copies,))],
        ),
        compiler_params=pltpu.CompilerParams(vmem_limit_bytes=3 * size + (4 << 20)),
        cost_estimate=cost(1 + size / 1e6),
        name="place",
    )(places.astype(jnp.int32), *pieces)
    return result[0] if len(widths) == 1 else result


def after(values, *tokens):
    return lax.optimization_barrier((values,) + tokens)[0]


def settle(*values):
    return lax.optimization_barrier(values)


def seq_masks(parity):
    return [0, 1 + parity, 2 - parity, 3]


def swap_seq(values, turn):
    mem, seq = lax.axis_size("mem"), lax.axis_size("seq")
    pairs = []
    for m in range(mem):
        mask = 1 + (m + turn) % 2
        pairs += [(m * seq + s, m * seq + (s ^ mask)) for s in range(seq)]
    return lax.ppermute(values, ("mem", "seq"), pairs)


def seq_places():
    parity = lax.axis_index("mem") % 2
    return lax.axis_index("seq") ^ jnp.stack(seq_masks(parity)).astype(jnp.int32)


def stack_seq(pieces, widths=None):
    return place(pieces, seq_places(), widths)


def send_seq(pieces):
    return [pieces[0]] + [shift(piece, "seq", k) for k, piece in enumerate(pieces) if k]


def total_of(pieces):
    return functools.reduce(jnp.add, [piece.astype(F32) for piece in pieces])


def join(blocks):
    return blocks[0] if len(blocks) == 1 else jnp.concatenate(blocks, axis=0)


def orders(count):
    bits = list(range(1, count.bit_length() - 1))
    return bits, bits[::-1]


def slot_masks(count):
    half = count // 2
    low = [
        [sum(((s >> j) & 1) << bit for j, bit in enumerate(order)) for s in range(half)]
        for order in orders(count)
    ]
    return low[0] + [m | 1 for m in low[1]], low[1] + [m | 1 for m in low[0]]


def swap_mem(values, turn):
    count = lax.axis_size("mem")
    pairs = []
    for i in range(count):
        order = [*orders(count)[i % 2], 0]
        pairs.append((i, i ^ (1 << order[turn])))
    return lax.ppermute(values, "mem", pairs)


def mem_masks():
    count = lax.axis_size("mem")
    even, odd = slot_masks(count)
    return jnp.where(
        lax.axis_index("mem") % 2 == 0, jnp.array(even, jnp.int32), jnp.array(odd, jnp.int32)
    )


def stack_mem(halves, widths=None):
    return place(halves, lax.axis_index("mem") ^ mem_masks(), widths)


def spread_weight(halves):
    if halves[0].shape[1] % 16 == 0:
        return list(halves)
    stacked = stack_mem(halves)
    return [stacked.reshape(1, -1, stacked.shape[-1])]


def add_low(left, right):
    return (left.astype(F32) + right.astype(F32)).astype(BF16)


def total_kernel(plans, spot_ref, *refs):
    terms = sum(number for number, _ in plans)
    sources, refs = list(refs[:terms]), refs[terms:]
    outs, holds = list(refs[: len(refs) - len(plans)]), refs[len(refs) - len(plans) :]
    column = 0
    for (number, ends), hold in zip(plans, holds):
        mine, sources = sources[:number], sources[number:]
        groups, rows, width = mine[0].shape
        for g in range(groups):
            total = mine[0][g].astype(F32)
            for ref in mine[1:]:
                total = total + ref[g].astype(F32)
            if not ends:
                outs[0][g] = total.astype(BF16)
                continue
            count = hold.shape[0]
            unit = rows // count
            for j in range(count):
                hold[j] = total[j * unit : (j + 1) * unit]
            for k, mask in enumerate(seq_masks(lax.rem(spot_ref[0], 2))):
                piece = hold[jnp.bitwise_xor(spot_ref[1], mask)].astype(BF16)
                outs[-2 + k // 2][k % 2, :, column : column + width] = piece
            column += width
        if not ends:
            del outs[:1]


class Scatter:
    def __init__(self, kept, sent, taken=0):
        self.terms = [kept if kept.ndim == 3 else kept[None]]
        self.sent = sent if sent.ndim == 3 else sent[None]
        self.left = (lax.axis_size("mem") // 2).bit_length() - 1 - taken
        self.rows = self.terms[0].shape[1]

    def move(self):
        self.terms.append(swap_mem(self.sent, self.left))

    def hold(self):
        return [self.terms, self.sent]

    def take(self, held):
        self.terms, self.sent = held


def advance(scatters, spot):
    count = lax.axis_size("seq")
    plans, shapes, specs, flat, holds = [], [], [], [], []
    ended, exact = 0, True
    whole = lambda shape: pl.BlockSpec(shape, lambda i, spot: (0, 0, 0))
    for s in scatters:
        ends = s.left == 0
        groups, _, width = s.terms[0].shape
        rows = s.rows if ends else s.rows // 2
        exact = exact and rows // (count if ends else 1) % 8 == 0
        plans.append((len(s.terms), ends))
        part = (groups, rows, width)
        if ends:
            specs += [whole(part)] * len(s.terms)
            ended += groups * width
            unit = rows // count
            holds.append(pltpu.VMEM((count, unit, width), F32))
        else:
            specs += [pl.BlockSpec(part, lambda i, spot: (0, 1, 0))] * len(s.terms)
            shapes.append(part)
            holds.append(pltpu.VMEM((1, 8, 128), F32))
        flat += s.terms
    if ended:
        shapes += [(2, unit, ended)] * 2
    if exact:
        size = sum(spec.block_shape[0] * spec.block_shape[1] * spec.block_shape[2] for spec in specs)
        outs = pl.pallas_call(
            functools.partial(total_kernel, plans),
            out_shape=shaped([(shape, BF16) for shape in shapes]),
            grid_spec=pltpu.PrefetchScalarGridSpec(
                num_scalar_prefetch=1,
                grid=(1,),
                in_specs=specs,
                out_specs=[whole(shape) for shape in shapes],
                scratch_shapes=holds,
            ),
            compiler_params=vmem(6 + (size * 8 >> 20)),
            cost_estimate=cost(1 + size / 1e6),
            name="total",
        )(spot, *(far(*flat) if size > 1 << 20 else flat))
        outs = list(outs)
    else:
        outs, ends_at = [], []
        for s in scatters:
            low = 0 if s.left == 0 else s.rows // 2
            high = s.rows if s.left == 0 else 2 * low
            total = total_of([term[:, low:high] for term in s.terms]).astype(BF16)
            if s.left:
                outs.append(total)
                continue
            groups, rows, width = total.shape
            blocks = total.reshape(groups, count, rows // count, width)
            ends_at.append(jnp.take(jnp.concatenate(list(blocks), axis=2), seq_places(), axis=0))
        if ends_at:
            blocks = jnp.concatenate(ends_at, axis=2)
            outs += [blocks[:2], blocks[2:]]
    for s in scatters:
        if s.left:
            s.sent, s.rows = outs.pop(0), s.rows // 2
        s.left -= 1
    return outs or None


def onward(kept, arrived, summed=None):
    half = kept.shape[0] // 2
    mine, theirs = kept[half:], arrived[half:]
    if summed is None:
        return add_low(mine, theirs)
    return jnp.concatenate(
        [add_low(mine[..., :summed], theirs[..., :summed]), mine[..., summed:], theirs[..., summed:]],
        axis=-1,
    )


def part_blocks(blocks, turn):
    count = blocks.shape[0]
    parts = blocks.reshape((count >> (turn + 1), 2, 1 << turn) + blocks.shape[1:])
    return parts[:, 0], parts[:, 1]


def join_blocks(stay, arrived):
    joined = jnp.stack([stay, arrived], axis=1)
    return joined.reshape((-1,) + joined.shape[3:])


HBM = pl.BlockSpec(memory_space=pltpu.HBM)


def far(*arrays):
    return [pltpu.with_memory_space_constraint(array, pltpu.HBM) for array in arrays]


def shaped(shapes, distant=()):
    return [
        jax.ShapeDtypeStruct(shape, dtype)
        for i, (shape, dtype) in enumerate(shapes)
    ]


def vmem(mebibytes):
    return pltpu.CompilerParams(vmem_limit_bytes=mebibytes << 20)


def cost(microseconds):
    return pl.CostEstimate(
        flops=int(microseconds * 1.1e9), bytes_accessed=0, transcendentals=0
    )


def run(copies):
    for copy in copies:
        copy.start()
    for copy in copies:
        copy.wait()


def prepare_kernel(
    slim, broad, scalars_ref, spot_ref,
    q_ref, k_ref, v_ref, o1_ref, q2_ref, k2_ref, v2_ref, o2_ref, gate_ref, up_ref,
    gain_ref, memory_ref,
    own_ref, two_ref, one_ref, second_ref, blocks_ref, live_ref,
    turn, triple, held, done,
):
    mem_count, height = blocks_ref.shape[0], memory_ref.shape[1]
    share, width = q_ref.shape
    half = mem_count // 2
    me, seq = spot_ref[0], spot_ref[1]
    parity = lax.rem(me, 2)
    counts_at, tails_at, rows_at = 0, mem_count, 2 * mem_count
    moves = [(ref, triple.at[i]) for i, ref in enumerate((q_ref, k_ref, v_ref))]
    moves += [(memory_ref, held)]
    for ref, base in ((own_ref, 3 * broad), (one_ref, 3 * broad), (two_ref, 6 * broad)):
        for i, source in enumerate((o1_ref, q2_ref, k2_ref, v2_ref, o2_ref)):
            moves += [(source, ref.at[:, base + i * width : base + (i + 1) * width])]
    hidden = gate_ref.shape[1]
    moves += [(gate_ref, second_ref.at[:, :hidden]), (up_ref, second_ref.at[:, hidden:])]
    copies = [pltpu.make_async_copy(a, b, done.at[i]) for i, (a, b) in enumerate(moves)]
    for copy in copies:
        copy.start()
    turn[...] = jnp.zeros_like(turn)
    turn[0:3, 0:share] = gain_ref[...].astype(F32)
    gains = turn[...].T[:share]
    lane = lax.broadcasted_iota(jnp.int32, (share, broad - slim), 1)
    extra = jnp.zeros((share, broad - slim), F32)
    for i in range(3):
        extra = jnp.where(lane == i, gains[:, i : i + 1], extra)
    extra = extra.astype(BF16)
    blank = jnp.zeros((share, broad - slim), BF16)
    token = lax.broadcasted_iota(jnp.int32, (height, 1), 0)

    def first_block(example):
        return lax.fori_loop(
            0, example, lambda i, total: total + scalars_ref[counts_at + i], jnp.int32(0)
        )

    mine = scalars_ref[rows_at + me]
    mine_start = first_block(mine)
    mine_end = mine_start + scalars_ref[counts_at + mine]

    for copy in copies[:4]:
        copy.wait()

    order, contrary = orders(mem_count)

    def one(t, carry):
        low = lax.rem(t, half)
        first, second = jnp.int32(0), jnp.int32(0)
        for j in range(len(order)):
            bit = lax.rem(lax.shift_right_logical(low, jnp.int32(j)), 2)
            first = first + bit * (1 << order[j])
            second = second + bit * (1 << contrary[j])
        flip = parity == 1
        first, second = jnp.where(flip, second, first), jnp.where(flip, first, second)
        upper = t >= half
        goal = jnp.bitwise_xor(me, jnp.where(upper, first + 1, first))
        start = first_block(scalars_ref[rows_at + goal])
        block = start + lax.rem(me - lax.rem(start, mem_count) + mem_count, mem_count)
        slot = jnp.minimum(block // mem_count, memory_ref.shape[0] - 1)
        blocks_ref[t] = held[slot]
        holder = jnp.bitwise_xor(me, jnp.where(upper, second + 1, first))
        block = mine_start + lax.rem(
            holder - lax.rem(mine_start, mem_count) + mem_count, mem_count
        )
        bound = jnp.where(block == mine_end - 1, scalars_ref[tails_at + mine], height)
        bound = jnp.where(block < mine_end, bound, 0)
        live_ref[t] = jnp.where(token < bound, 0.0, MASKED)
        return carry

    lax.fori_loop(0, mem_count, one, 0)
    seq_steps = seq_masks(parity)
    for ref, base, mask in (
        (own_ref, 0, seq_steps[0]),
        (two_ref, 0, seq_steps[1]),
        (one_ref, 0, seq_steps[2]),
        (two_ref, 1, seq_steps[3]),
    ):
        goal = jnp.bitwise_xor(seq, mask)
        for i in range(3):
            weight = triple[i].astype(F32)
            chosen = weight[:, :slim]
            for j in range(1, width // slim):
                chosen = jnp.where(goal == j, weight[:, j * slim : (j + 1) * slim], chosen)
            start = (3 * base + i) * broad
            ref[:, start : start + broad] = jnp.concatenate(
                [chosen.astype(BF16), blank if i else extra], axis=1
            )
    for copy in copies[4:]:
        copy.wait()


def prepare(weights, gains, memory, scalars, spot, slim, broad):
    mem_count = lax.axis_size("mem")
    share, width = weights[0].shape
    first = 3 * broad + 5 * width
    second = sum(w.shape[1] for w in weights[8:])
    height = memory.shape[1]
    whole = lambda shape: pl.BlockSpec(shape, lambda *_: (0,) * len(shape))
    outs = [
        ((share, first), BF16),
        ((share, first + 3 * broad), BF16),
        ((share, first), BF16),
        ((share, second), BF16),
        ((mem_count, height, width), BF16),
        ((mem_count, height, 1), F32),
    ]
    return pl.pallas_call(
        functools.partial(prepare_kernel, slim, broad),
        out_shape=shaped(outs),
        grid_spec=pltpu.PrefetchScalarGridSpec(
            num_scalar_prefetch=2,
            grid=(1,),
            in_specs=[HBM] * len(weights) + [whole(gains.shape), HBM],
            out_specs=[whole(shape) for shape, _ in outs],
            scratch_shapes=[
                pltpu.VMEM((8, 128), F32),
                pltpu.VMEM((3, share, width), BF16),
                pltpu.VMEM(memory.shape, BF16),
                pltpu.SemaphoreType.DMA((4 + 15 + 2,)),
            ],
        ),
        compiler_params=vmem(16 + 3 * mem_count // 8),
        cost_estimate=cost(3),
        name="prepare",
    )(scalars, spot, *far(*weights), gains, *far(memory))


def slots_kernel(per, scalars_ref, spot_ref, blocks_ref, keep_ref, send_ref, done):
    mem_count = blocks_ref.shape[0]
    me, seq = spot_ref[0], spot_ref[1]
    parity = lax.rem(me, 2)
    copies = []
    for k, mask in enumerate(seq_masks(parity)):
        for s in range(per):
            slot = jnp.bitwise_xor(seq, mask) * per + s
            block = slot * mem_count + me

            def scan(i, carry):
                end, owner = carry
                end = end + scalars_ref[i]
                return end, owner + jnp.where(end <= block, 1, 0)

            _, owner = lax.fori_loop(0, mem_count, scan, (jnp.int32(0), jnp.int32(0)))
            row = lax.fori_loop(
                0,
                mem_count,
                lambda i, r: jnp.where(scalars_ref[2 * mem_count + i] == owner, i, r),
                jnp.int32(0),
            )
            gap = jnp.bitwise_xor(row, me)
            bit = lambda b: lax.rem(lax.shift_right_logical(gap, jnp.int32(b)), 2)
            spots = [
                sum(bit(b) * (1 << j) for j, b in enumerate(order)) for order in orders(mem_count)
            ]
            at = jnp.where(parity == 1, spots[1], spots[0]) + bit(0) * (mem_count // 2)
            copies.append(
                pltpu.make_async_copy(
                    blocks_ref.at[at],
                    (keep_ref, send_ref)[k // 2].at[k % 2 * per + s],
                    done.at[len(copies)],
                )
            )
    for copy in copies:
        copy.start()
    for copy in copies:
        copy.wait()


def pick_slots(blocks, slots, scalars, spot):
    per = slots // lax.axis_size("seq")
    shape = (2 * per,) + blocks.shape[1:]
    return pl.pallas_call(
        functools.partial(slots_kernel, per),
        out_shape=shaped([(shape, BF16)] * 2),
        grid_spec=pltpu.PrefetchScalarGridSpec(
            num_scalar_prefetch=2,
            grid=(1,),
            in_specs=[HBM],
            out_specs=[pl.BlockSpec(shape, lambda *_: (0, 0, 0))] * 2,
            scratch_shapes=[pltpu.SemaphoreType.DMA((slots,))],
        ),
        compiler_params=vmem(8),
        cost_estimate=cost(2),
        name="pick_slots",
    )(scalars, spot, blocks)


PAIR = 2


def feed_kernel(
    order_ref, h2_ref, c3_ref, gain_ref, source_ref,
    *refs,
):
    sides, refs = refs[: 4 * PAIR], refs[4 * PAIR :]
    down_refs, refs = refs[:-15], refs[-15:]
    out_ref, dh2_ref, c2_ref, gain_grad_ref, bundle_ref, act_near_ref, n3_near_ref = refs[:7]
    turn, n3_rel, total, dn3, gate_w, up_w, down_w, act_all = refs[7:]
    step, steps = pl.program_id(0), pl.num_programs(0)
    half, unit = sides[0].shape
    width = h2_ref.shape[1]
    hidden = unit * steps * PAIR
    slim = width // 2

    @pl.when(step == 0)
    def _():
        columns = lax.broadcasted_iota(jnp.int32, (width, width), 1)
        turn[...] = (columns == source_ref[...]).astype(F32).astype(BF16)
        h2 = h2_ref[...]
        n3 = (h2 * norm_scale(h2) * gain_ref[2:3]).astype(BF16)
        rel = right_product(n3, turn[...]).astype(BF16)
        n3_rel[...] = rel
        n3_near_ref[...] = rel[:, :slim]
        bundle_ref[:, 2 * hidden + hidden // 2 :] = rel[:, slim:]
        total[...] = jnp.zeros_like(total)
        dn3[...] = jnp.zeros_like(dn3)

    base = 0
    for ref in down_refs:
        number = ref.shape[0]
        for block in range(number):

            @pl.when(step == (base + block) // PAIR)
            def _(ref=ref, block=block, at=(base + block) % PAIR):
                down_w[at * unit : (at + 1) * unit] = ref[block]

        base += number
    for n in range(PAIR):
        part = slice(n * unit, (n + 1) * unit)
        for k, target in enumerate((gate_w, up_w)):
            target[:half, part] = sides[4 * n + 2 * k][...]
            target[half:, part] = sides[4 * n + 2 * k + 1][...]
    down = down_w[...]
    n3, c3 = n3_rel[...], c3_ref[...]
    gate = product(n3, gate_w[...])
    upper = product(n3, up_w[...])
    dact = right_product(c3, down)
    inner = 0.7978845608028654 * (gate + 0.044715 * gate * gate * gate)
    bent = jnp.tanh(inner)
    gelu = 0.5 * gate * (1.0 + bent)
    slope = 0.5 * (1.0 + bent) + 0.5 * gate * (1.0 - bent * bent) * (
        0.7978845608028654 * (1.0 + 3.0 * 0.044715 * gate * gate)
    )
    act = (gelu * upper).astype(BF16)
    dgate = (dact * upper * slope).astype(BF16)
    dupper = (dact * gelu).astype(BF16)
    total[...] += product(act, down)
    for n in range(PAIR):
        part = slice(n * unit, (n + 1) * unit)
        act_all[step * PAIR + n] = act[:, part]
        column = pl.multiple_of(order_ref[step * PAIR + n] * unit, LANES)
        bundle_ref[:, pl.ds(column, unit)] = dgate[:, part]
        bundle_ref[:, pl.ds(pl.multiple_of(hidden + column, LANES), unit)] = dupper[:, part]
    dn3[...] += right_product(dgate, gate_w[...]) + right_product(dupper, up_w[...])

    @pl.when(step == steps - 1)
    def _():
        middle = act_all.shape[0] // 2
        for t in range(middle):
            act_near_ref[:, t * unit : (t + 1) * unit] = act_all[t]
            first = 2 * hidden + t * unit
            bundle_ref[:, first : first + unit] = act_all[middle + t]
        h2 = h2_ref[...]
        out_ref[...] = (h2 + total[...]).astype(BF16)
        high = dn3[...].astype(BF16)
        rest = (dn3[...] - high.astype(F32)).astype(BF16)
        upstream = product(high, turn[...]) + product(rest, turn[...])
        scale = norm_scale(h2)
        dh2 = c3_ref[...].astype(F32) + norm_hidden_grad(h2, scale, gain_ref[2:3], upstream)
        dh2_ref[...] = dh2
        c2_ref[...] = dh2.astype(BF16)
        gain_grad_ref[...] = jnp.sum(upstream * h2 * scale, axis=0, keepdims=True)


def feed(order, h2, c3, gains, source, both, down):
    rows, width = h2.shape
    half, hidden = both[0].shape
    hidden = hidden // 2
    steps = order.shape[0]
    unit = hidden // steps
    whole = lambda shape: pl.BlockSpec(shape, lambda i, o: (0, 0))
    sides = []
    for n in range(PAIR):
        sides += [pl.BlockSpec((half, unit), lambda i, o, n=n: (0, o[i * PAIR + n]))] * 2
        sides += [pl.BlockSpec((half, unit), lambda i, o, n=n: (0, o[i * PAIR + n] + steps))] * 2
    flat = (rows, width)
    shapes = [
        (flat, BF16),
        (flat, F32),
        (flat, BF16),
        ((1, width), F32),
        ((rows, 2 * hidden + hidden // 2 + width // 2), BF16),
        ((rows, hidden // 2), BF16),
        ((rows, width // 2), BF16),
    ]
    return pl.pallas_call(
        feed_kernel,
        out_shape=shaped(shapes, (0,)),
        grid_spec=pltpu.PrefetchScalarGridSpec(
            num_scalar_prefetch=1,
            grid=(steps // PAIR,),
            in_specs=[whole(flat)] * 2
            + [whole(gains.shape), whole((width, 1))]
            + sides
            + [pl.BlockSpec(w.shape, lambda i, o: (0, 0, 0)) for w in down],
            out_specs=[whole(shape) for shape, _ in shapes],
            scratch_shapes=[
                pltpu.VMEM((width, width), BF16),
                pltpu.VMEM(flat, BF16),
                pltpu.VMEM(flat, F32),
                pltpu.VMEM(flat, F32),
                pltpu.VMEM((2 * half, PAIR * unit), BF16),
                pltpu.VMEM((2 * half, PAIR * unit), BF16),
                pltpu.VMEM((PAIR * unit, width), BF16),
                pltpu.VMEM((steps, rows, unit), BF16),
            ],
        ),
        compiler_params=vmem(28),
        cost_estimate=cost(13),
        name="feed",
    )(order, h2, *far(c3), gains, source, *far(*both * (2 * PAIR)), *down)


def feed_weights_kernel(
    own_ref, other_ref, act_ref, n3_ref, c3_ref, c3_other_ref,
    both_keep_ref, both_send_ref, down_keep_ref, down_send_ref,
):
    hidden = both_keep_ref.shape[2]
    units = act_ref.shape[1]
    quarter, third = both_keep_ref.shape[1], down_keep_ref.shape[0]
    edge = 2 * hidden + units
    mine = transposed(n3_ref[...])
    theirs = transposed(other_ref[:, edge:])
    step = hidden // 2
    for first in range(0, 2 * hidden, step):
        grad = product(mine, own_ref[:, first : first + step])
        grad = grad + product(theirs, other_ref[:, first : first + step])
        grad = grad.astype(BF16)
        part, column = first // hidden, first % hidden
        both_keep_ref[part, :, column : column + step] = grad[:quarter]
        both_send_ref[part, :, column : column + step] = grad[quarter:]
    c3, c3_other = c3_ref[...], c3_other_ref[...]
    for k, ref in enumerate((down_keep_ref, down_send_ref)):
        first = k * third
        mine = transposed(act_ref[:, first : first + third])
        theirs = transposed(other_ref[:, 2 * hidden + first : 2 * hidden + first + third])
        ref[...] = (product(mine, c3) + product(theirs, c3_other)).astype(BF16)


def feed_weights(own, other, act, n3, c3, c3_other):
    rows, width = c3.shape
    units = act.shape[1]
    hidden = 2 * units
    pair = ((2, width // 4, hidden), BF16)
    single = ((units // 2, width), BF16)
    return pl.pallas_call(
        feed_weights_kernel,
        out_shape=shaped([pair, pair, single, single]),
        compiler_params=vmem(24),
        cost_estimate=cost(5),
        name="feed_weights",
    )(own, other, act, n3, c3, c3_other)


def head_mask(shape, head):
    return lax.broadcasted_iota(jnp.int32, shape, 1) // HEAD_DIM == head


def pick_head(values, head):
    return jnp.where(head_mask(values.shape, head), values, jnp.zeros_like(values))


def stack_heads(values, heads):
    return jnp.concatenate([pick_head(values, head) for head in heads], axis=0)


def head_groups(keys, heads):
    return [list(range(heads))] if keys <= 2048 else [[head] for head in range(heads)]


def transposed(values):
    return values.astype(F32).T.astype(values.dtype)


LOG2E = 1.4426950408889634
SHRINK = SCALING * LOG2E


def soft_parts(scores, axis=0):
    peak = jnp.max(scores, axis=0, keepdims=True)
    powers = jnp.exp2(scores - peak)
    total = jnp.sum(powers, axis=0, keepdims=True)
    return powers, 1.0 / total, peak + jnp.log2(total)


def causal_scores(keys, queries, count):
    scores = right_product(keys, queries) * SHRINK
    last = scores.shape[0] - count
    corner = scores[last:]
    key_place = lax.broadcasted_iota(jnp.int32, corner.shape, 0)
    query_place = lax.rem(lax.broadcasted_iota(jnp.int32, corner.shape, 1), count)
    corner = jnp.where(key_place <= query_place, corner, MASKED)
    return corner if last == 0 else jnp.concatenate([scores[:last], corner], axis=0)


def cross_scores(keys, queries, bias):
    return right_product(keys, queries) * SHRINK + bias


def score_grads(scores, logs, inner):
    chance = jnp.exp2(scores - logs)
    spread = jnp.sum(chance * inner, axis=0, keepdims=True)
    return chance.astype(BF16), (chance * (inner - spread)).astype(BF16)


def weight_copies(refs, masks, me, columns, target, done, base):
    copies = []
    for ref in refs:
        for block in range(ref.shape[0]):
            number = len(copies)
            spot = 0
            if len(refs) > 1:
                mask = masks[0][number]
                if masks[1][number] != mask:
                    mask = jnp.where(lax.rem(me, 2) == 1, masks[1][number], mask)
                spot = pl.multiple_of(jnp.bitwise_xor(me, mask) * ref.shape[1], 16)
            copies.append(
                pltpu.make_async_copy(
                    ref.at[block, :, columns[0] : columns[1]],
                    target.at[pl.ds(spot, ref.shape[1])],
                    done.at[base + number],
                )
            )
    return copies


def blocks_in(refs):
    return sum(ref.shape[0] for ref in refs)


def self_rows_kernel(heads, masks, counts, spot_ref, *refs):
    seq_count, weights = counts
    x_refs, refs = refs[:3], refs[3:]
    x_list = [x_refs[0], x_refs[1], x_refs[2].at[0], x_refs[2].at[1]]
    w_refs, refs = refs[:weights], refs[weights:]
    o_refs, refs = refs[:seq_count], refs[seq_count:]
    n1_ref, qkv_ref, gain_ref, log_ref, x_all, w_all, o_all, done = refs
    rows, width = x_refs[0].shape
    broad = w_all.shape[1] // 3
    me, seq = spot_ref[0], spot_ref[1]
    copies = weight_copies(w_refs, masks, me, (0, 3 * broad), w_all, done, 0)
    base = len(copies)
    copies += [
        pltpu.make_async_copy(ref, x_all.at[jnp.bitwise_xor(seq, mask)], done.at[base + k])
        for k, (ref, mask) in enumerate(zip(x_list, seq_masks(lax.rem(me, 2))))
    ]
    run(copies)
    slim = heads * HEAD_DIM
    edge = slim // LANES * LANES
    gains = w_all[:, edge : edge + LANES].astype(F32).T[slim - edge : slim - edge + 8]
    gain_ref[...] = gains
    for j in range(seq_count):
        x = x_all[j].astype(F32)
        n1 = (x * norm_scale(x) * gains[0:1]).astype(BF16)
        n1_ref[j * rows : (j + 1) * rows] = n1
        qkv_ref[j * rows : (j + 1) * rows] = product(n1, w_all[...]).astype(BF16)
    values_t = transposed(qkv_ref[:, 2 * broad :])
    for j in range(seq_count):
        first, last = j * rows, (j + 1) * rows
        queries = qkv_ref[first:last, :broad]
        parts = []
        scores = causal_scores(
            qkv_ref[:last, broad : 2 * broad], stack_heads(queries, range(heads)), rows
        )
        powers, inverse, logs = soft_parts(scores)
        powers = powers.astype(BF16)
        for head in range(heads):
            part = slice(head * rows, (head + 1) * rows)
            log_ref[head : head + 1, first:last] = logs[:, part]
            lines = values_t[head * HEAD_DIM : (head + 1) * HEAD_DIM, :last]
            parts.append(product(lines, powers[:, part]) * inverse[:, part])
        o_all[j] = jnp.concatenate(parts, axis=0).T.astype(BF16)
    for k, ref in enumerate(o_refs):
        ref[...] = o_all[lax.rem(seq + k, seq_count)]


def self_rows(x_pieces, weights, spot, heads, broad, masks):
    count = lax.axis_size("seq")
    rows, width = x_pieces[0].shape
    length, slim = rows * count, heads * HEAD_DIM
    whole = lambda shape: pl.BlockSpec(shape, lambda i, spot: (0, 0))
    shapes = [((rows, slim), BF16)] * count + [
        ((length, width), BF16),
        ((length, 3 * broad), BF16),
        ((8, width), F32),
        ((8, length), F32),
    ]
    outs = pl.pallas_call(
        functools.partial(self_rows_kernel, heads, masks, (count, len(weights))),
        out_shape=shaped(shapes, (count, count + 1, count + 3)),
        grid_spec=pltpu.PrefetchScalarGridSpec(
            num_scalar_prefetch=1,
            grid=(1,),
            in_specs=[HBM] * (3 + len(weights)),
            out_specs=[whole(s) for s, _ in shapes],
            scratch_shapes=[
                pltpu.VMEM((count, rows, width), BF16),
                pltpu.VMEM((width, 3 * broad), BF16),
                pltpu.VMEM((count, rows, slim), BF16),
                pltpu.SemaphoreType.DMA((blocks_in(weights) + count,)),
            ],
        ),
        compiler_params=vmem(14),
        cost_estimate=cost(10),
        name="self_rows",
    )(spot, *x_pieces, *weights)
    return outs[:count], *outs[count:]


def key_values_kernel(masks, number, edge, spot_ref, keys_ref, *refs):
    w_refs, (out_ref, w_all, done) = refs[:number], refs[number:]

    @pl.when(pl.program_id(0) == 0)
    def _():
        columns = (edge, edge + w_all.shape[1])
        run(weight_copies(w_refs, masks, spot_ref[0], columns, w_all, done, 0))

    out_ref[...] = product(keys_ref[...], w_all[...]).astype(BF16)


def key_values(keys, weights, spot, chunk, edge, masks):
    width = keys.shape[1]
    columns = 2 * width
    return pl.pallas_call(
        functools.partial(key_values_kernel, masks, len(weights), edge),
        out_shape=jax.ShapeDtypeStruct((keys.shape[0], columns), BF16),
        grid_spec=pltpu.PrefetchScalarGridSpec(
            num_scalar_prefetch=1,
            grid=(keys.shape[0] // chunk,),
            in_specs=[pl.BlockSpec((chunk, width), lambda i, spot: (i, 0))] + [HBM] * len(weights),
            out_specs=pl.BlockSpec((chunk, columns), lambda i, spot: (i, 0)),
            scratch_shapes=[
                pltpu.VMEM((width, columns), BF16),
                pltpu.SemaphoreType.DMA((blocks_in(weights),)),
            ],
        ),
        compiler_params=vmem(12),
        cost_estimate=cost(4),
        name="key_values",
    )(spot, keys, *weights)


def cross_attend(queries, keys, values, live, log_ref):
    values_t = transposed(values)
    pieces = []
    rows = queries.shape[0]
    for group in head_groups(keys.shape[0], LANES // HEAD_DIM):
        powers, inverse, logs = soft_parts(cross_scores(keys, stack_heads(queries, group), live))
        powers = powers.astype(BF16)
        for n, head in enumerate(group):
            part = slice(n * rows, (n + 1) * rows)
            log_ref[0, head : head + 1] = logs[:, part]
            lines = values_t[head * HEAD_DIM : (head + 1) * HEAD_DIM]
            pieces.append(product(lines, powers[:, part]) * inverse[:, part])
    return jnp.concatenate(pieces, axis=0).T.astype(BF16)


def rows_first_kernel(masks, counts, edge, spot_ref, *refs):
    seq_count, weights = counts
    a_refs, refs = refs[:seq_count], refs[seq_count:]
    w_refs, refs = refs[:weights], refs[weights:]
    x_ref, gain_ref, live_ref, k_ref, v_ref = refs[:5]
    q2_ref, a2_ref, h1_ref, log_ref = refs[5:9]
    a_all, w_o1, w_q2, q_parts, done = refs[9:]
    step = pl.program_id(0)
    me, seq = spot_ref[0], spot_ref[1]
    width = x_ref.shape[1]

    @pl.when(step == 0)
    def _():
        copies = [
            pltpu.make_async_copy(
                ref, a_all.at[lax.rem(seq - k + seq_count, seq_count)], done.at[k]
            )
            for k, ref in enumerate(a_refs)
        ]
        copies += weight_copies(w_refs, masks, me, (edge, edge + width), w_o1, done, seq_count)
        later = weight_copies(
            w_refs, masks, me, (edge + width, edge + 2 * width), w_q2, done, len(copies)
        )
        for copy in copies + later:
            copy.start()
        for copy in copies:
            copy.wait()
        a1 = jnp.concatenate([a_all[j] for j in range(seq_count)], axis=1)
        h1 = x_ref[...].astype(F32) + right_product(a1, w_o1[...])
        h1_ref[...] = h1
        n2 = (h1 * norm_scale(h1) * gain_ref[1:2]).astype(BF16)
        for copy in later:
            copy.wait()
        q2 = product(n2, w_q2[...]).astype(BF16)
        q2_ref[...] = q2
        for i in range(q_parts.shape[0]):
            q_parts[i] = q2[:, i * LANES : (i + 1) * LANES]

    a2_ref[...] = cross_attend(q_parts[step], k_ref[...], v_ref[...], live_ref[...], log_ref)


def rows_second_kernel(masks, weights, edge, spot_ref, *refs):
    w_refs, refs = refs[:weights], refs[weights:]
    h1_ref, early_ref, live_ref, q_ref, k_ref, v_ref, a2_ref, h2_ref, log_ref = refs[:9]
    w_o2, o_parts, done = refs[9:]
    step, parts = pl.program_id(0), o_parts.shape[0]
    width = h1_ref.shape[1]
    columns = (edge + 4 * width, edge + 5 * width)
    copies = weight_copies(w_refs, masks, spot_ref[0], columns, w_o2, done, 0)

    @pl.when(step == 0)
    def _():
        for copy in copies:
            copy.start()

    o_parts[step] = cross_attend(q_ref[...], k_ref[...], v_ref[...], live_ref[...], log_ref)

    @pl.when(step == parts - 1)
    def _():
        for copy in copies:
            copy.wait()
        a2 = jnp.concatenate([early_ref[...]] + [o_parts[i] for i in range(parts)], axis=1)
        a2_ref[...] = a2
        h2_ref[...] = h1_ref[...] + right_product(a2, w_o2[...])


def rows_first(a_pieces, weights, x, gains, live, kv, spot, edge, masks):
    count = len(a_pieces)
    rows, width = x.shape
    keys = kv.shape[0]
    parts = width // LANES
    flat = (rows, width)
    whole = lambda shape: pl.BlockSpec(shape, lambda i, spot: (0, 0))
    _, row, key, value = rows_specs(rows, keys, width, 0)
    log = pl.BlockSpec((1, 8, rows), lambda i, spot: (i, 0, 0))
    shapes = [
        (flat, BF16), ((rows, width // 2), BF16), (flat, F32), ((parts // 2, 8, rows), F32)
    ]
    square = pltpu.VMEM((width, width), BF16)
    return pl.pallas_call(
        functools.partial(rows_first_kernel, masks, (count, len(weights)), edge),
        out_shape=shaped(shapes),
        grid_spec=pltpu.PrefetchScalarGridSpec(
            num_scalar_prefetch=1,
            grid=(parts // 2,),
            in_specs=[HBM] * (count + len(weights))
            + [whole(flat), whole(gains.shape), whole(live.shape), key, value],
            out_specs=[whole(flat), row, whole(flat), log],
            scratch_shapes=[
                pltpu.VMEM((count,) + a_pieces[0].shape, BF16),
                square, square,
                pltpu.VMEM((parts, rows, LANES), BF16),
                pltpu.SemaphoreType.DMA((count + 2 * blocks_in(weights),)),
            ],
        ),
        compiler_params=vmem(max(16, keys * 8 // 1024 + 8)),
        cost_estimate=cost(7),
        name="rows_first",
    )(spot, *a_pieces, *weights, x, gains, live, kv, kv)


def rows_second(weights, h1, early, live, q2, kv, spot, edge, masks):
    rows, width = h1.shape
    keys = kv.shape[0]
    parts = width // LANES // 2
    flat = (rows, width)
    whole = lambda shape: pl.BlockSpec(shape, lambda i, spot: (0, 0))
    _, row, key, value = rows_specs(rows, keys, width, parts)
    log = pl.BlockSpec((1, 8, rows), lambda i, spot: (i, 0, 0))
    return pl.pallas_call(
        functools.partial(rows_second_kernel, masks, len(weights), edge),
        out_shape=shaped([(flat, BF16), (flat, F32), ((parts, 8, rows), F32)]),
        grid_spec=pltpu.PrefetchScalarGridSpec(
            num_scalar_prefetch=1,
            grid=(parts,),
            in_specs=[HBM] * len(weights)
            + [whole(flat), whole(early.shape), whole(live.shape), row, key, value],
            out_specs=[whole(flat), whole(flat), log],
            scratch_shapes=[
                pltpu.VMEM((width, width), BF16),
                pltpu.VMEM((parts, rows, LANES), BF16),
                pltpu.SemaphoreType.DMA((blocks_in(weights),)),
            ],
        ),
        compiler_params=vmem(max(14, keys * 8 // 1024 + 8)),
        cost_estimate=cost(6),
        name="rows_second",
    )(spot, *weights, h1, early, live, q2, kv, kv)


def cross_backward(queries, upstream, live, keys, values, logs):
    keys_t = transposed(keys)
    pieces, dk, dv = [], 0.0, 0.0
    rows = queries.shape[0]
    for group in head_groups(keys.shape[0], LANES // HEAD_DIM):
        own = stack_heads(queries, group)
        up_own = stack_heads(upstream, group)
        inner = right_product(values, up_own)
        log = jnp.concatenate([logs[head : head + 1] for head in group], axis=1)
        chance, grad = score_grads(cross_scores(keys, own, live), log, inner)
        dv = dv + product(chance, up_own)
        dk = dk + product(grad, own)
        for n, head in enumerate(group):
            lines = keys_t[head * HEAD_DIM : (head + 1) * HEAD_DIM]
            pieces.append(product(lines, grad[:, n * rows : (n + 1) * rows]))
    dq = jnp.concatenate(pieces, axis=0).T * SCALING
    return dq.astype(BF16), (dk * SCALING).astype(BF16), dv.astype(BF16)


def rows_early_kernel(masks, weights, edge, spot_ref, *refs):
    w_refs, refs = refs[:weights], refs[weights:]
    c2_ref, live_ref, log_ref, q_ref, k_ref, v_ref, up_ref, dq_ref, dk_ref, dv_ref = refs[:10]
    w_o2, up_parts, done = refs[10:]
    width = c2_ref.shape[1]

    @pl.when(pl.program_id(0) == 0)
    def _():
        columns = (edge + 4 * width, edge + 5 * width)
        run(weight_copies(w_refs, masks, spot_ref[0], columns, w_o2, done, 0))
        up = product(c2_ref[...], w_o2[...]).astype(BF16)
        up_ref[...] = up
        for i in range(up_parts.shape[0]):
            up_parts[i] = up[:, i * LANES : (i + 1) * LANES]

    dq_ref[...], dk_ref[...], dv_ref[...] = cross_backward(
        q_ref[...], up_parts[pl.program_id(0)], live_ref[...], k_ref[...], v_ref[...], log_ref[0]
    )


def rows_late_kernel(masks, counts, edge, spot_ref, *refs):
    seq_count, weights = counts
    w_refs, refs = refs[:weights], refs[weights:]
    up_ref, dq_early_ref, dh2_ref, h1_ref, gain_ref, live_ref, log_ref, q_ref, k_ref, v_ref = refs[:10]
    da_refs, refs = refs[10 : 10 + seq_count], refs[10 + seq_count :]
    dq2_ref, dk_ref, dv_ref, dh1_ref, gain_grad_ref = refs[:5]
    w_o1, w_q2, dq_parts, da_all, done = refs[5:]
    step = pl.program_id(0)
    me, seq = spot_ref[0], spot_ref[1]
    width = dh2_ref.shape[1]
    parts = dq_parts.shape[0]
    copies = weight_copies(
        w_refs, masks, me, (edge + width, edge + 2 * width), w_q2, done, 0
    )
    copies += weight_copies(w_refs, masks, me, (edge, edge + width), w_o1, done, len(copies))

    @pl.when(step == 0)
    def _():
        for copy in copies:
            copy.start()

    dq_parts[step], dk_ref[...], dv_ref[...] = cross_backward(
        q_ref[...], up_ref[...], live_ref[...], k_ref[...], v_ref[...], log_ref[0]
    )

    @pl.when(step == parts - 1)
    def _():
        for copy in copies:
            copy.wait()
        dq2 = jnp.concatenate([dq_early_ref[...]] + [dq_parts[i] for i in range(parts)], axis=1)
        dq2_ref[...] = dq2
        dn2 = right_product(dq2, w_q2[...])
        h1 = h1_ref[...]
        scale = norm_scale(h1)
        dh1 = dh2_ref[...] + norm_hidden_grad(h1, scale, gain_ref[1:2], dn2)
        dh1_ref[...] = dh1
        gain_grad_ref[...] = jnp.sum(dn2 * h1 * scale, axis=0, keepdims=True)
        c1 = dh1.astype(BF16)
        up = product(c1, w_o1[...])
        slim = da_all.shape[2]
        for j in range(seq_count):
            da_all[j] = up[:, j * slim : (j + 1) * slim].astype(BF16)
        for k, ref in enumerate(da_refs):
            ref[...] = da_all[lax.rem(seq + k, seq_count)]


def rows_specs(rows, keys, width, start):
    parts = width // LANES
    row = pl.BlockSpec((rows, LANES), lambda i, spot: (0, i + start))
    key = pl.BlockSpec((keys, LANES), lambda i, spot: (0, i + start))
    value = pl.BlockSpec((keys, LANES), lambda i, spot: (0, i + start + parts))
    log = pl.BlockSpec((1, 8, rows), lambda i, spot: (i, 0, 0))
    return log, row, key, value


def rows_early(weights, c2, live, logs, q2, kv, spot, edge, masks):
    rows, width = c2.shape
    keys = kv.shape[0]
    parts = width // LANES // 2
    whole = lambda shape: pl.BlockSpec(shape, lambda i, spot: (0, 0))
    log, row, key, value = rows_specs(rows, keys, width, 0)
    half = width // 2
    shapes = [((rows, width), BF16), ((rows, half), BF16)] + [((keys, half), BF16)] * 2
    return pl.pallas_call(
        functools.partial(rows_early_kernel, masks, len(weights), edge),
        out_shape=shaped(shapes, (2, 3)),
        grid_spec=pltpu.PrefetchScalarGridSpec(
            num_scalar_prefetch=1,
            grid=(parts,),
            in_specs=[HBM] * len(weights)
            + [whole((rows, width)), whole(live.shape), log, row, key, value],
            out_specs=[whole((rows, width)), row, key, key],
            scratch_shapes=[
                pltpu.VMEM((width, width), BF16),
                pltpu.VMEM((2 * parts, rows, LANES), BF16),
                pltpu.SemaphoreType.DMA((blocks_in(weights),)),
            ],
        ),
        compiler_params=vmem(max(12, keys * 8 // 1024 + 12)),
        cost_estimate=cost(10),
        name="rows_early",
    )(spot, *weights, c2, live, logs, q2, kv, kv)


def rows_late(weights, up, dq_early, dh2, h1, gains, live, logs, q2, kv, spot, edge, masks):
    count = lax.axis_size("seq")
    rows, width = dh2.shape
    keys = kv.shape[0]
    parts = width // LANES // 2
    slim = width // count
    flat = (rows, width)
    half = width // 2
    whole = lambda shape: pl.BlockSpec(shape, lambda i, spot: (0, 0))
    log, row, key, value = rows_specs(rows, keys, width, parts)
    key_out = pl.BlockSpec((keys, LANES), lambda i, spot: (0, i))
    shapes = [((rows, slim), BF16)] * count + [
        (flat, BF16), ((keys, half), BF16), ((keys, half), BF16),
        (flat, F32), ((1, width), F32),
    ]
    square = pltpu.VMEM((width, width), BF16)
    outs = pl.pallas_call(
        functools.partial(rows_late_kernel, masks, (count, len(weights)), edge),
        out_shape=shaped(shapes, range(count, count + 6)),
        grid_spec=pltpu.PrefetchScalarGridSpec(
            num_scalar_prefetch=1,
            grid=(parts,),
            in_specs=[HBM] * len(weights)
            + [row, whole((rows, half)), whole(flat), whole(flat)]
            + [whole(gains.shape), whole(live.shape), log, row, key, value],
            out_specs=[whole((rows, slim))] * count
            + [whole(flat), key_out, key_out, whole(flat), whole((1, width))],
            scratch_shapes=[
                square, square,
                pltpu.VMEM((parts, rows, LANES), BF16),
                pltpu.VMEM((count, rows, slim), BF16),
                pltpu.SemaphoreType.DMA((2 * blocks_in(weights),)),
            ],
        ),
        compiler_params=vmem(max(18, keys * 8 // 1024 + 12)),
        cost_estimate=cost(11),
        name="rows_late",
    )(spot, *weights, up, dq_early, dh2, h1, gains, live, logs, q2, kv, kv)
    return outs[:count], *outs[count:]


def turn_of(source_ref, width):
    columns = lax.broadcasted_iota(jnp.int32, (width, width), 1)
    return (columns == source_ref[...]).astype(F32).astype(BF16)


def cross_weights_kernel(masks, number, edge, spot_ref, *refs):
    w_refs, refs = refs[:number], refs[number:]
    source_ref, h1_ref, gain_ref, dq2_ref, c2_ref, a2_ref, keys_ref = refs[:7]
    parts, refs = refs[7:11], refs[11:]
    near_ref, far_ref, dmem_ref = refs[:3]
    w_all, turn, dk_sum, dv_sum, done = refs[3:]
    dk = jnp.concatenate([parts[0][...], parts[1][...]], axis=1)
    dv = jnp.concatenate([parts[2][...], parts[3][...]], axis=1)
    step, steps = pl.program_id(0), pl.num_programs(0)
    width = dq2_ref.shape[1]
    half = width // 2
    columns = (edge + 2 * width, edge + 4 * width)
    copies = weight_copies(w_refs, masks, spot_ref[0], columns, w_all, done, 0)

    def put(column, values):
        values = values.astype(BF16)
        near_ref[:, column : column + width] = values[:half]
        far_ref[:, column : column + width] = values[half:]

    @pl.when(step == 0)
    def _():
        for copy in copies:
            copy.start()
        turn[...] = turn_of(source_ref, width)
        h1 = h1_ref[...]
        n2 = (h1 * norm_scale(h1) * gain_ref[1:2]).astype(BF16)
        n2_t = right_product(turn[...], n2).astype(BF16)
        put(0, product(n2_t, dq2_ref[...]))
        c2_t = right_product(turn[...], c2_ref[...]).astype(BF16)
        put(3 * width, product(c2_t, a2_ref[...]))
        dk_sum[...] = jnp.zeros_like(dk_sum)
        dv_sum[...] = jnp.zeros_like(dv_sum)

    keys_t = right_product(turn[...], keys_ref[...]).astype(BF16)
    dk_sum[...] += product(keys_t, dk)
    dv_sum[...] += product(keys_t, dv)

    @pl.when(step == 0)
    def _():
        for copy in copies:
            copy.wait()

    dmem_ref[...] = (
        right_product(dk, w_all[:, :width]) + right_product(dv, w_all[:, width:])
    ).astype(BF16)

    @pl.when(step == steps - 1)
    def _():
        put(width, dk_sum[...])
        put(2 * width, dv_sum[...])


def cross_weights(weights, source, h1, gains, dq2, c2, a2, keys, grads, spot, chunk, edge, masks):
    rows, width = h1.shape
    whole = lambda shape: pl.BlockSpec(shape, lambda i, spot: (0, 0))
    part = pl.BlockSpec((chunk, width), lambda i, spot: (i, 0))
    half = ((width // 2, 4 * width), BF16)
    return pl.pallas_call(
        functools.partial(cross_weights_kernel, masks, len(weights), edge),
        out_shape=shaped([half, half, (keys.shape, BF16)], (0,)),
        grid_spec=pltpu.PrefetchScalarGridSpec(
            num_scalar_prefetch=1,
            grid=(keys.shape[0] // chunk,),
            in_specs=[HBM] * len(weights)
            + [whole(source.shape), whole((rows, width)), whole(gains.shape)]
            + [whole((rows, width))] * 3
            + [part]
            + [pl.BlockSpec((chunk, width // 2), lambda i, spot: (i, 0))] * 4,
            out_specs=[whole(half[0]), whole(half[0]), part],
            scratch_shapes=[
                pltpu.VMEM((width, 2 * width), BF16),
                pltpu.VMEM((width, width), BF16),
                pltpu.VMEM((width, width), F32),
                pltpu.VMEM((width, width), F32),
                pltpu.SemaphoreType.DMA((blocks_in(weights),)),
            ],
        ),
        compiler_params=vmem(24),
        cost_estimate=cost(10),
        name="cross_weights",
    )(spot, *weights, source, h1, gains, dq2, c2, a2, keys, *grads)


def self_backward_kernel(heads, masks, counts, spot_ref, *refs):
    seq_count, weights = counts
    up_refs, refs = refs[:seq_count], refs[seq_count:]
    x_refs, refs = refs[:3], refs[3:]
    x_list = [x_refs[0], x_refs[1], x_refs[2].at[0], x_refs[2].at[1]]
    w_refs, refs = refs[:weights], refs[weights:]
    qkv_ref, log_ref, refs = refs[0], refs[1], refs[2:]
    dn_refs, refs = refs[:2], refs[2:]
    steps = seq_masks(lax.rem(spot_ref[0], 2))
    dqkv_ref, gain_grad_ref = refs[:2]
    up_all, x_all, w_all, dn_all, dk_sum, dv_sum, done = refs[2:]
    rows = up_refs[0].shape[0]
    broad = w_all.shape[1] // 3
    slim = heads * HEAD_DIM
    me, seq = spot_ref[0], spot_ref[1]
    spots = [lax.rem(seq - k + seq_count, seq_count) for k in range(seq_count)]
    early = [
        pltpu.make_async_copy(ref, up_all.at[spots[k]], done.at[k])
        for k, ref in enumerate(up_refs)
    ]
    late = [
        pltpu.make_async_copy(ref, x_all.at[jnp.bitwise_xor(seq, mask)], done.at[seq_count + k])
        for k, (ref, mask) in enumerate(zip(x_list, steps))
    ]
    late += weight_copies(w_refs, masks, me, (0, 3 * broad), w_all, done, 2 * seq_count)
    for copy in early + late:
        copy.start()
    keys_t = transposed(qkv_ref[:, broad : 2 * broad])
    dk_sum[...] = jnp.zeros_like(dk_sum)
    dv_sum[...] = jnp.zeros_like(dv_sum)
    blank = jnp.zeros((rows, broad - slim), BF16)
    for copy in early:
        copy.wait()
    for j in range(seq_count):
        first, last = j * rows, (j + 1) * rows
        queries = qkv_ref[first:last, :broad]
        upstream = jnp.concatenate([up_all[j], blank], axis=1)
        parts = []
        own = stack_heads(queries, range(heads))
        up_own = stack_heads(upstream, range(heads))
        logs = jnp.concatenate(
            [log_ref[head : head + 1, first:last] for head in range(heads)], axis=1
        )
        inner = right_product(qkv_ref[:last, 2 * broad :], up_own)
        scores = causal_scores(qkv_ref[:last, broad : 2 * broad], own, rows)
        chance, grad = score_grads(scores, logs, inner)
        dv_sum[:last] += product(chance, up_own)
        dk_sum[:last] += product(grad, own)
        for head in range(heads):
            lines = keys_t[head * HEAD_DIM : (head + 1) * HEAD_DIM, :last]
            parts.append(product(lines, grad[:, head * rows : (head + 1) * rows]))
        rest = jnp.zeros((broad - slim, rows), F32)
        dq = jnp.concatenate(parts + [rest], axis=0).T * SCALING
        dqkv_ref[first:last, :broad] = dq.astype(BF16)
    dqkv_ref[:, broad : 2 * broad] = (dk_sum[...] * SCALING).astype(BF16)
    dqkv_ref[:, 2 * broad :] = dv_sum[...].astype(BF16)
    for copy in late:
        copy.wait()
    total = 0.0
    for j in range(seq_count):
        dn1 = right_product(dqkv_ref[j * rows : (j + 1) * rows], w_all[...])
        x = x_all[j].astype(F32)
        total = total + jnp.sum(dn1 * x * norm_scale(x), axis=0, keepdims=True)
        dn_all[j] = dn1.astype(BF16)
    gain_grad_ref[...] = total
    for k, mask in enumerate(steps):
        dn_refs[k // 2][k % 2] = dn_all[jnp.bitwise_xor(seq, mask)]


def self_backward(up_pieces, x_pieces, weights, qkv, logs, spot, heads, masks):
    count = len(up_pieces)
    rows, width = x_pieces[0].shape
    slim = up_pieces[0].shape[1]
    length, broad = qkv.shape[0], qkv.shape[1] // 3
    whole = lambda shape: pl.BlockSpec(shape, lambda i, spot: (0, 0))
    shapes = [((2, rows, width), BF16)] * 2 + [(qkv.shape, BF16), ((1, width), F32)]
    outs = pl.pallas_call(
        functools.partial(self_backward_kernel, heads, masks, (count, len(weights))),
        out_shape=shaped(shapes),
        grid_spec=pltpu.PrefetchScalarGridSpec(
            num_scalar_prefetch=1,
            grid=(1,),
            in_specs=[HBM] * (count + 3 + len(weights)) + [whole(qkv.shape), whole(logs.shape)],
            out_specs=[
                pl.BlockSpec(s, lambda i, spot, n=len(s): (0,) * n) for s, _ in shapes
            ],
            scratch_shapes=[
                pltpu.VMEM((count, rows, slim), BF16),
                pltpu.VMEM((count, rows, width), BF16),
                pltpu.VMEM((width, 3 * broad), BF16),
                pltpu.VMEM((count, rows, width), BF16),
                pltpu.VMEM((length, broad), F32),
                pltpu.VMEM((length, broad), F32),
                pltpu.SemaphoreType.DMA((2 * count + blocks_in(weights),)),
            ],
        ),
        compiler_params=vmem(18),
        cost_estimate=cost(13),
        name="self_backward",
    )(spot, *up_pieces, *x_pieces, *weights, qkv, logs)
    return outs


def self_weights_kernel(
    spot_ref, source_ref, n1_ref, dqkv_ref, dh1_ref, gain_ref, *refs
):
    a_refs, (near_ref, far_ref, a_all) = refs[:-3], refs[-3:]
    width = n1_ref.shape[1]
    half = width // 2
    count = len(a_refs)
    turn = turn_of(source_ref, width)
    column = 0

    def put(values):
        nonlocal column
        values = values.astype(BF16)
        near_ref[:, column : column + values.shape[1]] = values[:half]
        far_ref[:, column : column + values.shape[1]] = values[half:]
        column += values.shape[1]

    for k, ref in enumerate(a_refs):
        a_all[lax.rem(spot_ref[1] - k + count, count)] = ref[...]
    a1 = jnp.concatenate([a_all[j] for j in range(count)], axis=1)
    c1_t = right_product(turn, dh1_ref[...].astype(BF16)).astype(BF16)
    put(product(c1_t, a1))
    put(right_product(turn, gain_ref[...].astype(BF16)))
    n1_t = right_product(turn, n1_ref[...]).astype(BF16)
    put(product(n1_t, dqkv_ref[...]))


def self_weights(source, n1, dqkv, dh1, gain_grads, a_pieces, spot):
    width = n1.shape[1]
    half = ((width // 2, width + LANES + dqkv.shape[1]), BF16)
    whole = lambda shape: pl.BlockSpec(shape, lambda i, spot: (0, 0))
    ins = [source, n1, dqkv, dh1, gain_grads, *a_pieces]
    return pl.pallas_call(
        self_weights_kernel,
        out_shape=shaped([half, half]),
        grid_spec=pltpu.PrefetchScalarGridSpec(
            num_scalar_prefetch=1,
            grid=(1,),
            in_specs=[whole(a.shape) for a in ins],
            out_specs=[whole(half[0])] * 2,
            scratch_shapes=[pltpu.VMEM((len(a_pieces),) + a_pieces[0].shape, BF16)],
        ),
        compiler_params=vmem(16),
        cost_estimate=cost(6),
        name="self_weights",
    )(spot, *ins)


def last_rows_kernel(keep_ref, one_ref, two_ref, x_ref, dh1_ref, gain_ref, out_ref):
    dn1 = keep_ref[0].astype(F32) + one_ref[0].astype(F32) + two_ref[...].astype(F32)
    x = x_ref[...].astype(F32)
    out_ref[...] = (
        dh1_ref[...] + norm_hidden_grad(x, norm_scale(x), gain_ref[0:1], dn1)
    ).astype(BF16)


def last_rows(keep, one, two, x, dh1, gains):
    return pl.pallas_call(
        last_rows_kernel,
        out_shape=jax.ShapeDtypeStruct(x.shape, BF16),
        compiler_params=vmem(8),
        cost_estimate=cost(2),
        name="last_rows",
    )(keep, one, two, x, dh1, gains)


def finish_kernel(slim, broad, spot_ref, *refs):
    sources, outs, hold = refs[:12], refs[12:-1], refs[-1]

    def total(refs, columns):
        keep, one, two = refs
        return (
            keep[0, :, columns[0] : columns[1]].astype(F32)
            + one[0, :, columns[0] : columns[1]].astype(F32)
            + two[0, :, columns[0] : columns[1]].astype(F32)
        )

    pair, down, cross, rest = sources[0:3], sources[3:6], sources[6:9], sources[9:12]
    hidden, width = outs[0].shape[1], outs[2].shape[1]
    outs[0][...] = total(pair, (0, hidden))
    outs[1][...] = total(pair, (hidden, 2 * hidden))
    outs[2][...] = total(down, (0, width))
    for i in range(4):
        outs[3 + i][...] = total(cross, (i * width, (i + 1) * width))
    outs[7][...] = total(rest, (0, width))
    edge = width
    outs[-1][...] = total(rest, (edge, edge + LANES))
    edge = edge + LANES
    far_edge = edge + 3 * broad
    keep, one, two = rest
    steps = [jnp.bitwise_xor(spot_ref[1], m) for m in seq_masks(lax.rem(spot_ref[0], 2))]
    hold[steps[0]] = keep[0, :, edge:far_edge].astype(F32)
    hold[steps[1]] = two[0, :, edge:far_edge].astype(F32)
    hold[steps[2]] = one[0, :, edge:far_edge].astype(F32)
    hold[steps[3]] = two[0, :, far_edge : far_edge + 3 * broad].astype(F32)
    for i in range(3):
        outs[8 + i][...] = jnp.concatenate(
            [hold[j][:, i * broad : i * broad + slim] for j in range(hold.shape[0])], axis=1
        )


def finish(pair, down, cross, rest, spot, hidden, slim, broad):
    share, feed_share, width = pair[0].shape[1], down[0].shape[1], down[0].shape[2]
    count = lax.axis_size("seq")
    shapes = (
        [(share, hidden)] * 2 + [(feed_share, width)] + [(share, width)] * 8 + [(share, LANES)]
    )
    whole = lambda shape: pl.BlockSpec(shape, lambda i, spot: (0,) * len(shape))
    flat = [*pair, *down, *cross, *rest]
    return pl.pallas_call(
        functools.partial(finish_kernel, slim, broad),
        out_shape=shaped([(shape, F32) for shape in shapes]),
        grid_spec=pltpu.PrefetchScalarGridSpec(
            num_scalar_prefetch=1,
            grid=(1,),
            in_specs=[whole(a.shape) for a in flat],
            out_specs=[whole(shape) for shape in shapes],
            scratch_shapes=[pltpu.VMEM((count, share, 3 * broad), F32)],
        ),
        compiler_params=vmem(12),
        cost_estimate=cost(3),
        name="finish",
    )(spot, *flat)


def local(
    hidden_in,
    memory,
    cotangent,
    norm_self,
    query_self,
    key_self,
    value_self,
    output_self,
    norm_cross,
    query_cross,
    key_cross,
    value_cross,
    output_cross,
    norm_feed,
    gate_weight,
    up_weight,
    down_weight,
    block_counts,
    memory_tail,
    row_example,
):
    mem_count, seq_count = lax.axis_size("mem"), lax.axis_size("seq")
    mem_place, seq_place = lax.axis_index("mem"), lax.axis_index("seq")
    rows, width = hidden_in.shape[1], hidden_in.shape[2]
    inner = HEADS * HEAD_DIM
    near = HEADS // seq_count
    slim = near * HEAD_DIM
    broad = -(-(slim + 8) // LANES) * LANES
    share = norm_self.shape[0]
    hidden_width = gate_weight.shape[1]
    spot = jnp.stack([mem_place, seq_place]).astype(jnp.int32)
    scalars = jnp.concatenate([block_counts, memory_tail, row_example])
    masks = slot_masks(mem_count)
    mask_array = mem_masks()
    block = width // mem_count
    column = jnp.arange(width, dtype=jnp.int32)
    source = (block * (mem_place ^ jnp.repeat(mask_array, block)) + column % block).reshape(width, 1)
    gain_stack = jnp.stack([norm_self, norm_cross, norm_feed], axis=0)
    x_own = hidden_in[0]
    edge = 3 * broad
    turns = mem_count.bit_length() - 2
    flat = lambda stacked: stacked.reshape((1, -1) + stacked.shape[2:])

    with jax.named_scope("gather"):
        own, two, one, second, blocks, live = prepare(
            (query_self, key_self, value_self, output_self, query_cross)
            + (key_cross, value_cross, output_cross, gate_weight, up_weight),
            gain_stack, memory, scalars, spot, slim, broad,
        )
        live = live.reshape(-1, 1)
        stay, go = part_blocks(blocks, 0)
        two, arrived = swap_seq(two, 0), swap_mem(go, 0)
        c3 = cotangent[0]
        c3_other = swap_mem(c3, turns)
        blocks, x_in, down_in = join_blocks(stay, arrived), x_own, down_weight
        three = swap_seq(jnp.stack([one, two[:, edge:]]), 1)
        second_a = swap_seq(second, 0)
        for turn in range(1, turns):
            stay, go = part_blocks(blocks, turn)
            blocks = join_blocks(stay, swap_mem(go, turn))
        three, blocks, second_a, second, x_in, down_in, source = settle(
            three, blocks, second_a, second, x_in, down_in, source
        )
        plain = [(0, 0, 0, edge), (1, 0, edge, 5 * width)]
        skipping = [(0, 0, 0, edge), (1, 0, 2 * edge, 5 * width)]
        heads, outer = place(
            [own[None], two[None], three],
            seq_places(),
            [edge, 5 * width],
            [plain, skipping, plain],
        )
        heads, outer = [flat(heads)], [flat(outer)]
        heads.append(swap_mem(heads[0], 0))
        outer.append(swap_mem(outer[0], 0))
        stay, go = part_blocks(blocks, turns)
        keys_in = join_blocks(stay, swap_mem(go, turns)).reshape(-1, width)
        second_b = swap_seq(jnp.stack([second, second_a]), 1)
        heads, outer, keys_in, second_a, second_b, second, x_in, down_in = settle(
            heads, outer, keys_in, second_a, second_b, second, x_in, down_in
        )
        x_a = swap_seq(x_in, 0)
        for turn in range(1, turns):
            heads.append(swap_mem(join(heads), turn))
            outer.append(swap_mem(join(outer), turn))
        both = [flat(stack_seq([second[None], second_a[None], second_b]))]
        x_a, x_in, both, down_in = settle(x_a, x_in, both, down_in)
        x_b = swap_seq(jnp.stack([x_in, x_a]), 1)
        both.append(swap_mem(both[0], 0))
        down_a = swap_seq(down_in, 0)
        heads, outer, both, x_b, x_a, x_in, down_a, down_in = settle(
            heads, outer, both, x_b, x_a, x_in, down_a, down_in
        )
        heads, outer = join(heads), join(outer)
        heads = [heads, swap_mem(heads, turns)]
        outer = [outer, swap_mem(outer, turns)]
        for turn in range(1, turns):
            both.append(swap_mem(join(both), turn))
        down_b = swap_seq(jnp.stack([down_in, down_a]), 1)
        heads, x_in, x_a, x_b = settle(heads, x_in, x_a, x_b)
        packed_heads = spread_weight(heads)

    key_chunk = width

    with jax.named_scope("forward"):
        x_pieces = [x_in, x_a, x_b]
        o_pieces, n1, qkv, gains, self_logs = self_rows(
            x_pieces, packed_heads, spot, near, broad, masks
        )
        o_pieces, gains, outer, down_a, down_b, down_in = settle(
            o_pieces, gains, outer, down_a, down_b, down_in
        )
        packed = spread_weight(outer)
        downs = [flat(stack_seq([down_in[None], down_a[None], down_b]))]
        a_pieces = send_seq(o_pieces)
        kv2 = key_values(keys_in, packed, spot, key_chunk, 2 * width, masks)
        downs.append(swap_mem(downs[0], 0))
        a_pieces, kv2, downs, keys_in, both = settle(a_pieces, kv2, downs, keys_in, both)
        q2, a2_early, h1, logs_first = rows_first(
            a_pieces, packed, x_own, gains, live, kv2, spot, 0, masks
        )
        both = join(both)
        both_other = swap_mem(both, turns)
        for turn in range(1, turns):
            downs.append(swap_mem(join(downs), turn))
        others = [swap_mem(downs[0], turns), swap_mem(downs[1], turns)]
        a2_early, h1, q2, both, both_other, others, downs = settle(
            a2_early, h1, q2, both, both_other, others, downs
        )
        a2, h2, logs_second = rows_second(
            packed, h1, a2_early, live, q2, kv2, spot, 0, masks
        )
        others += [swap_mem(piece, turns) for piece in downs[2:]]
        h2, both_other, both, downs, others = settle(h2, both_other, both, downs, others)
        both = [w.reshape(-1, 2 * hidden_width) for w in (both, both_other)]
        unit = hidden_width // mem_count
        narrow = unit % LANES != 0
        if narrow:
            unit = 2 * LANES
            downs = [stack_mem(downs + others).reshape(-1, unit, width)]
            feed_order = jnp.arange(hidden_width // unit, dtype=jnp.int32)
        else:
            feed_order = mem_place ^ mask_array
            downs = downs + others
        layer_out, dh2, c2, gain_feed_terms, bundle, act_near, n3_near = feed(
            feed_order, h2, c3, gains, source, both, downs
        )

    with jax.named_scope("backward"):
        bundle_other = swap_mem(bundle, turns)
        up, dq_early, dk_early, dv_early = rows_early(
            packed, c2, live, logs_first, q2, kv2, spot, 0, masks
        )
        bundle_other, up, dq_early = settle(bundle_other, up, dq_early)
        if narrow:
            acts = jnp.concatenate([act_near, bundle[:, 2 * hidden_width : -(width // 2)]], axis=1)
            g_down = left_product(acts, c3).astype(BF16).reshape(mem_count, -1, width)
            g_down = place([g_down], jnp.argsort(mem_place ^ mask_array)).reshape(2, -1, width)
            normed = jnp.concatenate([n3_near, bundle[:, -(width // 2) :]], axis=1)
            g_both = jnp.stack(
                [
                    left_product(normed, bundle[:, k * hidden_width : (k + 1) * hidden_width])
                    for k in range(2)
                ]
            ).astype(BF16)
            feeding = Scatter(g_both[:, : width // 2], g_both[:, width // 2 :])
            downing = Scatter(g_down[0], g_down[1])
            for s in (feeding, downing):
                s.move()
            advance([feeding, downing], spot)
        else:
            g_feed = feed_weights(bundle, bundle_other, act_near, n3_near, c3, c3_other)
            feeding, downing = Scatter(*g_feed[0:2], 1), Scatter(*g_feed[2:4], 1)
        feeding.sent, up = settle(feeding.sent, up)
        feeding.move()
        da_pieces, dq2, dk_late, dv_late, dh1, gain_cross_terms = rows_late(
            packed, up, dq_early, dh2, h1, gains, live, logs_second, q2, kv2, spot, 0, masks
        )
        da_pieces, dq2 = settle(da_pieces, dq2)
        da_pieces = send_seq(da_pieces)
        *g_cross, dmem = cross_weights(
            packed, source, h1, gains, dq2, c2, a2, keys_in,
            [dk_early, dk_late, dv_early, dv_late], spot, key_chunk, 0, masks,
        )
        crossing = Scatter(*g_cross)
        advance([feeding], spot)
        da_pieces, crossing.sent, feeding.sent, downing.sent, dmem = settle(
            da_pieces, crossing.sent, feeding.sent, downing.sent, dmem
        )
        crossing.move()
        feeding.move()
        keep_dn, send_dn, dqkv, gain_self_terms = self_backward(
            da_pieces, x_pieces, packed_heads, qkv, self_logs, spot, near, masks
        )
        dmem = dmem.reshape(mem_count, -1, width)
        stay, go = part_blocks(dmem, turns)
        dmem = join_blocks(stay, swap_mem(go, turns))
        crossing.terms, feeding.terms, downing.sent, keep_dn, send_dn, dqkv, dmem = settle(
            crossing.terms, feeding.terms, downing.sent, keep_dn, send_dn, dqkv, dmem
        )
        one_dn = swap_seq(send_dn, 1)
        downing.move()
        stay, go = part_blocks(dmem, 0)
        dmem = join_blocks(stay, swap_mem(go, 0))
        while feeding.left > 0:
            advance([feeding], spot)
            feeding.move()
        ends = [advance([feeding], spot), None, None, None]
        advance([crossing], spot)
        gain_grads = jnp.concatenate(
            [gain_self_terms, gain_cross_terms, gain_feed_terms, jnp.zeros((LANES - 3, width), F32)]
        )
        g_self = self_weights(source, n1, dqkv, dh1, gain_grads, a_pieces, spot)
        selfing = Scatter(*g_self)
        crossing.move()
        one_dn, keep_dn, downing.terms, dmem, ends[0], selfing.sent = settle(
            one_dn, keep_dn, downing.terms, dmem, ends[0], selfing.sent
        )
        two_dn = swap_seq(onward(keep_dn, one_dn)[0], 0)
        one_both = swap_seq(ends[0][1], 1)
        selfing.move()
        for turn in range(1, turns):
            stay, go = part_blocks(dmem, turn)
            dmem = join_blocks(stay, swap_mem(go, turn))
        while downing.left > 0:
            advance([downing], spot)
            downing.move()
        ends[1] = advance([downing], spot)
        while crossing.left > 0:
            advance([crossing], spot)
            crossing.move()
        while selfing.left > 0:
            advance([selfing], spot)
            selfing.move()
        two_both = swap_seq(onward(ends[0][0], one_both), 0)
        mem_keep, mem_send = pick_slots(dmem, memory.shape[0], scalars, spot)
        mem_one = swap_seq(mem_send, 1)
        one_down = swap_seq(ends[1][1], 1)
        ends[2] = advance([crossing], spot)
        one_cross = swap_seq(ends[2][1], 1)
        mem_two = swap_seq(onward(mem_keep, mem_one), 0)
        ends[3] = advance([selfing], spot)
        one_self = swap_seq(ends[3][1], 1)
        two_down = swap_seq(onward(ends[1][0], one_down), 0)
        two_cross = swap_seq(onward(ends[2][0], one_cross), 0)
        two_self = swap_seq(onward(ends[3][0], one_self, width + LANES), 0)
        hidden_grad = last_rows(keep_dn, one_dn, after(two_dn, ends[3][1]), x_own, dh1, gains)
        per = mem_two.shape[0]
        memory_grad = total_of([mem_keep[:per], mem_one[:per], mem_two]).astype(BF16)
        *finals, gain_finals = finish(
            (ends[0][0], one_both, two_both),
            (ends[1][0], one_down, two_down),
            (ends[2][0], one_cross, two_cross),
            (ends[3][0], one_self, two_self),
            spot, hidden_width, slim, broad,
        )
    g_gate, g_up, g_down, g_q2, g_k2, g_v2, g_o2, g_o1, g_q1, g_k1, g_v1 = finals
    return (
        layer_out[None],
        hidden_grad[None],
        memory_grad,
        gain_finals[:, 0],
        g_q1,
        g_k1,
        g_v1,
        g_o1,
        gain_finals[:, 1],
        g_q2,
        g_k2,
        g_v2,
        g_o2,
        gain_finals[:, 2],
        g_gate,
        g_up,
        g_down,
    )


def solution(mesh):
    every = P(("mem", "seq"), None)
    gain = P(("mem", "seq"))
    in_specs = (
        (P("mem", "seq", None), P(None, "mem", None), P("mem", "seq", None), gain)
        + (every,) * 4
        + (gain,)
        + (every,) * 4
        + (gain,)
        + (every,) * 3
        + (P(),) * 3
    )
    out_specs = (
        (P("mem", "seq", None), P("mem", "seq", None), P("seq", "mem", None), gain)
        + (every,) * 4
        + (gain,)
        + (every,) * 4
        + (gain,)
        + (every,) * 3
    )
    return jax.shard_map(local, mesh=mesh, in_specs=in_specs, out_specs=out_specs, check_vma=False)
```

```python
import functools

import jax
import jax.numpy as jnp
from jax import lax
from jax.experimental import pallas as pl
from jax.experimental.pallas import tpu as pltpu
from jax.sharding import PartitionSpec as P

HEADS = 12
HEAD_DIM = 64
SCALING = HEAD_DIM ** (-0.5)
LANES = 128
MASKED = -1e30
F32 = jnp.float32
BF16 = jnp.bfloat16


def product(left, right):
    return jnp.dot(left, right, preferred_element_type=F32)


def left_product(left, right):
    return lax.dot_general(left, right, (((0,), (0,)), ((), ())), preferred_element_type=F32)


def right_product(left, right):
    return lax.dot_general(left, right, (((1,), (1,)), ((), ())), preferred_element_type=F32)


def gelu_tanh(values):
    return (
        0.5
        * values
        * (1.0 + jnp.tanh(0.7978845608028654 * (values + 0.044715 * values * values * values)))
    )


def gated_unit(gate, upper):
    return gelu_tanh(gate) * upper


def norm_scale(hidden):
    return lax.rsqrt(jnp.mean(hidden * hidden, axis=-1, keepdims=True) + 1e-06)


def norm_hidden_grad(hidden, scale, gain, upstream):
    lifted = upstream * gain
    return scale * lifted - hidden * (scale * scale * scale) * jnp.mean(
        lifted * hidden, axis=-1, keepdims=True
    )


def shift(values, axis, step):
    size = lax.axis_size(axis)
    return lax.ppermute(values, axis, [(i, (i + step) % size) for i in range(size)])


def swap(values, axis, mask):
    size = lax.axis_size(axis)
    return lax.ppermute(values, axis, [(i, i ^ mask) for i in range(size)])


def place_kernel(counts, maps, places, *refs):
    sources = refs[: len(counts)]
    targets, done = refs[len(counts) : -1], refs[-1]
    copies = []
    number = 0
    for source, count, moves in zip(sources, counts, maps):
        for block in range(count):
            for goal, to, start, width in moves:
                part, target = source.at[block], targets[goal].at[places[number]]
                if len(moves) > 1 or width != source.shape[2]:
                    part = source.at[block, :, start : start + width]
                    target = targets[goal].at[places[number], :, to : to + width]
                copies.append(pltpu.make_async_copy(part, target, done.at[len(copies)]))
            number += 1
    for copy in copies:
        copy.start()
    for copy in copies:
        copy.wait()


def place(pieces, places, widths=None, maps=None):
    counts = [piece.shape[0] for piece in pieces]
    total = sum(counts)
    _, height, width = pieces[0].shape
    widths = widths or [width]
    if maps is None:
        plain = [(i, 0, sum(widths[:i]), w) for i, w in enumerate(widths)]
        maps = [plain] * len(pieces)
    copies = sum(count * len(moves) for count, moves in zip(counts, maps))
    outs = [((total, height, w), pieces[0].dtype) for w in widths]
    size = total * height * sum(widths) * 2
    result = pl.pallas_call(
        functools.partial(place_kernel, counts, maps),
        out_shape=shaped(outs),
        grid_spec=pltpu.PrefetchScalarGridSpec(
            num_scalar_prefetch=1,
            grid=(1,),
            in_specs=[HBM] * len(pieces),
            out_specs=[
                pl.BlockSpec((total, height, w), lambda i, places: (0, 0, 0)) for w in widths
            ],
            scratch_shapes=[pltpu.SemaphoreType.DMA((copies,))],
        ),
        compiler_params=pltpu.CompilerParams(vmem_limit_bytes=3 * size + (4 << 20)),
        cost_estimate=cost(1 + size / 1e6),
        name="place",
    )(places.astype(jnp.int32), *pieces)
    return result[0] if len(widths) == 1 else result


def after(values, *tokens):
    return lax.optimization_barrier((values,) + tokens)[0]


def settle(*values):
    return lax.optimization_barrier(values)


def seq_masks(parity):
    return [0, 1 + parity, 2 - parity, 3]


def swap_seq(values, turn):
    mem, seq = lax.axis_size("mem"), lax.axis_size("seq")
    pairs = []
    for m in range(mem):
        mask = 1 + (m + turn) % 2
        pairs += [(m * seq + s, m * seq + (s ^ mask)) for s in range(seq)]
    return lax.ppermute(values, ("mem", "seq"), pairs)


def seq_places():
    parity = lax.axis_index("mem") % 2
    return lax.axis_index("seq") ^ jnp.stack(seq_masks(parity)).astype(jnp.int32)


def stack_seq(pieces, widths=None):
    return place(pieces, seq_places(), widths)


def send_seq(pieces):
    return [pieces[0]] + [shift(piece, "seq", k) for k, piece in enumerate(pieces) if k]


def total_of(pieces):
    return functools.reduce(jnp.add, [piece.astype(F32) for piece in pieces])


def join(blocks):
    return blocks[0] if len(blocks) == 1 else jnp.concatenate(blocks, axis=0)


def orders(count):
    bits = list(range(1, count.bit_length() - 1))
    return bits, bits[::-1]


def slot_masks(count):
    half = count // 2
    low = [
        [sum(((s >> j) & 1) << bit for j, bit in enumerate(order)) for s in range(half)]
        for order in orders(count)
    ]
    return low[0] + [m | 1 for m in low[1]], low[1] + [m | 1 for m in low[0]]


def swap_mem(values, turn):
    count = lax.axis_size("mem")
    pairs = []
    for i in range(count):
        order = [*orders(count)[i % 2], 0]
        pairs.append((i, i ^ (1 << order[turn])))
    return lax.ppermute(values, "mem", pairs)


def mem_masks():
    count = lax.axis_size("mem")
    even, odd = slot_masks(count)
    return jnp.where(
        lax.axis_index("mem") % 2 == 0, jnp.array(even, jnp.int32), jnp.array(odd, jnp.int32)
    )


def stack_mem(halves, widths=None):
    return place(halves, lax.axis_index("mem") ^ mem_masks(), widths)


def spread_weight(halves):
    if halves[0].shape[1] % 16 == 0:
        return list(halves)
    stacked = stack_mem(halves)
    return [stacked.reshape(1, -1, stacked.shape[-1])]


def add_low(left, right):
    return (left.astype(F32) + right.astype(F32)).astype(BF16)


def total_kernel(plans, spot_ref, *refs):
    terms = sum(number for number, _ in plans)
    sources, refs = list(refs[:terms]), refs[terms:]
    outs, holds = list(refs[: len(refs) - len(plans)]), refs[len(refs) - len(plans) :]
    column = 0
    for (number, ends), hold in zip(plans, holds):
        mine, sources = sources[:number], sources[number:]
        groups, rows, width = mine[0].shape
        for g in range(groups):
            total = mine[0][g].astype(F32)
            for ref in mine[1:]:
                total = total + ref[g].astype(F32)
            if not ends:
                outs[0][g] = total.astype(BF16)
                continue
            count = hold.shape[0]
            unit = rows // count
            for j in range(count):
                hold[j] = total[j * unit : (j + 1) * unit]
            for k, mask in enumerate(seq_masks(lax.rem(spot_ref[0], 2))):
                piece = hold[jnp.bitwise_xor(spot_ref[1], mask)].astype(BF16)
                outs[-2 + k // 2][k % 2, :, column : column + width] = piece
            column += width
        if not ends:
            del outs[:1]


class Scatter:
    def __init__(self, kept, sent, taken=0):
        self.terms = [kept if kept.ndim == 3 else kept[None]]
        self.sent = sent if sent.ndim == 3 else sent[None]
        self.left = (lax.axis_size("mem") // 2).bit_length() - 1 - taken
        self.rows = self.terms[0].shape[1]

    def move(self):
        self.terms.append(swap_mem(self.sent, self.left))

    def hold(self):
        return [self.terms, self.sent]

    def take(self, held):
        self.terms, self.sent = held


def advance(scatters, spot):
    count = lax.axis_size("seq")
    plans, shapes, specs, flat, holds = [], [], [], [], []
    ended, exact = 0, True
    whole = lambda shape: pl.BlockSpec(shape, lambda i, spot: (0, 0, 0))
    for s in scatters:
        ends = s.left == 0
        groups, _, width = s.terms[0].shape
        rows = s.rows if ends else s.rows // 2
        exact = exact and rows // (count if ends else 1) % 8 == 0
        plans.append((len(s.terms), ends))
        part = (groups, rows, width)
        if ends:
            specs += [whole(part)] * len(s.terms)
            ended += groups * width
            unit = rows // count
            holds.append(pltpu.VMEM((count, unit, width), F32))
        else:
            specs += [pl.BlockSpec(part, lambda i, spot: (0, 1, 0))] * len(s.terms)
            shapes.append(part)
            holds.append(pltpu.VMEM((1, 8, 128), F32))
        flat += s.terms
    if ended:
        shapes += [(2, unit, ended)] * 2
    if exact:
        size = sum(spec.block_shape[0] * spec.block_shape[1] * spec.block_shape[2] for spec in specs)
        outs = pl.pallas_call(
            functools.partial(total_kernel, plans),
            out_shape=shaped([(shape, BF16) for shape in shapes]),
            grid_spec=pltpu.PrefetchScalarGridSpec(
                num_scalar_prefetch=1,
                grid=(1,),
                in_specs=specs,
                out_specs=[whole(shape) for shape in shapes],
                scratch_shapes=holds,
            ),
            compiler_params=vmem(6 + (size * 8 >> 20)),
            cost_estimate=cost(1 + size / 1e6),
            name="total",
        )(spot, *(far(*flat) if size > 1 << 20 else flat))
        outs = list(outs)
    else:
        outs, ends_at = [], []
        for s in scatters:
            low = 0 if s.left == 0 else s.rows // 2
            high = s.rows if s.left == 0 else 2 * low
            total = total_of([term[:, low:high] for term in s.terms]).astype(BF16)
            if s.left:
                outs.append(total)
                continue
            groups, rows, width = total.shape
            blocks = total.reshape(groups, count, rows // count, width)
            ends_at.append(jnp.take(jnp.concatenate(list(blocks), axis=2), seq_places(), axis=0))
        if ends_at:
            blocks = jnp.concatenate(ends_at, axis=2)
            outs += [blocks[:2], blocks[2:]]
    for s in scatters:
        if s.left:
            s.sent, s.rows = outs.pop(0), s.rows // 2
        s.left -= 1
    return outs or None


def onward(kept, arrived, summed=None):
    half = kept.shape[0] // 2
    mine, theirs = kept[half:], arrived[half:]
    if summed is None:
        return add_low(mine, theirs)
    return jnp.concatenate(
        [add_low(mine[..., :summed], theirs[..., :summed]), mine[..., summed:], theirs[..., summed:]],
        axis=-1,
    )


def part_blocks(blocks, turn):
    count = blocks.shape[0]
    parts = blocks.reshape((count >> (turn + 1), 2, 1 << turn) + blocks.shape[1:])
    return parts[:, 0], parts[:, 1]


def join_blocks(stay, arrived):
    joined = jnp.stack([stay, arrived], axis=1)
    return joined.reshape((-1,) + joined.shape[3:])


HBM = pl.BlockSpec(memory_space=pltpu.HBM)


def far(*arrays):
    return [pltpu.with_memory_space_constraint(array, pltpu.HBM) for array in arrays]


def shaped(shapes, distant=()):
    return [
        jax.ShapeDtypeStruct(shape, dtype)
        for i, (shape, dtype) in enumerate(shapes)
    ]


def vmem(mebibytes):
    return pltpu.CompilerParams(vmem_limit_bytes=mebibytes << 20)


def cost(microseconds):
    return pl.CostEstimate(
        flops=int(microseconds * 1.1e9), bytes_accessed=0, transcendentals=0
    )


def run(copies):
    for copy in copies:
        copy.start()
    for copy in copies:
        copy.wait()


def prepare_kernel(
    slim, broad, scalars_ref, spot_ref,
    q_ref, k_ref, v_ref, o1_ref, q2_ref, k2_ref, v2_ref, o2_ref, gate_ref, up_ref,
    gain_ref, memory_ref,
    own_ref, two_ref, one_ref, second_ref, blocks_ref, live_ref,
    turn, triple, held, done,
):
    mem_count, height = blocks_ref.shape[0], memory_ref.shape[1]
    share, width = q_ref.shape
    half = mem_count // 2
    me, seq = spot_ref[0], spot_ref[1]
    parity = lax.rem(me, 2)
    counts_at, tails_at, rows_at = 0, mem_count, 2 * mem_count
    moves = [(ref, triple.at[i]) for i, ref in enumerate((q_ref, k_ref, v_ref))]
    moves += [(memory_ref, held)]
    for ref, base in ((own_ref, 3 * broad), (one_ref, 3 * broad), (two_ref, 6 * broad)):
        for i, source in enumerate((o1_ref, q2_ref, k2_ref, v2_ref, o2_ref)):
            moves += [(source, ref.at[:, base + i * width : base + (i + 1) * width])]
    hidden = gate_ref.shape[1]
    moves += [(gate_ref, second_ref.at[:, :hidden]), (up_ref, second_ref.at[:, hidden:])]
    copies = [pltpu.make_async_copy(a, b, done.at[i]) for i, (a, b) in enumerate(moves)]
    for copy in copies:
        copy.start()
    turn[...] = jnp.zeros_like(turn)
    turn[0:3, 0:share] = gain_ref[...].astype(F32)
    gains = turn[...].T[:share]
    lane = lax.broadcasted_iota(jnp.int32, (share, broad - slim), 1)
    extra = jnp.zeros((share, broad - slim), F32)
    for i in range(3):
        extra = jnp.where(lane == i, gains[:, i : i + 1], extra)
    extra = extra.astype(BF16)
    blank = jnp.zeros((share, broad - slim), BF16)
    token = lax.broadcasted_iota(jnp.int32, (height, 1), 0)

    def first_block(example):
        return lax.fori_loop(
            0, example, lambda i, total: total + scalars_ref[counts_at + i], jnp.int32(0)
        )

    mine = scalars_ref[rows_at + me]
    mine_start = first_block(mine)
    mine_end = mine_start + scalars_ref[counts_at + mine]

    for copy in copies[:4]:
        copy.wait()

    order, contrary = orders(mem_count)

    def one(t, carry):
        low = lax.rem(t, half)
        first, second = jnp.int32(0), jnp.int32(0)
        for j in range(len(order)):
            bit = lax.rem(lax.shift_right_logical(low, jnp.int32(j)), 2)
            first = first + bit * (1 << order[j])
            second = second + bit * (1 << contrary[j])
        flip = parity == 1
        first, second = jnp.where(flip, second, first), jnp.where(flip, first, second)
        upper = t >= half
        goal = jnp.bitwise_xor(me, jnp.where(upper, first + 1, first))
        start = first_block(scalars_ref[rows_at + goal])
        block = start + lax.rem(me - lax.rem(start, mem_count) + mem_count, mem_count)
        slot = jnp.minimum(block // mem_count, memory_ref.shape[0] - 1)
        blocks_ref[t] = held[slot]
        holder = jnp.bitwise_xor(me, jnp.where(upper, second + 1, first))
        block = mine_start + lax.rem(
            holder - lax.rem(mine_start, mem_count) + mem_count, mem_count
        )
        bound = jnp.where(block == mine_end - 1, scalars_ref[tails_at + mine], height)
        bound = jnp.where(block < mine_end, bound, 0)
        live_ref[t] = jnp.where(token < bound, 0.0, MASKED)
        return carry

    lax.fori_loop(0, mem_count, one, 0)
    seq_steps = seq_masks(parity)
    for ref, base, mask in (
        (own_ref, 0, seq_steps[0]),
        (two_ref, 0, seq_steps[1]),
        (one_ref, 0, seq_steps[2]),
        (two_ref, 1, seq_steps[3]),
    ):
        goal = jnp.bitwise_xor(seq, mask)
        for i in range(3):
            weight = triple[i].astype(F32)
            chosen = weight[:, :slim]
            for j in range(1, width // slim):
                chosen = jnp.where(goal == j, weight[:, j * slim : (j + 1) * slim], chosen)
            start = (3 * base + i) * broad
            ref[:, start : start + broad] = jnp.concatenate(
                [chosen.astype(BF16), blank if i else extra], axis=1
            )
    for copy in copies[4:]:
        copy.wait()


def prepare(weights, gains, memory, scalars, spot, slim, broad):
    mem_count = lax.axis_size("mem")
    share, width = weights[0].shape
    first = 3 * broad + 5 * width
    second = sum(w.shape[1] for w in weights[8:])
    height = memory.shape[1]
    whole = lambda shape: pl.BlockSpec(shape, lambda *_: (0,) * len(shape))
    outs = [
        ((share, first), BF16),
        ((share, first + 3 * broad), BF16),
        ((share, first), BF16),
        ((share, second), BF16),
        ((mem_count, height, width), BF16),
        ((mem_count, height, 1), F32),
    ]
    return pl.pallas_call(
        functools.partial(prepare_kernel, slim, broad),
        out_shape=shaped(outs),
        grid_spec=pltpu.PrefetchScalarGridSpec(
            num_scalar_prefetch=2,
            grid=(1,),
            in_specs=[HBM] * len(weights) + [whole(gains.shape), HBM],
            out_specs=[whole(shape) for shape, _ in outs],
            scratch_shapes=[
                pltpu.VMEM((8, 128), F32),
                pltpu.VMEM((3, share, width), BF16),
                pltpu.VMEM(memory.shape, BF16),
                pltpu.SemaphoreType.DMA((4 + 15 + 2,)),
            ],
        ),
        compiler_params=vmem(16 + 3 * mem_count // 8),
        cost_estimate=cost(3),
        name="prepare",
    )(scalars, spot, *far(*weights), gains, *far(memory))


def slots_kernel(per, scalars_ref, spot_ref, blocks_ref, keep_ref, send_ref, done):
    mem_count = blocks_ref.shape[0]
    me, seq = spot_ref[0], spot_ref[1]
    parity = lax.rem(me, 2)
    copies = []
    for k, mask in enumerate(seq_masks(parity)):
        for s in range(per):
            slot = jnp.bitwise_xor(seq, mask) * per + s
            block = slot * mem_count + me

            def scan(i, carry):
                end, owner = carry
                end = end + scalars_ref[i]
                return end, owner + jnp.where(end <= block, 1, 0)

            _, owner = lax.fori_loop(0, mem_count, scan, (jnp.int32(0), jnp.int32(0)))
            row = lax.fori_loop(
                0,
                mem_count,
                lambda i, r: jnp.where(scalars_ref[2 * mem_count + i] == owner, i, r),
                jnp.int32(0),
            )
            gap = jnp.bitwise_xor(row, me)
            bit = lambda b: lax.rem(lax.shift_right_logical(gap, jnp.int32(b)), 2)
            spots = [
                sum(bit(b) * (1 << j) for j, b in enumerate(order)) for order in orders(mem_count)
            ]
            at = jnp.where(parity == 1, spots[1], spots[0]) + bit(0) * (mem_count // 2)
            copies.append(
                pltpu.make_async_copy(
                    blocks_ref.at[at],
                    (keep_ref, send_ref)[k // 2].at[k % 2 * per + s],
                    done.at[len(copies)],
                )
            )
    for copy in copies:
        copy.start()
    for copy in copies:
        copy.wait()


def pick_slots(blocks, slots, scalars, spot):
    per = slots // lax.axis_size("seq")
    shape = (2 * per,) + blocks.shape[1:]
    return pl.pallas_call(
        functools.partial(slots_kernel, per),
        out_shape=shaped([(shape, BF16)] * 2),
        grid_spec=pltpu.PrefetchScalarGridSpec(
            num_scalar_prefetch=2,
            grid=(1,),
            in_specs=[HBM],
            out_specs=[pl.BlockSpec(shape, lambda *_: (0, 0, 0))] * 2,
            scratch_shapes=[pltpu.SemaphoreType.DMA((slots,))],
        ),
        compiler_params=vmem(8),
        cost_estimate=cost(2),
        name="pick_slots",
    )(scalars, spot, blocks)


PAIR = 2


def feed_kernel(
    order_ref, h2_ref, c3_ref, gain_ref, source_ref,
    *refs,
):
    sides, refs = refs[: 4 * PAIR], refs[4 * PAIR :]
    down_refs, refs = refs[:-15], refs[-15:]
    out_ref, dh2_ref, c2_ref, gain_grad_ref, bundle_ref, act_near_ref, n3_near_ref = refs[:7]
    turn, n3_rel, total, dn3, gate_w, up_w, down_w, act_all = refs[7:]
    step, steps = pl.program_id(0), pl.num_programs(0)
    half, unit = sides[0].shape
    width = h2_ref.shape[1]
    hidden = unit * steps * PAIR
    slim = width // 2

    @pl.when(step == 0)
    def _():
        columns = lax.broadcasted_iota(jnp.int32, (width, width), 1)
        turn[...] = (columns == source_ref[...]).astype(F32).astype(BF16)
        h2 = h2_ref[...]
        n3 = (h2 * norm_scale(h2) * gain_ref[2:3]).astype(BF16)
        rel = right_product(n3, turn[...]).astype(BF16)
        n3_rel[...] = rel
        n3_near_ref[...] = rel[:, :slim]
        bundle_ref[:, 2 * hidden + hidden // 2 :] = rel[:, slim:]
        total[...] = jnp.zeros_like(total)
        dn3[...] = jnp.zeros_like(dn3)

    base = 0
    for ref in down_refs:
        number = ref.shape[0]
        for block in range(number):

            @pl.when(step == (base + block) // PAIR)
            def _(ref=ref, block=block, at=(base + block) % PAIR):
                down_w[at * unit : (at + 1) * unit] = ref[block]

        base += number
    for n in range(PAIR):
        part = slice(n * unit, (n + 1) * unit)
        for k, target in enumerate((gate_w, up_w)):
            target[:half, part] = sides[4 * n + 2 * k][...]
            target[half:, part] = sides[4 * n + 2 * k + 1][...]
    down = down_w[...]
    n3, c3 = n3_rel[...], c3_ref[...]
    gate = product(n3, gate_w[...])
    upper = product(n3, up_w[...])
    dact = right_product(c3, down)
    inner = 0.7978845608028654 * (gate + 0.044715 * gate * gate * gate)
    bent = jnp.tanh(inner)
    gelu = 0.5 * gate * (1.0 + bent)
    slope = 0.5 * (1.0 + bent) + 0.5 * gate * (1.0 - bent * bent) * (
        0.7978845608028654 * (1.0 + 3.0 * 0.044715 * gate * gate)
    )
    act = (gelu * upper).astype(BF16)
    dgate = (dact * upper * slope).astype(BF16)
    dupper = (dact * gelu).astype(BF16)
    total[...] += product(act, down)
    for n in range(PAIR):
        part = slice(n * unit, (n + 1) * unit)
        act_all[step * PAIR + n] = act[:, part]
        column = pl.multiple_of(order_ref[step * PAIR + n] * unit, LANES)
        bundle_ref[:, pl.ds(column, unit)] = dgate[:, part]
        bundle_ref[:, pl.ds(pl.multiple_of(hidden + column, LANES), unit)] = dupper[:, part]
    dn3[...] += right_product(dgate, gate_w[...]) + right_product(dupper, up_w[...])

    @pl.when(step == steps - 1)
    def _():
        middle = act_all.shape[0] // 2
        for t in range(middle):
            act_near_ref[:, t * unit : (t + 1) * unit] = act_all[t]
            first = 2 * hidden + t * unit
            bundle_ref[:, first : first + unit] = act_all[middle + t]
        h2 = h2_ref[...]
        out_ref[...] = (h2 + total[...]).astype(BF16)
        high = dn3[...].astype(BF16)
        rest = (dn3[...] - high.astype(F32)).astype(BF16)
        upstream = product(high, turn[...]) + product(rest, turn[...])
        scale = norm_scale(h2)
        dh2 = c3_ref[...].astype(F32) + norm_hidden_grad(h2, scale, gain_ref[2:3], upstream)
        dh2_ref[...] = dh2
        c2_ref[...] = dh2.astype(BF16)
        gain_grad_ref[...] = jnp.sum(upstream * h2 * scale, axis=0, keepdims=True)


def feed(order, h2, c3, gains, source, both, down):
    rows, width = h2.shape
    half, hidden = both[0].shape
    hidden = hidden // 2
    steps = order.shape[0]
    unit = hidden // steps
    whole = lambda shape: pl.BlockSpec(shape, lambda i, o: (0, 0))
    sides = []
    for n in range(PAIR):
        sides += [pl.BlockSpec((half, unit), lambda i, o, n=n: (0, o[i * PAIR + n]))] * 2
        sides += [pl.BlockSpec((half, unit), lambda i, o, n=n: (0, o[i * PAIR + n] + steps))] * 2
    flat = (rows, width)
    shapes = [
        (flat, BF16),
        (flat, F32),
        (flat, BF16),
        ((1, width), F32),
        ((rows, 2 * hidden + hidden // 2 + width // 2), BF16),
        ((rows, hidden // 2), BF16),
        ((rows, width // 2), BF16),
    ]
    return pl.pallas_call(
        feed_kernel,
        out_shape=shaped(shapes, (0,)),
        grid_spec=pltpu.PrefetchScalarGridSpec(
            num_scalar_prefetch=1,
            grid=(steps // PAIR,),
            in_specs=[whole(flat)] * 2
            + [whole(gains.shape), whole((width, 1))]
            + sides
            + [pl.BlockSpec(w.shape, lambda i, o: (0, 0, 0)) for w in down],
            out_specs=[whole(shape) for shape, _ in shapes],
            scratch_shapes=[
                pltpu.VMEM((width, width), BF16),
                pltpu.VMEM(flat, BF16),
                pltpu.VMEM(flat, F32),
                pltpu.VMEM(flat, F32),
                pltpu.VMEM((2 * half, PAIR * unit), BF16),
                pltpu.VMEM((2 * half, PAIR * unit), BF16),
                pltpu.VMEM((PAIR * unit, width), BF16),
                pltpu.VMEM((steps, rows, unit), BF16),
            ],
        ),
        compiler_params=vmem(28),
        cost_estimate=cost(13),
        name="feed",
    )(order, h2, *far(c3), gains, source, *far(*both * (2 * PAIR)), *down)


def feed_weights_kernel(
    own_ref, other_ref, act_ref, n3_ref, c3_ref, c3_other_ref,
    both_keep_ref, both_send_ref, down_keep_ref, down_send_ref,
):
    hidden = both_keep_ref.shape[2]
    units = act_ref.shape[1]
    quarter, third = both_keep_ref.shape[1], down_keep_ref.shape[0]
    edge = 2 * hidden + units
    mine = transposed(n3_ref[...])
    theirs = transposed(other_ref[:, edge:])
    step = hidden // 2
    for first in range(0, 2 * hidden, step):
        grad = product(mine, own_ref[:, first : first + step])
        grad = grad + product(theirs, other_ref[:, first : first + step])
        grad = grad.astype(BF16)
        part, column = first // hidden, first % hidden
        both_keep_ref[part, :, column : column + step] = grad[:quarter]
        both_send_ref[part, :, column : column + step] = grad[quarter:]
    c3, c3_other = c3_ref[...], c3_other_ref[...]
    for k, ref in enumerate((down_keep_ref, down_send_ref)):
        first = k * third
        mine = transposed(act_ref[:, first : first + third])
        theirs = transposed(other_ref[:, 2 * hidden + first : 2 * hidden + first + third])
        ref[...] = (product(mine, c3) + product(theirs, c3_other)).astype(BF16)


def feed_weights(own, other, act, n3, c3, c3_other):
    rows, width = c3.shape
    units = act.shape[1]
    hidden = 2 * units
    pair = ((2, width // 4, hidden), BF16)
    single = ((units // 2, width), BF16)
    return pl.pallas_call(
        feed_weights_kernel,
        out_shape=shaped([pair, pair, single, single]),
        compiler_params=vmem(24),
        cost_estimate=cost(5),
        name="feed_weights",
    )(own, other, act, n3, c3, c3_other)


def head_mask(shape, head):
    return lax.broadcasted_iota(jnp.int32, shape, 1) // HEAD_DIM == head


def pick_head(values, head):
    return jnp.where(head_mask(values.shape, head), values, jnp.zeros_like(values))


def stack_heads(values, heads):
    return jnp.concatenate([pick_head(values, head) for head in heads], axis=0)


def head_groups(keys, heads):
    return [list(range(heads))] if keys <= 2048 else [[head] for head in range(heads)]


def transposed(values):
    return values.astype(F32).T.astype(values.dtype)


LOG2E = 1.4426950408889634
SHRINK = SCALING * LOG2E


def soft_parts(scores, axis=0):
    peak = jnp.max(scores, axis=0, keepdims=True)
    powers = jnp.exp2(scores - peak)
    total = jnp.sum(powers, axis=0, keepdims=True)
    return powers, 1.0 / total, peak + jnp.log2(total)


def causal_scores(keys, queries, count):
    scores = right_product(keys, queries) * SHRINK
    last = scores.shape[0] - count
    corner = scores[last:]
    key_place = lax.broadcasted_iota(jnp.int32, corner.shape, 0)
    query_place = lax.rem(lax.broadcasted_iota(jnp.int32, corner.shape, 1), count)
    corner = jnp.where(key_place <= query_place, corner, MASKED)
    return corner if last == 0 else jnp.concatenate([scores[:last], corner], axis=0)


def cross_scores(keys, queries, bias):
    return right_product(keys, queries) * SHRINK + bias


def score_grads(scores, logs, inner):
    chance = jnp.exp2(scores - logs)
    spread = jnp.sum(chance * inner, axis=0, keepdims=True)
    return chance.astype(BF16), (chance * (inner - spread)).astype(BF16)


def weight_copies(refs, masks, me, columns, target, done, base):
    copies = []
    for ref in refs:
        for block in range(ref.shape[0]):
            number = len(copies)
            spot = 0
            if len(refs) > 1:
                mask = masks[0][number]
                if masks[1][number] != mask:
                    mask = jnp.where(lax.rem(me, 2) == 1, masks[1][number], mask)
                spot = pl.multiple_of(jnp.bitwise_xor(me, mask) * ref.shape[1], 16)
            copies.append(
                pltpu.make_async_copy(
                    ref.at[block, :, columns[0] : columns[1]],
                    target.at[pl.ds(spot, ref.shape[1])],
                    done.at[base + number],
                )
            )
    return copies


def blocks_in(refs):
    return sum(ref.shape[0] for ref in refs)


def self_rows_kernel(heads, masks, counts, spot_ref, *refs):
    seq_count, weights = counts
    x_refs, refs = refs[:3], refs[3:]
    x_list = [x_refs[0], x_refs[1], x_refs[2].at[0], x_refs[2].at[1]]
    w_refs, refs = refs[:weights], refs[weights:]
    o_refs, refs = refs[:seq_count], refs[seq_count:]
    n1_ref, qkv_ref, gain_ref, log_ref, x_all, w_all, o_all, done = refs
    rows, width = x_refs[0].shape
    broad = w_all.shape[1] // 3
    me, seq = spot_ref[0], spot_ref[1]
    copies = weight_copies(w_refs, masks, me, (0, 3 * broad), w_all, done, 0)
    base = len(copies)
    copies += [
        pltpu.make_async_copy(ref, x_all.at[jnp.bitwise_xor(seq, mask)], done.at[base + k])
        for k, (ref, mask) in enumerate(zip(x_list, seq_masks(lax.rem(me, 2))))
    ]
    run(copies)
    slim = heads * HEAD_DIM
    edge = slim // LANES * LANES
    gains = w_all[:, edge : edge + LANES].astype(F32).T[slim - edge : slim - edge + 8]
    gain_ref[...] = gains
    for j in range(seq_count):
        x = x_all[j].astype(F32)
        n1 = (x * norm_scale(x) * gains[0:1]).astype(BF16)
        n1_ref[j * rows : (j + 1) * rows] = n1
        qkv_ref[j * rows : (j + 1) * rows] = product(n1, w_all[...]).astype(BF16)
    values_t = transposed(qkv_ref[:, 2 * broad :])
    for j in range(seq_count):
        first, last = j * rows, (j + 1) * rows
        queries = qkv_ref[first:last, :broad]
        parts = []
        scores = causal_scores(
            qkv_ref[:last, broad : 2 * broad], stack_heads(queries, range(heads)), rows
        )
        powers, inverse, logs = soft_parts(scores)
        powers = powers.astype(BF16)
        for head in range(heads):
            part = slice(head * rows, (head + 1) * rows)
            log_ref[head : head + 1, first:last] = logs[:, part]
            lines = values_t[head * HEAD_DIM : (head + 1) * HEAD_DIM, :last]
            parts.append(product(lines, powers[:, part]) * inverse[:, part])
        o_all[j] = jnp.concatenate(parts, axis=0).T.astype(BF16)
    for k, ref in enumerate(o_refs):
        ref[...] = o_all[lax.rem(seq + k, seq_count)]


def self_rows(x_pieces, weights, spot, heads, broad, masks):
    count = lax.axis_size("seq")
    rows, width = x_pieces[0].shape
    length, slim = rows * count, heads * HEAD_DIM
    whole = lambda shape: pl.BlockSpec(shape, lambda i, spot: (0, 0))
    shapes = [((rows, slim), BF16)] * count + [
        ((length, width), BF16),
        ((length, 3 * broad), BF16),
        ((8, width), F32),
        ((8, length), F32),
    ]
    outs = pl.pallas_call(
        functools.partial(self_rows_kernel, heads, masks, (count, len(weights))),
        out_shape=shaped(shapes, (count, count + 1, count + 3)),
        grid_spec=pltpu.PrefetchScalarGridSpec(
            num_scalar_prefetch=1,
            grid=(1,),
            in_specs=[HBM] * (3 + len(weights)),
            out_specs=[whole(s) for s, _ in shapes],
            scratch_shapes=[
                pltpu.VMEM((count, rows, width), BF16),
                pltpu.VMEM((width, 3 * broad), BF16),
                pltpu.VMEM((count, rows, slim), BF16),
                pltpu.SemaphoreType.DMA((blocks_in(weights) + count,)),
            ],
        ),
        compiler_params=vmem(14),
        cost_estimate=cost(10),
        name="self_rows",
    )(spot, *x_pieces, *weights)
    return outs[:count], *outs[count:]


def key_values_kernel(masks, number, edge, spot_ref, keys_ref, *refs):
    w_refs, (out_ref, w_all, done) = refs[:number], refs[number:]

    @pl.when(pl.program_id(0) == 0)
    def _():
        columns = (edge, edge + w_all.shape[1])
        run(weight_copies(w_refs, masks, spot_ref[0], columns, w_all, done, 0))

    out_ref[...] = product(keys_ref[...], w_all[...]).astype(BF16)


def key_values(keys, weights, spot, chunk, edge, masks):
    width = keys.shape[1]
    columns = 2 * width
    return pl.pallas_call(
        functools.partial(key_values_kernel, masks, len(weights), edge),
        out_shape=jax.ShapeDtypeStruct((keys.shape[0], columns), BF16),
        grid_spec=pltpu.PrefetchScalarGridSpec(
            num_scalar_prefetch=1,
            grid=(keys.shape[0] // chunk,),
            in_specs=[pl.BlockSpec((chunk, width), lambda i, spot: (i, 0))] + [HBM] * len(weights),
            out_specs=pl.BlockSpec((chunk, columns), lambda i, spot: (i, 0)),
            scratch_shapes=[
                pltpu.VMEM((width, columns), BF16),
                pltpu.SemaphoreType.DMA((blocks_in(weights),)),
            ],
        ),
        compiler_params=vmem(12),
        cost_estimate=cost(4),
        name="key_values",
    )(spot, keys, *weights)


def cross_attend(queries, keys, values, live, log_ref):
    values_t = transposed(values)
    pieces = []
    rows = queries.shape[0]
    for group in head_groups(keys.shape[0], LANES // HEAD_DIM):
        powers, inverse, logs = soft_parts(cross_scores(keys, stack_heads(queries, group), live))
        powers = powers.astype(BF16)
        for n, head in enumerate(group):
            part = slice(n * rows, (n + 1) * rows)
            log_ref[0, head : head + 1] = logs[:, part]
            lines = values_t[head * HEAD_DIM : (head + 1) * HEAD_DIM]
            pieces.append(product(lines, powers[:, part]) * inverse[:, part])
    return jnp.concatenate(pieces, axis=0).T.astype(BF16)


def rows_first_kernel(masks, counts, edge, spot_ref, *refs):
    seq_count, weights = counts
    a_refs, refs = refs[:seq_count], refs[seq_count:]
    w_refs, refs = refs[:weights], refs[weights:]
    x_ref, gain_ref, live_ref, k_ref, v_ref = refs[:5]
    q2_ref, a2_ref, h1_ref, log_ref = refs[5:9]
    a_all, w_o1, w_q2, q_parts, done = refs[9:]
    step = pl.program_id(0)
    me, seq = spot_ref[0], spot_ref[1]
    width = x_ref.shape[1]

    @pl.when(step == 0)
    def _():
        copies = [
            pltpu.make_async_copy(
                ref, a_all.at[lax.rem(seq - k + seq_count, seq_count)], done.at[k]
            )
            for k, ref in enumerate(a_refs)
        ]
        copies += weight_copies(w_refs, masks, me, (edge, edge + width), w_o1, done, seq_count)
        later = weight_copies(
            w_refs, masks, me, (edge + width, edge + 2 * width), w_q2, done, len(copies)
        )
        for copy in copies + later:
            copy.start()
        for copy in copies:
            copy.wait()
        a1 = jnp.concatenate([a_all[j] for j in range(seq_count)], axis=1)
        h1 = x_ref[...].astype(F32) + right_product(a1, w_o1[...])
        h1_ref[...] = h1
        n2 = (h1 * norm_scale(h1) * gain_ref[1:2]).astype(BF16)
        for copy in later:
            copy.wait()
        q2 = product(n2, w_q2[...]).astype(BF16)
        q2_ref[...] = q2
        for i in range(q_parts.shape[0]):
            q_parts[i] = q2[:, i * LANES : (i + 1) * LANES]

    a2_ref[...] = cross_attend(q_parts[step], k_ref[...], v_ref[...], live_ref[...], log_ref)


def rows_second_kernel(masks, weights, edge, spot_ref, *refs):
    w_refs, refs = refs[:weights], refs[weights:]
    h1_ref, early_ref, live_ref, q_ref, k_ref, v_ref, a2_ref, h2_ref, log_ref = refs[:9]
    w_o2, o_parts, done = refs[9:]
    step, parts = pl.program_id(0), o_parts.shape[0]
    width = h1_ref.shape[1]
    columns = (edge + 4 * width, edge + 5 * width)
    copies = weight_copies(w_refs, masks, spot_ref[0], columns, w_o2, done, 0)

    @pl.when(step == 0)
    def _():
        for copy in copies:
            copy.start()

    o_parts[step] = cross_attend(q_ref[...], k_ref[...], v_ref[...], live_ref[...], log_ref)

    @pl.when(step == parts - 1)
    def _():
        for copy in copies:
            copy.wait()
        a2 = jnp.concatenate([early_ref[...]] + [o_parts[i] for i in range(parts)], axis=1)
        a2_ref[...] = a2
        h2_ref[...] = h1_ref[...] + right_product(a2, w_o2[...])


def rows_first(a_pieces, weights, x, gains, live, kv, spot, edge, masks):
    count = len(a_pieces)
    rows, width = x.shape
    keys = kv.shape[0]
    parts = width // LANES
    flat = (rows, width)
    whole = lambda shape: pl.BlockSpec(shape, lambda i, spot: (0, 0))
    _, row, key, value = rows_specs(rows, keys, width, 0)
    log = pl.BlockSpec((1, 8, rows), lambda i, spot: (i, 0, 0))
    shapes = [
        (flat, BF16), ((rows, width // 2), BF16), (flat, F32), ((parts // 2, 8, rows), F32)
    ]
    square = pltpu.VMEM((width, width), BF16)
    return pl.pallas_call(
        functools.partial(rows_first_kernel, masks, (count, len(weights)), edge),
        out_shape=shaped(shapes),
        grid_spec=pltpu.PrefetchScalarGridSpec(
            num_scalar_prefetch=1,
            grid=(parts // 2,),
            in_specs=[HBM] * (count + len(weights))
            + [whole(flat), whole(gains.shape), whole(live.shape), key, value],
            out_specs=[whole(flat), row, whole(flat), log],
            scratch_shapes=[
                pltpu.VMEM((count,) + a_pieces[0].shape, BF16),
                square, square,
                pltpu.VMEM((parts, rows, LANES), BF16),
                pltpu.SemaphoreType.DMA((count + 2 * blocks_in(weights),)),
            ],
        ),
        compiler_params=vmem(max(16, keys * 8 // 1024 + 8)),
        cost_estimate=cost(7),
        name="rows_first",
    )(spot, *a_pieces, *weights, x, gains, live, kv, kv)


def rows_second(weights, h1, early, live, q2, kv, spot, edge, masks):
    rows, width = h1.shape
    keys = kv.shape[0]
    parts = width // LANES // 2
    flat = (rows, width)
    whole = lambda shape: pl.BlockSpec(shape, lambda i, spot: (0, 0))
    _, row, key, value = rows_specs(rows, keys, width, parts)
    log = pl.BlockSpec((1, 8, rows), lambda i, spot: (i, 0, 0))
    return pl.pallas_call(
        functools.partial(rows_second_kernel, masks, len(weights), edge),
        out_shape=shaped([(flat, BF16), (flat, F32), ((parts, 8, rows), F32)]),
        grid_spec=pltpu.PrefetchScalarGridSpec(
            num_scalar_prefetch=1,
            grid=(parts,),
            in_specs=[HBM] * len(weights)
            + [whole(flat), whole(early.shape), whole(live.shape), row, key, value],
            out_specs=[whole(flat), whole(flat), log],
            scratch_shapes=[
                pltpu.VMEM((width, width), BF16),
                pltpu.VMEM((parts, rows, LANES), BF16),
                pltpu.SemaphoreType.DMA((blocks_in(weights),)),
            ],
        ),
        compiler_params=vmem(max(14, keys * 8 // 1024 + 8)),
        cost_estimate=cost(6),
        name="rows_second",
    )(spot, *weights, h1, early, live, q2, kv, kv)


def cross_backward(queries, upstream, live, keys, values, logs):
    keys_t = transposed(keys)
    pieces, dk, dv = [], 0.0, 0.0
    rows = queries.shape[0]
    for group in head_groups(keys.shape[0], LANES // HEAD_DIM):
        own = stack_heads(queries, group)
        up_own = stack_heads(upstream, group)
        inner = right_product(values, up_own)
        log = jnp.concatenate([logs[head : head + 1] for head in group], axis=1)
        chance, grad = score_grads(cross_scores(keys, own, live), log, inner)
        dv = dv + product(chance, up_own)
        dk = dk + product(grad, own)
        for n, head in enumerate(group):
            lines = keys_t[head * HEAD_DIM : (head + 1) * HEAD_DIM]
            pieces.append(product(lines, grad[:, n * rows : (n + 1) * rows]))
    dq = jnp.concatenate(pieces, axis=0).T * SCALING
    return dq.astype(BF16), (dk * SCALING).astype(BF16), dv.astype(BF16)


def rows_early_kernel(masks, weights, edge, spot_ref, *refs):
    w_refs, refs = refs[:weights], refs[weights:]
    c2_ref, live_ref, log_ref, q_ref, k_ref, v_ref, up_ref, dq_ref, dk_ref, dv_ref = refs[:10]
    w_o2, up_parts, done = refs[10:]
    width = c2_ref.shape[1]

    @pl.when(pl.program_id(0) == 0)
    def _():
        columns = (edge + 4 * width, edge + 5 * width)
        run(weight_copies(w_refs, masks, spot_ref[0], columns, w_o2, done, 0))
        up = product(c2_ref[...], w_o2[...]).astype(BF16)
        up_ref[...] = up
        for i in range(up_parts.shape[0]):
            up_parts[i] = up[:, i * LANES : (i + 1) * LANES]

    dq_ref[...], dk_ref[...], dv_ref[...] = cross_backward(
        q_ref[...], up_parts[pl.program_id(0)], live_ref[...], k_ref[...], v_ref[...], log_ref[0]
    )


def rows_late_kernel(masks, counts, edge, spot_ref, *refs):
    seq_count, weights = counts
    w_refs, refs = refs[:weights], refs[weights:]
    up_ref, dq_early_ref, dh2_ref, h1_ref, gain_ref, live_ref, log_ref, q_ref, k_ref, v_ref = refs[:10]
    da_refs, refs = refs[10 : 10 + seq_count], refs[10 + seq_count :]
    dq2_ref, dk_ref, dv_ref, dh1_ref, gain_grad_ref = refs[:5]
    w_o1, w_q2, dq_parts, da_all, done = refs[5:]
    step = pl.program_id(0)
    me, seq = spot_ref[0], spot_ref[1]
    width = dh2_ref.shape[1]
    parts = dq_parts.shape[0]
    copies = weight_copies(
        w_refs, masks, me, (edge + width, edge + 2 * width), w_q2, done, 0
    )
    copies += weight_copies(w_refs, masks, me, (edge, edge + width), w_o1, done, len(copies))

    @pl.when(step == 0)
    def _():
        for copy in copies:
            copy.start()

    dq_parts[step], dk_ref[...], dv_ref[...] = cross_backward(
        q_ref[...], up_ref[...], live_ref[...], k_ref[...], v_ref[...], log_ref[0]
    )

    @pl.when(step == parts - 1)
    def _():
        for copy in copies:
            copy.wait()
        dq2 = jnp.concatenate([dq_early_ref[...]] + [dq_parts[i] for i in range(parts)], axis=1)
        dq2_ref[...] = dq2
        dn2 = right_product(dq2, w_q2[...])
        h1 = h1_ref[...]
        scale = norm_scale(h1)
        dh1 = dh2_ref[...] + norm_hidden_grad(h1, scale, gain_ref[1:2], dn2)
        dh1_ref[...] = dh1
        gain_grad_ref[...] = jnp.sum(dn2 * h1 * scale, axis=0, keepdims=True)
        c1 = dh1.astype(BF16)
        up = product(c1, w_o1[...])
        slim = da_all.shape[2]
        for j in range(seq_count):
            da_all[j] = up[:, j * slim : (j + 1) * slim].astype(BF16)
        for k, ref in enumerate(da_refs):
            ref[...] = da_all[lax.rem(seq + k, seq_count)]


def rows_specs(rows, keys, width, start):
    parts = width // LANES
    row = pl.BlockSpec((rows, LANES), lambda i, spot: (0, i + start))
    key = pl.BlockSpec((keys, LANES), lambda i, spot: (0, i + start))
    value = pl.BlockSpec((keys, LANES), lambda i, spot: (0, i + start + parts))
    log = pl.BlockSpec((1, 8, rows), lambda i, spot: (i, 0, 0))
    return log, row, key, value


def rows_early(weights, c2, live, logs, q2, kv, spot, edge, masks):
    rows, width = c2.shape
    keys = kv.shape[0]
    parts = width // LANES // 2
    whole = lambda shape: pl.BlockSpec(shape, lambda i, spot: (0, 0))
    log, row, key, value = rows_specs(rows, keys, width, 0)
    half = width // 2
    shapes = [((rows, width), BF16), ((rows, half), BF16)] + [((keys, half), BF16)] * 2
    return pl.pallas_call(
        functools.partial(rows_early_kernel, masks, len(weights), edge),
        out_shape=shaped(shapes, (2, 3)),
        grid_spec=pltpu.PrefetchScalarGridSpec(
            num_scalar_prefetch=1,
            grid=(parts,),
            in_specs=[HBM] * len(weights)
            + [whole((rows, width)), whole(live.shape), log, row, key, value],
            out_specs=[whole((rows, width)), row, key, key],
            scratch_shapes=[
                pltpu.VMEM((width, width), BF16),
                pltpu.VMEM((2 * parts, rows, LANES), BF16),
                pltpu.SemaphoreType.DMA((blocks_in(weights),)),
            ],
        ),
        compiler_params=vmem(max(12, keys * 8 // 1024 + 12)),
        cost_estimate=cost(10),
        name="rows_early",
    )(spot, *weights, c2, live, logs, q2, kv, kv)


def rows_late(weights, up, dq_early, dh2, h1, gains, live, logs, q2, kv, spot, edge, masks):
    count = lax.axis_size("seq")
    rows, width = dh2.shape
    keys = kv.shape[0]
    parts = width // LANES // 2
    slim = width // count
    flat = (rows, width)
    half = width // 2
    whole = lambda shape: pl.BlockSpec(shape, lambda i, spot: (0, 0))
    log, row, key, value = rows_specs(rows, keys, width, parts)
    key_out = pl.BlockSpec((keys, LANES), lambda i, spot: (0, i))
    shapes = [((rows, slim), BF16)] * count + [
        (flat, BF16), ((keys, half), BF16), ((keys, half), BF16),
        (flat, F32), ((1, width), F32),
    ]
    square = pltpu.VMEM((width, width), BF16)
    outs = pl.pallas_call(
        functools.partial(rows_late_kernel, masks, (count, len(weights)), edge),
        out_shape=shaped(shapes, range(count, count + 6)),
        grid_spec=pltpu.PrefetchScalarGridSpec(
            num_scalar_prefetch=1,
            grid=(parts,),
            in_specs=[HBM] * len(weights)
            + [row, whole((rows, half)), whole(flat), whole(flat)]
            + [whole(gains.shape), whole(live.shape), log, row, key, value],
            out_specs=[whole((rows, slim))] * count
            + [whole(flat), key_out, key_out, whole(flat), whole((1, width))],
            scratch_shapes=[
                square, square,
                pltpu.VMEM((parts, rows, LANES), BF16),
                pltpu.VMEM((count, rows, slim), BF16),
                pltpu.SemaphoreType.DMA((2 * blocks_in(weights),)),
            ],
        ),
        compiler_params=vmem(max(18, keys * 8 // 1024 + 12)),
        cost_estimate=cost(11),
        name="rows_late",
    )(spot, *weights, up, dq_early, dh2, h1, gains, live, logs, q2, kv, kv)
    return outs[:count], *outs[count:]


def turn_of(source_ref, width):
    columns = lax.broadcasted_iota(jnp.int32, (width, width), 1)
    return (columns == source_ref[...]).astype(F32).astype(BF16)


def cross_weights_kernel(masks, number, edge, spot_ref, *refs):
    w_refs, refs = refs[:number], refs[number:]
    source_ref, h1_ref, gain_ref, dq2_ref, c2_ref, a2_ref, keys_ref = refs[:7]
    parts, refs = refs[7:11], refs[11:]
    near_ref, far_ref, dmem_ref = refs[:3]
    w_all, turn, dk_sum, dv_sum, done = refs[3:]
    dk = jnp.concatenate([parts[0][...], parts[1][...]], axis=1)
    dv = jnp.concatenate([parts[2][...], parts[3][...]], axis=1)
    step, steps = pl.program_id(0), pl.num_programs(0)
    width = dq2_ref.shape[1]
    half = width // 2
    columns = (edge + 2 * width, edge + 4 * width)
    copies = weight_copies(w_refs, masks, spot_ref[0], columns, w_all, done, 0)

    def put(column, values):
        values = values.astype(BF16)
        near_ref[:, column : column + width] = values[:half]
        far_ref[:, column : column + width] = values[half:]

    @pl.when(step == 0)
    def _():
        for copy in copies:
            copy.start()
        turn[...] = turn_of(source_ref, width)
        h1 = h1_ref[...]
        n2 = (h1 * norm_scale(h1) * gain_ref[1:2]).astype(BF16)
        n2_t = right_product(turn[...], n2).astype(BF16)
        put(0, product(n2_t, dq2_ref[...]))
        c2_t = right_product(turn[...], c2_ref[...]).astype(BF16)
        put(3 * width, product(c2_t, a2_ref[...]))
        dk_sum[...] = jnp.zeros_like(dk_sum)
        dv_sum[...] = jnp.zeros_like(dv_sum)

    keys_t = right_product(turn[...], keys_ref[...]).astype(BF16)
    dk_sum[...] += product(keys_t, dk)
    dv_sum[...] += product(keys_t, dv)

    @pl.when(step == 0)
    def _():
        for copy in copies:
            copy.wait()

    dmem_ref[...] = (
        right_product(dk, w_all[:, :width]) + right_product(dv, w_all[:, width:])
    ).astype(BF16)

    @pl.when(step == steps - 1)
    def _():
        put(width, dk_sum[...])
        put(2 * width, dv_sum[...])


def cross_weights(weights, source, h1, gains, dq2, c2, a2, keys, grads, spot, chunk, edge, masks):
    rows, width = h1.shape
    whole = lambda shape: pl.BlockSpec(shape, lambda i, spot: (0, 0))
    part = pl.BlockSpec((chunk, width), lambda i, spot: (i, 0))
    half = ((width // 2, 4 * width), BF16)
    return pl.pallas_call(
        functools.partial(cross_weights_kernel, masks, len(weights), edge),
        out_shape=shaped([half, half, (keys.shape, BF16)], (0,)),
        grid_spec=pltpu.PrefetchScalarGridSpec(
            num_scalar_prefetch=1,
            grid=(keys.shape[0] // chunk,),
            in_specs=[HBM] * len(weights)
            + [whole(source.shape), whole((rows, width)), whole(gains.shape)]
            + [whole((rows, width))] * 3
            + [part]
            + [pl.BlockSpec((chunk, width // 2), lambda i, spot: (i, 0))] * 4,
            out_specs=[whole(half[0]), whole(half[0]), part],
            scratch_shapes=[
                pltpu.VMEM((width, 2 * width), BF16),
                pltpu.VMEM((width, width), BF16),
                pltpu.VMEM((width, width), F32),
                pltpu.VMEM((width, width), F32),
                pltpu.SemaphoreType.DMA((blocks_in(weights),)),
            ],
        ),
        compiler_params=vmem(24),
        cost_estimate=cost(10),
        name="cross_weights",
    )(spot, *weights, source, h1, gains, dq2, c2, a2, keys, *grads)


def self_backward_kernel(heads, masks, counts, spot_ref, *refs):
    seq_count, weights = counts
    up_refs, refs = refs[:seq_count], refs[seq_count:]
    x_refs, refs = refs[:3], refs[3:]
    x_list = [x_refs[0], x_refs[1], x_refs[2].at[0], x_refs[2].at[1]]
    w_refs, refs = refs[:weights], refs[weights:]
    qkv_ref, log_ref, refs = refs[0], refs[1], refs[2:]
    dn_refs, refs = refs[:2], refs[2:]
    steps = seq_masks(lax.rem(spot_ref[0], 2))
    dqkv_ref, gain_grad_ref = refs[:2]
    up_all, x_all, w_all, dn_all, dk_sum, dv_sum, done = refs[2:]
    rows = up_refs[0].shape[0]
    broad = w_all.shape[1] // 3
    slim = heads * HEAD_DIM
    me, seq = spot_ref[0], spot_ref[1]
    spots = [lax.rem(seq - k + seq_count, seq_count) for k in range(seq_count)]
    early = [
        pltpu.make_async_copy(ref, up_all.at[spots[k]], done.at[k])
        for k, ref in enumerate(up_refs)
    ]
    late = [
        pltpu.make_async_copy(ref, x_all.at[jnp.bitwise_xor(seq, mask)], done.at[seq_count + k])
        for k, (ref, mask) in enumerate(zip(x_list, steps))
    ]
    late += weight_copies(w_refs, masks, me, (0, 3 * broad), w_all, done, 2 * seq_count)
    for copy in early + late:
        copy.start()
    keys_t = transposed(qkv_ref[:, broad : 2 * broad])
    dk_sum[...] = jnp.zeros_like(dk_sum)
    dv_sum[...] = jnp.zeros_like(dv_sum)
    blank = jnp.zeros((rows, broad - slim), BF16)
    for copy in early:
        copy.wait()
    for j in range(seq_count):
        first, last = j * rows, (j + 1) * rows
        queries = qkv_ref[first:last, :broad]
        upstream = jnp.concatenate([up_all[j], blank], axis=1)
        parts = []
        own = stack_heads(queries, range(heads))
        up_own = stack_heads(upstream, range(heads))
        logs = jnp.concatenate(
            [log_ref[head : head + 1, first:last] for head in range(heads)], axis=1
        )
        inner = right_product(qkv_ref[:last, 2 * broad :], up_own)
        scores = causal_scores(qkv_ref[:last, broad : 2 * broad], own, rows)
        chance, grad = score_grads(scores, logs, inner)
        dv_sum[:last] += product(chance, up_own)
        dk_sum[:last] += product(grad, own)
        for head in range(heads):
            lines = keys_t[head * HEAD_DIM : (head + 1) * HEAD_DIM, :last]
            parts.append(product(lines, grad[:, head * rows : (head + 1) * rows]))
        rest = jnp.zeros((broad - slim, rows), F32)
        dq = jnp.concatenate(parts + [rest], axis=0).T * SCALING
        dqkv_ref[first:last, :broad] = dq.astype(BF16)
    dqkv_ref[:, broad : 2 * broad] = (dk_sum[...] * SCALING).astype(BF16)
    dqkv_ref[:, 2 * broad :] = dv_sum[...].astype(BF16)
    for copy in late:
        copy.wait()
    total = 0.0
    for j in range(seq_count):
        dn1 = right_product(dqkv_ref[j * rows : (j + 1) * rows], w_all[...])
        x = x_all[j].astype(F32)
        total = total + jnp.sum(dn1 * x * norm_scale(x), axis=0, keepdims=True)
        dn_all[j] = dn1.astype(BF16)
    gain_grad_ref[...] = total
    for k, mask in enumerate(steps):
        dn_refs[k // 2][k % 2] = dn_all[jnp.bitwise_xor(seq, mask)]


def self_backward(up_pieces, x_pieces, weights, qkv, logs, spot, heads, masks):
    count = len(up_pieces)
    rows, width = x_pieces[0].shape
    slim = up_pieces[0].shape[1]
    length, broad = qkv.shape[0], qkv.shape[1] // 3
    whole = lambda shape: pl.BlockSpec(shape, lambda i, spot: (0, 0))
    shapes = [((2, rows, width), BF16)] * 2 + [(qkv.shape, BF16), ((1, width), F32)]
    outs = pl.pallas_call(
        functools.partial(self_backward_kernel, heads, masks, (count, len(weights))),
        out_shape=shaped(shapes),
        grid_spec=pltpu.PrefetchScalarGridSpec(
            num_scalar_prefetch=1,
            grid=(1,),
            in_specs=[HBM] * (count + 3 + len(weights)) + [whole(qkv.shape), whole(logs.shape)],
            out_specs=[
                pl.BlockSpec(s, lambda i, spot, n=len(s): (0,) * n) for s, _ in shapes
            ],
            scratch_shapes=[
                pltpu.VMEM((count, rows, slim), BF16),
                pltpu.VMEM((count, rows, width), BF16),
                pltpu.VMEM((width, 3 * broad), BF16),
                pltpu.VMEM((count, rows, width), BF16),
                pltpu.VMEM((length, broad), F32),
                pltpu.VMEM((length, broad), F32),
                pltpu.SemaphoreType.DMA((2 * count + blocks_in(weights),)),
            ],
        ),
        compiler_params=vmem(18),
        cost_estimate=cost(13),
        name="self_backward",
    )(spot, *up_pieces, *x_pieces, *weights, qkv, logs)
    return outs


def self_weights_kernel(
    spot_ref, source_ref, n1_ref, dqkv_ref, dh1_ref, gain_ref, *refs
):
    a_refs, (near_ref, far_ref, a_all) = refs[:-3], refs[-3:]
    width = n1_ref.shape[1]
    half = width // 2
    count = len(a_refs)
    turn = turn_of(source_ref, width)
    column = 0

    def put(values):
        nonlocal column
        values = values.astype(BF16)
        near_ref[:, column : column + values.shape[1]] = values[:half]
        far_ref[:, column : column + values.shape[1]] = values[half:]
        column += values.shape[1]

    for k, ref in enumerate(a_refs):
        a_all[lax.rem(spot_ref[1] - k + count, count)] = ref[...]
    a1 = jnp.concatenate([a_all[j] for j in range(count)], axis=1)
    c1_t = right_product(turn, dh1_ref[...].astype(BF16)).astype(BF16)
    put(product(c1_t, a1))
    put(right_product(turn, gain_ref[...].astype(BF16)))
    n1_t = right_product(turn, n1_ref[...]).astype(BF16)
    put(product(n1_t, dqkv_ref[...]))


def self_weights(source, n1, dqkv, dh1, gain_grads, a_pieces, spot):
    width = n1.shape[1]
    half = ((width // 2, width + LANES + dqkv.shape[1]), BF16)
    whole = lambda shape: pl.BlockSpec(shape, lambda i, spot: (0, 0))
    ins = [source, n1, dqkv, dh1, gain_grads, *a_pieces]
    return pl.pallas_call(
        self_weights_kernel,
        out_shape=shaped([half, half]),
        grid_spec=pltpu.PrefetchScalarGridSpec(
            num_scalar_prefetch=1,
            grid=(1,),
            in_specs=[whole(a.shape) for a in ins],
            out_specs=[whole(half[0])] * 2,
            scratch_shapes=[pltpu.VMEM((len(a_pieces),) + a_pieces[0].shape, BF16)],
        ),
        compiler_params=vmem(16),
        cost_estimate=cost(6),
        name="self_weights",
    )(spot, *ins)


def last_rows_kernel(keep_ref, one_ref, two_ref, x_ref, dh1_ref, gain_ref, out_ref):
    dn1 = keep_ref[0].astype(F32) + one_ref[0].astype(F32) + two_ref[...].astype(F32)
    x = x_ref[...].astype(F32)
    out_ref[...] = (
        dh1_ref[...] + norm_hidden_grad(x, norm_scale(x), gain_ref[0:1], dn1)
    ).astype(BF16)


def last_rows(keep, one, two, x, dh1, gains):
    return pl.pallas_call(
        last_rows_kernel,
        out_shape=jax.ShapeDtypeStruct(x.shape, BF16),
        compiler_params=vmem(8),
        cost_estimate=cost(2),
        name="last_rows",
    )(keep, one, two, x, dh1, gains)


def finish_kernel(slim, broad, spot_ref, *refs):
    sources, outs, hold = refs[:12], refs[12:-1], refs[-1]

    def total(refs, columns):
        keep, one, two = refs
        return (
            keep[0, :, columns[0] : columns[1]].astype(F32)
            + one[0, :, columns[0] : columns[1]].astype(F32)
            + two[0, :, columns[0] : columns[1]].astype(F32)
        )

    pair, down, cross, rest = sources[0:3], sources[3:6], sources[6:9], sources[9:12]
    hidden, width = outs[0].shape[1], outs[2].shape[1]
    outs[0][...] = total(pair, (0, hidden))
    outs[1][...] = total(pair, (hidden, 2 * hidden))
    outs[2][...] = total(down, (0, width))
    for i in range(4):
        outs[3 + i][...] = total(cross, (i * width, (i + 1) * width))
    outs[7][...] = total(rest, (0, width))
    edge = width
    outs[-1][...] = total(rest, (edge, edge + LANES))
    edge = edge + LANES
    far_edge = edge + 3 * broad
    keep, one, two = rest
    steps = [jnp.bitwise_xor(spot_ref[1], m) for m in seq_masks(lax.rem(spot_ref[0], 2))]
    hold[steps[0]] = keep[0, :, edge:far_edge].astype(F32)
    hold[steps[1]] = two[0, :, edge:far_edge].astype(F32)
    hold[steps[2]] = one[0, :, edge:far_edge].astype(F32)
    hold[steps[3]] = two[0, :, far_edge : far_edge + 3 * broad].astype(F32)
    for i in range(3):
        outs[8 + i][...] = jnp.concatenate(
            [hold[j][:, i * broad : i * broad + slim] for j in range(hold.shape[0])], axis=1
        )


def finish(pair, down, cross, rest, spot, hidden, slim, broad):
    share, feed_share, width = pair[0].shape[1], down[0].shape[1], down[0].shape[2]
    count = lax.axis_size("seq")
    shapes = (
        [(share, hidden)] * 2 + [(feed_share, width)] + [(share, width)] * 8 + [(share, LANES)]
    )
    whole = lambda shape: pl.BlockSpec(shape, lambda i, spot: (0,) * len(shape))
    flat = [*pair, *down, *cross, *rest]
    return pl.pallas_call(
        functools.partial(finish_kernel, slim, broad),
        out_shape=shaped([(shape, F32) for shape in shapes]),
        grid_spec=pltpu.PrefetchScalarGridSpec(
            num_scalar_prefetch=1,
            grid=(1,),
            in_specs=[whole(a.shape) for a in flat],
            out_specs=[whole(shape) for shape in shapes],
            scratch_shapes=[pltpu.VMEM((count, share, 3 * broad), F32)],
        ),
        compiler_params=vmem(12),
        cost_estimate=cost(3),
        name="finish",
    )(spot, *flat)


def local(
    hidden_in,
    memory,
    cotangent,
    norm_self,
    query_self,
    key_self,
    value_self,
    output_self,
    norm_cross,
    query_cross,
    key_cross,
    value_cross,
    output_cross,
    norm_feed,
    gate_weight,
    up_weight,
    down_weight,
    block_counts,
    memory_tail,
    row_example,
):
    mem_count, seq_count = lax.axis_size("mem"), lax.axis_size("seq")
    mem_place, seq_place = lax.axis_index("mem"), lax.axis_index("seq")
    rows, width = hidden_in.shape[1], hidden_in.shape[2]
    inner = HEADS * HEAD_DIM
    near = HEADS // seq_count
    slim = near * HEAD_DIM
    broad = -(-(slim + 8) // LANES) * LANES
    share = norm_self.shape[0]
    hidden_width = gate_weight.shape[1]
    spot = jnp.stack([mem_place, seq_place]).astype(jnp.int32)
    scalars = jnp.concatenate([block_counts, memory_tail, row_example])
    masks = slot_masks(mem_count)
    mask_array = mem_masks()
    block = width // mem_count
    column = jnp.arange(width, dtype=jnp.int32)
    source = (block * (mem_place ^ jnp.repeat(mask_array, block)) + column % block).reshape(width, 1)
    gain_stack = jnp.stack([norm_self, norm_cross, norm_feed], axis=0)
    x_own = hidden_in[0]
    edge = 3 * broad
    turns = mem_count.bit_length() - 2
    flat = lambda stacked: stacked.reshape((1, -1) + stacked.shape[2:])

    with jax.named_scope("gather"):
        own, two, one, second, blocks, live = prepare(
            (query_self, key_self, value_self, output_self, query_cross)
            + (key_cross, value_cross, output_cross, gate_weight, up_weight),
            gain_stack, memory, scalars, spot, slim, broad,
        )
        live = live.reshape(-1, 1)
        stay, go = part_blocks(blocks, 0)
        two, arrived = swap_seq(two, 0), swap_mem(go, 0)
        c3 = cotangent[0]
        c3_other = swap_mem(c3, turns)
        blocks, x_in, down_in = join_blocks(stay, arrived), x_own, down_weight
        three = swap_seq(jnp.stack([one, two[:, edge:]]), 1)
        second_a = swap_seq(second, 0)
        for turn in range(1, turns):
            stay, go = part_blocks(blocks, turn)
            blocks = join_blocks(stay, swap_mem(go, turn))
        three, blocks, second_a, second, x_in, down_in, source = settle(
            three, blocks, second_a, second, x_in, down_in, source
        )
        plain = [(0, 0, 0, edge), (1, 0, edge, 5 * width)]
        skipping = [(0, 0, 0, edge), (1, 0, 2 * edge, 5 * width)]
        heads, outer = place(
            [own[None], two[None], three],
            seq_places(),
            [edge, 5 * width],
            [plain, skipping, plain],
        )
        heads, outer = [flat(heads)], [flat(outer)]
        heads.append(swap_mem(heads[0], 0))
        outer.append(swap_mem(outer[0], 0))
        stay, go = part_blocks(blocks, turns)
        keys_in = join_blocks(stay, swap_mem(go, turns)).reshape(-1, width)
        second_b = swap_seq(jnp.stack([second, second_a]), 1)
        heads, outer, keys_in, second_a, second_b, second, x_in, down_in = settle(
            heads, outer, keys_in, second_a, second_b, second, x_in, down_in
        )
        x_a = swap_seq(x_in, 0)
        for turn in range(1, turns):
            heads.append(swap_mem(join(heads), turn))
            outer.append(swap_mem(join(outer), turn))
        both = [flat(stack_seq([second[None], second_a[None], second_b]))]
        x_a, x_in, both, down_in = settle(x_a, x_in, both, down_in)
        x_b = swap_seq(jnp.stack([x_in, x_a]), 1)
        both.append(swap_mem(both[0], 0))
        down_a = swap_seq(down_in, 0)
        heads, outer, both, x_b, x_a, x_in, down_a, down_in = settle(
            heads, outer, both, x_b, x_a, x_in, down_a, down_in
        )
        heads, outer = join(heads), join(outer)
        heads = [heads, swap_mem(heads, turns)]
        outer = [outer, swap_mem(outer, turns)]
        for turn in range(1, turns):
            both.append(swap_mem(join(both), turn))
        down_b = swap_seq(jnp.stack([down_in, down_a]), 1)
        heads, x_in, x_a, x_b = settle(heads, x_in, x_a, x_b)
        packed_heads = spread_weight(heads)

    key_chunk = width

    with jax.named_scope("forward"):
        x_pieces = [x_in, x_a, x_b]
        o_pieces, n1, qkv, gains, self_logs = self_rows(
            x_pieces, packed_heads, spot, near, broad, masks
        )
        o_pieces, gains, outer, down_a, down_b, down_in = settle(
            o_pieces, gains, outer, down_a, down_b, down_in
        )
        packed = spread_weight(outer)
        downs = [flat(stack_seq([down_in[None], down_a[None], down_b]))]
        a_pieces = send_seq(o_pieces)
        kv2 = key_values(keys_in, packed, spot, key_chunk, 2 * width, masks)
        downs.append(swap_mem(downs[0], 0))
        a_pieces, kv2, downs, keys_in, both = settle(a_pieces, kv2, downs, keys_in, both)
        q2, a2_early, h1, logs_first = rows_first(
            a_pieces, packed, x_own, gains, live, kv2, spot, 0, masks
        )
        both = join(both)
        both_other = swap_mem(both, turns)
        for turn in range(1, turns):
            downs.append(swap_mem(join(downs), turn))
        others = [swap_mem(downs[0], turns), swap_mem(downs[1], turns)]
        a2_early, h1, q2, both, both_other, others = settle(
            a2_early, h1, q2, both, both_other, others
        )
        a2, h2, logs_second = rows_second(
            packed, h1, a2_early, live, q2, kv2, spot, 0, masks
        )
        h2, both_other, both, downs, others = settle(h2, both_other, both, downs, others)
        others += [swap_mem(piece, turns) for piece in downs[2:]]
        both = [w.reshape(-1, 2 * hidden_width) for w in (both, both_other)]
        unit = hidden_width // mem_count
        narrow = unit % LANES != 0
        if narrow:
            unit = 2 * LANES
            downs = [stack_mem(downs + others).reshape(-1, unit, width)]
            feed_order = jnp.arange(hidden_width // unit, dtype=jnp.int32)
        else:
            feed_order = mem_place ^ mask_array
            downs = downs + others
        layer_out, dh2, c2, gain_feed_terms, bundle, act_near, n3_near = feed(
            feed_order, h2, c3, gains, source, both, downs
        )

    with jax.named_scope("backward"):
        bundle_other = swap_mem(bundle, turns)
        up, dq_early, dk_early, dv_early = rows_early(
            packed, c2, live, logs_first, q2, kv2, spot, 0, masks
        )
        bundle_other, up, dq_early = settle(bundle_other, up, dq_early)
        if narrow:
            acts = jnp.concatenate([act_near, bundle[:, 2 * hidden_width : -(width // 2)]], axis=1)
            g_down = left_product(acts, c3).astype(BF16).reshape(mem_count, -1, width)
            g_down = place([g_down], jnp.argsort(mem_place ^ mask_array)).reshape(2, -1, width)
            normed = jnp.concatenate([n3_near, bundle[:, -(width // 2) :]], axis=1)
            g_both = jnp.stack(
                [
                    left_product(normed, bundle[:, k * hidden_width : (k + 1) * hidden_width])
                    for k in range(2)
                ]
            ).astype(BF16)
            feeding = Scatter(g_both[:, : width // 2], g_both[:, width // 2 :])
            downing = Scatter(g_down[0], g_down[1])
            for s in (feeding, downing):
                s.move()
            advance([feeding, downing], spot)
        else:
            g_feed = feed_weights(bundle, bundle_other, act_near, n3_near, c3, c3_other)
            feeding, downing = Scatter(*g_feed[0:2], 1), Scatter(*g_feed[2:4], 1)
        feeding.sent, up = settle(feeding.sent, up)
        feeding.move()
        da_pieces, dq2, dk_late, dv_late, dh1, gain_cross_terms = rows_late(
            packed, up, dq_early, dh2, h1, gains, live, logs_second, q2, kv2, spot, 0, masks
        )
        da_pieces, dq2 = settle(da_pieces, dq2)
        da_pieces = send_seq(da_pieces)
        *g_cross, dmem = cross_weights(
            packed, source, h1, gains, dq2, c2, a2, keys_in,
            [dk_early, dk_late, dv_early, dv_late], spot, key_chunk, 0, masks,
        )
        crossing = Scatter(*g_cross)
        advance([feeding], spot)
        da_pieces, crossing.sent, feeding.sent, downing.sent, dmem = settle(
            da_pieces, crossing.sent, feeding.sent, downing.sent, dmem
        )
        crossing.move()
        feeding.move()
        keep_dn, send_dn, dqkv, gain_self_terms = self_backward(
            da_pieces, x_pieces, packed_heads, qkv, self_logs, spot, near, masks
        )
        dmem = dmem.reshape(mem_count, -1, width)
        stay, go = part_blocks(dmem, turns)
        dmem = join_blocks(stay, swap_mem(go, turns))
        crossing.terms, feeding.terms, downing.sent, keep_dn, send_dn, dqkv, dmem = settle(
            crossing.terms, feeding.terms, downing.sent, keep_dn, send_dn, dqkv, dmem
        )
        one_dn = swap_seq(send_dn, 1)
        downing.move()
        stay, go = part_blocks(dmem, 0)
        dmem = join_blocks(stay, swap_mem(go, 0))
        while feeding.left > 0:
            advance([feeding], spot)
            feeding.move()
        ends = [advance([feeding], spot), None, None, None]
        advance([crossing], spot)
        gain_grads = jnp.concatenate(
            [gain_self_terms, gain_cross_terms, gain_feed_terms, jnp.zeros((LANES - 3, width), F32)]
        )
        g_self = self_weights(source, n1, dqkv, dh1, gain_grads, a_pieces, spot)
        selfing = Scatter(*g_self)
        crossing.move()
        one_dn, keep_dn, downing.terms, dmem, ends[0], selfing.sent = settle(
            one_dn, keep_dn, downing.terms, dmem, ends[0], selfing.sent
        )
        two_dn = swap_seq(onward(keep_dn, one_dn)[0], 0)
        one_both = swap_seq(ends[0][1], 1)
        selfing.move()
        for turn in range(1, turns):
            stay, go = part_blocks(dmem, turn)
            dmem = join_blocks(stay, swap_mem(go, turn))
        while downing.left > 0:
            advance([downing], spot)
            downing.move()
        ends[1] = advance([downing], spot)
        while crossing.left > 0:
            advance([crossing], spot)
            crossing.move()
        while selfing.left > 0:
            advance([selfing], spot)
            selfing.move()
        two_both = swap_seq(onward(ends[0][0], one_both), 0)
        mem_keep, mem_send = pick_slots(dmem, memory.shape[0], scalars, spot)
        mem_one = swap_seq(mem_send, 1)
        one_down = swap_seq(ends[1][1], 1)
        ends[2] = advance([crossing], spot)
        one_cross = swap_seq(ends[2][1], 1)
        mem_one = after(mem_one, ends[2][1])
        mem_two = swap_seq(onward(mem_keep, mem_one), 0)
        ends[3] = advance([selfing], spot)
        one_self = swap_seq(ends[3][1], 1)
        one_down = after(one_down, ends[2][1])
        two_down = swap_seq(onward(ends[1][0], one_down), 0)
        two_cross = swap_seq(onward(ends[2][0], one_cross), 0)
        two_self = swap_seq(onward(ends[3][0], one_self, width + LANES), 0)
        hidden_grad = last_rows(keep_dn, one_dn, after(two_dn, ends[3][1]), x_own, dh1, gains)
        per = mem_two.shape[0]
        memory_grad = total_of([mem_keep[:per], mem_one[:per], mem_two]).astype(BF16)
        *finals, gain_finals = finish(
            (ends[0][0], one_both, two_both),
            (ends[1][0], one_down, two_down),
            (ends[2][0], one_cross, two_cross),
            (ends[3][0], one_self, two_self),
            spot, hidden_width, slim, broad,
        )
    g_gate, g_up, g_down, g_q2, g_k2, g_v2, g_o2, g_o1, g_q1, g_k1, g_v1 = finals
    return (
        layer_out[None],
        hidden_grad[None],
        memory_grad,
        gain_finals[:, 0],
        g_q1,
        g_k1,
        g_v1,
        g_o1,
        gain_finals[:, 1],
        g_q2,
        g_k2,
        g_v2,
        g_o2,
        gain_finals[:, 2],
        g_gate,
        g_up,
        g_down,
    )


def solution(mesh):
    every = P(("mem", "seq"), None)
    gain = P(("mem", "seq"))
    in_specs = (
        (P("mem", "seq", None), P(None, "mem", None), P("mem", "seq", None), gain)
        + (every,) * 4
        + (gain,)
        + (every,) * 4
        + (gain,)
        + (every,) * 3
        + (P(),) * 3
    )
    out_specs = (
        (P("mem", "seq", None), P("mem", "seq", None), P("seq", "mem", None), gain)
        + (every,) * 4
        + (gain,)
        + (every,) * 4
        + (gain,)
        + (every,) * 3
    )
    return jax.shard_map(local, mesh=mesh, in_specs=in_specs, out_specs=out_specs, check_vma=False)
```

```python
import functools

import jax
import jax.numpy as jnp
from jax import lax
from jax.experimental import pallas as pl
from jax.experimental.pallas import tpu as pltpu
from jax.sharding import PartitionSpec as P

HEADS = 12
HEAD_DIM = 64
SCALING = HEAD_DIM ** (-0.5)
LANES = 128
MASKED = -1e30
F32 = jnp.float32
BF16 = jnp.bfloat16


def product(left, right):
    return jnp.dot(left, right, preferred_element_type=F32)


def left_product(left, right):
    return lax.dot_general(left, right, (((0,), (0,)), ((), ())), preferred_element_type=F32)


def right_product(left, right):
    return lax.dot_general(left, right, (((1,), (1,)), ((), ())), preferred_element_type=F32)


def gelu_tanh(values):
    return (
        0.5
        * values
        * (1.0 + jnp.tanh(0.7978845608028654 * (values + 0.044715 * values * values * values)))
    )


def gated_unit(gate, upper):
    return gelu_tanh(gate) * upper


def norm_scale(hidden):
    return lax.rsqrt(jnp.mean(hidden * hidden, axis=-1, keepdims=True) + 1e-06)


def norm_hidden_grad(hidden, scale, gain, upstream):
    lifted = upstream * gain
    return scale * lifted - hidden * (scale * scale * scale) * jnp.mean(
        lifted * hidden, axis=-1, keepdims=True
    )


def shift(values, axis, step):
    size = lax.axis_size(axis)
    return lax.ppermute(values, axis, [(i, (i + step) % size) for i in range(size)])


def swap(values, axis, mask):
    size = lax.axis_size(axis)
    return lax.ppermute(values, axis, [(i, i ^ mask) for i in range(size)])


def place_kernel(counts, maps, places, *refs):
    sources = refs[: len(counts)]
    targets, done = refs[len(counts) : -1], refs[-1]
    copies = []
    number = 0
    for source, count, moves in zip(sources, counts, maps):
        for block in range(count):
            for goal, to, start, width in moves:
                part, target = source.at[block], targets[goal].at[places[number]]
                if len(moves) > 1 or width != source.shape[2]:
                    part = source.at[block, :, start : start + width]
                    target = targets[goal].at[places[number], :, to : to + width]
                copies.append(pltpu.make_async_copy(part, target, done.at[len(copies)]))
            number += 1
    for copy in copies:
        copy.start()
    for copy in copies:
        copy.wait()


def place(pieces, places, widths=None, maps=None):
    counts = [piece.shape[0] for piece in pieces]
    total = sum(counts)
    _, height, width = pieces[0].shape
    widths = widths or [width]
    if maps is None:
        plain = [(i, 0, sum(widths[:i]), w) for i, w in enumerate(widths)]
        maps = [plain] * len(pieces)
    copies = sum(count * len(moves) for count, moves in zip(counts, maps))
    outs = [((total, height, w), pieces[0].dtype) for w in widths]
    size = total * height * sum(widths) * 2
    result = pl.pallas_call(
        functools.partial(place_kernel, counts, maps),
        out_shape=shaped(outs),
        grid_spec=pltpu.PrefetchScalarGridSpec(
            num_scalar_prefetch=1,
            grid=(1,),
            in_specs=[HBM] * len(pieces),
            out_specs=[
                pl.BlockSpec((total, height, w), lambda i, places: (0, 0, 0)) for w in widths
            ],
            scratch_shapes=[pltpu.SemaphoreType.DMA((copies,))],
        ),
        compiler_params=pltpu.CompilerParams(vmem_limit_bytes=3 * size + (4 << 20)),
        cost_estimate=cost(1 + size / 1e6),
        name="place",
    )(places.astype(jnp.int32), *pieces)
    return result[0] if len(widths) == 1 else result


def after(values, *tokens):
    return lax.optimization_barrier((values,) + tokens)[0]


def settle(*values):
    return lax.optimization_barrier(values)


def seq_masks(parity):
    return [0, 1 + parity, 2 - parity, 3]


def swap_seq(values, turn):
    mem, seq = lax.axis_size("mem"), lax.axis_size("seq")
    pairs = []
    for m in range(mem):
        mask = 1 + (m + turn) % 2
        pairs += [(m * seq + s, m * seq + (s ^ mask)) for s in range(seq)]
    return lax.ppermute(values, ("mem", "seq"), pairs)


def seq_places():
    parity = lax.axis_index("mem") % 2
    return lax.axis_index("seq") ^ jnp.stack(seq_masks(parity)).astype(jnp.int32)


def stack_seq(pieces, widths=None):
    return place(pieces, seq_places(), widths)


def send_seq(pieces):
    return [pieces[0]] + [shift(piece, "seq", k) for k, piece in enumerate(pieces) if k]


def total_of(pieces):
    return functools.reduce(jnp.add, [piece.astype(F32) for piece in pieces])


def join(blocks):
    return blocks[0] if len(blocks) == 1 else jnp.concatenate(blocks, axis=0)


def orders(count):
    bits = list(range(1, count.bit_length() - 1))
    return bits, bits[::-1]


def slot_masks(count):
    half = count // 2
    low = [
        [sum(((s >> j) & 1) << bit for j, bit in enumerate(order)) for s in range(half)]
        for order in orders(count)
    ]
    return low[0] + [m | 1 for m in low[1]], low[1] + [m | 1 for m in low[0]]


def swap_mem(values, turn):
    count = lax.axis_size("mem")
    pairs = []
    for i in range(count):
        order = [*orders(count)[i % 2], 0]
        pairs.append((i, i ^ (1 << order[turn])))
    return lax.ppermute(values, "mem", pairs)


def mem_masks():
    count = lax.axis_size("mem")
    even, odd = slot_masks(count)
    return jnp.where(
        lax.axis_index("mem") % 2 == 0, jnp.array(even, jnp.int32), jnp.array(odd, jnp.int32)
    )


def stack_mem(halves, widths=None):
    return place(halves, lax.axis_index("mem") ^ mem_masks(), widths)


def spread_weight(halves):
    if halves[0].shape[1] % 16 == 0:
        return list(halves)
    stacked = stack_mem(halves)
    return [stacked.reshape(1, -1, stacked.shape[-1])]


def add_low(left, right):
    return (left.astype(F32) + right.astype(F32)).astype(BF16)


def total_kernel(plans, spot_ref, *refs):
    terms = sum(number for number, _ in plans)
    sources, refs = list(refs[:terms]), refs[terms:]
    outs, holds = list(refs[: len(refs) - len(plans)]), refs[len(refs) - len(plans) :]
    column = 0
    for (number, ends), hold in zip(plans, holds):
        mine, sources = sources[:number], sources[number:]
        groups, rows, width = mine[0].shape
        for g in range(groups):
            total = mine[0][g].astype(F32)
            for ref in mine[1:]:
                total = total + ref[g].astype(F32)
            if not ends:
                outs[0][g] = total.astype(BF16)
                continue
            count = hold.shape[0]
            unit = rows // count
            for j in range(count):
                hold[j] = total[j * unit : (j + 1) * unit]
            for k, mask in enumerate(seq_masks(lax.rem(spot_ref[0], 2))):
                piece = hold[jnp.bitwise_xor(spot_ref[1], mask)].astype(BF16)
                outs[-2 + k // 2][k % 2, :, column : column + width] = piece
            column += width
        if not ends:
            del outs[:1]


class Scatter:
    def __init__(self, kept, sent, taken=0):
        self.terms = [kept if kept.ndim == 3 else kept[None]]
        self.sent = sent if sent.ndim == 3 else sent[None]
        self.left = (lax.axis_size("mem") // 2).bit_length() - 1 - taken
        self.rows = self.terms[0].shape[1]

    def move(self):
        self.terms.append(swap_mem(self.sent, self.left))

    def hold(self):
        return [self.terms, self.sent]

    def take(self, held):
        self.terms, self.sent = held


def advance(scatters, spot):
    count = lax.axis_size("seq")
    plans, shapes, specs, flat, holds = [], [], [], [], []
    ended, exact = 0, True
    whole = lambda shape: pl.BlockSpec(shape, lambda i, spot: (0, 0, 0))
    for s in scatters:
        ends = s.left == 0
        groups, _, width = s.terms[0].shape
        rows = s.rows if ends else s.rows // 2
        exact = exact and rows // (count if ends else 1) % 8 == 0
        plans.append((len(s.terms), ends))
        part = (groups, rows, width)
        if ends:
            specs += [whole(part)] * len(s.terms)
            ended += groups * width
            unit = rows // count
            holds.append(pltpu.VMEM((count, unit, width), F32))
        else:
            specs += [pl.BlockSpec(part, lambda i, spot: (0, 1, 0))] * len(s.terms)
            shapes.append(part)
            holds.append(pltpu.VMEM((1, 8, 128), F32))
        flat += s.terms
    if ended:
        shapes += [(2, unit, ended)] * 2
    if exact:
        size = sum(spec.block_shape[0] * spec.block_shape[1] * spec.block_shape[2] for spec in specs)
        outs = pl.pallas_call(
            functools.partial(total_kernel, plans),
            out_shape=shaped([(shape, BF16) for shape in shapes]),
            grid_spec=pltpu.PrefetchScalarGridSpec(
                num_scalar_prefetch=1,
                grid=(1,),
                in_specs=specs,
                out_specs=[whole(shape) for shape in shapes],
                scratch_shapes=holds,
            ),
            compiler_params=vmem(6 + (size * 8 >> 20)),
            cost_estimate=cost(1 + size / 1e6),
            name="total",
        )(spot, *(far(*flat) if size > 1 << 20 else flat))
        outs = list(outs)
    else:
        outs, ends_at = [], []
        for s in scatters:
            low = 0 if s.left == 0 else s.rows // 2
            high = s.rows if s.left == 0 else 2 * low
            total = total_of([term[:, low:high] for term in s.terms]).astype(BF16)
            if s.left:
                outs.append(total)
                continue
            groups, rows, width = total.shape
            blocks = total.reshape(groups, count, rows // count, width)
            ends_at.append(jnp.take(jnp.concatenate(list(blocks), axis=2), seq_places(), axis=0))
        if ends_at:
            blocks = jnp.concatenate(ends_at, axis=2)
            outs += [blocks[:2], blocks[2:]]
    for s in scatters:
        if s.left:
            s.sent, s.rows = outs.pop(0), s.rows // 2
        s.left -= 1
    return outs or None


def onward(kept, arrived, summed=None):
    half = kept.shape[0] // 2
    mine, theirs = kept[half:], arrived[half:]
    if summed is None:
        return add_low(mine, theirs)
    return jnp.concatenate(
        [add_low(mine[..., :summed], theirs[..., :summed]), mine[..., summed:], theirs[..., summed:]],
        axis=-1,
    )


def part_blocks(blocks, turn):
    count = blocks.shape[0]
    parts = blocks.reshape((count >> (turn + 1), 2, 1 << turn) + blocks.shape[1:])
    return parts[:, 0], parts[:, 1]


def join_blocks(stay, arrived):
    joined = jnp.stack([stay, arrived], axis=1)
    return joined.reshape((-1,) + joined.shape[3:])


HBM = pl.BlockSpec(memory_space=pltpu.HBM)


def far(*arrays):
    return [pltpu.with_memory_space_constraint(array, pltpu.HBM) for array in arrays]


def shaped(shapes, distant=()):
    return [
        jax.ShapeDtypeStruct(shape, dtype)
        for i, (shape, dtype) in enumerate(shapes)
    ]


def vmem(mebibytes):
    return pltpu.CompilerParams(vmem_limit_bytes=mebibytes << 20)


def cost(microseconds):
    return pl.CostEstimate(
        flops=int(microseconds * 1.1e9), bytes_accessed=0, transcendentals=0
    )


def run(copies):
    for copy in copies:
        copy.start()
    for copy in copies:
        copy.wait()


def prepare_kernel(
    slim, broad, scalars_ref, spot_ref,
    q_ref, k_ref, v_ref, o1_ref, q2_ref, k2_ref, v2_ref, o2_ref, gate_ref, up_ref,
    gain_ref, memory_ref,
    own_ref, two_ref, one_ref, second_ref, blocks_ref, live_ref,
    turn, triple, held, done,
):
    mem_count, height = blocks_ref.shape[0], memory_ref.shape[1]
    share, width = q_ref.shape
    half = mem_count // 2
    me, seq = spot_ref[0], spot_ref[1]
    parity = lax.rem(me, 2)
    counts_at, tails_at, rows_at = 0, mem_count, 2 * mem_count
    moves = [(ref, triple.at[i]) for i, ref in enumerate((q_ref, k_ref, v_ref))]
    moves += [(memory_ref, held)]
    for ref, base in ((own_ref, 3 * broad), (one_ref, 3 * broad), (two_ref, 6 * broad)):
        for i, source in enumerate((o1_ref, q2_ref, k2_ref, v2_ref, o2_ref)):
            moves += [(source, ref.at[:, base + i * width : base + (i + 1) * width])]
    hidden = gate_ref.shape[1]
    moves += [(gate_ref, second_ref.at[:, :hidden]), (up_ref, second_ref.at[:, hidden:])]
    copies = [pltpu.make_async_copy(a, b, done.at[i]) for i, (a, b) in enumerate(moves)]
    for copy in copies:
        copy.start()
    turn[...] = jnp.zeros_like(turn)
    turn[0:3, 0:share] = gain_ref[...].astype(F32)
    gains = turn[...].T[:share]
    lane = lax.broadcasted_iota(jnp.int32, (share, broad - slim), 1)
    extra = jnp.zeros((share, broad - slim), F32)
    for i in range(3):
        extra = jnp.where(lane == i, gains[:, i : i + 1], extra)
    extra = extra.astype(BF16)
    blank = jnp.zeros((share, broad - slim), BF16)
    token = lax.broadcasted_iota(jnp.int32, (height, 1), 0)

    def first_block(example):
        return lax.fori_loop(
            0, example, lambda i, total: total + scalars_ref[counts_at + i], jnp.int32(0)
        )

    mine = scalars_ref[rows_at + me]
    mine_start = first_block(mine)
    mine_end = mine_start + scalars_ref[counts_at + mine]

    for copy in copies[:4]:
        copy.wait()

    order, contrary = orders(mem_count)

    def one(t, carry):
        low = lax.rem(t, half)
        first, second = jnp.int32(0), jnp.int32(0)
        for j in range(len(order)):
            bit = lax.rem(lax.shift_right_logical(low, jnp.int32(j)), 2)
            first = first + bit * (1 << order[j])
            second = second + bit * (1 << contrary[j])
        flip = parity == 1
        first, second = jnp.where(flip, second, first), jnp.where(flip, first, second)
        upper = t >= half
        goal = jnp.bitwise_xor(me, jnp.where(upper, first + 1, first))
        start = first_block(scalars_ref[rows_at + goal])
        block = start + lax.rem(me - lax.rem(start, mem_count) + mem_count, mem_count)
        slot = jnp.minimum(block // mem_count, memory_ref.shape[0] - 1)
        blocks_ref[t] = held[slot]
        holder = jnp.bitwise_xor(me, jnp.where(upper, second + 1, first))
        block = mine_start + lax.rem(
            holder - lax.rem(mine_start, mem_count) + mem_count, mem_count
        )
        bound = jnp.where(block == mine_end - 1, scalars_ref[tails_at + mine], height)
        bound = jnp.where(block < mine_end, bound, 0)
        live_ref[t] = jnp.where(token < bound, 0.0, MASKED)
        return carry

    lax.fori_loop(0, mem_count, one, 0)
    seq_steps = seq_masks(parity)
    for ref, base, mask in (
        (own_ref, 0, seq_steps[0]),
        (two_ref, 0, seq_steps[1]),
        (one_ref, 0, seq_steps[2]),
        (two_ref, 1, seq_steps[3]),
    ):
        goal = jnp.bitwise_xor(seq, mask)
        for i in range(3):
            weight = triple[i].astype(F32)
            chosen = weight[:, :slim]
            for j in range(1, width // slim):
                chosen = jnp.where(goal == j, weight[:, j * slim : (j + 1) * slim], chosen)
            start = (3 * base + i) * broad
            ref[:, start : start + broad] = jnp.concatenate(
                [chosen.astype(BF16), blank if i else extra], axis=1
            )
    for copy in copies[4:]:
        copy.wait()


def prepare(weights, gains, memory, scalars, spot, slim, broad):
    mem_count = lax.axis_size("mem")
    share, width = weights[0].shape
    first = 3 * broad + 5 * width
    second = sum(w.shape[1] for w in weights[8:])
    height = memory.shape[1]
    whole = lambda shape: pl.BlockSpec(shape, lambda *_: (0,) * len(shape))
    outs = [
        ((share, first), BF16),
        ((share, first + 3 * broad), BF16),
        ((share, first), BF16),
        ((share, second), BF16),
        ((mem_count, height, width), BF16),
        ((mem_count, height, 1), F32),
    ]
    return pl.pallas_call(
        functools.partial(prepare_kernel, slim, broad),
        out_shape=shaped(outs),
        grid_spec=pltpu.PrefetchScalarGridSpec(
            num_scalar_prefetch=2,
            grid=(1,),
            in_specs=[HBM] * len(weights) + [whole(gains.shape), HBM],
            out_specs=[whole(shape) for shape, _ in outs],
            scratch_shapes=[
                pltpu.VMEM((8, 128), F32),
                pltpu.VMEM((3, share, width), BF16),
                pltpu.VMEM(memory.shape, BF16),
                pltpu.SemaphoreType.DMA((4 + 15 + 2,)),
            ],
        ),
        compiler_params=vmem(16 + 3 * mem_count // 8),
        cost_estimate=cost(3),
        name="prepare",
    )(scalars, spot, *far(*weights), gains, *far(memory))


def slots_kernel(per, scalars_ref, spot_ref, blocks_ref, keep_ref, send_ref, done):
    mem_count = blocks_ref.shape[0]
    me, seq = spot_ref[0], spot_ref[1]
    parity = lax.rem(me, 2)
    copies = []
    for k, mask in enumerate(seq_masks(parity)):
        for s in range(per):
            slot = jnp.bitwise_xor(seq, mask) * per + s
            block = slot * mem_count + me

            def scan(i, carry):
                end, owner = carry
                end = end + scalars_ref[i]
                return end, owner + jnp.where(end <= block, 1, 0)

            _, owner = lax.fori_loop(0, mem_count, scan, (jnp.int32(0), jnp.int32(0)))
            row = lax.fori_loop(
                0,
                mem_count,
                lambda i, r: jnp.where(scalars_ref[2 * mem_count + i] == owner, i, r),
                jnp.int32(0),
            )
            gap = jnp.bitwise_xor(row, me)
            bit = lambda b: lax.rem(lax.shift_right_logical(gap, jnp.int32(b)), 2)
            spots = [
                sum(bit(b) * (1 << j) for j, b in enumerate(order)) for order in orders(mem_count)
            ]
            at = jnp.where(parity == 1, spots[1], spots[0]) + bit(0) * (mem_count // 2)
            copies.append(
                pltpu.make_async_copy(
                    blocks_ref.at[at],
                    (keep_ref, send_ref)[k // 2].at[k % 2 * per + s],
                    done.at[len(copies)],
                )
            )
    for copy in copies:
        copy.start()
    for copy in copies:
        copy.wait()


def pick_slots(blocks, slots, scalars, spot):
    per = slots // lax.axis_size("seq")
    shape = (2 * per,) + blocks.shape[1:]
    return pl.pallas_call(
        functools.partial(slots_kernel, per),
        out_shape=shaped([(shape, BF16)] * 2),
        grid_spec=pltpu.PrefetchScalarGridSpec(
            num_scalar_prefetch=2,
            grid=(1,),
            in_specs=[HBM],
            out_specs=[pl.BlockSpec(shape, lambda *_: (0, 0, 0))] * 2,
            scratch_shapes=[pltpu.SemaphoreType.DMA((slots,))],
        ),
        compiler_params=vmem(8),
        cost_estimate=cost(2),
        name="pick_slots",
    )(scalars, spot, blocks)


PAIR = 2


def feed_kernel(
    order_ref, h2_ref, c3_ref, gain_ref, turn,
    *refs,
):
    sides, refs = refs[: 4 * PAIR], refs[4 * PAIR :]
    down_refs, refs = refs[:-14], refs[-14:]
    out_ref, dh2_ref, c2_ref, gain_grad_ref, bundle_ref, act_near_ref, n3_near_ref = refs[:7]
    n3_rel, total, dn3, gate_w, up_w, down_w, act_all = refs[7:]
    step, steps = pl.program_id(0), pl.num_programs(0)
    half, unit = sides[0].shape
    width = h2_ref.shape[1]
    hidden = unit * steps * PAIR
    slim = width // 2

    @pl.when(step == 0)
    def _():
        h2 = h2_ref[...]
        n3 = (h2 * norm_scale(h2) * gain_ref[2:3]).astype(BF16)
        rel = right_product(n3, turn[...]).astype(BF16)
        n3_rel[...] = rel
        n3_near_ref[...] = rel[:, :slim]
        bundle_ref[:, 2 * hidden + hidden // 2 :] = rel[:, slim:]
        total[...] = jnp.zeros_like(total)
        dn3[...] = jnp.zeros_like(dn3)

    base = 0
    for ref in down_refs:
        number = ref.shape[0]
        for block in range(number):

            @pl.when(step == (base + block) // PAIR)
            def _(ref=ref, block=block, at=(base + block) % PAIR):
                down_w[at * unit : (at + 1) * unit] = ref[block]

        base += number
    for n in range(PAIR):
        part = slice(n * unit, (n + 1) * unit)
        for k, target in enumerate((gate_w, up_w)):
            target[:half, part] = sides[4 * n + 2 * k][...]
            target[half:, part] = sides[4 * n + 2 * k + 1][...]
    down = down_w[...]
    n3, c3 = n3_rel[...], c3_ref[...]
    gate = product(n3, gate_w[...])
    upper = product(n3, up_w[...])
    dact = right_product(c3, down)
    inner = 0.7978845608028654 * (gate + 0.044715 * gate * gate * gate)
    bent = jnp.tanh(inner)
    gelu = 0.5 * gate * (1.0 + bent)
    slope = 0.5 * (1.0 + bent) + 0.5 * gate * (1.0 - bent * bent) * (
        0.7978845608028654 * (1.0 + 3.0 * 0.044715 * gate * gate)
    )
    act = (gelu * upper).astype(BF16)
    dgate = (dact * upper * slope).astype(BF16)
    dupper = (dact * gelu).astype(BF16)
    total[...] += product(act, down)
    for n in range(PAIR):
        part = slice(n * unit, (n + 1) * unit)
        act_all[step * PAIR + n] = act[:, part]
        column = pl.multiple_of(order_ref[step * PAIR + n] * unit, LANES)
        bundle_ref[:, pl.ds(column, unit)] = dgate[:, part]
        bundle_ref[:, pl.ds(pl.multiple_of(hidden + column, LANES), unit)] = dupper[:, part]
    dn3[...] += right_product(dgate, gate_w[...]) + right_product(dupper, up_w[...])

    @pl.when(step == steps - 1)
    def _():
        middle = act_all.shape[0] // 2
        for t in range(middle):
            act_near_ref[:, t * unit : (t + 1) * unit] = act_all[t]
            first = 2 * hidden + t * unit
            bundle_ref[:, first : first + unit] = act_all[middle + t]
        h2 = h2_ref[...]
        out_ref[...] = (h2 + total[...]).astype(BF16)
        high = dn3[...].astype(BF16)
        rest = (dn3[...] - high.astype(F32)).astype(BF16)
        upstream = product(high, turn[...]) + product(rest, turn[...])
        scale = norm_scale(h2)
        dh2 = c3_ref[...].astype(F32) + norm_hidden_grad(h2, scale, gain_ref[2:3], upstream)
        dh2_ref[...] = dh2
        c2_ref[...] = dh2.astype(BF16)
        gain_grad_ref[...] = jnp.sum(upstream * h2 * scale, axis=0, keepdims=True)


def feed(order, h2, c3, gains, source, both, down):
    rows, width = h2.shape
    half, hidden = both[0].shape
    hidden = hidden // 2
    steps = order.shape[0]
    unit = hidden // steps
    whole = lambda shape: pl.BlockSpec(shape, lambda i, o: (0, 0))
    sides = []
    for n in range(PAIR):
        sides += [pl.BlockSpec((half, unit), lambda i, o, n=n: (0, o[i * PAIR + n]))] * 2
        sides += [pl.BlockSpec((half, unit), lambda i, o, n=n: (0, o[i * PAIR + n] + steps))] * 2
    flat = (rows, width)
    shapes = [
        (flat, BF16),
        (flat, F32),
        (flat, BF16),
        ((1, width), F32),
        ((rows, 2 * hidden + hidden // 2 + width // 2), BF16),
        ((rows, hidden // 2), BF16),
        ((rows, width // 2), BF16),
    ]
    return pl.pallas_call(
        feed_kernel,
        out_shape=shaped(shapes, (0,)),
        grid_spec=pltpu.PrefetchScalarGridSpec(
            num_scalar_prefetch=1,
            grid=(steps // PAIR,),
            in_specs=[whole(flat)] * 2
            + [whole(gains.shape), whole((width, width))]
            + sides
            + [pl.BlockSpec(w.shape, lambda i, o: (0, 0, 0)) for w in down],
            out_specs=[whole(shape) for shape, _ in shapes],
            scratch_shapes=[
                pltpu.VMEM(flat, BF16),
                pltpu.VMEM(flat, F32),
                pltpu.VMEM(flat, F32),
                pltpu.VMEM((2 * half, PAIR * unit), BF16),
                pltpu.VMEM((2 * half, PAIR * unit), BF16),
                pltpu.VMEM((PAIR * unit, width), BF16),
                pltpu.VMEM((steps, rows, unit), BF16),
            ],
        ),
        compiler_params=vmem(28),
        cost_estimate=cost(13),
        name="feed",
    )(order, h2, *far(c3), gains, source, *far(*both * (2 * PAIR)), *down)


def feed_weights_kernel(
    own_ref, other_ref, act_ref, n3_ref, c3_ref, c3_other_ref,
    both_keep_ref, both_send_ref, down_keep_ref, down_send_ref,
):
    hidden = both_keep_ref.shape[2]
    units = act_ref.shape[1]
    quarter, third = both_keep_ref.shape[1], down_keep_ref.shape[0]
    edge = 2 * hidden + units
    mine = transposed(n3_ref[...])
    theirs = transposed(other_ref[:, edge:])
    step = hidden // 2
    for first in range(0, 2 * hidden, step):
        grad = product(mine, own_ref[:, first : first + step])
        grad = grad + product(theirs, other_ref[:, first : first + step])
        grad = grad.astype(BF16)
        part, column = first // hidden, first % hidden
        both_keep_ref[part, :, column : column + step] = grad[:quarter]
        both_send_ref[part, :, column : column + step] = grad[quarter:]
    c3, c3_other = c3_ref[...], c3_other_ref[...]
    for k, ref in enumerate((down_keep_ref, down_send_ref)):
        first = k * third
        mine = transposed(act_ref[:, first : first + third])
        theirs = transposed(other_ref[:, 2 * hidden + first : 2 * hidden + first + third])
        ref[...] = (product(mine, c3) + product(theirs, c3_other)).astype(BF16)


def feed_weights(own, other, act, n3, c3, c3_other):
    rows, width = c3.shape
    units = act.shape[1]
    hidden = 2 * units
    pair = ((2, width // 4, hidden), BF16)
    single = ((units // 2, width), BF16)
    return pl.pallas_call(
        feed_weights_kernel,
        out_shape=shaped([pair, pair, single, single]),
        compiler_params=vmem(24),
        cost_estimate=cost(5),
        name="feed_weights",
    )(own, other, act, n3, c3, c3_other)


def head_mask(shape, head):
    return lax.broadcasted_iota(jnp.int32, shape, 1) // HEAD_DIM == head


def pick_head(values, head):
    return jnp.where(head_mask(values.shape, head), values, jnp.zeros_like(values))


def stack_heads(values, heads):
    return jnp.concatenate([pick_head(values, head) for head in heads], axis=0)


def head_groups(keys, heads):
    return [list(range(heads))] if keys <= 2048 else [[head] for head in range(heads)]


def transposed(values):
    return values.astype(F32).T.astype(values.dtype)


LOG2E = 1.4426950408889634
SHRINK = SCALING * LOG2E


def soft_parts(scores, axis=0):
    peak = jnp.max(scores, axis=0, keepdims=True)
    powers = jnp.exp2(scores - peak)
    total = jnp.sum(powers, axis=0, keepdims=True)
    return powers, 1.0 / total, peak + jnp.log2(total)


def causal_scores(keys, queries, count):
    scores = right_product(keys, queries) * SHRINK
    last = scores.shape[0] - count
    corner = scores[last:]
    key_place = lax.broadcasted_iota(jnp.int32, corner.shape, 0)
    query_place = lax.rem(lax.broadcasted_iota(jnp.int32, corner.shape, 1), count)
    corner = jnp.where(key_place <= query_place, corner, MASKED)
    return corner if last == 0 else jnp.concatenate([scores[:last], corner], axis=0)


def cross_scores(keys, queries, bias):
    return right_product(keys, queries) * SHRINK + bias


def score_grads(scores, logs, inner):
    chance = jnp.exp2(scores - logs)
    spread = jnp.sum(chance * inner, axis=0, keepdims=True)
    return chance.astype(BF16), (chance * (inner - spread)).astype(BF16)


def weight_copies(refs, masks, me, columns, target, done, base):
    copies = []
    for ref in refs:
        for block in range(ref.shape[0]):
            number = len(copies)
            spot = 0
            if len(refs) > 1:
                mask = masks[0][number]
                if masks[1][number] != mask:
                    mask = jnp.where(lax.rem(me, 2) == 1, masks[1][number], mask)
                spot = pl.multiple_of(jnp.bitwise_xor(me, mask) * ref.shape[1], 16)
            copies.append(
                pltpu.make_async_copy(
                    ref.at[block, :, columns[0] : columns[1]],
                    target.at[pl.ds(spot, ref.shape[1])],
                    done.at[base + number],
                )
            )
    return copies


def blocks_in(refs):
    return sum(ref.shape[0] for ref in refs)


def self_rows_kernel(heads, masks, counts, spot_ref, *refs):
    seq_count, weights = counts
    x_refs, refs = refs[:3], refs[3:]
    x_list = [x_refs[0], x_refs[1], x_refs[2].at[0], x_refs[2].at[1]]
    w_refs, refs = refs[:weights], refs[weights:]
    o_refs, refs = refs[:seq_count], refs[seq_count:]
    n1_ref, qkv_ref, gain_ref, log_ref, x_all, w_all, o_all, done = refs
    rows, width = x_refs[0].shape
    broad = w_all.shape[1] // 3
    me, seq = spot_ref[0], spot_ref[1]
    copies = weight_copies(w_refs, masks, me, (0, 3 * broad), w_all, done, 0)
    base = len(copies)
    copies += [
        pltpu.make_async_copy(ref, x_all.at[jnp.bitwise_xor(seq, mask)], done.at[base + k])
        for k, (ref, mask) in enumerate(zip(x_list, seq_masks(lax.rem(me, 2))))
    ]
    run(copies)
    slim = heads * HEAD_DIM
    edge = slim // LANES * LANES
    gains = w_all[:, edge : edge + LANES].astype(F32).T[slim - edge : slim - edge + 8]
    gain_ref[...] = gains
    for j in range(seq_count):
        x = x_all[j].astype(F32)
        n1 = (x * norm_scale(x) * gains[0:1]).astype(BF16)
        n1_ref[j * rows : (j + 1) * rows] = n1
        qkv_ref[j * rows : (j + 1) * rows] = product(n1, w_all[...]).astype(BF16)
    values_t = transposed(qkv_ref[:, 2 * broad :])
    for j in range(seq_count):
        first, last = j * rows, (j + 1) * rows
        queries = qkv_ref[first:last, :broad]
        parts = []
        scores = causal_scores(
            qkv_ref[:last, broad : 2 * broad], stack_heads(queries, range(heads)), rows
        )
        powers, inverse, logs = soft_parts(scores)
        powers = powers.astype(BF16)
        for head in range(heads):
            part = slice(head * rows, (head + 1) * rows)
            log_ref[head : head + 1, first:last] = logs[:, part]
            lines = values_t[head * HEAD_DIM : (head + 1) * HEAD_DIM, :last]
            parts.append(product(lines, powers[:, part]) * inverse[:, part])
        o_all[j] = jnp.concatenate(parts, axis=0).T.astype(BF16)
    for k, ref in enumerate(o_refs):
        ref[...] = o_all[lax.rem(seq + k, seq_count)]


def self_rows(x_pieces, weights, spot, heads, broad, masks):
    count = lax.axis_size("seq")
    rows, width = x_pieces[0].shape
    length, slim = rows * count, heads * HEAD_DIM
    whole = lambda shape: pl.BlockSpec(shape, lambda i, spot: (0, 0))
    shapes = [((rows, slim), BF16)] * count + [
        ((length, width), BF16),
        ((length, 3 * broad), BF16),
        ((8, width), F32),
        ((8, length), F32),
    ]
    outs = pl.pallas_call(
        functools.partial(self_rows_kernel, heads, masks, (count, len(weights))),
        out_shape=shaped(shapes, (count, count + 1, count + 3)),
        grid_spec=pltpu.PrefetchScalarGridSpec(
            num_scalar_prefetch=1,
            grid=(1,),
            in_specs=[HBM] * (3 + len(weights)),
            out_specs=[whole(s) for s, _ in shapes],
            scratch_shapes=[
                pltpu.VMEM((count, rows, width), BF16),
                pltpu.VMEM((width, 3 * broad), BF16),
                pltpu.VMEM((count, rows, slim), BF16),
                pltpu.SemaphoreType.DMA((blocks_in(weights) + count,)),
            ],
        ),
        compiler_params=vmem(14),
        cost_estimate=cost(10),
        name="self_rows",
    )(spot, *x_pieces, *weights)
    return outs[:count], *outs[count:]


def key_values_kernel(masks, number, edge, spot_ref, turn_ref, keys_ref, *refs):
    w_refs, (out_ref, keys_t_ref, w_all, done) = refs[:number], refs[number:]

    @pl.when(pl.program_id(0) == 0)
    def _():
        columns = (edge, edge + w_all.shape[1])
        run(weight_copies(w_refs, masks, spot_ref[0], columns, w_all, done, 0))

    keys_t_ref[...] = right_product(turn_ref[...], keys_ref[...]).astype(BF16)
    out_ref[...] = product(keys_ref[...], w_all[...]).astype(BF16)


def key_values(turn, keys, weights, spot, chunk, edge, masks):
    width = keys.shape[1]
    columns = 2 * width
    return pl.pallas_call(
        functools.partial(key_values_kernel, masks, len(weights), edge),
        out_shape=shaped([((keys.shape[0], columns), BF16), ((width, keys.shape[0]), BF16)]),
        grid_spec=pltpu.PrefetchScalarGridSpec(
            num_scalar_prefetch=1,
            grid=(keys.shape[0] // chunk,),
            in_specs=[
                pl.BlockSpec((width, width), lambda i, spot: (0, 0)),
                pl.BlockSpec((chunk, width), lambda i, spot: (i, 0)),
            ]
            + [HBM] * len(weights),
            out_specs=[
                pl.BlockSpec((chunk, columns), lambda i, spot: (i, 0)),
                pl.BlockSpec((width, chunk), lambda i, spot: (0, i)),
            ],
            scratch_shapes=[
                pltpu.VMEM((width, columns), BF16),
                pltpu.SemaphoreType.DMA((blocks_in(weights),)),
            ],
        ),
        compiler_params=vmem(12),
        cost_estimate=cost(4),
        name="key_values",
    )(spot, turn, keys, *weights)


def cross_attend(queries, keys, values, live, log_ref):
    values_t = transposed(values)
    pieces = []
    rows = queries.shape[0]
    for group in head_groups(keys.shape[0], LANES // HEAD_DIM):
        powers, inverse, logs = soft_parts(cross_scores(keys, stack_heads(queries, group), live))
        powers = powers.astype(BF16)
        for n, head in enumerate(group):
            part = slice(n * rows, (n + 1) * rows)
            log_ref[0, head : head + 1] = logs[:, part]
            lines = values_t[head * HEAD_DIM : (head + 1) * HEAD_DIM]
            pieces.append(product(lines, powers[:, part]) * inverse[:, part])
    return jnp.concatenate(pieces, axis=0).T.astype(BF16)


def rows_first_kernel(masks, counts, edge, spot_ref, *refs):
    seq_count, weights = counts
    a_refs, refs = refs[:seq_count], refs[seq_count:]
    w_refs, refs = refs[:weights], refs[weights:]
    x_ref, gain_ref, live_ref, k_ref, v_ref = refs[:5]
    q2_ref, a2_ref, h1_ref, log_ref = refs[5:9]
    a_all, w_o1, w_q2, q_parts, done = refs[9:]
    step = pl.program_id(0)
    me, seq = spot_ref[0], spot_ref[1]
    width = x_ref.shape[1]

    @pl.when(step == 0)
    def _():
        copies = [
            pltpu.make_async_copy(
                ref, a_all.at[lax.rem(seq - k + seq_count, seq_count)], done.at[k]
            )
            for k, ref in enumerate(a_refs)
        ]
        copies += weight_copies(w_refs, masks, me, (edge, edge + width), w_o1, done, seq_count)
        later = weight_copies(
            w_refs, masks, me, (edge + width, edge + 2 * width), w_q2, done, len(copies)
        )
        for copy in copies + later:
            copy.start()
        for copy in copies:
            copy.wait()
        a1 = jnp.concatenate([a_all[j] for j in range(seq_count)], axis=1)
        h1 = x_ref[...].astype(F32) + right_product(a1, w_o1[...])
        h1_ref[...] = h1
        n2 = (h1 * norm_scale(h1) * gain_ref[1:2]).astype(BF16)
        for copy in later:
            copy.wait()
        q2 = product(n2, w_q2[...]).astype(BF16)
        q2_ref[...] = q2
        for i in range(q_parts.shape[0]):
            q_parts[i] = q2[:, i * LANES : (i + 1) * LANES]

    a2_ref[...] = cross_attend(q_parts[step], k_ref[...], v_ref[...], live_ref[...], log_ref)


def rows_second_kernel(masks, weights, edge, spot_ref, *refs):
    w_refs, refs = refs[:weights], refs[weights:]
    h1_ref, early_ref, live_ref, q_ref, k_ref, v_ref, a2_ref, h2_ref, log_ref = refs[:9]
    w_o2, o_parts, done = refs[9:]
    step, parts = pl.program_id(0), o_parts.shape[0]
    width = h1_ref.shape[1]
    columns = (edge + 4 * width, edge + 5 * width)
    copies = weight_copies(w_refs, masks, spot_ref[0], columns, w_o2, done, 0)

    @pl.when(step == 0)
    def _():
        for copy in copies:
            copy.start()

    o_parts[step] = cross_attend(q_ref[...], k_ref[...], v_ref[...], live_ref[...], log_ref)

    @pl.when(step == parts - 1)
    def _():
        for copy in copies:
            copy.wait()
        a2 = jnp.concatenate([early_ref[...]] + [o_parts[i] for i in range(parts)], axis=1)
        a2_ref[...] = a2
        h2_ref[...] = h1_ref[...] + right_product(a2, w_o2[...])


def rows_first(a_pieces, weights, x, gains, live, kv, spot, edge, masks):
    count = len(a_pieces)
    rows, width = x.shape
    keys = kv.shape[0]
    parts = width // LANES
    flat = (rows, width)
    whole = lambda shape: pl.BlockSpec(shape, lambda i, spot: (0, 0))
    _, row, key, value = rows_specs(rows, keys, width, 0)
    log = pl.BlockSpec((1, 8, rows), lambda i, spot: (i, 0, 0))
    shapes = [
        (flat, BF16), ((rows, width // 2), BF16), (flat, F32), ((parts // 2, 8, rows), F32)
    ]
    square = pltpu.VMEM((width, width), BF16)
    return pl.pallas_call(
        functools.partial(rows_first_kernel, masks, (count, len(weights)), edge),
        out_shape=shaped(shapes),
        grid_spec=pltpu.PrefetchScalarGridSpec(
            num_scalar_prefetch=1,
            grid=(parts // 2,),
            in_specs=[HBM] * (count + len(weights))
            + [whole(flat), whole(gains.shape), whole(live.shape), key, value],
            out_specs=[whole(flat), row, whole(flat), log],
            scratch_shapes=[
                pltpu.VMEM((count,) + a_pieces[0].shape, BF16),
                square, square,
                pltpu.VMEM((parts, rows, LANES), BF16),
                pltpu.SemaphoreType.DMA((count + 2 * blocks_in(weights),)),
            ],
        ),
        compiler_params=vmem(max(16, keys * 8 // 1024 + 8)),
        cost_estimate=cost(7),
        name="rows_first",
    )(spot, *a_pieces, *weights, x, gains, live, kv, kv)


def rows_second(weights, h1, early, live, q2, kv, spot, edge, masks):
    rows, width = h1.shape
    keys = kv.shape[0]
    parts = width // LANES // 2
    flat = (rows, width)
    whole = lambda shape: pl.BlockSpec(shape, lambda i, spot: (0, 0))
    _, row, key, value = rows_specs(rows, keys, width, parts)
    log = pl.BlockSpec((1, 8, rows), lambda i, spot: (i, 0, 0))
    return pl.pallas_call(
        functools.partial(rows_second_kernel, masks, len(weights), edge),
        out_shape=shaped([(flat, BF16), (flat, F32), ((parts, 8, rows), F32)]),
        grid_spec=pltpu.PrefetchScalarGridSpec(
            num_scalar_prefetch=1,
            grid=(parts,),
            in_specs=[HBM] * len(weights)
            + [whole(flat), whole(early.shape), whole(live.shape), row, key, value],
            out_specs=[whole(flat), whole(flat), log],
            scratch_shapes=[
                pltpu.VMEM((width, width), BF16),
                pltpu.VMEM((parts, rows, LANES), BF16),
                pltpu.SemaphoreType.DMA((blocks_in(weights),)),
            ],
        ),
        compiler_params=vmem(max(14, keys * 8 // 1024 + 8)),
        cost_estimate=cost(6),
        name="rows_second",
    )(spot, *weights, h1, early, live, q2, kv, kv)


def cross_backward(queries, upstream, live, keys, values, logs):
    keys_t = transposed(keys)
    pieces, dk, dv = [], 0.0, 0.0
    rows = queries.shape[0]
    for group in head_groups(keys.shape[0], LANES // HEAD_DIM):
        own = stack_heads(queries, group)
        up_own = stack_heads(upstream, group)
        inner = right_product(values, up_own)
        log = jnp.concatenate([logs[head : head + 1] for head in group], axis=1)
        chance, grad = score_grads(cross_scores(keys, own, live), log, inner)
        dv = dv + product(chance, up_own)
        dk = dk + product(grad, own)
        for n, head in enumerate(group):
            lines = keys_t[head * HEAD_DIM : (head + 1) * HEAD_DIM]
            pieces.append(product(lines, grad[:, n * rows : (n + 1) * rows]))
    dq = jnp.concatenate(pieces, axis=0).T * SCALING
    return dq.astype(BF16), (dk * SCALING).astype(BF16), dv.astype(BF16)


def rows_early_kernel(masks, weights, edge, spot_ref, *refs):
    w_refs, refs = refs[:weights], refs[weights:]
    c2_ref, live_ref, log_ref, q_ref, k_ref, v_ref, up_ref, dq_ref, dk_ref, dv_ref = refs[:10]
    w_o2, up_parts, done = refs[10:]
    width = c2_ref.shape[1]

    @pl.when(pl.program_id(0) == 0)
    def _():
        columns = (edge + 4 * width, edge + 5 * width)
        run(weight_copies(w_refs, masks, spot_ref[0], columns, w_o2, done, 0))
        up = product(c2_ref[...], w_o2[...]).astype(BF16)
        up_ref[...] = up
        for i in range(up_parts.shape[0]):
            up_parts[i] = up[:, i * LANES : (i + 1) * LANES]

    dq_ref[...], dk_ref[...], dv_ref[...] = cross_backward(
        q_ref[...], up_parts[pl.program_id(0)], live_ref[...], k_ref[...], v_ref[...], log_ref[0]
    )


def rows_late_kernel(masks, counts, edge, spot_ref, *refs):
    seq_count, weights = counts
    w_refs, refs = refs[:weights], refs[weights:]
    up_ref, dq_early_ref, dh2_ref, h1_ref, gain_ref, live_ref, log_ref, q_ref, k_ref, v_ref = refs[:10]
    da_refs, refs = refs[10 : 10 + seq_count], refs[10 + seq_count :]
    dq2_ref, dk_ref, dv_ref, dh1_ref, gain_grad_ref = refs[:5]
    w_o1, w_q2, dq_parts, da_all, done = refs[5:]
    step = pl.program_id(0)
    me, seq = spot_ref[0], spot_ref[1]
    width = dh2_ref.shape[1]
    parts = dq_parts.shape[0]
    copies = weight_copies(
        w_refs, masks, me, (edge + width, edge + 2 * width), w_q2, done, 0
    )
    copies += weight_copies(w_refs, masks, me, (edge, edge + width), w_o1, done, len(copies))

    @pl.when(step == 0)
    def _():
        for copy in copies:
            copy.start()

    dq_parts[step], dk_ref[...], dv_ref[...] = cross_backward(
        q_ref[...], up_ref[...], live_ref[...], k_ref[...], v_ref[...], log_ref[0]
    )

    @pl.when(step == parts - 1)
    def _():
        for copy in copies:
            copy.wait()
        dq2 = jnp.concatenate([dq_early_ref[...]] + [dq_parts[i] for i in range(parts)], axis=1)
        dq2_ref[...] = dq2
        dn2 = right_product(dq2, w_q2[...])
        h1 = h1_ref[...]
        scale = norm_scale(h1)
        dh1 = dh2_ref[...] + norm_hidden_grad(h1, scale, gain_ref[1:2], dn2)
        dh1_ref[...] = dh1
        gain_grad_ref[...] = jnp.sum(dn2 * h1 * scale, axis=0, keepdims=True)
        c1 = dh1.astype(BF16)
        up = product(c1, w_o1[...])
        slim = da_all.shape[2]
        for j in range(seq_count):
            da_all[j] = up[:, j * slim : (j + 1) * slim].astype(BF16)
        for k, ref in enumerate(da_refs):
            ref[...] = da_all[lax.rem(seq + k, seq_count)]


def rows_specs(rows, keys, width, start):
    parts = width // LANES
    row = pl.BlockSpec((rows, LANES), lambda i, spot: (0, i + start))
    key = pl.BlockSpec((keys, LANES), lambda i, spot: (0, i + start))
    value = pl.BlockSpec((keys, LANES), lambda i, spot: (0, i + start + parts))
    log = pl.BlockSpec((1, 8, rows), lambda i, spot: (i, 0, 0))
    return log, row, key, value


def rows_early(weights, c2, live, logs, q2, kv, spot, edge, masks):
    rows, width = c2.shape
    keys = kv.shape[0]
    parts = width // LANES // 2
    whole = lambda shape: pl.BlockSpec(shape, lambda i, spot: (0, 0))
    log, row, key, value = rows_specs(rows, keys, width, 0)
    half = width // 2
    shapes = [((rows, width), BF16), ((rows, half), BF16)] + [((keys, half), BF16)] * 2
    return pl.pallas_call(
        functools.partial(rows_early_kernel, masks, len(weights), edge),
        out_shape=shaped(shapes, (2, 3)),
        grid_spec=pltpu.PrefetchScalarGridSpec(
            num_scalar_prefetch=1,
            grid=(parts,),
            in_specs=[HBM] * len(weights)
            + [whole((rows, width)), whole(live.shape), log, row, key, value],
            out_specs=[whole((rows, width)), row, key, key],
            scratch_shapes=[
                pltpu.VMEM((width, width), BF16),
                pltpu.VMEM((2 * parts, rows, LANES), BF16),
                pltpu.SemaphoreType.DMA((blocks_in(weights),)),
            ],
        ),
        compiler_params=vmem(max(12, keys * 8 // 1024 + 12)),
        cost_estimate=cost(10),
        name="rows_early",
    )(spot, *weights, c2, live, logs, q2, kv, kv)


def rows_late(weights, up, dq_early, dh2, h1, gains, live, logs, q2, kv, spot, edge, masks):
    count = lax.axis_size("seq")
    rows, width = dh2.shape
    keys = kv.shape[0]
    parts = width // LANES // 2
    slim = width // count
    flat = (rows, width)
    half = width // 2
    whole = lambda shape: pl.BlockSpec(shape, lambda i, spot: (0, 0))
    log, row, key, value = rows_specs(rows, keys, width, parts)
    key_out = pl.BlockSpec((keys, LANES), lambda i, spot: (0, i))
    shapes = [((rows, slim), BF16)] * count + [
        (flat, BF16), ((keys, half), BF16), ((keys, half), BF16),
        (flat, F32), ((1, width), F32),
    ]
    square = pltpu.VMEM((width, width), BF16)
    outs = pl.pallas_call(
        functools.partial(rows_late_kernel, masks, (count, len(weights)), edge),
        out_shape=shaped(shapes, range(count, count + 6)),
        grid_spec=pltpu.PrefetchScalarGridSpec(
            num_scalar_prefetch=1,
            grid=(parts,),
            in_specs=[HBM] * len(weights)
            + [row, whole((rows, half)), whole(flat), whole(flat)]
            + [whole(gains.shape), whole(live.shape), log, row, key, value],
            out_specs=[whole((rows, slim))] * count
            + [whole(flat), key_out, key_out, whole(flat), whole((1, width))],
            scratch_shapes=[
                square, square,
                pltpu.VMEM((parts, rows, LANES), BF16),
                pltpu.VMEM((count, rows, slim), BF16),
                pltpu.SemaphoreType.DMA((2 * blocks_in(weights),)),
            ],
        ),
        compiler_params=vmem(max(18, keys * 8 // 1024 + 12)),
        cost_estimate=cost(11),
        name="rows_late",
    )(spot, *weights, up, dq_early, dh2, h1, gains, live, logs, q2, kv, kv)
    return outs[:count], *outs[count:]


def cross_weights_kernel(masks, number, edge, spot_ref, *refs):
    w_refs, refs = refs[:number], refs[number:]
    turn, h1_ref, gain_ref, dq2_ref, c2_ref, a2_ref, keys_ref = refs[:7]
    parts, refs = refs[7:11], refs[11:]
    near_ref, far_ref, dmem_ref = refs[:3]
    w_all, dk_sum, dv_sum, done = refs[3:]
    dk = jnp.concatenate([parts[0][...], parts[1][...]], axis=1)
    dv = jnp.concatenate([parts[2][...], parts[3][...]], axis=1)
    step, steps = pl.program_id(0), pl.num_programs(0)
    width = dq2_ref.shape[1]
    half = width // 2
    columns = (edge + 2 * width, edge + 4 * width)
    copies = weight_copies(w_refs, masks, spot_ref[0], columns, w_all, done, 0)

    def put(column, values):
        values = values.astype(BF16)
        near_ref[:, column : column + width] = values[:half]
        far_ref[:, column : column + width] = values[half:]

    @pl.when(step == 0)
    def _():
        for copy in copies:
            copy.start()
        h1 = h1_ref[...]
        n2 = (h1 * norm_scale(h1) * gain_ref[1:2]).astype(BF16)
        n2_t = right_product(turn[...], n2).astype(BF16)
        put(0, product(n2_t, dq2_ref[...]))
        c2_t = right_product(turn[...], c2_ref[...]).astype(BF16)
        put(3 * width, product(c2_t, a2_ref[...]))
        dk_sum[...] = jnp.zeros_like(dk_sum)
        dv_sum[...] = jnp.zeros_like(dv_sum)

    keys_t = keys_ref[...]
    dk_sum[...] += product(keys_t, dk)
    dv_sum[...] += product(keys_t, dv)

    @pl.when(step == 0)
    def _():
        for copy in copies:
            copy.wait()

    dmem_ref[...] = (
        right_product(dk, w_all[:, :width]) + right_product(dv, w_all[:, width:])
    ).astype(BF16)

    @pl.when(step == steps - 1)
    def _():
        put(width, dk_sum[...])
        put(2 * width, dv_sum[...])


def cross_weights(weights, source, h1, gains, dq2, c2, a2, keys, grads, spot, chunk, edge, masks):
    rows, width = h1.shape
    whole = lambda shape: pl.BlockSpec(shape, lambda i, spot: (0, 0))
    part = pl.BlockSpec((chunk, width), lambda i, spot: (i, 0))
    half = ((width // 2, 4 * width), BF16)
    return pl.pallas_call(
        functools.partial(cross_weights_kernel, masks, len(weights), edge),
        out_shape=shaped([half, half, ((keys.shape[1], keys.shape[0]), BF16)], (0,)),
        grid_spec=pltpu.PrefetchScalarGridSpec(
            num_scalar_prefetch=1,
            grid=(keys.shape[1] // chunk,),
            in_specs=[HBM] * len(weights)
            + [whole(source.shape), whole((rows, width)), whole(gains.shape)]
            + [whole((rows, width))] * 3
            + [pl.BlockSpec((width, chunk), lambda i, spot: (0, i))]
            + [pl.BlockSpec((chunk, width // 2), lambda i, spot: (i, 0))] * 4,
            out_specs=[whole(half[0]), whole(half[0]), part],
            scratch_shapes=[
                pltpu.VMEM((width, 2 * width), BF16),
                pltpu.VMEM((width, width), F32),
                pltpu.VMEM((width, width), F32),
                pltpu.SemaphoreType.DMA((blocks_in(weights),)),
            ],
        ),
        compiler_params=vmem(24),
        cost_estimate=cost(10),
        name="cross_weights",
    )(spot, *weights, source, h1, gains, dq2, c2, a2, keys, *grads)


def self_backward_kernel(heads, masks, counts, spot_ref, *refs):
    seq_count, weights = counts
    up_refs, refs = refs[:seq_count], refs[seq_count:]
    x_refs, refs = refs[:3], refs[3:]
    x_list = [x_refs[0], x_refs[1], x_refs[2].at[0], x_refs[2].at[1]]
    w_refs, refs = refs[:weights], refs[weights:]
    qkv_ref, log_ref, refs = refs[0], refs[1], refs[2:]
    dn_refs, refs = refs[:2], refs[2:]
    steps = seq_masks(lax.rem(spot_ref[0], 2))
    dqkv_ref, gain_grad_ref = refs[:2]
    up_all, x_all, w_all, dn_all, dk_sum, dv_sum, done = refs[2:]
    rows = up_refs[0].shape[0]
    broad = w_all.shape[1] // 3
    slim = heads * HEAD_DIM
    me, seq = spot_ref[0], spot_ref[1]
    spots = [lax.rem(seq - k + seq_count, seq_count) for k in range(seq_count)]
    early = [
        pltpu.make_async_copy(ref, up_all.at[spots[k]], done.at[k])
        for k, ref in enumerate(up_refs)
    ]
    late = [
        pltpu.make_async_copy(ref, x_all.at[jnp.bitwise_xor(seq, mask)], done.at[seq_count + k])
        for k, (ref, mask) in enumerate(zip(x_list, steps))
    ]
    late += weight_copies(w_refs, masks, me, (0, 3 * broad), w_all, done, 2 * seq_count)
    for copy in early + late:
        copy.start()
    keys_t = transposed(qkv_ref[:, broad : 2 * broad])
    dk_sum[...] = jnp.zeros_like(dk_sum)
    dv_sum[...] = jnp.zeros_like(dv_sum)
    blank = jnp.zeros((rows, broad - slim), BF16)
    for copy in early:
        copy.wait()
    for j in range(seq_count):
        first, last = j * rows, (j + 1) * rows
        queries = qkv_ref[first:last, :broad]
        upstream = jnp.concatenate([up_all[j], blank], axis=1)
        parts = []
        own = stack_heads(queries, range(heads))
        up_own = stack_heads(upstream, range(heads))
        logs = jnp.concatenate(
            [log_ref[head : head + 1, first:last] for head in range(heads)], axis=1
        )
        inner = right_product(qkv_ref[:last, 2 * broad :], up_own)
        scores = causal_scores(qkv_ref[:last, broad : 2 * broad], own, rows)
        chance, grad = score_grads(scores, logs, inner)
        dv_sum[:last] += product(chance, up_own)
        dk_sum[:last] += product(grad, own)
        for head in range(heads):
            lines = keys_t[head * HEAD_DIM : (head + 1) * HEAD_DIM, :last]
            parts.append(product(lines, grad[:, head * rows : (head + 1) * rows]))
        rest = jnp.zeros((broad - slim, rows), F32)
        dq = jnp.concatenate(parts + [rest], axis=0).T * SCALING
        dqkv_ref[first:last, :broad] = dq.astype(BF16)
    dqkv_ref[:, broad : 2 * broad] = (dk_sum[...] * SCALING).astype(BF16)
    dqkv_ref[:, 2 * broad :] = dv_sum[...].astype(BF16)
    for copy in late:
        copy.wait()
    total = 0.0
    for j in range(seq_count):
        dn1 = right_product(dqkv_ref[j * rows : (j + 1) * rows], w_all[...])
        x = x_all[j].astype(F32)
        total = total + jnp.sum(dn1 * x * norm_scale(x), axis=0, keepdims=True)
        dn_all[j] = dn1.astype(BF16)
    gain_grad_ref[...] = total
    for k, mask in enumerate(steps):
        dn_refs[k // 2][k % 2] = dn_all[jnp.bitwise_xor(seq, mask)]


def self_backward(up_pieces, x_pieces, weights, qkv, logs, spot, heads, masks):
    count = len(up_pieces)
    rows, width = x_pieces[0].shape
    slim = up_pieces[0].shape[1]
    length, broad = qkv.shape[0], qkv.shape[1] // 3
    whole = lambda shape: pl.BlockSpec(shape, lambda i, spot: (0, 0))
    shapes = [((2, rows, width), BF16)] * 2 + [(qkv.shape, BF16), ((1, width), F32)]
    outs = pl.pallas_call(
        functools.partial(self_backward_kernel, heads, masks, (count, len(weights))),
        out_shape=shaped(shapes),
        grid_spec=pltpu.PrefetchScalarGridSpec(
            num_scalar_prefetch=1,
            grid=(1,),
            in_specs=[HBM] * (count + 3 + len(weights)) + [whole(qkv.shape), whole(logs.shape)],
            out_specs=[
                pl.BlockSpec(s, lambda i, spot, n=len(s): (0,) * n) for s, _ in shapes
            ],
            scratch_shapes=[
                pltpu.VMEM((count, rows, slim), BF16),
                pltpu.VMEM((count, rows, width), BF16),
                pltpu.VMEM((width, 3 * broad), BF16),
                pltpu.VMEM((count, rows, width), BF16),
                pltpu.VMEM((length, broad), F32),
                pltpu.VMEM((length, broad), F32),
                pltpu.SemaphoreType.DMA((2 * count + blocks_in(weights),)),
            ],
        ),
        compiler_params=vmem(18),
        cost_estimate=cost(13),
        name="self_backward",
    )(spot, *up_pieces, *x_pieces, *weights, qkv, logs)
    return outs


def self_weights_kernel(
    spot_ref, source_ref, n1_ref, dqkv_ref, dh1_ref, gain_ref, *refs
):
    a_refs, (near_ref, far_ref, a_all) = refs[:-3], refs[-3:]
    width = n1_ref.shape[1]
    half = width // 2
    count = len(a_refs)
    turn = source_ref[...]
    column = 0

    def put(values):
        nonlocal column
        values = values.astype(BF16)
        near_ref[:, column : column + values.shape[1]] = values[:half]
        far_ref[:, column : column + values.shape[1]] = values[half:]
        column += values.shape[1]

    for k, ref in enumerate(a_refs):
        a_all[lax.rem(spot_ref[1] - k + count, count)] = ref[...]
    a1 = jnp.concatenate([a_all[j] for j in range(count)], axis=1)
    c1_t = right_product(turn, dh1_ref[...].astype(BF16)).astype(BF16)
    put(product(c1_t, a1))
    put(right_product(turn, gain_ref[...].astype(BF16)))
    n1_t = right_product(turn, n1_ref[...]).astype(BF16)
    put(product(n1_t, dqkv_ref[...]))


def self_weights(source, n1, dqkv, dh1, gain_grads, a_pieces, spot):
    width = n1.shape[1]
    half = ((width // 2, width + LANES + dqkv.shape[1]), BF16)
    whole = lambda shape: pl.BlockSpec(shape, lambda i, spot: (0, 0))
    ins = [source, n1, dqkv, dh1, gain_grads, *a_pieces]
    return pl.pallas_call(
        self_weights_kernel,
        out_shape=shaped([half, half]),
        grid_spec=pltpu.PrefetchScalarGridSpec(
            num_scalar_prefetch=1,
            grid=(1,),
            in_specs=[whole(a.shape) for a in ins],
            out_specs=[whole(half[0])] * 2,
            scratch_shapes=[pltpu.VMEM((len(a_pieces),) + a_pieces[0].shape, BF16)],
        ),
        compiler_params=vmem(16),
        cost_estimate=cost(6),
        name="self_weights",
    )(spot, *ins)


def last_rows_kernel(keep_ref, one_ref, two_ref, x_ref, dh1_ref, gain_ref, out_ref):
    dn1 = keep_ref[0].astype(F32) + one_ref[0].astype(F32) + two_ref[...].astype(F32)
    x = x_ref[...].astype(F32)
    out_ref[...] = (
        dh1_ref[...] + norm_hidden_grad(x, norm_scale(x), gain_ref[0:1], dn1)
    ).astype(BF16)


def last_rows(keep, one, two, x, dh1, gains):
    return pl.pallas_call(
        last_rows_kernel,
        out_shape=jax.ShapeDtypeStruct(x.shape, BF16),
        compiler_params=vmem(8),
        cost_estimate=cost(2),
        name="last_rows",
    )(keep, one, two, x, dh1, gains)


def finish_kernel(slim, broad, spot_ref, *refs):
    sources, outs, hold = refs[:12], refs[12:-1], refs[-1]

    def total(refs, columns):
        keep, one, two = refs
        return (
            keep[0, :, columns[0] : columns[1]].astype(F32)
            + one[0, :, columns[0] : columns[1]].astype(F32)
            + two[0, :, columns[0] : columns[1]].astype(F32)
        )

    pair, down, cross, rest = sources[0:3], sources[3:6], sources[6:9], sources[9:12]
    hidden, width = outs[0].shape[1], outs[2].shape[1]
    outs[0][...] = total(pair, (0, hidden))
    outs[1][...] = total(pair, (hidden, 2 * hidden))
    outs[2][...] = total(down, (0, width))
    for i in range(4):
        outs[3 + i][...] = total(cross, (i * width, (i + 1) * width))
    outs[7][...] = total(rest, (0, width))
    edge = width
    outs[-1][...] = total(rest, (edge, edge + LANES))
    edge = edge + LANES
    far_edge = edge + 3 * broad
    keep, one, two = rest
    steps = [jnp.bitwise_xor(spot_ref[1], m) for m in seq_masks(lax.rem(spot_ref[0], 2))]
    hold[steps[0]] = keep[0, :, edge:far_edge].astype(F32)
    hold[steps[1]] = two[0, :, edge:far_edge].astype(F32)
    hold[steps[2]] = one[0, :, edge:far_edge].astype(F32)
    hold[steps[3]] = two[0, :, far_edge : far_edge + 3 * broad].astype(F32)
    for i in range(3):
        outs[8 + i][...] = jnp.concatenate(
            [hold[j][:, i * broad : i * broad + slim] for j in range(hold.shape[0])], axis=1
        )


def finish(pair, down, cross, rest, spot, hidden, slim, broad):
    share, feed_share, width = pair[0].shape[1], down[0].shape[1], down[0].shape[2]
    count = lax.axis_size("seq")
    shapes = (
        [(share, hidden)] * 2 + [(feed_share, width)] + [(share, width)] * 8 + [(share, LANES)]
    )
    whole = lambda shape: pl.BlockSpec(shape, lambda i, spot: (0,) * len(shape))
    flat = [*pair, *down, *cross, *rest]
    return pl.pallas_call(
        functools.partial(finish_kernel, slim, broad),
        out_shape=shaped([(shape, F32) for shape in shapes]),
        grid_spec=pltpu.PrefetchScalarGridSpec(
            num_scalar_prefetch=1,
            grid=(1,),
            in_specs=[whole(a.shape) for a in flat],
            out_specs=[whole(shape) for shape in shapes],
            scratch_shapes=[pltpu.VMEM((count, share, 3 * broad), F32)],
        ),
        compiler_params=vmem(12),
        cost_estimate=cost(3),
        name="finish",
    )(spot, *flat)


def local(
    hidden_in,
    memory,
    cotangent,
    norm_self,
    query_self,
    key_self,
    value_self,
    output_self,
    norm_cross,
    query_cross,
    key_cross,
    value_cross,
    output_cross,
    norm_feed,
    gate_weight,
    up_weight,
    down_weight,
    block_counts,
    memory_tail,
    row_example,
):
    mem_count, seq_count = lax.axis_size("mem"), lax.axis_size("seq")
    mem_place, seq_place = lax.axis_index("mem"), lax.axis_index("seq")
    rows, width = hidden_in.shape[1], hidden_in.shape[2]
    inner = HEADS * HEAD_DIM
    near = HEADS // seq_count
    slim = near * HEAD_DIM
    broad = -(-(slim + 8) // LANES) * LANES
    share = norm_self.shape[0]
    hidden_width = gate_weight.shape[1]
    spot = jnp.stack([mem_place, seq_place]).astype(jnp.int32)
    scalars = jnp.concatenate([block_counts, memory_tail, row_example])
    masks = slot_masks(mem_count)
    mask_array = mem_masks()
    block = width // mem_count
    column = jnp.arange(width, dtype=jnp.int32)
    source = block * (mem_place ^ jnp.repeat(mask_array, block)) + column % block
    source = (column[None, :] == source[:, None]).astype(BF16)
    gain_stack = jnp.stack([norm_self, norm_cross, norm_feed], axis=0)
    x_own = hidden_in[0]
    edge = 3 * broad
    turns = mem_count.bit_length() - 2
    flat = lambda stacked: stacked.reshape((1, -1) + stacked.shape[2:])

    with jax.named_scope("gather"):
        own, two, one, second, blocks, live = prepare(
            (query_self, key_self, value_self, output_self, query_cross)
            + (key_cross, value_cross, output_cross, gate_weight, up_weight),
            gain_stack, memory, scalars, spot, slim, broad,
        )
        live = live.reshape(-1, 1)
        stay, go = part_blocks(blocks, 0)
        two, arrived = swap_seq(two, 0), swap_mem(go, 0)
        c3 = cotangent[0]
        c3_other = swap_mem(c3, turns)
        blocks, x_in, down_in = join_blocks(stay, arrived), x_own, down_weight
        three = swap_seq(jnp.stack([one, two[:, edge:]]), 1)
        second_a = swap_seq(second, 0)
        for turn in range(1, turns):
            stay, go = part_blocks(blocks, turn)
            blocks = join_blocks(stay, swap_mem(go, turn))
        three, blocks, second_a, second, x_in, down_in, source = settle(
            three, blocks, second_a, second, x_in, down_in, source
        )
        plain = [(0, 0, 0, edge), (1, 0, edge, 5 * width)]
        skipping = [(0, 0, 0, edge), (1, 0, 2 * edge, 5 * width)]
        heads, outer = place(
            [own[None], two[None], three],
            seq_places(),
            [edge, 5 * width],
            [plain, skipping, plain],
        )
        heads, outer = [flat(heads)], [flat(outer)]
        heads.append(swap_mem(heads[0], 0))
        outer.append(swap_mem(outer[0], 0))
        stay, go = part_blocks(blocks, turns)
        keys_in = join_blocks(stay, swap_mem(go, turns)).reshape(-1, width)
        second_b = swap_seq(jnp.stack([second, second_a]), 1)
        heads, outer, keys_in, second_a, second_b, second, x_in, down_in = settle(
            heads, outer, keys_in, second_a, second_b, second, x_in, down_in
        )
        x_a = swap_seq(x_in, 0)
        for turn in range(1, turns):
            heads.append(swap_mem(join(heads), turn))
            outer.append(swap_mem(join(outer), turn))
        both = [flat(stack_seq([second[None], second_a[None], second_b]))]
        x_a, x_in, both, down_in = settle(x_a, x_in, both, down_in)
        x_b = swap_seq(jnp.stack([x_in, x_a]), 1)
        both.append(swap_mem(both[0], 0))
        down_a = swap_seq(down_in, 0)
        heads, outer, both, x_b, x_a, x_in, down_a, down_in = settle(
            heads, outer, both, x_b, x_a, x_in, down_a, down_in
        )
        heads, outer = join(heads), join(outer)
        heads = [heads, swap_mem(heads, turns)]
        outer = [outer, swap_mem(outer, turns)]
        for turn in range(1, turns):
            both.append(swap_mem(join(both), turn))
        down_b = swap_seq(jnp.stack([down_in, down_a]), 1)
        heads, x_in, x_a, x_b = settle(heads, x_in, x_a, x_b)
        packed_heads = spread_weight(heads)

    key_chunk = width

    with jax.named_scope("forward"):
        x_pieces = [x_in, x_a, x_b]
        o_pieces, n1, qkv, gains, self_logs = self_rows(
            x_pieces, packed_heads, spot, near, broad, masks
        )
        o_pieces, gains, outer, down_a, down_b, down_in = settle(
            o_pieces, gains, outer, down_a, down_b, down_in
        )
        packed = spread_weight(outer)
        downs = [flat(stack_seq([down_in[None], down_a[None], down_b]))]
        a_pieces = send_seq(o_pieces)
        kv2, keys_t = key_values(source, keys_in, packed, spot, key_chunk, 2 * width, masks)
        downs.append(swap_mem(downs[0], 0))
        a_pieces, kv2, downs, keys_in, both = settle(a_pieces, kv2, downs, keys_in, both)
        q2, a2_early, h1, logs_first = rows_first(
            a_pieces, packed, x_own, gains, live, kv2, spot, 0, masks
        )
        both = join(both)
        both_other = swap_mem(both, turns)
        for turn in range(1, turns):
            downs.append(swap_mem(join(downs), turn))
        others = [swap_mem(downs[0], turns), swap_mem(downs[1], turns)]
        a2_early, h1, q2, both, both_other, others = settle(
            a2_early, h1, q2, both, both_other, others
        )
        a2, h2, logs_second = rows_second(
            packed, h1, a2_early, live, q2, kv2, spot, 0, masks
        )
        h2, both_other, both, downs, others = settle(h2, both_other, both, downs, others)
        others += [swap_mem(piece, turns) for piece in downs[2:]]
        both = [w.reshape(-1, 2 * hidden_width) for w in (both, both_other)]
        unit = hidden_width // mem_count
        narrow = unit % LANES != 0
        if narrow:
            unit = 2 * LANES
            downs = [stack_mem(downs + others).reshape(-1, unit, width)]
            feed_order = jnp.arange(hidden_width // unit, dtype=jnp.int32)
        else:
            feed_order = mem_place ^ mask_array
            downs = downs + others
        layer_out, dh2, c2, gain_feed_terms, bundle, act_near, n3_near = feed(
            feed_order, h2, c3, gains, source, both, downs
        )

    with jax.named_scope("backward"):
        bundle_other = swap_mem(bundle, turns)
        up, dq_early, dk_early, dv_early = rows_early(
            packed, c2, live, logs_first, q2, kv2, spot, 0, masks
        )
        bundle_other, up, dq_early = settle(bundle_other, up, dq_early)
        if narrow:
            acts = jnp.concatenate([act_near, bundle[:, 2 * hidden_width : -(width // 2)]], axis=1)
            g_down = left_product(acts, c3).astype(BF16).reshape(mem_count, -1, width)
            g_down = place([g_down], jnp.argsort(mem_place ^ mask_array)).reshape(2, -1, width)
            normed = jnp.concatenate([n3_near, bundle[:, -(width // 2) :]], axis=1)
            g_both = jnp.stack(
                [
                    left_product(normed, bundle[:, k * hidden_width : (k + 1) * hidden_width])
                    for k in range(2)
                ]
            ).astype(BF16)
            feeding = Scatter(g_both[:, : width // 2], g_both[:, width // 2 :])
            downing = Scatter(g_down[0], g_down[1])
            for s in (feeding, downing):
                s.move()
            advance([feeding, downing], spot)
        else:
            g_feed = feed_weights(bundle, bundle_other, act_near, n3_near, c3, c3_other)
            feeding, downing = Scatter(*g_feed[0:2], 1), Scatter(*g_feed[2:4], 1)
        feeding.sent, up = settle(feeding.sent, up)
        feeding.move()
        da_pieces, dq2, dk_late, dv_late, dh1, gain_cross_terms = rows_late(
            packed, up, dq_early, dh2, h1, gains, live, logs_second, q2, kv2, spot, 0, masks
        )
        da_pieces, dq2 = settle(da_pieces, dq2)
        da_pieces = send_seq(da_pieces)
        *g_cross, dmem = cross_weights(
            packed, source, h1, gains, dq2, c2, a2, keys_t,
            [dk_early, dk_late, dv_early, dv_late], spot, key_chunk, 0, masks,
        )
        crossing = Scatter(*g_cross)
        advance([feeding], spot)
        da_pieces, crossing.sent, feeding.sent, downing.sent, dmem = settle(
            da_pieces, crossing.sent, feeding.sent, downing.sent, dmem
        )
        crossing.move()
        feeding.move()
        keep_dn, send_dn, dqkv, gain_self_terms = self_backward(
            da_pieces, x_pieces, packed_heads, qkv, self_logs, spot, near, masks
        )
        dmem = dmem.reshape(mem_count, -1, width)
        stay, go = part_blocks(dmem, turns)
        dmem = join_blocks(stay, swap_mem(go, turns))
        crossing.terms, feeding.terms, downing.sent, keep_dn, send_dn, dqkv, dmem = settle(
            crossing.terms, feeding.terms, downing.sent, keep_dn, send_dn, dqkv, dmem
        )
        one_dn = swap_seq(send_dn, 1)
        downing.move()
        stay, go = part_blocks(dmem, 0)
        dmem = join_blocks(stay, swap_mem(go, 0))
        while feeding.left > 0:
            advance([feeding], spot)
            feeding.move()
        ends = [advance([feeding], spot), None, None, None]
        advance([crossing], spot)
        gain_grads = jnp.concatenate(
            [gain_self_terms, gain_cross_terms, gain_feed_terms, jnp.zeros((LANES - 3, width), F32)]
        )
        g_self = self_weights(source, n1, dqkv, dh1, gain_grads, a_pieces, spot)
        selfing = Scatter(*g_self)
        crossing.move()
        one_dn, keep_dn, downing.terms, dmem, ends[0], selfing.sent = settle(
            one_dn, keep_dn, downing.terms, dmem, ends[0], selfing.sent
        )
        two_dn = swap_seq(onward(keep_dn, one_dn)[0], 0)
        one_both = swap_seq(ends[0][1], 1)
        selfing.move()
        for turn in range(1, turns):
            stay, go = part_blocks(dmem, turn)
            dmem = join_blocks(stay, swap_mem(go, turn))
        while downing.left > 0:
            advance([downing], spot)
            downing.move()
        ends[1] = advance([downing], spot)
        while crossing.left > 0:
            advance([crossing], spot)
            crossing.move()
        while selfing.left > 0:
            advance([selfing], spot)
            selfing.move()
        two_both = swap_seq(onward(ends[0][0], one_both), 0)
        mem_keep, mem_send = pick_slots(dmem, memory.shape[0], scalars, spot)
        mem_one = swap_seq(mem_send, 1)
        one_down = swap_seq(ends[1][1], 1)
        ends[2] = advance([crossing], spot)
        one_cross = swap_seq(ends[2][1], 1)
        mem_one = after(mem_one, ends[2][1])
        mem_two = swap_seq(onward(mem_keep, mem_one), 0)
        ends[3] = advance([selfing], spot)
        one_self = swap_seq(ends[3][1], 1)
        one_down = after(one_down, ends[2][1])
        two_down = swap_seq(onward(ends[1][0], one_down), 0)
        two_cross = swap_seq(onward(ends[2][0], one_cross), 0)
        two_self = swap_seq(onward(ends[3][0], one_self, width + LANES), 0)
        hidden_grad = last_rows(keep_dn, one_dn, after(two_dn, ends[3][1]), x_own, dh1, gains)
        per = mem_two.shape[0]
        memory_grad = total_of([mem_keep[:per], mem_one[:per], mem_two]).astype(BF16)
        *finals, gain_finals = finish(
            (ends[0][0], one_both, two_both),
            (ends[1][0], one_down, two_down),
            (ends[2][0], one_cross, two_cross),
            (ends[3][0], one_self, two_self),
            spot, hidden_width, slim, broad,
        )
    g_gate, g_up, g_down, g_q2, g_k2, g_v2, g_o2, g_o1, g_q1, g_k1, g_v1 = finals
    return (
        layer_out[None],
        hidden_grad[None],
        memory_grad,
        gain_finals[:, 0],
        g_q1,
        g_k1,
        g_v1,
        g_o1,
        gain_finals[:, 1],
        g_q2,
        g_k2,
        g_v2,
        g_o2,
        gain_finals[:, 2],
        g_gate,
        g_up,
        g_down,
    )


def solution(mesh):
    every = P(("mem", "seq"), None)
    gain = P(("mem", "seq"))
    in_specs = (
        (P("mem", "seq", None), P(None, "mem", None), P("mem", "seq", None), gain)
        + (every,) * 4
        + (gain,)
        + (every,) * 4
        + (gain,)
        + (every,) * 3
        + (P(),) * 3
    )
    out_specs = (
        (P("mem", "seq", None), P("mem", "seq", None), P("seq", "mem", None), gain)
        + (every,) * 4
        + (gain,)
        + (every,) * 4
        + (gain,)
        + (every,) * 3
    )
    return jax.shard_map(local, mesh=mesh, in_specs=in_specs, out_specs=out_specs, check_vma=False)
```

```python
import functools

import jax
import jax.numpy as jnp
from jax import lax
from jax.experimental import pallas as pl
from jax.experimental.pallas import tpu as pltpu
from jax.sharding import PartitionSpec as P

HEADS = 12
HEAD_DIM = 64
SCALING = HEAD_DIM ** (-0.5)
LANES = 128
MASKED = -1e30
F32 = jnp.float32
BF16 = jnp.bfloat16


def product(left, right):
    return jnp.dot(left, right, preferred_element_type=F32)


def left_product(left, right):
    return lax.dot_general(left, right, (((0,), (0,)), ((), ())), preferred_element_type=F32)


def right_product(left, right):
    return lax.dot_general(left, right, (((1,), (1,)), ((), ())), preferred_element_type=F32)


def gelu_tanh(values):
    return (
        0.5
        * values
        * (1.0 + jnp.tanh(0.7978845608028654 * (values + 0.044715 * values * values * values)))
    )


def gated_unit(gate, upper):
    return gelu_tanh(gate) * upper


def norm_scale(hidden):
    return lax.rsqrt(jnp.mean(hidden * hidden, axis=-1, keepdims=True) + 1e-06)


def norm_hidden_grad(hidden, scale, gain, upstream):
    lifted = upstream * gain
    return scale * lifted - hidden * (scale * scale * scale) * jnp.mean(
        lifted * hidden, axis=-1, keepdims=True
    )


def shift(values, axis, step):
    size = lax.axis_size(axis)
    return lax.ppermute(values, axis, [(i, (i + step) % size) for i in range(size)])


def swap(values, axis, mask):
    size = lax.axis_size(axis)
    return lax.ppermute(values, axis, [(i, i ^ mask) for i in range(size)])


def place_kernel(counts, maps, places, *refs):
    sources = refs[: len(counts)]
    targets, done = refs[len(counts) : -1], refs[-1]
    copies = []
    number = 0
    for source, count, moves in zip(sources, counts, maps):
        for block in range(count):
            for goal, to, start, width in moves:
                part, target = source.at[block], targets[goal].at[places[number]]
                if len(moves) > 1 or width != source.shape[2]:
                    part = source.at[block, :, start : start + width]
                    target = targets[goal].at[places[number], :, to : to + width]
                copies.append(pltpu.make_async_copy(part, target, done.at[len(copies)]))
            number += 1
    for copy in copies:
        copy.start()
    for copy in copies:
        copy.wait()


def place(pieces, places, widths=None, maps=None):
    counts = [piece.shape[0] for piece in pieces]
    total = sum(counts)
    _, height, width = pieces[0].shape
    widths = widths or [width]
    if maps is None:
        plain = [(i, 0, sum(widths[:i]), w) for i, w in enumerate(widths)]
        maps = [plain] * len(pieces)
    copies = sum(count * len(moves) for count, moves in zip(counts, maps))
    outs = [((total, height, w), pieces[0].dtype) for w in widths]
    size = total * height * sum(widths) * 2
    result = pl.pallas_call(
        functools.partial(place_kernel, counts, maps),
        out_shape=shaped(outs),
        grid_spec=pltpu.PrefetchScalarGridSpec(
            num_scalar_prefetch=1,
            grid=(1,),
            in_specs=[HBM] * len(pieces),
            out_specs=[
                pl.BlockSpec((total, height, w), lambda i, places: (0, 0, 0)) for w in widths
            ],
            scratch_shapes=[pltpu.SemaphoreType.DMA((copies,))],
        ),
        compiler_params=pltpu.CompilerParams(vmem_limit_bytes=3 * size + (4 << 20)),
        cost_estimate=cost(1 + size / 1e6),
        name="place",
    )(places.astype(jnp.int32), *pieces)
    return result[0] if len(widths) == 1 else result


def after(values, *tokens):
    return lax.optimization_barrier((values,) + tokens)[0]


def settle(*values):
    return lax.optimization_barrier(values)


def seq_masks(parity):
    return [0, 1 + parity, 2 - parity, 3]


def swap_seq(values, turn):
    mem, seq = lax.axis_size("mem"), lax.axis_size("seq")
    pairs = []
    for m in range(mem):
        mask = 1 + (m + turn) % 2
        pairs += [(m * seq + s, m * seq + (s ^ mask)) for s in range(seq)]
    return lax.ppermute(values, ("mem", "seq"), pairs)


def seq_places():
    parity = lax.axis_index("mem") % 2
    return lax.axis_index("seq") ^ jnp.stack(seq_masks(parity)).astype(jnp.int32)


def stack_seq(pieces, widths=None):
    return place(pieces, seq_places(), widths)


def send_seq(pieces):
    return [pieces[0]] + [shift(piece, "seq", k) for k, piece in enumerate(pieces) if k]


def total_of(pieces):
    return functools.reduce(jnp.add, [piece.astype(F32) for piece in pieces])


def join(blocks):
    return blocks[0] if len(blocks) == 1 else jnp.concatenate(blocks, axis=0)


def orders(count):
    bits = list(range(1, count.bit_length() - 1))
    return bits, bits[::-1]


def slot_masks(count):
    half = count // 2
    low = [
        [sum(((s >> j) & 1) << bit for j, bit in enumerate(order)) for s in range(half)]
        for order in orders(count)
    ]
    return low[0] + [m | 1 for m in low[1]], low[1] + [m | 1 for m in low[0]]


def swap_mem(values, turn):
    count = lax.axis_size("mem")
    pairs = []
    for i in range(count):
        order = [*orders(count)[i % 2], 0]
        pairs.append((i, i ^ (1 << order[turn])))
    return lax.ppermute(values, "mem", pairs)


def mem_masks():
    count = lax.axis_size("mem")
    even, odd = slot_masks(count)
    return jnp.where(
        lax.axis_index("mem") % 2 == 0, jnp.array(even, jnp.int32), jnp.array(odd, jnp.int32)
    )


def stack_mem(halves, widths=None):
    return place(halves, lax.axis_index("mem") ^ mem_masks(), widths)


def spread_weight(halves):
    if halves[0].shape[1] % 16 == 0:
        return list(halves)
    stacked = stack_mem(halves)
    return [stacked.reshape(1, -1, stacked.shape[-1])]


def add_low(left, right):
    return (left.astype(F32) + right.astype(F32)).astype(BF16)


def total_kernel(plans, spot_ref, *refs):
    terms = sum(number for number, _ in plans)
    sources, refs = list(refs[:terms]), refs[terms:]
    outs, holds = list(refs[: len(refs) - len(plans)]), refs[len(refs) - len(plans) :]
    column = 0
    for (number, ends), hold in zip(plans, holds):
        mine, sources = sources[:number], sources[number:]
        groups, rows, width = mine[0].shape
        for g in range(groups):
            total = mine[0][g].astype(F32)
            for ref in mine[1:]:
                total = total + ref[g].astype(F32)
            if not ends:
                outs[0][g] = total.astype(BF16)
                continue
            count = hold.shape[0]
            unit = rows // count
            for j in range(count):
                hold[j] = total[j * unit : (j + 1) * unit]
            for k, mask in enumerate(seq_masks(lax.rem(spot_ref[0], 2))):
                piece = hold[jnp.bitwise_xor(spot_ref[1], mask)].astype(BF16)
                outs[-2 + k // 2][k % 2, :, column : column + width] = piece
            column += width
        if not ends:
            del outs[:1]


class Scatter:
    def __init__(self, kept, sent, taken=0):
        self.terms = [kept if kept.ndim == 3 else kept[None]]
        self.sent = sent if sent.ndim == 3 else sent[None]
        self.left = (lax.axis_size("mem") // 2).bit_length() - 1 - taken
        self.rows = self.terms[0].shape[1]

    def move(self):
        self.terms.append(swap_mem(self.sent, self.left))

    def hold(self):
        return [self.terms, self.sent]

    def take(self, held):
        self.terms, self.sent = held


def advance(scatters, spot):
    count = lax.axis_size("seq")
    plans, shapes, specs, flat, holds = [], [], [], [], []
    ended, exact = 0, True
    whole = lambda shape: pl.BlockSpec(shape, lambda i, spot: (0, 0, 0))
    for s in scatters:
        ends = s.left == 0
        groups, _, width = s.terms[0].shape
        rows = s.rows if ends else s.rows // 2
        exact = exact and rows // (count if ends else 1) % 8 == 0
        plans.append((len(s.terms), ends))
        part = (groups, rows, width)
        if ends:
            specs += [whole(part)] * len(s.terms)
            ended += groups * width
            unit = rows // count
            holds.append(pltpu.VMEM((count, unit, width), F32))
        else:
            specs += [pl.BlockSpec(part, lambda i, spot: (0, 1, 0))] * len(s.terms)
            shapes.append(part)
            holds.append(pltpu.VMEM((1, 8, 128), F32))
        flat += s.terms
    if ended:
        shapes += [(2, unit, ended)] * 2
    if exact:
        size = sum(spec.block_shape[0] * spec.block_shape[1] * spec.block_shape[2] for spec in specs)
        outs = pl.pallas_call(
            functools.partial(total_kernel, plans),
            out_shape=shaped([(shape, BF16) for shape in shapes]),
            grid_spec=pltpu.PrefetchScalarGridSpec(
                num_scalar_prefetch=1,
                grid=(1,),
                in_specs=specs,
                out_specs=[whole(shape) for shape in shapes],
                scratch_shapes=holds,
            ),
            compiler_params=vmem(6 + (size * 8 >> 20)),
            cost_estimate=cost(1 + size / 1e6),
            name="total",
        )(spot, *(far(*flat) if size > 1 << 20 else flat))
        outs = list(outs)
    else:
        outs, ends_at = [], []
        for s in scatters:
            low = 0 if s.left == 0 else s.rows // 2
            high = s.rows if s.left == 0 else 2 * low
            total = total_of([term[:, low:high] for term in s.terms]).astype(BF16)
            if s.left:
                outs.append(total)
                continue
            groups, rows, width = total.shape
            blocks = total.reshape(groups, count, rows // count, width)
            ends_at.append(jnp.take(jnp.concatenate(list(blocks), axis=2), seq_places(), axis=0))
        if ends_at:
            blocks = jnp.concatenate(ends_at, axis=2)
            outs += [blocks[:2], blocks[2:]]
    for s in scatters:
        if s.left:
            s.sent, s.rows = outs.pop(0), s.rows // 2
        s.left -= 1
    return outs or None


def onward(kept, arrived, summed=None):
    half = kept.shape[0] // 2
    mine, theirs = kept[half:], arrived[half:]
    if summed is None:
        return add_low(mine, theirs)
    return jnp.concatenate(
        [add_low(mine[..., :summed], theirs[..., :summed]), mine[..., summed:], theirs[..., summed:]],
        axis=-1,
    )


def part_blocks(blocks, turn):
    count = blocks.shape[0]
    parts = blocks.reshape((count >> (turn + 1), 2, 1 << turn) + blocks.shape[1:])
    return parts[:, 0], parts[:, 1]


def join_blocks(stay, arrived):
    joined = jnp.stack([stay, arrived], axis=1)
    return joined.reshape((-1,) + joined.shape[3:])


HBM = pl.BlockSpec(memory_space=pltpu.HBM)


def far(*arrays):
    return [pltpu.with_memory_space_constraint(array, pltpu.HBM) for array in arrays]


def shaped(shapes, distant=()):
    return [
        jax.ShapeDtypeStruct(shape, dtype)
        for i, (shape, dtype) in enumerate(shapes)
    ]


def vmem(mebibytes):
    return pltpu.CompilerParams(vmem_limit_bytes=mebibytes << 20)


def cost(microseconds):
    return pl.CostEstimate(
        flops=int(microseconds * 1.1e9), bytes_accessed=0, transcendentals=0
    )


def run(copies):
    for copy in copies:
        copy.start()
    for copy in copies:
        copy.wait()


def prepare_kernel(
    slim, broad, spot_ref, counts_ref, tails_ref, rows_ref,
    q_ref, k_ref, v_ref, o1_ref, q2_ref, k2_ref, v2_ref, o2_ref, gate_ref, up_ref,
    gain_ref, memory_ref,
    own_ref, two_ref, one_ref, second_ref, blocks_ref, live_ref,
    turn, triple, held, counts, tails, rows, done,
):
    mem_count, height = blocks_ref.shape[0], memory_ref.shape[1]
    share, width = q_ref.shape
    half = mem_count // 2
    me, seq = spot_ref[0], spot_ref[1]
    parity = lax.rem(me, 2)
    moves = [(counts_ref, counts), (tails_ref, tails), (rows_ref, rows)]
    moves += [(ref, triple.at[i]) for i, ref in enumerate((q_ref, k_ref, v_ref))]
    moves += [(memory_ref, held)]
    for ref, base in ((own_ref, 3 * broad), (one_ref, 3 * broad), (two_ref, 6 * broad)):
        for i, source in enumerate((o1_ref, q2_ref, k2_ref, v2_ref, o2_ref)):
            moves += [(source, ref.at[:, base + i * width : base + (i + 1) * width])]
    hidden = gate_ref.shape[1]
    moves += [(gate_ref, second_ref.at[:, :hidden]), (up_ref, second_ref.at[:, hidden:])]
    copies = [pltpu.make_async_copy(a, b, done.at[i]) for i, (a, b) in enumerate(moves)]
    for copy in copies:
        copy.start()
    turn[...] = jnp.zeros_like(turn)
    turn[0:3, 0:share] = gain_ref[...].astype(F32)
    gains = turn[...].T[:share]
    lane = lax.broadcasted_iota(jnp.int32, (share, broad - slim), 1)
    extra = jnp.zeros((share, broad - slim), F32)
    for i in range(3):
        extra = jnp.where(lane == i, gains[:, i : i + 1], extra)
    extra = extra.astype(BF16)
    blank = jnp.zeros((share, broad - slim), BF16)
    token = lax.broadcasted_iota(jnp.int32, (height, 1), 0)

    def first_block(example):
        return lax.fori_loop(
            0, example, lambda i, total: total + counts[i], jnp.int32(0)
        )

    for copy in copies[:3]:
        copy.wait()
    mine = rows[me]
    mine_start = first_block(mine)
    mine_end = mine_start + counts[mine]

    for copy in copies[3:7]:
        copy.wait()

    order, contrary = orders(mem_count)

    def one(t, carry):
        low = lax.rem(t, half)
        first, second = jnp.int32(0), jnp.int32(0)
        for j in range(len(order)):
            bit = lax.rem(lax.shift_right_logical(low, jnp.int32(j)), 2)
            first = first + bit * (1 << order[j])
            second = second + bit * (1 << contrary[j])
        flip = parity == 1
        first, second = jnp.where(flip, second, first), jnp.where(flip, first, second)
        upper = t >= half
        goal = jnp.bitwise_xor(me, jnp.where(upper, first + 1, first))
        start = first_block(rows[goal])
        block = start + lax.rem(me - lax.rem(start, mem_count) + mem_count, mem_count)
        slot = jnp.minimum(block // mem_count, memory_ref.shape[0] - 1)
        blocks_ref[t] = held[slot]
        holder = jnp.bitwise_xor(me, jnp.where(upper, second + 1, first))
        block = mine_start + lax.rem(
            holder - lax.rem(mine_start, mem_count) + mem_count, mem_count
        )
        bound = jnp.where(block == mine_end - 1, tails[mine], height)
        bound = jnp.where(block < mine_end, bound, 0)
        live_ref[t] = jnp.where(token < bound, 0.0, MASKED)
        return carry

    lax.fori_loop(0, mem_count, one, 0)
    seq_steps = seq_masks(parity)
    for ref, base, mask in (
        (own_ref, 0, seq_steps[0]),
        (two_ref, 0, seq_steps[1]),
        (one_ref, 0, seq_steps[2]),
        (two_ref, 1, seq_steps[3]),
    ):
        goal = jnp.bitwise_xor(seq, mask)
        for i in range(3):
            weight = triple[i].astype(F32)
            chosen = weight[:, :slim]
            for j in range(1, width // slim):
                chosen = jnp.where(goal == j, weight[:, j * slim : (j + 1) * slim], chosen)
            start = (3 * base + i) * broad
            ref[:, start : start + broad] = jnp.concatenate(
                [chosen.astype(BF16), blank if i else extra], axis=1
            )
    for copy in copies[7:]:
        copy.wait()


def prepare(weights, gains, memory, tables, spot, slim, broad):
    mem_count = lax.axis_size("mem")
    share, width = weights[0].shape
    first = 3 * broad + 5 * width
    second = sum(w.shape[1] for w in weights[8:])
    height = memory.shape[1]
    whole = lambda shape: pl.BlockSpec(shape, lambda *_: (0,) * len(shape))
    outs = [
        ((share, first), BF16),
        ((share, first + 3 * broad), BF16),
        ((share, first), BF16),
        ((share, second), BF16),
        ((mem_count, height, width), BF16),
        ((mem_count, height, 1), F32),
    ]
    return pl.pallas_call(
        functools.partial(prepare_kernel, slim, broad),
        out_shape=shaped(outs),
        grid_spec=pltpu.PrefetchScalarGridSpec(
            num_scalar_prefetch=1,
            grid=(1,),
            in_specs=[HBM] * (3 + len(weights)) + [whole(gains.shape), HBM],
            out_specs=[whole(shape) for shape, _ in outs],
            scratch_shapes=[
                pltpu.VMEM((8, 128), F32),
                pltpu.VMEM((3, share, width), BF16),
                pltpu.VMEM(memory.shape, BF16),
                pltpu.SMEM((mem_count,), jnp.int32),
                pltpu.SMEM((mem_count,), jnp.int32),
                pltpu.SMEM((mem_count,), jnp.int32),
                pltpu.SemaphoreType.DMA((3 + 4 + 15 + 2,)),
            ],
        ),
        compiler_params=vmem(16 + 3 * mem_count // 8),
        cost_estimate=cost(3),
        name="prepare",
    )(spot, *far(*tables, *weights), gains, *far(memory))


def slots_kernel(per, scalars_ref, spot_ref, blocks_ref, keep_ref, send_ref, done):
    mem_count = blocks_ref.shape[0]
    me, seq = spot_ref[0], spot_ref[1]
    parity = lax.rem(me, 2)
    copies = []
    for k, mask in enumerate(seq_masks(parity)):
        for s in range(per):
            slot = jnp.bitwise_xor(seq, mask) * per + s
            block = slot * mem_count + me

            def scan(i, carry):
                end, owner = carry
                end = end + scalars_ref[i]
                return end, owner + jnp.where(end <= block, 1, 0)

            _, owner = lax.fori_loop(0, mem_count, scan, (jnp.int32(0), jnp.int32(0)))
            row = lax.fori_loop(
                0,
                mem_count,
                lambda i, r: jnp.where(scalars_ref[2 * mem_count + i] == owner, i, r),
                jnp.int32(0),
            )
            gap = jnp.bitwise_xor(row, me)
            bit = lambda b: lax.rem(lax.shift_right_logical(gap, jnp.int32(b)), 2)
            spots = [
                sum(bit(b) * (1 << j) for j, b in enumerate(order)) for order in orders(mem_count)
            ]
            at = jnp.where(parity == 1, spots[1], spots[0]) + bit(0) * (mem_count // 2)
            copies.append(
                pltpu.make_async_copy(
                    blocks_ref.at[at],
                    (keep_ref, send_ref)[k // 2].at[k % 2 * per + s],
                    done.at[len(copies)],
                )
            )
    for copy in copies:
        copy.start()
    for copy in copies:
        copy.wait()


def pick_slots(blocks, slots, scalars, spot):
    per = slots // lax.axis_size("seq")
    shape = (2 * per,) + blocks.shape[1:]
    return pl.pallas_call(
        functools.partial(slots_kernel, per),
        out_shape=shaped([(shape, BF16)] * 2),
        grid_spec=pltpu.PrefetchScalarGridSpec(
            num_scalar_prefetch=2,
            grid=(1,),
            in_specs=[HBM],
            out_specs=[pl.BlockSpec(shape, lambda *_: (0, 0, 0))] * 2,
            scratch_shapes=[pltpu.SemaphoreType.DMA((slots,))],
        ),
        compiler_params=vmem(8),
        cost_estimate=cost(2),
        name="pick_slots",
    )(scalars, spot, blocks)


PAIR = 2


def feed_kernel(
    order_ref, h2_ref, c3_ref, gain_ref, turn,
    *refs,
):
    sides, refs = refs[: 4 * PAIR], refs[4 * PAIR :]
    down_refs, refs = refs[:-14], refs[-14:]
    out_ref, dh2_ref, c2_ref, gain_grad_ref, bundle_ref, act_near_ref, n3_near_ref = refs[:7]
    n3_rel, total, dn3, gate_w, up_w, down_w, act_all = refs[7:]
    step, steps = pl.program_id(0), pl.num_programs(0)
    half, unit = sides[0].shape
    width = h2_ref.shape[1]
    hidden = unit * steps * PAIR
    slim = width // 2

    @pl.when(step == 0)
    def _():
        h2 = h2_ref[...]
        n3 = (h2 * norm_scale(h2) * gain_ref[2:3]).astype(BF16)
        rel = right_product(n3, turn[...]).astype(BF16)
        n3_rel[...] = rel
        n3_near_ref[...] = rel[:, :slim]
        bundle_ref[:, 2 * hidden + hidden // 2 :] = rel[:, slim:]
        total[...] = jnp.zeros_like(total)
        dn3[...] = jnp.zeros_like(dn3)

    base = 0
    for ref in down_refs:
        number = ref.shape[0]
        for block in range(number):

            @pl.when(step == (base + block) // PAIR)
            def _(ref=ref, block=block, at=(base + block) % PAIR):
                down_w[at * unit : (at + 1) * unit] = ref[block]

        base += number
    for n in range(PAIR):
        part = slice(n * unit, (n + 1) * unit)
        for k, target in enumerate((gate_w, up_w)):
            target[:half, part] = sides[4 * n + 2 * k][...]
            target[half:, part] = sides[4 * n + 2 * k + 1][...]
    down = down_w[...]
    n3, c3 = n3_rel[...], c3_ref[...]
    gate = product(n3, gate_w[...])
    upper = product(n3, up_w[...])
    dact = right_product(c3, down)
    inner = 0.7978845608028654 * (gate + 0.044715 * gate * gate * gate)
    bent = jnp.tanh(inner)
    gelu = 0.5 * gate * (1.0 + bent)
    slope = 0.5 * (1.0 + bent) + 0.5 * gate * (1.0 - bent * bent) * (
        0.7978845608028654 * (1.0 + 3.0 * 0.044715 * gate * gate)
    )
    act = (gelu * upper).astype(BF16)
    dgate = (dact * upper * slope).astype(BF16)
    dupper = (dact * gelu).astype(BF16)
    total[...] += product(act, down)
    for n in range(PAIR):
        part = slice(n * unit, (n + 1) * unit)
        act_all[step * PAIR + n] = act[:, part]
        column = pl.multiple_of(order_ref[step * PAIR + n] * unit, LANES)
        bundle_ref[:, pl.ds(column, unit)] = dgate[:, part]
        bundle_ref[:, pl.ds(pl.multiple_of(hidden + column, LANES), unit)] = dupper[:, part]
    dn3[...] += right_product(dgate, gate_w[...]) + right_product(dupper, up_w[...])

    @pl.when(step == steps - 1)
    def _():
        middle = act_all.shape[0] // 2
        for t in range(middle):
            act_near_ref[:, t * unit : (t + 1) * unit] = act_all[t]
            first = 2 * hidden + t * unit
            bundle_ref[:, first : first + unit] = act_all[middle + t]
        h2 = h2_ref[...]
        out_ref[...] = (h2 + total[...]).astype(BF16)
        high = dn3[...].astype(BF16)
        rest = (dn3[...] - high.astype(F32)).astype(BF16)
        upstream = product(high, turn[...]) + product(rest, turn[...])
        scale = norm_scale(h2)
        dh2 = c3_ref[...].astype(F32) + norm_hidden_grad(h2, scale, gain_ref[2:3], upstream)
        dh2_ref[...] = dh2
        c2_ref[...] = dh2.astype(BF16)
        gain_grad_ref[...] = jnp.sum(upstream * h2 * scale, axis=0, keepdims=True)


def feed(order, h2, c3, gains, source, both, down):
    rows, width = h2.shape
    half, hidden = both[0].shape
    hidden = hidden // 2
    steps = order.shape[0]
    unit = hidden // steps
    whole = lambda shape: pl.BlockSpec(shape, lambda i, o: (0, 0))
    sides = []
    for n in range(PAIR):
        sides += [pl.BlockSpec((half, unit), lambda i, o, n=n: (0, o[i * PAIR + n]))] * 2
        sides += [pl.BlockSpec((half, unit), lambda i, o, n=n: (0, o[i * PAIR + n] + steps))] * 2
    flat = (rows, width)
    shapes = [
        (flat, BF16),
        (flat, F32),
        (flat, BF16),
        ((1, width), F32),
        ((rows, 2 * hidden + hidden // 2 + width // 2), BF16),
        ((rows, hidden // 2), BF16),
        ((rows, width // 2), BF16),
    ]
    return pl.pallas_call(
        feed_kernel,
        out_shape=shaped(shapes, (0,)),
        grid_spec=pltpu.PrefetchScalarGridSpec(
            num_scalar_prefetch=1,
            grid=(steps // PAIR,),
            in_specs=[whole(flat)] * 2
            + [whole(gains.shape), whole((width, width))]
            + sides
            + [pl.BlockSpec(w.shape, lambda i, o: (0, 0, 0)) for w in down],
            out_specs=[whole(shape) for shape, _ in shapes],
            scratch_shapes=[
                pltpu.VMEM(flat, BF16),
                pltpu.VMEM(flat, F32),
                pltpu.VMEM(flat, F32),
                pltpu.VMEM((2 * half, PAIR * unit), BF16),
                pltpu.VMEM((2 * half, PAIR * unit), BF16),
                pltpu.VMEM((PAIR * unit, width), BF16),
                pltpu.VMEM((steps, rows, unit), BF16),
            ],
        ),
        compiler_params=vmem(28),
        cost_estimate=cost(13),
        name="feed",
    )(order, h2, *far(c3), gains, source, *far(*both * (2 * PAIR)), *down)


def feed_weights_kernel(
    own_ref, other_ref, act_ref, n3_ref, c3_ref, c3_other_ref,
    both_keep_ref, both_send_ref, down_keep_ref, down_send_ref,
):
    hidden = both_keep_ref.shape[2]
    units = act_ref.shape[1]
    quarter, third = both_keep_ref.shape[1], down_keep_ref.shape[0]
    edge = 2 * hidden + units
    mine = transposed(n3_ref[...])
    theirs = transposed(other_ref[:, edge:])
    step = hidden // 2
    for first in range(0, 2 * hidden, step):
        grad = product(mine, own_ref[:, first : first + step])
        grad = grad + product(theirs, other_ref[:, first : first + step])
        grad = grad.astype(BF16)
        part, column = first // hidden, first % hidden
        both_keep_ref[part, :, column : column + step] = grad[:quarter]
        both_send_ref[part, :, column : column + step] = grad[quarter:]
    c3, c3_other = c3_ref[...], c3_other_ref[...]
    for k, ref in enumerate((down_keep_ref, down_send_ref)):
        first = k * third
        mine = transposed(act_ref[:, first : first + third])
        theirs = transposed(other_ref[:, 2 * hidden + first : 2 * hidden + first + third])
        ref[...] = (product(mine, c3) + product(theirs, c3_other)).astype(BF16)


def feed_weights(own, other, act, n3, c3, c3_other):
    rows, width = c3.shape
    units = act.shape[1]
    hidden = 2 * units
    pair = ((2, width // 4, hidden), BF16)
    single = ((units // 2, width), BF16)
    return pl.pallas_call(
        feed_weights_kernel,
        out_shape=shaped([pair, pair, single, single]),
        compiler_params=vmem(24),
        cost_estimate=cost(5),
        name="feed_weights",
    )(own, other, act, n3, c3, c3_other)


def head_mask(shape, head):
    return lax.broadcasted_iota(jnp.int32, shape, 1) // HEAD_DIM == head


def pick_head(values, head):
    return jnp.where(head_mask(values.shape, head), values, jnp.zeros_like(values))


def stack_heads(values, heads):
    return jnp.concatenate([pick_head(values, head) for head in heads], axis=0)


def head_groups(keys, heads):
    return [list(range(heads))] if keys <= 2048 else [[head] for head in range(heads)]


def transposed(values):
    return values.astype(F32).T.astype(values.dtype)


LOG2E = 1.4426950408889634
SHRINK = SCALING * LOG2E


def soft_parts(scores, axis=0):
    peak = jnp.max(scores, axis=0, keepdims=True)
    powers = jnp.exp2(scores - peak)
    total = jnp.sum(powers, axis=0, keepdims=True)
    return powers, 1.0 / total, peak + jnp.log2(total)


def causal_scores(keys, queries, count):
    scores = right_product(keys, queries) * SHRINK
    last = scores.shape[0] - count
    corner = scores[last:]
    key_place = lax.broadcasted_iota(jnp.int32, corner.shape, 0)
    query_place = lax.rem(lax.broadcasted_iota(jnp.int32, corner.shape, 1), count)
    corner = jnp.where(key_place <= query_place, corner, MASKED)
    return corner if last == 0 else jnp.concatenate([scores[:last], corner], axis=0)


def cross_scores(keys, queries, bias):
    return right_product(keys, queries) * SHRINK + bias


def score_grads(scores, logs, inner):
    chance = jnp.exp2(scores - logs)
    spread = jnp.sum(chance * inner, axis=0, keepdims=True)
    return chance.astype(BF16), (chance * (inner - spread)).astype(BF16)


def weight_copies(refs, masks, me, columns, target, done, base):
    copies = []
    for ref in refs:
        for block in range(ref.shape[0]):
            number = len(copies)
            spot = 0
            if len(refs) > 1:
                mask = masks[0][number]
                if masks[1][number] != mask:
                    mask = jnp.where(lax.rem(me, 2) == 1, masks[1][number], mask)
                spot = pl.multiple_of(jnp.bitwise_xor(me, mask) * ref.shape[1], 16)
            copies.append(
                pltpu.make_async_copy(
                    ref.at[block, :, columns[0] : columns[1]],
                    target.at[pl.ds(spot, ref.shape[1])],
                    done.at[base + number],
                )
            )
    return copies


def blocks_in(refs):
    return sum(ref.shape[0] for ref in refs)


def self_rows_kernel(heads, masks, counts, spot_ref, *refs):
    seq_count, weights = counts
    x_refs, refs = refs[:3], refs[3:]
    x_list = [x_refs[0], x_refs[1], x_refs[2].at[0], x_refs[2].at[1]]
    w_refs, refs = refs[:weights], refs[weights:]
    o_refs, refs = refs[:seq_count], refs[seq_count:]
    n1_ref, qkv_ref, gain_ref, log_ref, x_all, w_all, o_all, done = refs
    rows, width = x_refs[0].shape
    broad = w_all.shape[1] // 3
    me, seq = spot_ref[0], spot_ref[1]
    copies = weight_copies(w_refs, masks, me, (0, 3 * broad), w_all, done, 0)
    base = len(copies)
    copies += [
        pltpu.make_async_copy(ref, x_all.at[jnp.bitwise_xor(seq, mask)], done.at[base + k])
        for k, (ref, mask) in enumerate(zip(x_list, seq_masks(lax.rem(me, 2))))
    ]
    run(copies)
    slim = heads * HEAD_DIM
    edge = slim // LANES * LANES
    gains = w_all[:, edge : edge + LANES].astype(F32).T[slim - edge : slim - edge + 8]
    gain_ref[...] = gains
    for j in range(seq_count):
        x = x_all[j].astype(F32)
        n1 = (x * norm_scale(x) * gains[0:1]).astype(BF16)
        n1_ref[j * rows : (j + 1) * rows] = n1
        qkv_ref[j * rows : (j + 1) * rows] = product(n1, w_all[...]).astype(BF16)
    values_t = transposed(qkv_ref[:, 2 * broad :])
    for j in range(seq_count):
        first, last = j * rows, (j + 1) * rows
        queries = qkv_ref[first:last, :broad]
        parts = []
        scores = causal_scores(
            qkv_ref[:last, broad : 2 * broad], stack_heads(queries, range(heads)), rows
        )
        powers, inverse, logs = soft_parts(scores)
        powers = powers.astype(BF16)
        for head in range(heads):
            part = slice(head * rows, (head + 1) * rows)
            log_ref[head : head + 1, first:last] = logs[:, part]
            lines = values_t[head * HEAD_DIM : (head + 1) * HEAD_DIM, :last]
            parts.append(product(lines, powers[:, part]) * inverse[:, part])
        o_all[j] = jnp.concatenate(parts, axis=0).T.astype(BF16)
    for k, ref in enumerate(o_refs):
        ref[...] = o_all[lax.rem(seq + k, seq_count)]


def self_rows(x_pieces, weights, spot, heads, broad, masks):
    count = lax.axis_size("seq")
    rows, width = x_pieces[0].shape
    length, slim = rows * count, heads * HEAD_DIM
    whole = lambda shape: pl.BlockSpec(shape, lambda i, spot: (0, 0))
    shapes = [((rows, slim), BF16)] * count + [
        ((length, width), BF16),
        ((length, 3 * broad), BF16),
        ((8, width), F32),
        ((8, length), F32),
    ]
    outs = pl.pallas_call(
        functools.partial(self_rows_kernel, heads, masks, (count, len(weights))),
        out_shape=shaped(shapes, (count, count + 1, count + 3)),
        grid_spec=pltpu.PrefetchScalarGridSpec(
            num_scalar_prefetch=1,
            grid=(1,),
            in_specs=[HBM] * (3 + len(weights)),
            out_specs=[whole(s) for s, _ in shapes],
            scratch_shapes=[
                pltpu.VMEM((count, rows, width), BF16),
                pltpu.VMEM((width, 3 * broad), BF16),
                pltpu.VMEM((count, rows, slim), BF16),
                pltpu.SemaphoreType.DMA((blocks_in(weights) + count,)),
            ],
        ),
        compiler_params=vmem(14),
        cost_estimate=cost(10),
        name="self_rows",
    )(spot, *x_pieces, *weights)
    return outs[:count], *outs[count:]


def key_values_kernel(masks, number, edge, spot_ref, turn_ref, keys_ref, *refs):
    w_refs, (out_ref, keys_t_ref, w_all, done) = refs[:number], refs[number:]

    @pl.when(pl.program_id(0) == 0)
    def _():
        columns = (edge, edge + w_all.shape[1])
        run(weight_copies(w_refs, masks, spot_ref[0], columns, w_all, done, 0))

    keys_t_ref[...] = right_product(turn_ref[...], keys_ref[...]).astype(BF16)
    out_ref[...] = product(keys_ref[...], w_all[...]).astype(BF16)


def key_values(turn, keys, weights, spot, chunk, edge, masks):
    width = keys.shape[1]
    columns = 2 * width
    return pl.pallas_call(
        functools.partial(key_values_kernel, masks, len(weights), edge),
        out_shape=shaped([((keys.shape[0], columns), BF16), ((width, keys.shape[0]), BF16)]),
        grid_spec=pltpu.PrefetchScalarGridSpec(
            num_scalar_prefetch=1,
            grid=(keys.shape[0] // chunk,),
            in_specs=[
                pl.BlockSpec((width, width), lambda i, spot: (0, 0)),
                pl.BlockSpec((chunk, width), lambda i, spot: (i, 0)),
            ]
            + [HBM] * len(weights),
            out_specs=[
                pl.BlockSpec((chunk, columns), lambda i, spot: (i, 0)),
                pl.BlockSpec((width, chunk), lambda i, spot: (0, i)),
            ],
            scratch_shapes=[
                pltpu.VMEM((width, columns), BF16),
                pltpu.SemaphoreType.DMA((blocks_in(weights),)),
            ],
        ),
        compiler_params=vmem(12),
        cost_estimate=cost(4),
        name="key_values",
    )(spot, turn, keys, *weights)


def cross_attend(queries, keys, values, live, log_ref):
    values_t = transposed(values)
    pieces = []
    rows = queries.shape[0]
    for group in head_groups(keys.shape[0], LANES // HEAD_DIM):
        powers, inverse, logs = soft_parts(cross_scores(keys, stack_heads(queries, group), live))
        powers = powers.astype(BF16)
        for n, head in enumerate(group):
            part = slice(n * rows, (n + 1) * rows)
            log_ref[0, head : head + 1] = logs[:, part]
            lines = values_t[head * HEAD_DIM : (head + 1) * HEAD_DIM]
            pieces.append(product(lines, powers[:, part]) * inverse[:, part])
    return jnp.concatenate(pieces, axis=0).T.astype(BF16)


def rows_first_kernel(masks, counts, edge, spot_ref, *refs):
    seq_count, weights = counts
    a_refs, refs = refs[:seq_count], refs[seq_count:]
    w_refs, refs = refs[:weights], refs[weights:]
    x_ref, gain_ref, live_ref, k_ref, v_ref = refs[:5]
    q2_ref, a2_ref, h1_ref, log_ref = refs[5:9]
    a_all, w_o1, w_q2, q_parts, done = refs[9:]
    step = pl.program_id(0)
    me, seq = spot_ref[0], spot_ref[1]
    width = x_ref.shape[1]

    @pl.when(step == 0)
    def _():
        copies = [
            pltpu.make_async_copy(
                ref, a_all.at[lax.rem(seq - k + seq_count, seq_count)], done.at[k]
            )
            for k, ref in enumerate(a_refs)
        ]
        copies += weight_copies(w_refs, masks, me, (edge, edge + width), w_o1, done, seq_count)
        later = weight_copies(
            w_refs, masks, me, (edge + width, edge + 2 * width), w_q2, done, len(copies)
        )
        for copy in copies + later:
            copy.start()
        for copy in copies:
            copy.wait()
        a1 = jnp.concatenate([a_all[j] for j in range(seq_count)], axis=1)
        h1 = x_ref[...].astype(F32) + right_product(a1, w_o1[...])
        h1_ref[...] = h1
        n2 = (h1 * norm_scale(h1) * gain_ref[1:2]).astype(BF16)
        for copy in later:
            copy.wait()
        q2 = product(n2, w_q2[...]).astype(BF16)
        q2_ref[...] = q2
        for i in range(q_parts.shape[0]):
            q_parts[i] = q2[:, i * LANES : (i + 1) * LANES]

    a2_ref[...] = cross_attend(q_parts[step], k_ref[...], v_ref[...], live_ref[...], log_ref)


def rows_second_kernel(masks, weights, edge, spot_ref, *refs):
    w_refs, refs = refs[:weights], refs[weights:]
    h1_ref, early_ref, live_ref, q_ref, k_ref, v_ref, a2_ref, h2_ref, log_ref = refs[:9]
    w_o2, o_parts, done = refs[9:]
    step, parts = pl.program_id(0), o_parts.shape[0]
    width = h1_ref.shape[1]
    columns = (edge + 4 * width, edge + 5 * width)
    copies = weight_copies(w_refs, masks, spot_ref[0], columns, w_o2, done, 0)

    @pl.when(step == 0)
    def _():
        for copy in copies:
            copy.start()

    o_parts[step] = cross_attend(q_ref[...], k_ref[...], v_ref[...], live_ref[...], log_ref)

    @pl.when(step == parts - 1)
    def _():
        for copy in copies:
            copy.wait()
        a2 = jnp.concatenate([early_ref[...]] + [o_parts[i] for i in range(parts)], axis=1)
        a2_ref[...] = a2
        h2_ref[...] = h1_ref[...] + right_product(a2, w_o2[...])


def rows_first(a_pieces, weights, x, gains, live, kv, spot, edge, masks):
    count = len(a_pieces)
    rows, width = x.shape
    keys = kv.shape[0]
    parts = width // LANES
    flat = (rows, width)
    whole = lambda shape: pl.BlockSpec(shape, lambda i, spot: (0, 0))
    _, row, key, value = rows_specs(rows, keys, width, 0)
    log = pl.BlockSpec((1, 8, rows), lambda i, spot: (i, 0, 0))
    shapes = [
        (flat, BF16), ((rows, width // 2), BF16), (flat, F32), ((parts // 2, 8, rows), F32)
    ]
    square = pltpu.VMEM((width, width), BF16)
    return pl.pallas_call(
        functools.partial(rows_first_kernel, masks, (count, len(weights)), edge),
        out_shape=shaped(shapes),
        grid_spec=pltpu.PrefetchScalarGridSpec(
            num_scalar_prefetch=1,
            grid=(parts // 2,),
            in_specs=[HBM] * (count + len(weights))
            + [whole(flat), whole(gains.shape), whole(live.shape), key, value],
            out_specs=[whole(flat), row, whole(flat), log],
            scratch_shapes=[
                pltpu.VMEM((count,) + a_pieces[0].shape, BF16),
                square, square,
                pltpu.VMEM((parts, rows, LANES), BF16),
                pltpu.SemaphoreType.DMA((count + 2 * blocks_in(weights),)),
            ],
        ),
        compiler_params=vmem(max(16, keys * 8 // 1024 + 8)),
        cost_estimate=cost(7),
        name="rows_first",
    )(spot, *a_pieces, *weights, x, gains, live, kv, kv)


def rows_second(weights, h1, early, live, q2, kv, spot, edge, masks):
    rows, width = h1.shape
    keys = kv.shape[0]
    parts = width // LANES // 2
    flat = (rows, width)
    whole = lambda shape: pl.BlockSpec(shape, lambda i, spot: (0, 0))
    _, row, key, value = rows_specs(rows, keys, width, parts)
    log = pl.BlockSpec((1, 8, rows), lambda i, spot: (i, 0, 0))
    return pl.pallas_call(
        functools.partial(rows_second_kernel, masks, len(weights), edge),
        out_shape=shaped([(flat, BF16), (flat, F32), ((parts, 8, rows), F32)]),
        grid_spec=pltpu.PrefetchScalarGridSpec(
            num_scalar_prefetch=1,
            grid=(parts,),
            in_specs=[HBM] * len(weights)
            + [whole(flat), whole(early.shape), whole(live.shape), row, key, value],
            out_specs=[whole(flat), whole(flat), log],
            scratch_shapes=[
                pltpu.VMEM((width, width), BF16),
                pltpu.VMEM((parts, rows, LANES), BF16),
                pltpu.SemaphoreType.DMA((blocks_in(weights),)),
            ],
        ),
        compiler_params=vmem(max(14, keys * 8 // 1024 + 8)),
        cost_estimate=cost(6),
        name="rows_second",
    )(spot, *weights, h1, early, live, q2, kv, kv)


def cross_backward(queries, upstream, live, keys, values, logs):
    keys_t = transposed(keys)
    pieces, dk, dv = [], 0.0, 0.0
    rows = queries.shape[0]
    for group in head_groups(keys.shape[0], LANES // HEAD_DIM):
        own = stack_heads(queries, group)
        up_own = stack_heads(upstream, group)
        inner = right_product(values, up_own)
        log = jnp.concatenate([logs[head : head + 1] for head in group], axis=1)
        chance, grad = score_grads(cross_scores(keys, own, live), log, inner)
        dv = dv + product(chance, up_own)
        dk = dk + product(grad, own)
        for n, head in enumerate(group):
            lines = keys_t[head * HEAD_DIM : (head + 1) * HEAD_DIM]
            pieces.append(product(lines, grad[:, n * rows : (n + 1) * rows]))
    dq = jnp.concatenate(pieces, axis=0).T * SCALING
    return dq.astype(BF16), (dk * SCALING).astype(BF16), dv.astype(BF16)


def rows_early_kernel(masks, weights, edge, spot_ref, *refs):
    w_refs, refs = refs[:weights], refs[weights:]
    c2_ref, live_ref, log_ref, q_ref, k_ref, v_ref, up_ref, dq_ref, dk_ref, dv_ref = refs[:10]
    w_o2, up_parts, done = refs[10:]
    width = c2_ref.shape[1]

    @pl.when(pl.program_id(0) == 0)
    def _():
        columns = (edge + 4 * width, edge + 5 * width)
        run(weight_copies(w_refs, masks, spot_ref[0], columns, w_o2, done, 0))
        up = product(c2_ref[...], w_o2[...]).astype(BF16)
        up_ref[...] = up
        for i in range(up_parts.shape[0]):
            up_parts[i] = up[:, i * LANES : (i + 1) * LANES]

    dq_ref[...], dk_ref[...], dv_ref[...] = cross_backward(
        q_ref[...], up_parts[pl.program_id(0)], live_ref[...], k_ref[...], v_ref[...], log_ref[0]
    )


def rows_late_kernel(masks, counts, edge, spot_ref, *refs):
    seq_count, weights = counts
    w_refs, refs = refs[:weights], refs[weights:]
    up_ref, dq_early_ref, dh2_ref, h1_ref, gain_ref, live_ref, log_ref, q_ref, k_ref, v_ref = refs[:10]
    da_refs, refs = refs[10 : 10 + seq_count], refs[10 + seq_count :]
    dq2_ref, dk_ref, dv_ref, dh1_ref, gain_grad_ref = refs[:5]
    w_o1, w_q2, dq_parts, da_all, done = refs[5:]
    step = pl.program_id(0)
    me, seq = spot_ref[0], spot_ref[1]
    width = dh2_ref.shape[1]
    parts = dq_parts.shape[0]
    copies = weight_copies(
        w_refs, masks, me, (edge + width, edge + 2 * width), w_q2, done, 0
    )
    copies += weight_copies(w_refs, masks, me, (edge, edge + width), w_o1, done, len(copies))

    @pl.when(step == 0)
    def _():
        for copy in copies:
            copy.start()

    dq_parts[step], dk_ref[...], dv_ref[...] = cross_backward(
        q_ref[...], up_ref[...], live_ref[...], k_ref[...], v_ref[...], log_ref[0]
    )

    @pl.when(step == parts - 1)
    def _():
        for copy in copies:
            copy.wait()
        dq2 = jnp.concatenate([dq_early_ref[...]] + [dq_parts[i] for i in range(parts)], axis=1)
        dq2_ref[...] = dq2
        dn2 = right_product(dq2, w_q2[...])
        h1 = h1_ref[...]
        scale = norm_scale(h1)
        dh1 = dh2_ref[...] + norm_hidden_grad(h1, scale, gain_ref[1:2], dn2)
        dh1_ref[...] = dh1
        gain_grad_ref[...] = jnp.sum(dn2 * h1 * scale, axis=0, keepdims=True)
        c1 = dh1.astype(BF16)
        up = product(c1, w_o1[...])
        slim = da_all.shape[2]
        for j in range(seq_count):
            da_all[j] = up[:, j * slim : (j + 1) * slim].astype(BF16)
        for k, ref in enumerate(da_refs):
            ref[...] = da_all[lax.rem(seq + k, seq_count)]


def rows_specs(rows, keys, width, start):
    parts = width // LANES
    row = pl.BlockSpec((rows, LANES), lambda i, spot: (0, i + start))
    key = pl.BlockSpec((keys, LANES), lambda i, spot: (0, i + start))
    value = pl.BlockSpec((keys, LANES), lambda i, spot: (0, i + start + parts))
    log = pl.BlockSpec((1, 8, rows), lambda i, spot: (i, 0, 0))
    return log, row, key, value


def rows_early(weights, c2, live, logs, q2, kv, spot, edge, masks):
    rows, width = c2.shape
    keys = kv.shape[0]
    parts = width // LANES // 2
    whole = lambda shape: pl.BlockSpec(shape, lambda i, spot: (0, 0))
    log, row, key, value = rows_specs(rows, keys, width, 0)
    half = width // 2
    shapes = [((rows, width), BF16), ((rows, half), BF16)] + [((keys, half), BF16)] * 2
    return pl.pallas_call(
        functools.partial(rows_early_kernel, masks, len(weights), edge),
        out_shape=shaped(shapes, (2, 3)),
        grid_spec=pltpu.PrefetchScalarGridSpec(
            num_scalar_prefetch=1,
            grid=(parts,),
            in_specs=[HBM] * len(weights)
            + [whole((rows, width)), whole(live.shape), log, row, key, value],
            out_specs=[whole((rows, width)), row, key, key],
            scratch_shapes=[
                pltpu.VMEM((width, width), BF16),
                pltpu.VMEM((2 * parts, rows, LANES), BF16),
                pltpu.SemaphoreType.DMA((blocks_in(weights),)),
            ],
        ),
        compiler_params=vmem(max(12, keys * 8 // 1024 + 12)),
        cost_estimate=cost(10),
        name="rows_early",
    )(spot, *weights, c2, live, logs, q2, kv, kv)


def rows_late(weights, up, dq_early, dh2, h1, gains, live, logs, q2, kv, spot, edge, masks):
    count = lax.axis_size("seq")
    rows, width = dh2.shape
    keys = kv.shape[0]
    parts = width // LANES // 2
    slim = width // count
    flat = (rows, width)
    half = width // 2
    whole = lambda shape: pl.BlockSpec(shape, lambda i, spot: (0, 0))
    log, row, key, value = rows_specs(rows, keys, width, parts)
    key_out = pl.BlockSpec((keys, LANES), lambda i, spot: (0, i))
    shapes = [((rows, slim), BF16)] * count + [
        (flat, BF16), ((keys, half), BF16), ((keys, half), BF16),
        (flat, F32), ((1, width), F32),
    ]
    square = pltpu.VMEM((width, width), BF16)
    outs = pl.pallas_call(
        functools.partial(rows_late_kernel, masks, (count, len(weights)), edge),
        out_shape=shaped(shapes, range(count, count + 6)),
        grid_spec=pltpu.PrefetchScalarGridSpec(
            num_scalar_prefetch=1,
            grid=(parts,),
            in_specs=[HBM] * len(weights)
            + [row, whole((rows, half)), whole(flat), whole(flat)]
            + [whole(gains.shape), whole(live.shape), log, row, key, value],
            out_specs=[whole((rows, slim))] * count
            + [whole(flat), key_out, key_out, whole(flat), whole((1, width))],
            scratch_shapes=[
                square, square,
                pltpu.VMEM((parts, rows, LANES), BF16),
                pltpu.VMEM((count, rows, slim), BF16),
                pltpu.SemaphoreType.DMA((2 * blocks_in(weights),)),
            ],
        ),
        compiler_params=vmem(max(18, keys * 8 // 1024 + 12)),
        cost_estimate=cost(11),
        name="rows_late",
    )(spot, *weights, up, dq_early, dh2, h1, gains, live, logs, q2, kv, kv)
    return outs[:count], *outs[count:]


def cross_weights_kernel(masks, number, edge, spot_ref, *refs):
    w_refs, refs = refs[:number], refs[number:]
    turn, h1_ref, gain_ref, dq2_ref, c2_ref, a2_ref, keys_ref = refs[:7]
    parts, refs = refs[7:11], refs[11:]
    near_ref, far_ref, dmem_ref = refs[:3]
    w_all, dk_sum, dv_sum, done = refs[3:]
    dk = jnp.concatenate([parts[0][...], parts[1][...]], axis=1)
    dv = jnp.concatenate([parts[2][...], parts[3][...]], axis=1)
    step, steps = pl.program_id(0), pl.num_programs(0)
    width = dq2_ref.shape[1]
    half = width // 2
    columns = (edge + 2 * width, edge + 4 * width)
    copies = weight_copies(w_refs, masks, spot_ref[0], columns, w_all, done, 0)

    def put(column, values):
        values = values.astype(BF16)
        near_ref[:, column : column + width] = values[:half]
        far_ref[:, column : column + width] = values[half:]

    @pl.when(step == 0)
    def _():
        for copy in copies:
            copy.start()
        h1 = h1_ref[...]
        n2 = (h1 * norm_scale(h1) * gain_ref[1:2]).astype(BF16)
        n2_t = right_product(turn[...], n2).astype(BF16)
        put(0, product(n2_t, dq2_ref[...]))
        c2_t = right_product(turn[...], c2_ref[...]).astype(BF16)
        put(3 * width, product(c2_t, a2_ref[...]))
        dk_sum[...] = jnp.zeros_like(dk_sum)
        dv_sum[...] = jnp.zeros_like(dv_sum)

    keys_t = keys_ref[...]
    dk_sum[...] += product(keys_t, dk)
    dv_sum[...] += product(keys_t, dv)

    @pl.when(step == 0)
    def _():
        for copy in copies:
            copy.wait()

    dmem_ref[...] = (
        right_product(dk, w_all[:, :width]) + right_product(dv, w_all[:, width:])
    ).astype(BF16)

    @pl.when(step == steps - 1)
    def _():
        put(width, dk_sum[...])
        put(2 * width, dv_sum[...])


def cross_weights(weights, source, h1, gains, dq2, c2, a2, keys, grads, spot, chunk, edge, masks):
    rows, width = h1.shape
    whole = lambda shape: pl.BlockSpec(shape, lambda i, spot: (0, 0))
    part = pl.BlockSpec((chunk, width), lambda i, spot: (i, 0))
    half = ((width // 2, 4 * width), BF16)
    return pl.pallas_call(
        functools.partial(cross_weights_kernel, masks, len(weights), edge),
        out_shape=shaped([half, half, ((keys.shape[1], keys.shape[0]), BF16)], (0,)),
        grid_spec=pltpu.PrefetchScalarGridSpec(
            num_scalar_prefetch=1,
            grid=(keys.shape[1] // chunk,),
            in_specs=[HBM] * len(weights)
            + [whole(source.shape), whole((rows, width)), whole(gains.shape)]
            + [whole((rows, width))] * 3
            + [pl.BlockSpec((width, chunk), lambda i, spot: (0, i))]
            + [pl.BlockSpec((chunk, width // 2), lambda i, spot: (i, 0))] * 4,
            out_specs=[whole(half[0]), whole(half[0]), part],
            scratch_shapes=[
                pltpu.VMEM((width, 2 * width), BF16),
                pltpu.VMEM((width, width), F32),
                pltpu.VMEM((width, width), F32),
                pltpu.SemaphoreType.DMA((blocks_in(weights),)),
            ],
        ),
        compiler_params=vmem(24),
        cost_estimate=cost(10),
        name="cross_weights",
    )(spot, *weights, source, h1, gains, dq2, c2, a2, keys, *grads)


def self_backward_kernel(heads, masks, counts, spot_ref, *refs):
    seq_count, weights = counts
    up_refs, refs = refs[:seq_count], refs[seq_count:]
    x_refs, refs = refs[:3], refs[3:]
    x_list = [x_refs[0], x_refs[1], x_refs[2].at[0], x_refs[2].at[1]]
    w_refs, refs = refs[:weights], refs[weights:]
    qkv_ref, log_ref, refs = refs[0], refs[1], refs[2:]
    dn_refs, refs = refs[:2], refs[2:]
    steps = seq_masks(lax.rem(spot_ref[0], 2))
    dqkv_ref, gain_grad_ref = refs[:2]
    up_all, x_all, w_all, dn_all, dk_sum, dv_sum, done = refs[2:]
    rows = up_refs[0].shape[0]
    broad = w_all.shape[1] // 3
    slim = heads * HEAD_DIM
    me, seq = spot_ref[0], spot_ref[1]
    spots = [lax.rem(seq - k + seq_count, seq_count) for k in range(seq_count)]
    early = [
        pltpu.make_async_copy(ref, up_all.at[spots[k]], done.at[k])
        for k, ref in enumerate(up_refs)
    ]
    late = [
        pltpu.make_async_copy(ref, x_all.at[jnp.bitwise_xor(seq, mask)], done.at[seq_count + k])
        for k, (ref, mask) in enumerate(zip(x_list, steps))
    ]
    late += weight_copies(w_refs, masks, me, (0, 3 * broad), w_all, done, 2 * seq_count)
    for copy in early + late:
        copy.start()
    keys_t = transposed(qkv_ref[:, broad : 2 * broad])
    dk_sum[...] = jnp.zeros_like(dk_sum)
    dv_sum[...] = jnp.zeros_like(dv_sum)
    blank = jnp.zeros((rows, broad - slim), BF16)
    for copy in early:
        copy.wait()
    for j in range(seq_count):
        first, last = j * rows, (j + 1) * rows
        queries = qkv_ref[first:last, :broad]
        upstream = jnp.concatenate([up_all[j], blank], axis=1)
        parts = []
        own = stack_heads(queries, range(heads))
        up_own = stack_heads(upstream, range(heads))
        logs = jnp.concatenate(
            [log_ref[head : head + 1, first:last] for head in range(heads)], axis=1
        )
        inner = right_product(qkv_ref[:last, 2 * broad :], up_own)
        scores = causal_scores(qkv_ref[:last, broad : 2 * broad], own, rows)
        chance, grad = score_grads(scores, logs, inner)
        dv_sum[:last] += product(chance, up_own)
        dk_sum[:last] += product(grad, own)
        for head in range(heads):
            lines = keys_t[head * HEAD_DIM : (head + 1) * HEAD_DIM, :last]
            parts.append(product(lines, grad[:, head * rows : (head + 1) * rows]))
        rest = jnp.zeros((broad - slim, rows), F32)
        dq = jnp.concatenate(parts + [rest], axis=0).T * SCALING
        dqkv_ref[first:last, :broad] = dq.astype(BF16)
    dqkv_ref[:, broad : 2 * broad] = (dk_sum[...] * SCALING).astype(BF16)
    dqkv_ref[:, 2 * broad :] = dv_sum[...].astype(BF16)
    for copy in late:
        copy.wait()
    total = 0.0
    for j in range(seq_count):
        dn1 = right_product(dqkv_ref[j * rows : (j + 1) * rows], w_all[...])
        x = x_all[j].astype(F32)
        total = total + jnp.sum(dn1 * x * norm_scale(x), axis=0, keepdims=True)
        dn_all[j] = dn1.astype(BF16)
    gain_grad_ref[...] = total
    for k, mask in enumerate(steps):
        dn_refs[k // 2][k % 2] = dn_all[jnp.bitwise_xor(seq, mask)]


def self_backward(up_pieces, x_pieces, weights, qkv, logs, spot, heads, masks):
    count = len(up_pieces)
    rows, width = x_pieces[0].shape
    slim = up_pieces[0].shape[1]
    length, broad = qkv.shape[0], qkv.shape[1] // 3
    whole = lambda shape: pl.BlockSpec(shape, lambda i, spot: (0, 0))
    shapes = [((2, rows, width), BF16)] * 2 + [(qkv.shape, BF16), ((1, width), F32)]
    outs = pl.pallas_call(
        functools.partial(self_backward_kernel, heads, masks, (count, len(weights))),
        out_shape=shaped(shapes),
        grid_spec=pltpu.PrefetchScalarGridSpec(
            num_scalar_prefetch=1,
            grid=(1,),
            in_specs=[HBM] * (count + 3 + len(weights)) + [whole(qkv.shape), whole(logs.shape)],
            out_specs=[
                pl.BlockSpec(s, lambda i, spot, n=len(s): (0,) * n) for s, _ in shapes
            ],
            scratch_shapes=[
                pltpu.VMEM((count, rows, slim), BF16),
                pltpu.VMEM((count, rows, width), BF16),
                pltpu.VMEM((width, 3 * broad), BF16),
                pltpu.VMEM((count, rows, width), BF16),
                pltpu.VMEM((length, broad), F32),
                pltpu.VMEM((length, broad), F32),
                pltpu.SemaphoreType.DMA((2 * count + blocks_in(weights),)),
            ],
        ),
        compiler_params=vmem(18),
        cost_estimate=cost(13),
        name="self_backward",
    )(spot, *up_pieces, *x_pieces, *weights, qkv, logs)
    return outs


def self_weights_kernel(
    spot_ref, source_ref, n1_ref, dqkv_ref, dh1_ref, gain_ref, *refs
):
    a_refs, (near_ref, far_ref, a_all) = refs[:-3], refs[-3:]
    width = n1_ref.shape[1]
    half = width // 2
    count = len(a_refs)
    turn = source_ref[...]
    column = 0

    def put(values):
        nonlocal column
        values = values.astype(BF16)
        near_ref[:, column : column + values.shape[1]] = values[:half]
        far_ref[:, column : column + values.shape[1]] = values[half:]
        column += values.shape[1]

    for k, ref in enumerate(a_refs):
        a_all[lax.rem(spot_ref[1] - k + count, count)] = ref[...]
    a1 = jnp.concatenate([a_all[j] for j in range(count)], axis=1)
    c1_t = right_product(turn, dh1_ref[...].astype(BF16)).astype(BF16)
    put(product(c1_t, a1))
    put(right_product(turn, gain_ref[...].astype(BF16)))
    n1_t = right_product(turn, n1_ref[...]).astype(BF16)
    put(product(n1_t, dqkv_ref[...]))


def self_weights(source, n1, dqkv, dh1, gain_grads, a_pieces, spot):
    width = n1.shape[1]
    half = ((width // 2, width + LANES + dqkv.shape[1]), BF16)
    whole = lambda shape: pl.BlockSpec(shape, lambda i, spot: (0, 0))
    ins = [source, n1, dqkv, dh1, gain_grads, *a_pieces]
    return pl.pallas_call(
        self_weights_kernel,
        out_shape=shaped([half, half]),
        grid_spec=pltpu.PrefetchScalarGridSpec(
            num_scalar_prefetch=1,
            grid=(1,),
            in_specs=[whole(a.shape) for a in ins],
            out_specs=[whole(half[0])] * 2,
            scratch_shapes=[pltpu.VMEM((len(a_pieces),) + a_pieces[0].shape, BF16)],
        ),
        compiler_params=vmem(16),
        cost_estimate=cost(6),
        name="self_weights",
    )(spot, *ins)


def last_rows_kernel(keep_ref, one_ref, two_ref, x_ref, dh1_ref, gain_ref, out_ref):
    dn1 = keep_ref[0].astype(F32) + one_ref[0].astype(F32) + two_ref[...].astype(F32)
    x = x_ref[...].astype(F32)
    out_ref[...] = (
        dh1_ref[...] + norm_hidden_grad(x, norm_scale(x), gain_ref[0:1], dn1)
    ).astype(BF16)


def last_rows(keep, one, two, x, dh1, gains):
    return pl.pallas_call(
        last_rows_kernel,
        out_shape=jax.ShapeDtypeStruct(x.shape, BF16),
        compiler_params=vmem(8),
        cost_estimate=cost(2),
        name="last_rows",
    )(keep, one, two, x, dh1, gains)


def finish_kernel(slim, broad, spot_ref, *refs):
    sources, outs, hold = refs[:12], refs[12:-1], refs[-1]

    def total(refs, columns):
        keep, one, two = refs
        return (
            keep[0, :, columns[0] : columns[1]].astype(F32)
            + one[0, :, columns[0] : columns[1]].astype(F32)
            + two[0, :, columns[0] : columns[1]].astype(F32)
        )

    pair, down, cross, rest = sources[0:3], sources[3:6], sources[6:9], sources[9:12]
    hidden, width = outs[0].shape[1], outs[2].shape[1]
    outs[0][...] = total(pair, (0, hidden))
    outs[1][...] = total(pair, (hidden, 2 * hidden))
    outs[2][...] = total(down, (0, width))
    for i in range(4):
        outs[3 + i][...] = total(cross, (i * width, (i + 1) * width))
    outs[7][...] = total(rest, (0, width))
    edge = width
    outs[-1][...] = total(rest, (edge, edge + LANES))
    edge = edge + LANES
    far_edge = edge + 3 * broad
    keep, one, two = rest
    steps = [jnp.bitwise_xor(spot_ref[1], m) for m in seq_masks(lax.rem(spot_ref[0], 2))]
    hold[steps[0]] = keep[0, :, edge:far_edge].astype(F32)
    hold[steps[1]] = two[0, :, edge:far_edge].astype(F32)
    hold[steps[2]] = one[0, :, edge:far_edge].astype(F32)
    hold[steps[3]] = two[0, :, far_edge : far_edge + 3 * broad].astype(F32)
    for i in range(3):
        outs[8 + i][...] = jnp.concatenate(
            [hold[j][:, i * broad : i * broad + slim] for j in range(hold.shape[0])], axis=1
        )


def finish(pair, down, cross, rest, spot, hidden, slim, broad):
    share, feed_share, width = pair[0].shape[1], down[0].shape[1], down[0].shape[2]
    count = lax.axis_size("seq")
    shapes = (
        [(share, hidden)] * 2 + [(feed_share, width)] + [(share, width)] * 8 + [(share, LANES)]
    )
    whole = lambda shape: pl.BlockSpec(shape, lambda i, spot: (0,) * len(shape))
    flat = [*pair, *down, *cross, *rest]
    return pl.pallas_call(
        functools.partial(finish_kernel, slim, broad),
        out_shape=shaped([(shape, F32) for shape in shapes]),
        grid_spec=pltpu.PrefetchScalarGridSpec(
            num_scalar_prefetch=1,
            grid=(1,),
            in_specs=[whole(a.shape) for a in flat],
            out_specs=[whole(shape) for shape in shapes],
            scratch_shapes=[pltpu.VMEM((count, share, 3 * broad), F32)],
        ),
        compiler_params=vmem(12),
        cost_estimate=cost(3),
        name="finish",
    )(spot, *flat)


def local(
    hidden_in,
    memory,
    cotangent,
    norm_self,
    query_self,
    key_self,
    value_self,
    output_self,
    norm_cross,
    query_cross,
    key_cross,
    value_cross,
    output_cross,
    norm_feed,
    gate_weight,
    up_weight,
    down_weight,
    block_counts,
    memory_tail,
    row_example,
):
    mem_count, seq_count = lax.axis_size("mem"), lax.axis_size("seq")
    mem_place, seq_place = lax.axis_index("mem"), lax.axis_index("seq")
    rows, width = hidden_in.shape[1], hidden_in.shape[2]
    inner = HEADS * HEAD_DIM
    near = HEADS // seq_count
    slim = near * HEAD_DIM
    broad = -(-(slim + 8) // LANES) * LANES
    share = norm_self.shape[0]
    hidden_width = gate_weight.shape[1]
    spot = jnp.stack([mem_place, seq_place]).astype(jnp.int32)
    scalars = jnp.concatenate([block_counts, memory_tail, row_example])
    masks = slot_masks(mem_count)
    mask_array = mem_masks()
    block = width // mem_count
    column = jnp.arange(width, dtype=jnp.int32)
    source = block * (mem_place ^ jnp.repeat(mask_array, block)) + column % block
    source = (column[None, :] == source[:, None]).astype(BF16)
    gain_stack = jnp.stack([norm_self, norm_cross, norm_feed], axis=0)
    x_own = hidden_in[0]
    edge = 3 * broad
    turns = mem_count.bit_length() - 2
    flat = lambda stacked: stacked.reshape((1, -1) + stacked.shape[2:])

    with jax.named_scope("gather"):
        own, two, one, second, blocks, live = prepare(
            (query_self, key_self, value_self, output_self, query_cross)
            + (key_cross, value_cross, output_cross, gate_weight, up_weight),
            gain_stack, memory, (block_counts, memory_tail, row_example), spot, slim, broad,
        )
        live = live.reshape(-1, 1)
        stay, go = part_blocks(blocks, 0)
        two, arrived = swap_seq(two, 0), swap_mem(go, 0)
        c3 = cotangent[0]
        c3_other = swap_mem(c3, turns)
        blocks, x_in, down_in = join_blocks(stay, arrived), x_own, down_weight
        three = swap_seq(jnp.stack([one, two[:, edge:]]), 1)
        second_a = swap_seq(second, 0)
        for turn in range(1, turns):
            stay, go = part_blocks(blocks, turn)
            blocks = join_blocks(stay, swap_mem(go, turn))
        three, blocks, second_a, second, x_in, down_in, source = settle(
            three, blocks, second_a, second, x_in, down_in, source
        )
        plain = [(0, 0, 0, edge), (1, 0, edge, 5 * width)]
        skipping = [(0, 0, 0, edge), (1, 0, 2 * edge, 5 * width)]
        heads, outer = place(
            [own[None], two[None], three],
            seq_places(),
            [edge, 5 * width],
            [plain, skipping, plain],
        )
        heads, outer = [flat(heads)], [flat(outer)]
        heads.append(swap_mem(heads[0], 0))
        outer.append(swap_mem(outer[0], 0))
        stay, go = part_blocks(blocks, turns)
        keys_in = join_blocks(stay, swap_mem(go, turns)).reshape(-1, width)
        second_b = swap_seq(jnp.stack([second, second_a]), 1)
        heads, outer, keys_in, second_a, second_b, second, x_in, down_in = settle(
            heads, outer, keys_in, second_a, second_b, second, x_in, down_in
        )
        x_a = swap_seq(x_in, 0)
        for turn in range(1, turns):
            heads.append(swap_mem(join(heads), turn))
            outer.append(swap_mem(join(outer), turn))
        both = [flat(stack_seq([second[None], second_a[None], second_b]))]
        x_a, x_in, both, down_in = settle(x_a, x_in, both, down_in)
        x_b = swap_seq(jnp.stack([x_in, x_a]), 1)
        both.append(swap_mem(both[0], 0))
        down_a = swap_seq(down_in, 0)
        heads, outer, both, x_b, x_a, x_in, down_a, down_in = settle(
            heads, outer, both, x_b, x_a, x_in, down_a, down_in
        )
        heads, outer = join(heads), join(outer)
        heads = [heads, swap_mem(heads, turns)]
        outer = [outer, swap_mem(outer, turns)]
        for turn in range(1, turns):
            both.append(swap_mem(join(both), turn))
        down_b = swap_seq(jnp.stack([down_in, down_a]), 1)
        heads, x_in, x_a, x_b = settle(heads, x_in, x_a, x_b)
        packed_heads = spread_weight(heads)

    key_chunk = width

    with jax.named_scope("forward"):
        x_pieces = [x_in, x_a, x_b]
        o_pieces, n1, qkv, gains, self_logs = self_rows(
            x_pieces, packed_heads, spot, near, broad, masks
        )
        o_pieces, gains, outer, down_a, down_b, down_in = settle(
            o_pieces, gains, outer, down_a, down_b, down_in
        )
        packed = spread_weight(outer)
        downs = [flat(stack_seq([down_in[None], down_a[None], down_b]))]
        a_pieces = send_seq(o_pieces)
        kv2, keys_t = key_values(source, keys_in, packed, spot, key_chunk, 2 * width, masks)
        downs.append(swap_mem(downs[0], 0))
        a_pieces, kv2, downs, keys_in, both = settle(a_pieces, kv2, downs, keys_in, both)
        q2, a2_early, h1, logs_first = rows_first(
            a_pieces, packed, x_own, gains, live, kv2, spot, 0, masks
        )
        both = join(both)
        both_other = swap_mem(both, turns)
        for turn in range(1, turns):
            downs.append(swap_mem(join(downs), turn))
        others = [swap_mem(downs[0], turns), swap_mem(downs[1], turns)]
        a2_early, h1, q2, both, both_other, others = settle(
            a2_early, h1, q2, both, both_other, others
        )
        a2, h2, logs_second = rows_second(
            packed, h1, a2_early, live, q2, kv2, spot, 0, masks
        )
        h2, both_other, both, downs, others = settle(h2, both_other, both, downs, others)
        others += [swap_mem(piece, turns) for piece in downs[2:]]
        both = [w.reshape(-1, 2 * hidden_width) for w in (both, both_other)]
        unit = hidden_width // mem_count
        narrow = unit % LANES != 0
        if narrow:
            unit = 2 * LANES
            downs = [stack_mem(downs + others).reshape(-1, unit, width)]
            feed_order = jnp.arange(hidden_width // unit, dtype=jnp.int32)
        else:
            feed_order = mem_place ^ mask_array
            downs = downs + others
        layer_out, dh2, c2, gain_feed_terms, bundle, act_near, n3_near = feed(
            feed_order, h2, c3, gains, source, both, downs
        )

    with jax.named_scope("backward"):
        bundle_other = swap_mem(bundle, turns)
        up, dq_early, dk_early, dv_early = rows_early(
            packed, c2, live, logs_first, q2, kv2, spot, 0, masks
        )
        bundle_other, up, dq_early = settle(bundle_other, up, dq_early)
        if narrow:
            acts = jnp.concatenate([act_near, bundle[:, 2 * hidden_width : -(width // 2)]], axis=1)
            g_down = left_product(acts, c3).astype(BF16).reshape(mem_count, -1, width)
            g_down = place([g_down], jnp.argsort(mem_place ^ mask_array)).reshape(2, -1, width)
            normed = jnp.concatenate([n3_near, bundle[:, -(width // 2) :]], axis=1)
            g_both = jnp.stack(
                [
                    left_product(normed, bundle[:, k * hidden_width : (k + 1) * hidden_width])
                    for k in range(2)
                ]
            ).astype(BF16)
            feeding = Scatter(g_both[:, : width // 2], g_both[:, width // 2 :])
            downing = Scatter(g_down[0], g_down[1])
            for s in (feeding, downing):
                s.move()
            advance([feeding, downing], spot)
        else:
            g_feed = feed_weights(bundle, bundle_other, act_near, n3_near, c3, c3_other)
            feeding, downing = Scatter(*g_feed[0:2], 1), Scatter(*g_feed[2:4], 1)
        feeding.sent, up = settle(feeding.sent, up)
        feeding.move()
        da_pieces, dq2, dk_late, dv_late, dh1, gain_cross_terms = rows_late(
            packed, up, dq_early, dh2, h1, gains, live, logs_second, q2, kv2, spot, 0, masks
        )
        da_pieces, dq2 = settle(da_pieces, dq2)
        da_pieces = send_seq(da_pieces)
        *g_cross, dmem = cross_weights(
            packed, source, h1, gains, dq2, c2, a2, keys_t,
            [dk_early, dk_late, dv_early, dv_late], spot, key_chunk, 0, masks,
        )
        crossing = Scatter(*g_cross)
        advance([feeding], spot)
        da_pieces, crossing.sent, feeding.sent, downing.sent, dmem = settle(
            da_pieces, crossing.sent, feeding.sent, downing.sent, dmem
        )
        crossing.move()
        feeding.move()
        keep_dn, send_dn, dqkv, gain_self_terms = self_backward(
            da_pieces, x_pieces, packed_heads, qkv, self_logs, spot, near, masks
        )
        dmem = dmem.reshape(mem_count, -1, width)
        stay, go = part_blocks(dmem, turns)
        dmem = join_blocks(stay, swap_mem(go, turns))
        crossing.terms, feeding.terms, downing.sent, keep_dn, send_dn, dqkv, dmem = settle(
            crossing.terms, feeding.terms, downing.sent, keep_dn, send_dn, dqkv, dmem
        )
        one_dn = swap_seq(send_dn, 1)
        downing.move()
        stay, go = part_blocks(dmem, 0)
        dmem = join_blocks(stay, swap_mem(go, 0))
        while feeding.left > 0:
            advance([feeding], spot)
            feeding.move()
        ends = [advance([feeding], spot), None, None, None]
        advance([crossing], spot)
        gain_grads = jnp.concatenate(
            [gain_self_terms, gain_cross_terms, gain_feed_terms, jnp.zeros((LANES - 3, width), F32)]
        )
        g_self = self_weights(source, n1, dqkv, dh1, gain_grads, a_pieces, spot)
        selfing = Scatter(*g_self)
        crossing.move()
        one_dn, keep_dn, downing.terms, dmem, ends[0], selfing.sent = settle(
            one_dn, keep_dn, downing.terms, dmem, ends[0], selfing.sent
        )
        two_dn = swap_seq(onward(keep_dn, one_dn)[0], 0)
        one_both = swap_seq(ends[0][1], 1)
        selfing.move()
        for turn in range(1, turns):
            stay, go = part_blocks(dmem, turn)
            dmem = join_blocks(stay, swap_mem(go, turn))
        while downing.left > 0:
            advance([downing], spot)
            downing.move()
        ends[1] = advance([downing], spot)
        while crossing.left > 0:
            advance([crossing], spot)
            crossing.move()
        while selfing.left > 0:
            advance([selfing], spot)
            selfing.move()
        two_both = swap_seq(onward(ends[0][0], one_both), 0)
        mem_keep, mem_send = pick_slots(dmem, memory.shape[0], scalars, spot)
        mem_one = swap_seq(mem_send, 1)
        one_down = swap_seq(ends[1][1], 1)
        ends[2] = advance([crossing], spot)
        one_cross = swap_seq(ends[2][1], 1)
        mem_one = after(mem_one, ends[2][1])
        mem_two = swap_seq(onward(mem_keep, mem_one), 0)
        ends[3] = advance([selfing], spot)
        one_self = swap_seq(ends[3][1], 1)
        one_down = after(one_down, ends[2][1])
        two_down = swap_seq(onward(ends[1][0], one_down), 0)
        two_cross = swap_seq(onward(ends[2][0], one_cross), 0)
        two_self = swap_seq(onward(ends[3][0], one_self, width + LANES), 0)
        hidden_grad = last_rows(keep_dn, one_dn, after(two_dn, ends[3][1]), x_own, dh1, gains)
        per = mem_two.shape[0]
        memory_grad = total_of([mem_keep[:per], mem_one[:per], mem_two]).astype(BF16)
        *finals, gain_finals = finish(
            (ends[0][0], one_both, two_both),
            (ends[1][0], one_down, two_down),
            (ends[2][0], one_cross, two_cross),
            (ends[3][0], one_self, two_self),
            spot, hidden_width, slim, broad,
        )
    g_gate, g_up, g_down, g_q2, g_k2, g_v2, g_o2, g_o1, g_q1, g_k1, g_v1 = finals
    return (
        layer_out[None],
        hidden_grad[None],
        memory_grad,
        gain_finals[:, 0],
        g_q1,
        g_k1,
        g_v1,
        g_o1,
        gain_finals[:, 1],
        g_q2,
        g_k2,
        g_v2,
        g_o2,
        gain_finals[:, 2],
        g_gate,
        g_up,
        g_down,
    )


def solution(mesh):
    every = P(("mem", "seq"), None)
    gain = P(("mem", "seq"))
    in_specs = (
        (P("mem", "seq", None), P(None, "mem", None), P("mem", "seq", None), gain)
        + (every,) * 4
        + (gain,)
        + (every,) * 4
        + (gain,)
        + (every,) * 3
        + (P(),) * 3
    )
    out_specs = (
        (P("mem", "seq", None), P("mem", "seq", None), P("seq", "mem", None), gain)
        + (every,) * 4
        + (gain,)
        + (every,) * 4
        + (gain,)
        + (every,) * 3
    )
    return jax.shard_map(local, mesh=mesh, in_specs=in_specs, out_specs=out_specs, check_vma=False)
```
